32 devices in a mesh: dp: 4 (over y, core), fsdp: 8 (over z, x).
Axes of the slice: x: 2, y: 2, z: 4, core: 2. Of those that a mesh axis runs over, the one named last changes fastest.
Arguments:
- hidden: bfloat16 [4096, 2048], P(('dp', 'fsdp')), may hold values from -6 to 6
- source: bfloat16 [4096, 2048], P(('dp', 'fsdp')), may hold values from -6 to 6
- cotangent: bfloat16 [4096, 2048], P(('dp', 'fsdp')), may hold values from -6 to 6
- row_counts: int32 [4, 8], P('dp'), may hold values from 96 to 128, as said below
- seq_lengths: int32 [4, 3], P('dp'), may hold values from 1 to 990, as said below
- kv_gain: bfloat16 [2048], P(('dp', 'fsdp')), may hold values from 0.25 to 1.75
- w_key: bfloat16 [2048, 2048], P(('dp', 'fsdp')), may hold values from -0.125 to 0.125
- w_value: bfloat16 [2048, 2048], P(('dp', 'fsdp')), may hold values from -0.125 to 0.125
- attn_gain: bfloat16 [2048], P(('dp', 'fsdp')), may hold values from 0.25 to 1.75
- w_query: bfloat16 [2048, 2048], P(('dp', 'fsdp')), may hold values from -0.125 to 0.125
- w_out: bfloat16 [2048, 2048], P(('dp', 'fsdp')), may hold values from -0.75 to 0.75
- ffn_gain: bfloat16 [2048], P(('dp', 'fsdp')), may hold values from 0.25 to 1.75
- w_gate: bfloat16 [5504, 2048], P(('dp', 'fsdp')), may hold values from -0.125 to 0.125
- w_up: bfloat16 [5504, 2048], P(('dp', 'fsdp')), may hold values from -0.125 to 0.125
- w_down: bfloat16 [5504, 2048], P(('dp', 'fsdp')), may hold values from -0.078125 to 0.078125
Outputs:
- output: bfloat16 [4096, 2048], P(('dp', 'fsdp'))
- grad_hidden: bfloat16 [4096, 2048], P(('dp', 'fsdp'))
- grad_source: bfloat16 [4096, 2048], P(('dp', 'fsdp'))
- grad_kv_gain: float32 [2048], P(('dp', 'fsdp'))
- grad_key: float32 [2048, 2048], P(('dp', 'fsdp'))
- grad_value: float32 [2048, 2048], P(('dp', 'fsdp'))
- grad_attn_gain: float32 [2048], P(('dp', 'fsdp'))
- grad_query: float32 [2048, 2048], P(('dp', 'fsdp'))
- grad_out: float32 [2048, 2048], P(('dp', 'fsdp'))
- grad_ffn_gain: float32 [2048], P(('dp', 'fsdp'))
- grad_gate: float32 [5504, 2048], P(('dp', 'fsdp'))
- grad_up: float32 [5504, 2048], P(('dp', 'fsdp'))
- grad_down: float32 [5504, 2048], P(('dp', 'fsdp'))
The draws below stay inside these ranges and needn't reach their ends.
Inputs may be any that keep to these rules, and one draw needn't show every extreme that they name: `row_counts`: each device's live rows are its first ones, and a group's live rows follow one another device by device; in every group some device has 128 live rows. `seq_lengths`: the 3 sequences of a group are packed in order into its live rows; their lengths add up to the sum of the group's row_counts.
All inputs are finite; a program needn't handle non-finite values.
Results may differ from the reference program's by a relative error of at most 0.017.
Values may be sent and summed in bfloat16 or wider, within the bound.
No kernel may reach another device: no remote copies, remote signals or barrier semaphores. Data moves between devices by JAX's collectives and lax.ppermute only.
A program may use at most 704 MiB of HBM per device.

```python
import math
import jax
import jax.numpy as jnp
from jax import lax

D = 2048
HEADS = 16
FF = 5504
TOK_DEV = 128
SEQS = 3
TOKENS = 4096
N_DP = 4
N_FSDP = 8


def layout_draw(anchor):
    key_counts, key_full, key_empty, key_span, key_short, key_peak = jax.random.split(anchor, 6)
    least = TOK_DEV - TOK_DEV // 4
    counts = jax.random.randint(key_counts, (N_DP, N_FSDP), least, TOK_DEV + 1)
    fullest = jax.random.randint(key_full, (N_DP,), 0, N_FSDP)
    emptiest = (fullest + jax.random.randint(key_empty, (N_DP,), 1, N_FSDP)) % N_FSDP
    peak_group = jax.random.randint(key_peak, (), 0, N_DP)
    groups = jnp.arange(N_DP)[:, None]
    columns = jnp.arange(N_FSDP)[None, :]
    counts = jnp.where(columns == fullest[:, None], TOK_DEV, counts)
    counts = jnp.where(groups == peak_group, TOK_DEV, counts)
    counts = jnp.where(columns == emptiest[:, None], least, counts)
    spanning = jax.random.randint(key_span, (N_DP,), 0, SEQS)
    shorter = jax.random.randint(key_short, (N_DP, SEQS), 1, TOK_DEV // 4)
    shorter = jnp.where(groups == peak_group, 1, shorter)
    places = jnp.arange(SEQS)[None, :]
    is_long = places == spanning[:, None]
    remainder = jnp.sum(jnp.where(is_long, 0, shorter), axis=1)
    longest = jnp.sum(counts, axis=1) - remainder
    lengths = jnp.where(is_long, longest[:, None], shorter)
    return (counts.astype(jnp.int32), lengths.astype(jnp.int32))


def draw_row_counts(key, part):
    counts, lengths = layout_draw(key)
    return counts


def draw_seq_lengths(key, part):
    counts, lengths = layout_draw(key)
    return lengths


def block_levels(rng, extent, cuts, smallest, high):
    level = 1.0
    for dim, blocks in cuts:
        draws = jax.random.uniform(jax.random.fold_in(jax.random.fold_in(rng, 6), dim), (blocks,), jnp.float32, smallest / len(cuts), high / len(cuts))
        level = level * jnp.repeat(jnp.exp(draws), extent[dim] // blocks).reshape((-1,) + (1,) * (len(extent) - 1 - dim))
    return level


def centred(stream_key, shape, spread, limit, cuts=(), kind=jnp.bfloat16):
    drawn = jax.random.normal(stream_key, shape, jnp.float32) * spread
    if len(cuts) > 0:
        drawn = block_levels(stream_key, shape, cuts, -0.22, 0.18) * drawn
    return jnp.clip(drawn, min=-limit, max=limit).astype(kind)


def setup_inputs(seed: int = 0) -> dict:
    splits = jax.random.split(jax.random.key(seed), 16)
    return {
        "hidden": centred(splits[0], (TOKENS, D), 1.0, 6.0, ((0, 32),)),
        "source": centred(splits[1], (TOKENS, D), 1.0, 6.0, ((0, 32),)),
        "cotangent": centred(splits[2], (TOKENS, D), 1.0, 6.0, ((0, 32),)),
        "row_counts": draw_row_counts(jax.random.fold_in(splits[15], 71), 0),
        "seq_lengths": draw_seq_lengths(jax.random.fold_in(splits[15], 71), 0),
        "kv_gain": jnp.clip(1.0 + 0.15 * jax.random.normal(splits[5], (D,), jnp.float32), 0.25, 1.75).astype(jnp.bfloat16),
        "w_key": centred(splits[6], (D, D), D ** -0.5, 0.125, ((0, 32),)),
        "w_value": centred(splits[7], (D, D), D ** -0.5, 0.125, ((0, 32),)),
        "attn_gain": jnp.clip(1.0 + 0.15 * jax.random.normal(splits[8], (D,), jnp.float32), 0.25, 1.75).astype(jnp.bfloat16),
        "w_query": centred(splits[9], (D, D), D ** -0.5, 0.125, ((0, 32),)),
        "w_out": centred(splits[10], (D, D), (max(4, D * 32 // (TOK_DEV * N_FSDP))) ** -0.5, 0.75, ((0, 32),)),
        "ffn_gain": jnp.clip(1.0 + 0.15 * jax.random.normal(splits[11], (D,), jnp.float32), 0.25, 1.75).astype(jnp.bfloat16),
        "w_gate": centred(splits[12], (FF, D), D ** -0.5, 0.125, ((0, 32),)),
        "w_up": centred(splits[13], (FF, D), D ** -0.5, 0.125, ((0, 32),)),
        "w_down": centred(splits[14], (FF, D), FF ** -0.5, 0.078125, ((0, 32),)),
    }


EPSILON = 1e-06
MASKED = -1000000000.0
HIGHEST = lax.Precision.HIGHEST

@jax.custom_vjp
def low(v):
    return lax.optimization_barrier(v.astype(jnp.bfloat16)).astype(jnp.float32)

@jax.custom_vjp
def low_back(v):
    return v

def low_keep(v):
    return (low(v), None)

def low_pass(kept, grad):
    return (grad,)

def back_keep(v):
    return (v, None)

def back_low(kept, grad):
    return (low(grad),)
low.defvjp(low_keep, low_pass)
low_back.defvjp(back_keep, back_low)

def high_product(left, right):
    return jnp.dot(left, right, precision=HIGHEST, preferred_element_type=jnp.float32)

def normalize(values, gain):
    return values * lax.rsqrt(lax.optimization_barrier(jnp.mean(values * values, axis=-1, keepdims=True)) + EPSILON) * gain

def slot_layout(row_counts, seq_lengths):
    group_rows = TOK_DEV * N_FSDP
    slots = jnp.arange(group_rows, dtype=jnp.int32)
    device_of = slots // TOK_DEV
    within = slots - device_of * TOK_DEV
    picker = device_of[None, :, None] == jnp.arange(N_FSDP, dtype=jnp.int32)[None, None, :]
    offsets = jnp.cumsum(row_counts, axis=1, dtype=jnp.int32) - row_counts
    count_here = lax.optimization_barrier(jnp.sum(jnp.where(picker, row_counts[:, None, :], 0), axis=2, dtype=jnp.int32))
    offset_here = lax.optimization_barrier(jnp.sum(jnp.where(picker, offsets[:, None, :], 0), axis=2, dtype=jnp.int32))
    position = offset_here + within[None, :]
    ends = jnp.cumsum(seq_lengths, axis=1, dtype=jnp.int32)
    sequence = lax.optimization_barrier(jnp.sum((ends[:, None, :] <= position[:, :, None]).astype(jnp.int32), axis=2, dtype=jnp.int32))
    live = within[None, :] < count_here
    return (live.reshape(-1), position.reshape(-1), sequence.reshape(-1))

def attend_block(index, query_group, key_group, value_group, live_group, position_group, sequence_group):
    group_rows = TOK_DEV * N_FSDP
    block_rows = math.gcd(group_rows, 512)
    head_size = D // HEADS
    factor = 1.0 / math.sqrt(head_size)
    first_row = index * block_rows
    query_block = lax.dynamic_slice_in_dim(query_group, first_row, block_rows, 0)
    query_position = lax.dynamic_slice_in_dim(position_group, first_row, block_rows, 0)
    query_sequence = lax.dynamic_slice_in_dim(sequence_group, first_row, block_rows, 0)
    scores = jnp.einsum('qhd,khd->hqk', query_block, key_group, precision=HIGHEST) * factor
    scores = low_back(scores)
    allowed = live_group[None, :] & (sequence_group[None, :] == query_sequence[:, None]) & (position_group[None, :] <= query_position[:, None])
    masked = jnp.where(allowed[None], scores, MASKED)
    largest = lax.optimization_barrier(jnp.max(masked, axis=-1, keepdims=True))
    exponent = jnp.exp(masked - largest)
    probs = low(exponent / lax.optimization_barrier(jnp.sum(exponent, axis=-1, keepdims=True)))
    return jnp.einsum('hqk,khd->qhd', probs, value_group, precision=HIGHEST).reshape(block_rows, D)

def attention(queries, keys, values, live, position, sequence):
    group_rows = TOK_DEV * N_FSDP
    block_rows = math.gcd(group_rows, 512)
    head_size = D // HEADS
    checked = jax.checkpoint(attend_block)

    def one_group(operands):
        query_group, key_group, value_group, live_group, position_group, sequence_group = operands

        def one_block(index):
            return checked(index, query_group, key_group, value_group, live_group, position_group, sequence_group)
        blocks = lax.map(one_block, jnp.arange(group_rows // block_rows, dtype=jnp.int32))
        return blocks.reshape(group_rows, D)
    operands = (queries.reshape(N_DP, group_rows, HEADS, head_size), keys.reshape(N_DP, group_rows, HEADS, head_size), values.reshape(N_DP, group_rows, HEADS, head_size), live.reshape(N_DP, group_rows), position.reshape(N_DP, group_rows), sequence.reshape(N_DP, group_rows))
    return lax.map(one_group, operands).reshape(N_DP * group_rows, D)

def forward(live, position, sequence, hidden, source, kv_gain, w_key, w_value, attn_gain, w_query, w_out, ffn_gain, w_gate, w_up, w_down):
    source_normed = low(normalize(source, kv_gain))
    keys = low_back(low(high_product(source_normed, w_key)))
    values = low_back(low(high_product(source_normed, w_value)))
    hidden_normed = low(normalize(hidden, attn_gain))
    queries = low_back(low(high_product(hidden_normed, w_query)))
    attended = low_back(low(attention(queries, keys, values, live, position, sequence)))
    middle = hidden + low_back(high_product(attended, w_out))
    middle_normed = low(normalize(middle, ffn_gain))
    gate_value = low_back(high_product(middle_normed, w_gate.T))
    up_value = low_back(high_product(middle_normed, w_up.T))
    inner = low(jax.nn.silu(gate_value) * up_value)
    return (middle + high_product(inner, w_down)) * live.astype(jnp.float32)[:, None]

def reference(hidden, source, cotangent, row_counts, seq_lengths, kv_gain, w_key, w_value, attn_gain, w_query, w_out, ffn_gain, w_gate, w_up, w_down):
    live, position, sequence = slot_layout(row_counts, seq_lengths)
    params = tuple((argument.astype(jnp.float32) for argument in (hidden, source, kv_gain, w_key, w_value, attn_gain, w_query, w_out, ffn_gain, w_gate, w_up, w_down)))

    def run(*floats):
        return forward(live, position, sequence, *floats)
    result, pullback = jax.vjp(run, *params)
    grads = pullback(cotangent.astype(jnp.float32))
    return (result.astype(jnp.bfloat16), grads[0].astype(jnp.bfloat16), grads[1].astype(jnp.bfloat16), grads[2], grads[3], grads[4], grads[5], grads[6], grads[7], grads[8], grads[9], grads[10], grads[11])
```

```python
import functools
import math

import jax
import jax.numpy as jnp
from jax import lax
from jax.experimental import pallas as pl
from jax.experimental.pallas import tpu as pltpu
from jax.sharding import PartitionSpec as P

HEADS = 16


EPSILON = 1e-06
MASKED = -1000000000.0


def product(left, right):
    return jnp.dot(left, right, preferred_element_type=jnp.float32)


def rows_by_rows(left, right):
    return lax.dot_general(
        left, right, (((1,), (1,)), ((), ())), preferred_element_type=jnp.float32
    )


def columns_by_columns(left, right):
    return lax.dot_general(
        left, right, (((0,), (0,)), ((), ())), preferred_element_type=jnp.float32
    )


def inverse_scale(values):
    return lax.rsqrt(jnp.mean(values * values, axis=-1, keepdims=True) + EPSILON)


def norm_backward(values, scale, gain, d_normed):
    weighted = d_normed * gain
    return scale * weighted - values * scale**3 * jnp.mean(
        values * weighted, axis=-1, keepdims=True
    )


def slot_layout(row_counts, seq_lengths, slots, per_device):
    counts = row_counts[0]
    offsets = jnp.cumsum(counts) - counts
    device_of = slots // per_device
    within = slots - device_of * per_device
    picker = device_of[:, None] == jnp.arange(counts.shape[0], dtype=jnp.int32)[None, :]
    count_here = jnp.sum(jnp.where(picker, counts[None, :], 0), axis=1)
    offset_here = jnp.sum(jnp.where(picker, offsets[None, :], 0), axis=1)
    position = offset_here + within
    ends = jnp.cumsum(seq_lengths[0])
    sequence = jnp.sum((ends[None, :] <= position[:, None]).astype(jnp.int32), axis=1)
    return (within < count_here, position, sequence)


def body(
    hidden,
    source,
    cotangent,
    row_counts,
    seq_lengths,
    kv_gain,
    w_key,
    w_value,
    attn_gain,
    w_query,
    w_out,
    ffn_gain,
    w_gate,
    w_up,
    w_down,
):
    local_rows, model_width = hidden.shape
    group_rows = local_rows * lax.axis_size("fsdp")
    head_size = model_width // HEADS
    factor = 1.0 / math.sqrt(head_size)
    block_rows = math.gcd(group_rows, 512)
    block_count = group_rows // block_rows
    own_slots = lax.axis_index("fsdp") * local_rows + jnp.arange(local_rows, dtype=jnp.int32)
    query_live, query_position, query_sequence = slot_layout(
        row_counts, seq_lengths, own_slots, local_rows
    )
    key_live, key_position, key_sequence = slot_layout(
        row_counts, seq_lengths, jnp.arange(group_rows, dtype=jnp.int32), local_rows
    )
    live_column = query_live.astype(jnp.float32)[:, None]
    source_f = source.astype(jnp.float32)
    hidden_f = hidden.astype(jnp.float32)
    source_scale = inverse_scale(source_f)
    hidden_scale = inverse_scale(hidden_f)
    source_unit = source_f * source_scale
    hidden_unit = hidden_f * hidden_scale
    piece_kv_gain = lax.all_gather(kv_gain, ("dp", "fsdp"), axis=0, tiled=True)
    piece_key = lax.all_gather(w_key, ("dp", "fsdp"), axis=0, tiled=True)
    piece_value = lax.all_gather(w_value, ("dp", "fsdp"), axis=0, tiled=True)
    piece_attn_gain = lax.all_gather(attn_gain, ("dp", "fsdp"), axis=0, tiled=True)
    piece_query = lax.all_gather(w_query, ("dp", "fsdp"), axis=0, tiled=True)
    piece_ffn_gain = lax.all_gather(ffn_gain, ("dp", "fsdp"), axis=0, tiled=True)
    source_cols = (source_unit * piece_kv_gain.astype(jnp.float32)[None, :]).astype(jnp.bfloat16)
    hidden_cols = (hidden_unit * piece_attn_gain.astype(jnp.float32)[None, :]).astype(jnp.bfloat16)
    key_sum = product(source_cols, piece_key)
    value_sum = product(source_cols, piece_value)
    query_sum = product(hidden_cols, piece_query)
    stacked = jnp.stack([piece_kv_gain, piece_attn_gain, piece_ffn_gain]).astype(jnp.float32)
    gains = stacked
    key_sum, value_sum, query_sum, gains = (key_sum, value_sum, query_sum, gains)
    kv_gain_full, attn_gain_full, ffn_gain_full = (gains[0], gains[1], gains[2])
    keys_low = key_sum.astype(jnp.bfloat16)
    values_low = value_sum.astype(jnp.bfloat16)
    queries_low = query_sum.astype(jnp.bfloat16)
    group_keys, group_values = (
        lax.all_gather(keys_low, "fsdp", axis=0, tiled=True),
        lax.all_gather(values_low, "fsdp", axis=0, tiled=True),
    )
    blocks = (
        group_keys.reshape(block_count, block_rows, HEADS, head_size),
        group_values.reshape(block_count, block_rows, HEADS, head_size),
        key_live.reshape(block_count, block_rows),
        key_position.reshape(block_count, block_rows),
        key_sequence.reshape(block_count, block_rows),
    )
    query_heads = queries_low.reshape(local_rows, HEADS, head_size)

    def block_scores(key_block, live_block, position_block, sequence_block):
        scores = (
            jnp.einsum("qhd,khd->hqk", query_heads, key_block, preferred_element_type=jnp.float32)
            * factor
        )
        allowed = (
            live_block[None, :]
            & (sequence_block[None, :] == query_sequence[:, None])
            & (position_block[None, :] <= query_position[:, None])
        )
        return jnp.where(allowed[None], scores, MASKED)

    def running_total(running, key_block_set):
        largest, summed = running
        key_block, value_block, live_block, position_block, sequence_block = key_block_set
        masked = block_scores(key_block, live_block, position_block, sequence_block)
        new_largest = jnp.maximum(largest, jnp.max(masked, axis=-1))
        summed = summed * jnp.exp(largest - new_largest) + jnp.sum(
            jnp.exp(masked - new_largest[:, :, None]), axis=-1
        )
        return ((new_largest, summed), None)

    (largest, summed), unused = lax.scan(
        running_total,
        (
            jnp.full((HEADS, local_rows), MASKED, jnp.float32),
            jnp.zeros((HEADS, local_rows), jnp.float32),
        ),
        blocks,
    )
    log_total = largest + jnp.log(summed)

    def weighted_sum(running, key_block_set):
        key_block, value_block, live_block, position_block, sequence_block = key_block_set
        probs_low = jnp.exp(
            block_scores(key_block, live_block, position_block, sequence_block)
            - log_total[:, :, None]
        ).astype(jnp.bfloat16)
        return (
            running
            + jnp.einsum(
                "hqk,khd->qhd", probs_low, value_block, preferred_element_type=jnp.float32
            ),
            None,
        )

    attended_f, unused = lax.scan(
        weighted_sum, jnp.zeros((local_rows, HEADS, head_size), jnp.float32), blocks
    )
    attended_low = attended_f.reshape(local_rows, model_width).astype(jnp.bfloat16)
    branch = product(attended_low, lax.all_gather(w_out, ("dp", "fsdp"), axis=0, tiled=True))
    middle = hidden_f + branch
    middle_scale = inverse_scale(middle)
    middle_unit = middle * middle_scale
    middle_low = (middle_unit * ffn_gain_full).astype(jnp.bfloat16)
    piece_gate = lax.all_gather(w_gate, ("dp", "fsdp"), axis=0, tiled=True)
    piece_up = lax.all_gather(w_up, ("dp", "fsdp"), axis=0, tiled=True)
    piece_down = lax.all_gather(w_down, ("dp", "fsdp"), axis=0, tiled=True)
    gate_value = rows_by_rows(middle_low, piece_gate)
    up_value = rows_by_rows(middle_low, piece_up)
    inner = (jax.nn.silu(gate_value) * up_value).astype(jnp.bfloat16)
    ffn_result = product(inner, piece_down)
    output = ((middle + ffn_result) * live_column).astype(jnp.bfloat16)
    d_out = cotangent.astype(jnp.float32) * live_column
    d_out_low = d_out.astype(jnp.bfloat16)
    piece_gate = lax.all_gather(w_gate, ("dp", "fsdp"), axis=0, tiled=True)
    piece_up = lax.all_gather(w_up, ("dp", "fsdp"), axis=0, tiled=True)
    piece_down = lax.all_gather(w_down, ("dp", "fsdp"), axis=0, tiled=True)
    gate_value = rows_by_rows(middle_low, piece_gate)
    up_value = rows_by_rows(middle_low, piece_up)
    sigmoid_gate = jax.nn.sigmoid(gate_value)
    swished = gate_value * sigmoid_gate
    inner = (swished * up_value).astype(jnp.bfloat16)
    d_inner = rows_by_rows(d_out_low, piece_down)
    d_gate = (d_inner * up_value * sigmoid_gate * (1.0 + gate_value * (1.0 - sigmoid_gate))).astype(
        jnp.bfloat16
    )
    d_up = (d_inner * swished).astype(jnp.bfloat16)
    d_normed = product(d_gate, piece_gate) + product(d_up, piece_up)
    ffn_grads = lax.psum_scatter(
        jnp.stack(
            [
                columns_by_columns(d_gate, middle_low),
                columns_by_columns(d_up, middle_low),
                columns_by_columns(inner, d_out_low),
            ],
            axis=1,
        ),
        ("dp", "fsdp"),
        scatter_dimension=0,
        tiled=True,
    )
    ffn_gain_part = jnp.sum(d_normed * middle_unit, axis=0)
    d_middle = d_out + norm_backward(middle, middle_scale, ffn_gain_full, d_normed)
    d_branch_low = d_middle.astype(jnp.bfloat16)
    d_attended = rows_by_rows(
        d_branch_low, lax.all_gather(w_out, ("dp", "fsdp"), axis=0, tiled=True)
    )
    d_heads = d_attended.astype(jnp.bfloat16).reshape(local_rows, HEADS, head_size)
    delta = jnp.sum(d_heads.astype(jnp.float32) * attended_f, axis=-1).T

    def attention_backward(d_query_sum, key_block_set):
        key_block, value_block, live_block, position_block, sequence_block = key_block_set
        probs = jnp.exp(
            block_scores(key_block, live_block, position_block, sequence_block)
            - log_total[:, :, None]
        )
        probs_low = probs.astype(jnp.bfloat16)
        d_values = jnp.einsum(
            "hqk,qhd->khd", probs_low, d_heads, preferred_element_type=jnp.float32
        )
        d_probs = jnp.einsum(
            "qhd,khd->hqk", d_heads, value_block, preferred_element_type=jnp.float32
        )
        d_scores = (probs * (d_probs - delta[:, :, None])).astype(jnp.bfloat16)
        d_query_sum = d_query_sum + jnp.einsum(
            "hqk,khd->qhd", d_scores, key_block, preferred_element_type=jnp.float32
        )
        d_keys = (
            jnp.einsum("hqk,qhd->khd", d_scores, query_heads, preferred_element_type=jnp.float32)
            * factor
        )
        return (d_query_sum, jnp.stack([d_keys, d_values], axis=1))

    d_query_sum, key_terms = lax.scan(
        attention_backward, jnp.zeros((local_rows, HEADS, head_size), jnp.float32), blocks
    )
    key_grads = lax.psum_scatter(
        key_terms.reshape(group_rows, 2, model_width).astype(jnp.bfloat16),
        "fsdp",
        scatter_dimension=0,
        tiled=True,
    ).astype(jnp.float32)
    d_keys_low = key_grads[:, 0].astype(jnp.bfloat16)
    d_values_low = key_grads[:, 1].astype(jnp.bfloat16)
    d_queries_low = (d_query_sum * factor).reshape(local_rows, model_width).astype(jnp.bfloat16)
    piece_query = lax.all_gather(w_query, ("dp", "fsdp"), axis=0, tiled=True)
    piece_key = lax.all_gather(w_key, ("dp", "fsdp"), axis=0, tiled=True)
    piece_value = lax.all_gather(w_value, ("dp", "fsdp"), axis=0, tiled=True)
    hidden_part = rows_by_rows(d_queries_low, piece_query)
    source_part = rows_by_rows(d_keys_low, piece_key) + rows_by_rows(d_values_low, piece_value)
    input_back = jnp.stack([hidden_part, source_part])
    grad_hidden = (
        d_middle + norm_backward(hidden_f, hidden_scale, attn_gain_full, input_back[0])
    ).astype(jnp.bfloat16)
    grad_source = norm_backward(source_f, source_scale, kv_gain_full, input_back[1]).astype(
        jnp.bfloat16
    )
    attn_gain_part = jnp.sum(input_back[0] * hidden_unit, axis=0)
    kv_gain_part = jnp.sum(input_back[1] * source_unit, axis=0)
    source_low = (source_unit * kv_gain_full).astype(jnp.bfloat16)
    hidden_low = (hidden_unit * attn_gain_full).astype(jnp.bfloat16)
    hidden_part = hidden_low
    source_part = source_low
    layer_stack = lax.psum_scatter(
        jnp.stack(
            [
                columns_by_columns(hidden_part, d_queries_low),
                columns_by_columns(source_part, d_keys_low),
                columns_by_columns(source_part, d_values_low),
                columns_by_columns(attended_low, d_branch_low),
            ],
            axis=1,
        ),
        ("dp", "fsdp"),
        scatter_dimension=0,
        tiled=True,
    )
    grad_query, grad_key, grad_value, grad_out = (
        layer_stack[:, 0],
        layer_stack[:, 1],
        layer_stack[:, 2],
        layer_stack[:, 3],
    )
    grad_kv_gain, grad_attn_gain, grad_ffn_gain = (
        lax.psum_scatter(kv_gain_part, ("dp", "fsdp"), scatter_dimension=0, tiled=True),
        lax.psum_scatter(attn_gain_part, ("dp", "fsdp"), scatter_dimension=0, tiled=True),
        lax.psum_scatter(ffn_gain_part, ("dp", "fsdp"), scatter_dimension=0, tiled=True),
    )
    return (
        output,
        grad_hidden,
        grad_source,
        grad_kv_gain,
        grad_key,
        grad_value,
        grad_attn_gain,
        grad_query,
        grad_out,
        grad_ffn_gain,
        ffn_grads[:, 0],
        ffn_grads[:, 1],
        ffn_grads[:, 2],
    )


RING = (0, 1, 3, 2)
BLOCK = 256


def swap_pairs(size, mask):
    return [(place, place ^ mask) for place in range(size)]


def ring_pairs():
    return [
        (2 * RING[place] + x, 2 * RING[(place + 1) % 4] + x) for place in range(4) for x in range(2)
    ]


def x_swap(value):
    return lax.ppermute(value, "fsdp", swap_pairs(8, 1))


def ring_step(value):
    return lax.ppermute(value, "fsdp", ring_pairs())


def y_swap(value):
    return lax.ppermute(value, "dp", swap_pairs(4, 2))


def core_swap(value):
    return lax.ppermute(value, "dp", swap_pairs(4, 1))


def in_order(flag, first, second):
    swapped = flag == 1
    return jnp.concatenate(
        [jnp.where(swapped, second, first), jnp.where(swapped, first, second)], axis=0
    )


def gather_rows(own):
    pieces = []
    held = own
    for step in range(4):
        pieces.append((held, x_swap(held)))
        if step < 3:
            held = ring_step(held)
    return pieces


def scatter_rows(part):
    total = None
    for step in (1, 2, 3, 0):
        other = x_swap(part(step, 1).astype(jnp.bfloat16))
        here = part(step, 0) + other.astype(jnp.float32)
        if total is not None:
            here = here + ring_step(total).astype(jnp.float32)
        total = here.astype(jnp.bfloat16) if step else here
    return total


def attend_kernel(
    factor, q_ref, k_ref, v_ref, first_ref, last_ref, place_ref, att_ref, low_ref, lse_ref
):
    scores = rows_by_rows(q_ref[...], k_ref[...]) * factor
    places = place_ref[...]
    allowed = (places >= first_ref[...]) & (places <= last_ref[...])
    masked = jnp.where(allowed, scores, MASKED)
    largest = jnp.max(masked, axis=-1, keepdims=True)
    raised = jnp.exp(masked - largest)
    summed = jnp.sum(raised, axis=-1, keepdims=True)
    probs_low = (raised * (1.0 / summed)).astype(jnp.bfloat16)
    attended = product(probs_low, v_ref[...])
    att_ref[...] = attended
    low_ref[...] = attended.astype(jnp.bfloat16)
    lse_ref[...] = (largest + jnp.log(summed))[None]


def attend_back_kernel(
    factor,
    q_ref,
    k_ref,
    v_ref,
    first_ref,
    last_ref,
    place_ref,
    lse_ref,
    att_ref,
    d_att_ref,
    dq_ref,
    dk_ref,
    dv_ref,
    dk_sum,
    dv_sum,
):
    step = pl.program_id(1)

    @pl.when(step == 0)
    def _():
        dk_sum[...] = jnp.zeros_like(dk_sum)
        dv_sum[...] = jnp.zeros_like(dv_sum)

    queries = q_ref[...]
    keys = k_ref[...]
    d_att = d_att_ref[...]
    scores = rows_by_rows(queries, keys) * factor
    places = place_ref[...]
    allowed = (places >= first_ref[...]) & (places <= last_ref[...])
    probs = jnp.exp(jnp.where(allowed, scores, MASKED) - lse_ref[0])
    delta = jnp.sum(d_att.astype(jnp.float32) * att_ref[...], axis=-1, keepdims=True)
    d_probs = rows_by_rows(d_att, v_ref[...])
    d_scores = (probs * (d_probs - delta)).astype(jnp.bfloat16)
    dq_ref[...] = (product(d_scores, keys) * factor).astype(jnp.bfloat16)
    dk_sum[...] += columns_by_columns(d_scores, queries)
    dv_sum[...] += columns_by_columns(probs.astype(jnp.bfloat16), d_att)

    @pl.when(step == pl.num_programs(1) - 1)
    def _():
        dk_ref[...] = (dk_sum[...] * factor).astype(jnp.bfloat16)
        dv_ref[...] = dv_sum[...].astype(jnp.bfloat16)


def attend_specs(count, head):
    by_query = pl.BlockSpec((BLOCK, head), lambda h, i: (i, h))
    by_key = pl.BlockSpec((count, head), lambda h, i: (0, h))
    bound = pl.BlockSpec((BLOCK, 1), lambda h, i: (i, 0))
    place = pl.BlockSpec((1, count), lambda h, i: (0, 0))
    lse = pl.BlockSpec((1, BLOCK, 1), lambda h, i: (h, i, 0))
    return by_query, by_key, bound, place, lse


def attend(queries, keys, values, first, last, place, head):
    count, width = queries.shape
    by_query, by_key, bound, places, lse = attend_specs(count, head)
    return pl.pallas_call(
        functools.partial(attend_kernel, 1.0 / math.sqrt(head)),
        grid=(width // head, count // BLOCK),
        in_specs=[by_query, by_key, by_key, bound, bound, places],
        out_specs=[by_query, by_query, lse],
        out_shape=[
            jax.ShapeDtypeStruct((count, width), jnp.float32),
            jax.ShapeDtypeStruct((count, width), jnp.bfloat16),
            jax.ShapeDtypeStruct((width // head, count, 1), jnp.float32),
        ],
        compiler_params=pltpu.CompilerParams(vmem_limit_bytes=40 * 2**20),
        cost_estimate=pl.CostEstimate(
            flops=4 * count * count * width,
            bytes_accessed=12 * count * width,
            transcendentals=count * count * width // head,
        ),
        name="attend",
    )(queries, keys, values, first, last, place)


def attend_back(queries, keys, values, first, last, place, lse, attended, d_attended, head):
    count, width = queries.shape
    by_query, by_key, bound, places, by_lse = attend_specs(count, head)
    return pl.pallas_call(
        functools.partial(attend_back_kernel, 1.0 / math.sqrt(head)),
        grid=(width // head, count // BLOCK),
        in_specs=[
            by_query,
            by_key,
            by_key,
            bound,
            bound,
            places,
            by_lse,
            by_query,
            by_query,
        ],
        out_specs=[by_query, by_key, by_key],
        out_shape=[jax.ShapeDtypeStruct((count, width), jnp.bfloat16)] * 3,
        scratch_shapes=[pltpu.VMEM((count, head), jnp.float32)] * 2,
        compiler_params=pltpu.CompilerParams(vmem_limit_bytes=40 * 2**20),
        cost_estimate=pl.CostEstimate(
            flops=10 * count * count * width,
            bytes_accessed=18 * count * width,
            transcendentals=count * count * width // head,
        ),
        name="attend_back",
    )(queries, keys, values, first, last, place, lse, attended, d_attended)


def spread_gains(gains, me):
    held = gains
    for bit in (1, 2, 4, 8, 16):
        held = jnp.concatenate(
            [held, lax.ppermute(held, ("dp", "fsdp"), swap_pairs(32, bit))], axis=0
        )
    count = held.shape[0]
    owner = jnp.arange(count, dtype=jnp.int32)
    picker = (owner[None, :] == (owner[:, None] ^ me)).astype(held.dtype)
    return product(picker, held)


def sum_to_owners(total, me):
    for bit in (16, 8, 4, 2, 1):
        half = total.shape[0] // 2
        high = (me & bit) != 0
        kept = jnp.where(high, total[half:], total[:half])
        given = jnp.where(high, total[:half], total[half:])
        total = kept + lax.ppermute(given, ("dp", "fsdp"), swap_pairs(32, bit))
    return total


def projection_columns(stacked, z, x, dp):
    rows, width = stacked.shape
    each = rows // 3
    half = width // 2
    kept = lax.dynamic_slice(stacked, (0, half * x), (rows, half))
    given = lax.dynamic_slice(stacked, (0, half * (1 - x)), (rows, half))
    pair = in_order(x, kept, x_swap(given))
    head = half // 8

    def for_z(place):
        return jnp.concatenate(
            [
                lax.dynamic_slice(pair, (0, head * (4 * j) + head * place), (2 * rows, head))
                for j in range(2)
            ],
            axis=1,
        )

    held = [for_z(z)]
    for mask in (1, 2, 3):
        held.append(lax.ppermute(for_z(z ^ mask), "fsdp", swap_pairs(8, 2 * mask)))
    held = jnp.stack(held)
    held = jnp.concatenate(
        [lax.dynamic_index_in_dim(held, place ^ z, 0, keepdims=False) for place in range(4)], axis=0
    )
    both = jnp.stack([held, y_swap(held)])
    other = core_swap(both)
    held = jnp.stack([both[0], other[0], both[1], other[1]])
    held = held.reshape(4, 8, 3, each, 2 * head)
    out = []
    for which in range(3):
        out.append(
            jnp.concatenate(
                [
                    lax.dynamic_index_in_dim(held[:, :, which], place ^ dp, 0, keepdims=False)
                    for place in range(4)
                ],
                axis=0,
            ).reshape(32 * each, 2 * head)
        )
    return out


def projection_grads(grads, z, x, y, c):
    width, mine = grads[0].shape
    block = width // 4
    each = width // 32
    head = mine // 2

    def dp_rows(grad, place):
        return lax.dynamic_slice(grad, (block * place, 0), (block, mine))

    given = jnp.concatenate(
        [
            jnp.concatenate([dp_rows(grad, 2 * row + 1 - c) for row in range(2)], axis=0)
            for grad in grads
        ],
        axis=1,
    ).astype(jnp.bfloat16)
    from_core = core_swap(given)

    def summed(which, row):
        return dp_rows(grads[which], 2 * row + c) + lax.dynamic_slice(
            from_core, (block * row, mine * which), (block, mine)
        ).astype(jnp.float32)

    given = jnp.concatenate([summed(which, 1 - y) for which in range(3)], axis=1)
    got = y_swap(given.astype(jnp.bfloat16))
    total = jnp.concatenate([summed(which, y) for which in range(3)], axis=1)
    total = (total + got.astype(jnp.float32)).astype(jnp.bfloat16)

    def z_rows(place):
        return lax.dynamic_slice(total, (2 * each * place, 0), (2 * each, 3 * mine))

    held = [z_rows(z)]
    for mask in (1, 2, 3):
        held.append(lax.ppermute(z_rows(z ^ mask), "fsdp", swap_pairs(8, 2 * mask)))
    held = jnp.stack(held)
    held = jnp.stack(
        [lax.dynamic_index_in_dim(held, place ^ z, 0, keepdims=False) for place in range(4)]
    )
    kept = lax.dynamic_slice(held, (0, each * x, 0), (4, each, 3 * mine))
    given = lax.dynamic_slice(held, (0, each * (1 - x), 0), (4, each, 3 * mine))
    both = in_order(x, kept[None], x_swap(given)[None])
    out = []
    for which in range(3):
        out.append(
            jnp.concatenate(
                [
                    both[side, place, :, mine * which + head * j : mine * which + head * (j + 1)]
                    for side in range(2)
                    for j in range(2)
                    for place in range(4)
                ],
                axis=1,
            ).astype(jnp.float32)
        )
    return out


def out_rows(own, x, y, c):
    head = in_order(x, own, x_swap(own))
    pairs = [(place, place ^ 16) for place in range(32) if place // 16 == place % 2]
    got = lax.ppermute(head, ("dp", "fsdp"), pairs)
    mine = jnp.where(x == y, head, got)
    return in_order(c, mine, core_swap(mine))


def out_grads(grad, x, y, c):
    head = grad.shape[0] // 2
    width = grad.shape[1]
    kept = lax.dynamic_slice(grad, (head * c, 0), (head, width))
    given = lax.dynamic_slice(grad, (head * (1 - c), 0), (head, width))
    total = kept + core_swap(given.astype(jnp.bfloat16)).astype(jnp.float32)
    pairs = [(place, place ^ 16) for place in range(32) if place // 16 != place % 2]
    got = lax.ppermute(total.astype(jnp.bfloat16), ("dp", "fsdp"), pairs)
    total = total + got.astype(jnp.float32)
    each = head // 2
    kept = lax.dynamic_slice(total, (each * x, 0), (each, width))
    given = lax.dynamic_slice(total, (each * (1 - x), 0), (each, width))
    pairs = [(place, place ^ 1) for place in range(32) if place // 16 == place % 2]
    got = lax.ppermute(given.astype(jnp.bfloat16), ("dp", "fsdp"), pairs)
    return jnp.where(x == y, kept, got.astype(jnp.float32))


def hidden_units(own, padded):
    rows = jnp.pad(own, ((0, padded - own.shape[0]), (0, 0)))
    rows = jnp.concatenate([rows, y_swap(rows)], axis=0)
    return jnp.concatenate([rows, core_swap(rows)], axis=0)


def hidden_grads(units, rows, count):
    half = units.shape[1] // 2
    got = core_swap(columns_by_columns(units[:, half:], rows).astype(jnp.bfloat16))
    total = columns_by_columns(units[:, :half], rows) + got.astype(jnp.float32)
    quarter = half // 2
    got = y_swap(total[quarter:].astype(jnp.bfloat16))
    return (total[:quarter] + got.astype(jnp.float32))[:count]


def fast_body(
    hidden,
    source,
    cotangent,
    row_counts,
    seq_lengths,
    kv_gain,
    w_key,
    w_value,
    attn_gain,
    w_query,
    w_out,
    ffn_gain,
    w_gate,
    w_up,
    w_down,
):
    local_rows, width = hidden.shape
    head = width // HEADS
    dp = lax.axis_index("dp")
    fsdp = lax.axis_index("fsdp")
    y, c = dp // 2, dp % 2
    z, x = fsdp // 2, fsdp % 2
    me = 8 * dp + fsdp

    src_pieces = gather_rows(source)
    hid_pieces = gather_rows(hidden)
    wq, wk, wv = projection_columns(jnp.concatenate([w_query, w_key, w_value], axis=0), z, x, dp)
    w_kv = jnp.concatenate([wk, wv], axis=1)
    each = kv_gain.shape[0]
    spread = spread_gains(jnp.concatenate([kv_gain, attn_gain, ffn_gain])[None, :], me)
    kv_gain_full, attn_gain_full, ffn_gain_full = (
        spread[:, which * each : (which + 1) * each].reshape(1, width) for which in range(3)
    )

    order = z ^ (z >> 1)
    devices = []
    for step in range(4):
        place = (order - step) % 4
        for side in range(2):
            devices.append(2 * (place ^ (place >> 1)) + (x ^ side))
    slots = (
        jnp.stack(devices).astype(jnp.int32)[:, None] * local_rows
        + jnp.arange(local_rows, dtype=jnp.int32)[None, :]
    ).reshape(-1)
    live, position, sequence = slot_layout(row_counts, seq_lengths, slots, local_rows)
    starts = jnp.concatenate([jnp.zeros((1,), jnp.int32), jnp.cumsum(seq_lengths[0])])
    first = jnp.sum(
        jnp.where(
            sequence[:, None] == jnp.arange(starts.shape[0], dtype=jnp.int32)[None, :],
            starts[None, :],
            0,
        ),
        axis=1,
    )
    first, last = first[:, None], position[:, None]
    place_of_key = jnp.where(live, position, -1)[None, :]
    own_live = live[:local_rows].astype(jnp.float32)[:, None]

    def normed(values, gain):
        values = values.astype(jnp.float32)
        return (values * inverse_scale(values) * gain).astype(jnp.bfloat16)

    hid_low, src_low, queries, pairs = [], [], [], []
    for step in range(4):
        rows = normed(jnp.concatenate(src_pieces[step], axis=0), kv_gain_full)
        src_low.append(rows)
        pairs.append(product(rows, w_kv).astype(jnp.bfloat16))
        rows = normed(jnp.concatenate(hid_pieces[step], axis=0), attn_gain_full)
        hid_low.append(rows)
        queries.append(product(rows, wq).astype(jnp.bfloat16))
    hid_low = jnp.concatenate(hid_low, axis=0)
    src_low = jnp.concatenate(src_low, axis=0)
    queries = jnp.concatenate(queries, axis=0)
    pairs = jnp.concatenate(pairs, axis=0)
    keys, values = pairs[:, : 2 * head], pairs[:, 2 * head :]
    attended_f, attended_low, lse = attend(queries, keys, values, first, last, place_of_key, head)

    wo = out_rows(w_out, x, y, c)

    def rows_of(array, step, side):
        start = (2 * step + side) * local_rows
        return array[start : start + local_rows]

    branch = scatter_rows(lambda step, side: product(rows_of(attended_low, step, side), wo))
    hidden_f = hidden.astype(jnp.float32)
    middle = hidden_f + branch
    middle_scale = inverse_scale(middle)
    middle_unit = middle * middle_scale
    mid_pieces = gather_rows((middle_unit * ffn_gain_full).astype(jnp.bfloat16))

    d_out = cotangent.astype(jnp.float32) * own_live
    cot_pieces = gather_rows(d_out.astype(jnp.bfloat16))
    units = w_gate.shape[0]
    padded = -(-units // 64) * 64
    wg = hidden_units(w_gate, padded)
    wu = hidden_units(w_up, padded)
    wd = hidden_units(w_down, padded)

    mids, cots, inners, d_gates, d_ups = [], [], [], [], []
    for step in range(4):
        mid = jnp.concatenate(mid_pieces[step], axis=0)
        cot = jnp.concatenate(cot_pieces[step], axis=0)
        gate_value = rows_by_rows(mid, wg)
        up_value = rows_by_rows(mid, wu)
        sigmoid_gate = jax.nn.sigmoid(gate_value)
        swished = gate_value * sigmoid_gate
        d_inner = rows_by_rows(cot, wd)
        mids.append(mid)
        cots.append(cot)
        inners.append((swished * up_value).astype(jnp.bfloat16))
        d_gates.append(
            (d_inner * up_value * sigmoid_gate * (1.0 + gate_value * (1.0 - sigmoid_gate))).astype(
                jnp.bfloat16
            )
        )
        d_ups.append((d_inner * swished).astype(jnp.bfloat16))

    def side_of(array, side):
        return array[side * local_rows : (side + 1) * local_rows]

    d_normed = scatter_rows(
        lambda step, side: product(side_of(d_gates[step], side), wg)
        + product(side_of(d_ups[step], side), wu)
    )
    ffn_result = scatter_rows(lambda step, side: product(side_of(inners[step], side), wd))
    output = ((middle + ffn_result) * own_live).astype(jnp.bfloat16)

    d_middle = d_out + norm_backward(middle, middle_scale, ffn_gain_full, d_normed)
    d_branch_low = d_middle.astype(jnp.bfloat16)
    branch_pieces = gather_rows(d_branch_low)
    ffn_gain_part = jnp.sum(d_normed * middle_unit, axis=0)
    grad_ffn_gain = sum_to_owners(ffn_gain_part.reshape(32, each), me).reshape(each)

    mids = jnp.concatenate(mids, axis=0)
    cots = jnp.concatenate(cots, axis=0)
    grad_gate = hidden_grads(jnp.concatenate(d_gates, axis=0), mids, units)
    grad_up = hidden_grads(jnp.concatenate(d_ups, axis=0), mids, units)
    grad_down = hidden_grads(jnp.concatenate(inners, axis=0), cots, units)

    d_branches = [jnp.concatenate(pair, axis=0) for pair in branch_pieces]
    d_attended = jnp.concatenate(
        [rows_by_rows(rows, wo).astype(jnp.bfloat16) for rows in d_branches], axis=0
    )
    d_queries, d_keys, d_values = attend_back(
        queries, keys, values, first, last, place_of_key, lse, attended_f, d_attended, head
    )
    d_pairs = jnp.concatenate([d_keys, d_values], axis=1)
    d_src = scatter_rows(lambda step, side: rows_by_rows(rows_of(d_pairs, step, side), w_kv))
    d_hid = scatter_rows(lambda step, side: rows_by_rows(rows_of(d_queries, step, side), wq))

    grad_out = out_grads(
        columns_by_columns(attended_low, jnp.concatenate(d_branches, axis=0)), x, y, c
    )
    pair_grads = columns_by_columns(src_low, d_pairs)
    grad_query, grad_key, grad_value = projection_grads(
        [
            columns_by_columns(hid_low, d_queries),
            pair_grads[:, : 2 * head],
            pair_grads[:, 2 * head :],
        ],
        z,
        x,
        y,
        c,
    )
    grad_attn_gain = jnp.sum(w_query.astype(jnp.float32) * grad_query, axis=1)
    grad_attn_gain = grad_attn_gain / attn_gain.astype(jnp.float32)
    grad_kv_gain = jnp.sum(
        w_key.astype(jnp.float32) * grad_key + w_value.astype(jnp.float32) * grad_value, axis=1
    )
    grad_kv_gain = grad_kv_gain / kv_gain.astype(jnp.float32)

    grad_hidden = (
        d_middle + norm_backward(hidden_f, inverse_scale(hidden_f), attn_gain_full, d_hid)
    ).astype(jnp.bfloat16)
    source_f = source.astype(jnp.float32)
    grad_source = norm_backward(source_f, inverse_scale(source_f), kv_gain_full, d_src).astype(
        jnp.bfloat16
    )
    return (
        output,
        grad_hidden,
        grad_source,
        grad_kv_gain,
        grad_key,
        grad_value,
        grad_attn_gain,
        grad_query,
        grad_out,
        grad_ffn_gain,
        grad_gate,
        grad_up,
        grad_down,
    )


def solution(mesh):
    in_specs = (
        P(("dp", "fsdp"), None),
        P(("dp", "fsdp"), None),
        P(("dp", "fsdp"), None),
        P("dp", None),
        P("dp", None),
        P(("dp", "fsdp")),
        P(("dp", "fsdp"), None),
        P(("dp", "fsdp"), None),
        P(("dp", "fsdp")),
        P(("dp", "fsdp"), None),
        P(("dp", "fsdp"), None),
        P(("dp", "fsdp")),
        P(("dp", "fsdp"), None),
        P(("dp", "fsdp"), None),
        P(("dp", "fsdp"), None),
    )
    out_specs = (
        P(("dp", "fsdp"), None),
        P(("dp", "fsdp"), None),
        P(("dp", "fsdp"), None),
        P(("dp", "fsdp")),
        P(("dp", "fsdp"), None),
        P(("dp", "fsdp"), None),
        P(("dp", "fsdp")),
        P(("dp", "fsdp"), None),
        P(("dp", "fsdp"), None),
        P(("dp", "fsdp")),
        P(("dp", "fsdp"), None),
        P(("dp", "fsdp"), None),
        P(("dp", "fsdp"), None),
    )
    placed = (
        mesh.shape["dp"] == 4 and mesh.shape["fsdp"] == 8 and HEADS == 2 * mesh.shape["fsdp"]
    )
    chosen = fast_body if placed else body
    return jax.shard_map(chosen, mesh=mesh, in_specs=in_specs, out_specs=out_specs, check_vma=False)
```

```python
import functools
import math

import jax
import jax.numpy as jnp
from jax import lax
from jax.experimental import pallas as pl
from jax.experimental.pallas import tpu as pltpu
from jax.sharding import PartitionSpec as P

HEADS = 16


EPSILON = 1e-06
MASKED = -1000000000.0


def product(left, right):
    return jnp.dot(left, right, preferred_element_type=jnp.float32)


def rows_by_rows(left, right):
    return lax.dot_general(
        left, right, (((1,), (1,)), ((), ())), preferred_element_type=jnp.float32
    )


def columns_by_columns(left, right):
    return lax.dot_general(
        left, right, (((0,), (0,)), ((), ())), preferred_element_type=jnp.float32
    )


def inverse_scale(values):
    return lax.rsqrt(jnp.mean(values * values, axis=-1, keepdims=True) + EPSILON)


def norm_backward(values, scale, gain, d_normed):
    weighted = d_normed * gain
    return scale * weighted - values * scale**3 * jnp.mean(
        values * weighted, axis=-1, keepdims=True
    )


def slot_layout(row_counts, seq_lengths, slots, per_device):
    counts = row_counts[0]
    offsets = jnp.cumsum(counts) - counts
    device_of = slots // per_device
    within = slots - device_of * per_device
    picker = device_of[:, None] == jnp.arange(counts.shape[0], dtype=jnp.int32)[None, :]
    count_here = jnp.sum(jnp.where(picker, counts[None, :], 0), axis=1)
    offset_here = jnp.sum(jnp.where(picker, offsets[None, :], 0), axis=1)
    position = offset_here + within
    ends = jnp.cumsum(seq_lengths[0])
    sequence = jnp.sum((ends[None, :] <= position[:, None]).astype(jnp.int32), axis=1)
    return (within < count_here, position, sequence)


def body(
    hidden,
    source,
    cotangent,
    row_counts,
    seq_lengths,
    kv_gain,
    w_key,
    w_value,
    attn_gain,
    w_query,
    w_out,
    ffn_gain,
    w_gate,
    w_up,
    w_down,
):
    local_rows, model_width = hidden.shape
    group_rows = local_rows * lax.axis_size("fsdp")
    head_size = model_width // HEADS
    factor = 1.0 / math.sqrt(head_size)
    block_rows = math.gcd(group_rows, 512)
    block_count = group_rows // block_rows
    own_slots = lax.axis_index("fsdp") * local_rows + jnp.arange(local_rows, dtype=jnp.int32)
    query_live, query_position, query_sequence = slot_layout(
        row_counts, seq_lengths, own_slots, local_rows
    )
    key_live, key_position, key_sequence = slot_layout(
        row_counts, seq_lengths, jnp.arange(group_rows, dtype=jnp.int32), local_rows
    )
    live_column = query_live.astype(jnp.float32)[:, None]
    source_f = source.astype(jnp.float32)
    hidden_f = hidden.astype(jnp.float32)
    source_scale = inverse_scale(source_f)
    hidden_scale = inverse_scale(hidden_f)
    source_unit = source_f * source_scale
    hidden_unit = hidden_f * hidden_scale
    piece_kv_gain = lax.all_gather(kv_gain, ("dp", "fsdp"), axis=0, tiled=True)
    piece_key = lax.all_gather(w_key, ("dp", "fsdp"), axis=0, tiled=True)
    piece_value = lax.all_gather(w_value, ("dp", "fsdp"), axis=0, tiled=True)
    piece_attn_gain = lax.all_gather(attn_gain, ("dp", "fsdp"), axis=0, tiled=True)
    piece_query = lax.all_gather(w_query, ("dp", "fsdp"), axis=0, tiled=True)
    piece_ffn_gain = lax.all_gather(ffn_gain, ("dp", "fsdp"), axis=0, tiled=True)
    source_cols = (source_unit * piece_kv_gain.astype(jnp.float32)[None, :]).astype(jnp.bfloat16)
    hidden_cols = (hidden_unit * piece_attn_gain.astype(jnp.float32)[None, :]).astype(jnp.bfloat16)
    key_sum = product(source_cols, piece_key)
    value_sum = product(source_cols, piece_value)
    query_sum = product(hidden_cols, piece_query)
    stacked = jnp.stack([piece_kv_gain, piece_attn_gain, piece_ffn_gain]).astype(jnp.float32)
    gains = stacked
    key_sum, value_sum, query_sum, gains = (key_sum, value_sum, query_sum, gains)
    kv_gain_full, attn_gain_full, ffn_gain_full = (gains[0], gains[1], gains[2])
    keys_low = key_sum.astype(jnp.bfloat16)
    values_low = value_sum.astype(jnp.bfloat16)
    queries_low = query_sum.astype(jnp.bfloat16)
    group_keys, group_values = (
        lax.all_gather(keys_low, "fsdp", axis=0, tiled=True),
        lax.all_gather(values_low, "fsdp", axis=0, tiled=True),
    )
    blocks = (
        group_keys.reshape(block_count, block_rows, HEADS, head_size),
        group_values.reshape(block_count, block_rows, HEADS, head_size),
        key_live.reshape(block_count, block_rows),
        key_position.reshape(block_count, block_rows),
        key_sequence.reshape(block_count, block_rows),
    )
    query_heads = queries_low.reshape(local_rows, HEADS, head_size)

    def block_scores(key_block, live_block, position_block, sequence_block):
        scores = (
            jnp.einsum("qhd,khd->hqk", query_heads, key_block, preferred_element_type=jnp.float32)
            * factor
        )
        allowed = (
            live_block[None, :]
            & (sequence_block[None, :] == query_sequence[:, None])
            & (position_block[None, :] <= query_position[:, None])
        )
        return jnp.where(allowed[None], scores, MASKED)

    def running_total(running, key_block_set):
        largest, summed = running
        key_block, value_block, live_block, position_block, sequence_block = key_block_set
        masked = block_scores(key_block, live_block, position_block, sequence_block)
        new_largest = jnp.maximum(largest, jnp.max(masked, axis=-1))
        summed = summed * jnp.exp(largest - new_largest) + jnp.sum(
            jnp.exp(masked - new_largest[:, :, None]), axis=-1
        )
        return ((new_largest, summed), None)

    (largest, summed), unused = lax.scan(
        running_total,
        (
            jnp.full((HEADS, local_rows), MASKED, jnp.float32),
            jnp.zeros((HEADS, local_rows), jnp.float32),
        ),
        blocks,
    )
    log_total = largest + jnp.log(summed)

    def weighted_sum(running, key_block_set):
        key_block, value_block, live_block, position_block, sequence_block = key_block_set
        probs_low = jnp.exp(
            block_scores(key_block, live_block, position_block, sequence_block)
            - log_total[:, :, None]
        ).astype(jnp.bfloat16)
        return (
            running
            + jnp.einsum(
                "hqk,khd->qhd", probs_low, value_block, preferred_element_type=jnp.float32
            ),
            None,
        )

    attended_f, unused = lax.scan(
        weighted_sum, jnp.zeros((local_rows, HEADS, head_size), jnp.float32), blocks
    )
    attended_low = attended_f.reshape(local_rows, model_width).astype(jnp.bfloat16)
    branch = product(attended_low, lax.all_gather(w_out, ("dp", "fsdp"), axis=0, tiled=True))
    middle = hidden_f + branch
    middle_scale = inverse_scale(middle)
    middle_unit = middle * middle_scale
    middle_low = (middle_unit * ffn_gain_full).astype(jnp.bfloat16)
    piece_gate = lax.all_gather(w_gate, ("dp", "fsdp"), axis=0, tiled=True)
    piece_up = lax.all_gather(w_up, ("dp", "fsdp"), axis=0, tiled=True)
    piece_down = lax.all_gather(w_down, ("dp", "fsdp"), axis=0, tiled=True)
    gate_value = rows_by_rows(middle_low, piece_gate)
    up_value = rows_by_rows(middle_low, piece_up)
    inner = (jax.nn.silu(gate_value) * up_value).astype(jnp.bfloat16)
    ffn_result = product(inner, piece_down)
    output = ((middle + ffn_result) * live_column).astype(jnp.bfloat16)
    d_out = cotangent.astype(jnp.float32) * live_column
    d_out_low = d_out.astype(jnp.bfloat16)
    piece_gate = lax.all_gather(w_gate, ("dp", "fsdp"), axis=0, tiled=True)
    piece_up = lax.all_gather(w_up, ("dp", "fsdp"), axis=0, tiled=True)
    piece_down = lax.all_gather(w_down, ("dp", "fsdp"), axis=0, tiled=True)
    gate_value = rows_by_rows(middle_low, piece_gate)
    up_value = rows_by_rows(middle_low, piece_up)
    sigmoid_gate = jax.nn.sigmoid(gate_value)
    swished = gate_value * sigmoid_gate
    inner = (swished * up_value).astype(jnp.bfloat16)
    d_inner = rows_by_rows(d_out_low, piece_down)
    d_gate = (d_inner * up_value * sigmoid_gate * (1.0 + gate_value * (1.0 - sigmoid_gate))).astype(
        jnp.bfloat16
    )
    d_up = (d_inner * swished).astype(jnp.bfloat16)
    d_normed = product(d_gate, piece_gate) + product(d_up, piece_up)
    ffn_grads = lax.psum_scatter(
        jnp.stack(
            [
                columns_by_columns(d_gate, middle_low),
                columns_by_columns(d_up, middle_low),
                columns_by_columns(inner, d_out_low),
            ],
            axis=1,
        ),
        ("dp", "fsdp"),
        scatter_dimension=0,
        tiled=True,
    )
    ffn_gain_part = jnp.sum(d_normed * middle_unit, axis=0)
    d_middle = d_out + norm_backward(middle, middle_scale, ffn_gain_full, d_normed)
    d_branch_low = d_middle.astype(jnp.bfloat16)
    d_attended = rows_by_rows(
        d_branch_low, lax.all_gather(w_out, ("dp", "fsdp"), axis=0, tiled=True)
    )
    d_heads = d_attended.astype(jnp.bfloat16).reshape(local_rows, HEADS, head_size)
    delta = jnp.sum(d_heads.astype(jnp.float32) * attended_f, axis=-1).T

    def attention_backward(d_query_sum, key_block_set):
        key_block, value_block, live_block, position_block, sequence_block = key_block_set
        probs = jnp.exp(
            block_scores(key_block, live_block, position_block, sequence_block)
            - log_total[:, :, None]
        )
        probs_low = probs.astype(jnp.bfloat16)
        d_values = jnp.einsum(
            "hqk,qhd->khd", probs_low, d_heads, preferred_element_type=jnp.float32
        )
        d_probs = jnp.einsum(
            "qhd,khd->hqk", d_heads, value_block, preferred_element_type=jnp.float32
        )
        d_scores = (probs * (d_probs - delta[:, :, None])).astype(jnp.bfloat16)
        d_query_sum = d_query_sum + jnp.einsum(
            "hqk,khd->qhd", d_scores, key_block, preferred_element_type=jnp.float32
        )
        d_keys = (
            jnp.einsum("hqk,qhd->khd", d_scores, query_heads, preferred_element_type=jnp.float32)
            * factor
        )
        return (d_query_sum, jnp.stack([d_keys, d_values], axis=1))

    d_query_sum, key_terms = lax.scan(
        attention_backward, jnp.zeros((local_rows, HEADS, head_size), jnp.float32), blocks
    )
    key_grads = lax.psum_scatter(
        key_terms.reshape(group_rows, 2, model_width).astype(jnp.bfloat16),
        "fsdp",
        scatter_dimension=0,
        tiled=True,
    ).astype(jnp.float32)
    d_keys_low = key_grads[:, 0].astype(jnp.bfloat16)
    d_values_low = key_grads[:, 1].astype(jnp.bfloat16)
    d_queries_low = (d_query_sum * factor).reshape(local_rows, model_width).astype(jnp.bfloat16)
    piece_query = lax.all_gather(w_query, ("dp", "fsdp"), axis=0, tiled=True)
    piece_key = lax.all_gather(w_key, ("dp", "fsdp"), axis=0, tiled=True)
    piece_value = lax.all_gather(w_value, ("dp", "fsdp"), axis=0, tiled=True)
    hidden_part = rows_by_rows(d_queries_low, piece_query)
    source_part = rows_by_rows(d_keys_low, piece_key) + rows_by_rows(d_values_low, piece_value)
    input_back = jnp.stack([hidden_part, source_part])
    grad_hidden = (
        d_middle + norm_backward(hidden_f, hidden_scale, attn_gain_full, input_back[0])
    ).astype(jnp.bfloat16)
    grad_source = norm_backward(source_f, source_scale, kv_gain_full, input_back[1]).astype(
        jnp.bfloat16
    )
    attn_gain_part = jnp.sum(input_back[0] * hidden_unit, axis=0)
    kv_gain_part = jnp.sum(input_back[1] * source_unit, axis=0)
    source_low = (source_unit * kv_gain_full).astype(jnp.bfloat16)
    hidden_low = (hidden_unit * attn_gain_full).astype(jnp.bfloat16)
    hidden_part = hidden_low
    source_part = source_low
    layer_stack = lax.psum_scatter(
        jnp.stack(
            [
                columns_by_columns(hidden_part, d_queries_low),
                columns_by_columns(source_part, d_keys_low),
                columns_by_columns(source_part, d_values_low),
                columns_by_columns(attended_low, d_branch_low),
            ],
            axis=1,
        ),
        ("dp", "fsdp"),
        scatter_dimension=0,
        tiled=True,
    )
    grad_query, grad_key, grad_value, grad_out = (
        layer_stack[:, 0],
        layer_stack[:, 1],
        layer_stack[:, 2],
        layer_stack[:, 3],
    )
    grad_kv_gain, grad_attn_gain, grad_ffn_gain = (
        lax.psum_scatter(kv_gain_part, ("dp", "fsdp"), scatter_dimension=0, tiled=True),
        lax.psum_scatter(attn_gain_part, ("dp", "fsdp"), scatter_dimension=0, tiled=True),
        lax.psum_scatter(ffn_gain_part, ("dp", "fsdp"), scatter_dimension=0, tiled=True),
    )
    return (
        output,
        grad_hidden,
        grad_source,
        grad_kv_gain,
        grad_key,
        grad_value,
        grad_attn_gain,
        grad_query,
        grad_out,
        grad_ffn_gain,
        ffn_grads[:, 0],
        ffn_grads[:, 1],
        ffn_grads[:, 2],
    )


RING = (0, 1, 3, 2)
BLOCK = 256


def swap_pairs(size, mask):
    return [(place, place ^ mask) for place in range(size)]


def ring_pairs():
    return [
        (2 * RING[place] + x, 2 * RING[(place + 1) % 4] + x) for place in range(4) for x in range(2)
    ]


def x_swap(value):
    return lax.ppermute(value, "fsdp", swap_pairs(8, 1))


def ring_step(value):
    return lax.ppermute(value, "fsdp", ring_pairs())


def y_swap(value):
    return lax.ppermute(value, "dp", swap_pairs(4, 2))


def core_swap(value):
    return lax.ppermute(value, "dp", swap_pairs(4, 1))


def in_order(flag, first, second):
    swapped = flag == 1
    return jnp.concatenate(
        [jnp.where(swapped, second, first), jnp.where(swapped, first, second)], axis=0
    )


def after(value, *earlier):
    if not earlier:
        return value
    return lax.optimization_barrier((value, *earlier))[0]


class Gather:
    def __init__(self, own):
        self.held = own
        self.pieces = []

    def send(self):
        if len(self.pieces) < 3:
            return self.held, self.held
        half = self.held.shape[0] // 2
        return self.held[:half], self.pieces[2][1][half:]

    def take(self, from_x, from_ring):
        if len(self.pieces) < 3:
            self.pieces.append((self.held, from_x))
            self.held = from_ring
        else:
            self.pieces.append((self.held, from_x, from_ring))

    def piece(self, step):
        return jnp.concatenate(self.pieces[step], axis=0)


class Scatter:
    def __init__(self):
        self.kept = []
        self.got = None
        self.terms = None

    def of(self, terms):
        self.terms = terms
        return self

    def send(self):
        terms = self.terms
        rows = terms.shape[0] // 2
        half = rows // 2
        if not self.kept:
            self.kept.append(terms[:rows])
            return terms[rows : rows + half], terms[rows + half :]
        if len(self.kept) == 1:
            from_x, from_ring = self.got
            total = jnp.concatenate(
                [
                    self.kept[0][:half].astype(jnp.float32) + from_x.astype(jnp.float32),
                    self.kept[0][half:].astype(jnp.float32),
                ],
                axis=0,
            )
            given = jnp.concatenate(
                [
                    terms[rows : rows + half].astype(jnp.float32),
                    terms[rows + half :].astype(jnp.float32) + from_ring.astype(jnp.float32),
                ],
                axis=0,
            ).astype(jnp.bfloat16)
        else:
            total, given = self.total(), terms[rows:]
        self.kept.append(terms[:rows])
        return given, total.astype(jnp.bfloat16)

    def take(self, from_x, from_ring):
        self.got = (from_x, from_ring)

    def total(self):
        from_x, from_ring = self.got
        return (
            self.kept[-1].astype(jnp.float32)
            + from_x.astype(jnp.float32)
            + from_ring.astype(jnp.float32)
        )


def move(parts, *gate):
    sent = [part.send() for part in parts]
    along_x, along_ring = (
        values[0] if len(values) == 1 else jnp.concatenate(values, axis=0) for values in zip(*sent)
    )
    along_x, along_ring = after((along_x, along_ring), *gate)
    from_x, from_ring = x_swap(along_x), ring_step(along_ring)
    x_row = ring_row = 0
    for part, (given_x, given_ring) in zip(parts, sent):
        x_end, ring_end = x_row + given_x.shape[0], ring_row + given_ring.shape[0]
        part.take(from_x[x_row:x_end], from_ring[ring_row:ring_end])
        x_row, ring_row = x_end, ring_end
    return [from_x, from_ring]


def attend_kernel(
    factor, q_ref, k_ref, v_ref, first_ref, last_ref, place_ref, att_ref, low_ref, lse_ref
):
    scores = rows_by_rows(q_ref[...], k_ref[...]) * factor
    places = place_ref[...]
    allowed = (places >= first_ref[...]) & (places <= last_ref[...])
    masked = jnp.where(allowed, scores, MASKED)
    largest = jnp.max(masked, axis=-1, keepdims=True)
    raised = jnp.exp(masked - largest)
    summed = jnp.sum(raised, axis=-1, keepdims=True)
    probs_low = (raised * (1.0 / summed)).astype(jnp.bfloat16)
    attended = product(probs_low, v_ref[...])
    att_ref[...] = attended
    low_ref[...] = attended.astype(jnp.bfloat16)
    lse_ref[...] = (largest + jnp.log(summed))[None]


def attend_back_kernel(
    factor,
    q_ref,
    k_ref,
    v_ref,
    first_ref,
    last_ref,
    place_ref,
    lse_ref,
    att_ref,
    d_att_ref,
    dq_ref,
    dkv_ref,
    dk_sum,
    dv_sum,
):
    head = pl.program_id(0)
    step = pl.program_id(1)
    size = q_ref.shape[1]
    mine = dkv_ref.shape[1] // 2

    @pl.when(step == 0)
    def _():
        dk_sum[...] = jnp.zeros_like(dk_sum)
        dv_sum[...] = jnp.zeros_like(dv_sum)

    queries = q_ref[...]
    keys = k_ref[...]
    d_att = d_att_ref[...]
    scores = rows_by_rows(queries, keys) * factor
    places = place_ref[...]
    allowed = (places >= first_ref[...]) & (places <= last_ref[...])
    probs = jnp.exp(jnp.where(allowed, scores, MASKED) - lse_ref[0])
    delta = jnp.sum(d_att.astype(jnp.float32) * att_ref[...], axis=-1, keepdims=True)
    d_probs = rows_by_rows(d_att, v_ref[...])
    d_scores = (probs * (d_probs - delta)).astype(jnp.bfloat16)
    dq_ref[...] = (product(d_scores, keys) * factor).astype(jnp.bfloat16)
    dk_sum[...] += columns_by_columns(d_scores, queries)
    dv_sum[...] += columns_by_columns(probs.astype(jnp.bfloat16), d_att)

    @pl.when(step == pl.num_programs(1) - 1)
    def _():
        first = pl.multiple_of(size * head, size)
        dkv_ref[:, pl.ds(first, size)] = (dk_sum[...] * factor).astype(jnp.bfloat16)
        dkv_ref[:, pl.ds(mine + first, size)] = dv_sum[...].astype(jnp.bfloat16)


def attend_specs(count, head):
    by_query = pl.BlockSpec((BLOCK, head), lambda h, i: (i, h))
    keys = pl.BlockSpec((count, head), lambda h, i: (0, h))
    values = pl.BlockSpec((count, head), lambda h, i: (0, 2 + h))
    bound = pl.BlockSpec((BLOCK, 1), lambda h, i: (i, 0))
    place = pl.BlockSpec((1, count), lambda h, i: (0, 0))
    lse = pl.BlockSpec((1, BLOCK, 1), lambda h, i: (h, i, 0))
    return by_query, keys, values, bound, place, lse


def attend(queries, pairs, first, last, place, head):
    count, width = queries.shape
    by_query, keys, values, bound, places, lse = attend_specs(count, head)
    return pl.pallas_call(
        functools.partial(attend_kernel, 1.0 / math.sqrt(head)),
        grid=(width // head, count // BLOCK),
        in_specs=[by_query, keys, values, bound, bound, places],
        out_specs=[by_query, by_query, lse],
        out_shape=[
            jax.ShapeDtypeStruct((count, width), jnp.float32),
            jax.ShapeDtypeStruct((count, width), jnp.bfloat16),
            jax.ShapeDtypeStruct((width // head, count, 1), jnp.float32),
        ],
        compiler_params=pltpu.CompilerParams(vmem_limit_bytes=40 * 2**20),
        cost_estimate=pl.CostEstimate(
            flops=count * count, bytes_accessed=count * width, transcendentals=0
        ),
        name="attend",
    )(queries, pairs, pairs, first, last, place)


def attend_back(queries, pairs, first, last, place, lse, attended, d_attended, head):
    count, width = queries.shape
    by_query, keys, values, bound, places, by_lse = attend_specs(count, head)
    return pl.pallas_call(
        functools.partial(attend_back_kernel, 1.0 / math.sqrt(head)),
        grid=(width // head, count // BLOCK),
        in_specs=[
            by_query,
            keys,
            values,
            bound,
            bound,
            places,
            by_lse,
            by_query,
            by_query,
        ],
        out_specs=[by_query, pl.BlockSpec((count, 2 * width), lambda h, i: (0, 0))],
        out_shape=[
            jax.ShapeDtypeStruct((count, width), jnp.bfloat16),
            jax.ShapeDtypeStruct((count, 2 * width), jnp.bfloat16),
        ],
        scratch_shapes=[pltpu.VMEM((count, head), jnp.float32)] * 2,
        compiler_params=pltpu.CompilerParams(vmem_limit_bytes=40 * 2**20),
        cost_estimate=pl.CostEstimate(
            flops=count * count, bytes_accessed=count * width, transcendentals=0
        ),
        name="attend_back",
    )(queries, pairs, pairs, first, last, place, lse, attended, d_attended)


def as_rows(values, columns):
    rows = 8 * -(-values.shape[0] // (8 * columns))
    return jnp.pad(values, (0, rows * columns - values.shape[0])).reshape(rows, columns)


def from_rows(rows, count):
    return rows.reshape(-1)[:count]


def heads_of(device, head):
    z, x = device // 2, device % 2
    return [slice(head * (8 * x + 4 * j + z), head * (8 * x + 4 * j + z + 1)) for j in range(2)]


def columns_kernel(dp_ref, held_ref, q_ref, kv_ref, gain_ref):
    each = q_ref.shape[0] // 8
    mine = q_ref.shape[1]
    rows = held_ref.shape[2] // 8
    for device in range(8):
        first = rows * device
        here = slice(each * device, each * (device + 1))
        q_ref[here, :] = held_ref[0, 0, first : first + each, :]
        kv_ref[here, :mine] = held_ref[0, 0, first + each : first + 2 * each, :]
        kv_ref[here, mine:] = held_ref[0, 0, first + 2 * each : first + 3 * each, :]
        extra = rows - 3 * each
        gain_ref[0, extra * device : extra * (device + 1), :] = held_ref[
            0, 0, first + 3 * each : first + rows, :
        ]


def payload_kernel(q_ref, k_ref, v_ref, gain_ref, out_ref):
    each = q_ref.shape[0]
    head = q_ref.shape[1] // 16
    rows = out_ref.shape[0] // 8
    for device in range(8):
        for which, w_ref in enumerate((q_ref, k_ref, v_ref)):
            first = rows * device + each * which
            for j, columns in enumerate(heads_of(device, head)):
                out_ref[first : first + each, head * j : head * (j + 1)] = w_ref[:, columns]
        out_ref[rows * device + 3 * each : rows * (device + 1), :] = gain_ref[...]


class Columns:
    def __init__(self, weights, gains, dp):
        self.weights, self.gains, self.dp = weights, gains, dp

    def along_fsdp(self, *gate):
        each, width = self.weights[0].shape
        extra = as_rows(self.gains, width // 8)
        given = pl.pallas_call(
            payload_kernel,
            out_shape=jax.ShapeDtypeStruct(
                (8 * (3 * each + extra.shape[0]), width // 8), self.weights[0].dtype
            ),
            compiler_params=pltpu.CompilerParams(vmem_limit_bytes=16 * 2**20),
            cost_estimate=pl.CostEstimate(flops=0, bytes_accessed=2**20, transcendentals=0),
            name="payload",
        )(*self.weights, extra)
        self.held = lax.all_to_all(after(given, *gate), "fsdp", 0, 0, tiled=True)
        return [self.held]

    def along_y(self, *gate):
        held = after(self.held, *gate)
        got, other = y_swap(held), core_swap(held)
        self.held = [held, got, other]
        return [got, other]

    def along_core(self, *gate):
        held, got, other = after(tuple(self.held), *gate)
        last = core_swap(got)
        self.held = jnp.stack([held, got, other, last]).reshape(2, 2, *held.shape)
        return [last]

    def whole(self):
        each, width = self.weights[0].shape
        rows, mine = self.held.shape[2:]
        extra = rows - 24 * each
        block = 8 * each
        low = self.held.dtype
        wq, w_kv, gains = pl.pallas_call(
            columns_kernel,
            grid_spec=pltpu.PrefetchScalarGridSpec(
                num_scalar_prefetch=1,
                grid=(4,),
                in_specs=[
                    pl.BlockSpec(
                        (1, 1, rows, mine),
                        lambda i, dp: ((dp[0] ^ i) % 2, (dp[0] ^ i) // 2, 0, 0),
                    )
                ],
                out_specs=[
                    pl.BlockSpec((block, mine), lambda i, dp: (i, 0)),
                    pl.BlockSpec((block, 2 * mine), lambda i, dp: (i, 0)),
                    pl.BlockSpec((1, extra, mine), lambda i, dp: (i, 0, 0)),
                ],
            ),
            out_shape=[
                jax.ShapeDtypeStruct((4 * block, mine), low),
                jax.ShapeDtypeStruct((4 * block, 2 * mine), low),
                jax.ShapeDtypeStruct((4, extra, mine), low),
            ],
            compiler_params=pltpu.CompilerParams(vmem_limit_bytes=32 * 2**20),
            cost_estimate=pl.CostEstimate(flops=0, bytes_accessed=2**20, transcendentals=0),
            name="columns",
        )(self.dp.reshape(1).astype(jnp.int32), self.held)
        gains = gains.reshape(32, -1)[:, : self.gains.shape[0]].astype(jnp.float32)
        return wq, w_kv, gains


def column_grads_kernel(dp_ref, *refs):
    sources, hiddens = refs[:4], refs[4:8]
    dq_ref, dkv_ref, given_ref, kept_ref = refs[8:]
    count = sources[0].shape[0]
    mine = dq_ref.shape[1]
    for_q, for_kv = 0.0, 0.0
    for step in range(4):
        here = slice(count * step, count * (step + 1))
        for_q = for_q + columns_by_columns(hiddens[step][...], dq_ref[here, :])
        for_kv = for_kv + columns_by_columns(sources[step][...], dkv_ref[here, :])

    @pl.when(pl.program_id(0) < 2)
    def _():
        given_ref[0, :, :mine] = for_q.astype(jnp.bfloat16)
        given_ref[0, :, mine:] = for_kv.astype(jnp.bfloat16)

    @pl.when(pl.program_id(0) >= 2)
    def _():
        kept_ref[0, :, :mine] = for_q
        kept_ref[0, :, mine:] = for_kv


def own_grads_kernel(got_ref, wq_ref, wk_ref, wv_ref, q_ref, k_ref, v_ref, q_sum_ref, kv_sum_ref):
    each = wq_ref.shape[0]
    head = wq_ref.shape[1] // 16
    sums = []
    for which, (w_ref, out_ref) in enumerate(((wq_ref, q_ref), (wk_ref, k_ref), (wv_ref, v_ref))):
        total = jnp.zeros((each, head), jnp.float32)
        for device in range(8):
            for j, columns in enumerate(heads_of(device, head)):
                first = head * (2 * which + j)
                grad = got_ref[device, :each, first : first + head].astype(jnp.float32)
                out_ref[:, columns] = grad
                total = total + grad * w_ref[:, columns].astype(jnp.float32)
        sums.append(jnp.sum(total, axis=1, keepdims=True))
    q_sum_ref[...] = sums[0]
    kv_sum_ref[...] = sums[1] + sums[2]


FREE = pl.CostEstimate(flops=0, bytes_accessed=0, transcendentals=0)


def whole_block(array):
    return pl.BlockSpec(array.shape, lambda *place: (0,) * array.ndim)


def project_kernel(held_ref, *refs):
    others = refs[:-8]
    kv_gain_ref, attn_gain_ref, w_kv_ref, wq_ref, src_ref, hid_ref, pair_ref, query_ref = refs[-8:]
    rows = src_ref.shape[0] // 2

    def other_rows(which):
        if len(others) == 1:
            return others[0][rows * which : rows * (which + 1), :]
        return others[which][...]

    for which, gain_ref, w_ref, low_ref, out_ref in (
        (0, kv_gain_ref, w_kv_ref, src_ref, pair_ref),
        (1, attn_gain_ref, wq_ref, hid_ref, query_ref),
    ):
        for side in range(2):
            here = slice(rows * side, rows * (side + 1))
            values = other_rows(which) if side else held_ref[rows * which : rows * (which + 1), :]
            values = values.astype(jnp.float32)
            low_ref[here, :] = (values * inverse_scale(values) * gain_ref[...]).astype(jnp.bfloat16)
        out_ref[...] = product(low_ref[...], w_ref[...]).astype(jnp.bfloat16)


def project(piece, kv_gain, attn_gain, w_kv, wq):
    rows, width = piece[0].shape
    low = piece[0].dtype
    return pl.pallas_call(
        project_kernel,
        out_shape=[
            jax.ShapeDtypeStruct((rows, width), low),
            jax.ShapeDtypeStruct((rows, width), low),
            jax.ShapeDtypeStruct((rows, w_kv.shape[1]), low),
            jax.ShapeDtypeStruct((rows, wq.shape[1]), low),
        ],
        compiler_params=pltpu.CompilerParams(vmem_limit_bytes=40 * 2**20),
        cost_estimate=FREE,
        name="project",
    )(*piece, kv_gain, attn_gain, w_kv, wq)


def input_terms_kernel(pair_ref, query_ref, w_kv_ref, wq_ref, src_ref, hid_ref):
    src_ref[...] = rows_by_rows(pair_ref[...], w_kv_ref[...]).astype(jnp.bfloat16)
    hid_ref[...] = rows_by_rows(query_ref[...], wq_ref[...]).astype(jnp.bfloat16)


def input_terms(step, d_pairs, d_queries, w_kv, wq):
    rows, width = d_pairs.shape[0] // 4, w_kv.shape[0]
    out = jax.ShapeDtypeStruct((rows, width), jnp.bfloat16)
    out_spec = pl.BlockSpec((rows, width), lambda i: (0, 0))
    return pl.pallas_call(
        input_terms_kernel,
        grid=(1,),
        in_specs=[
            pl.BlockSpec((rows, d_pairs.shape[1]), lambda i: (step, 0)),
            pl.BlockSpec((rows, d_queries.shape[1]), lambda i: (step, 0)),
            whole_block(w_kv),
            whole_block(wq),
        ],
        out_specs=[out_spec, out_spec],
        out_shape=[out, out],
        compiler_params=pltpu.CompilerParams(vmem_limit_bytes=40 * 2**20),
        cost_estimate=FREE,
        name="input_terms",
    )(d_pairs, d_queries, w_kv, wq)


def add_kernel(*refs):
    count = len(refs) // 3
    for kept_ref, got_ref, out_ref in zip(refs[:count], refs[count : 2 * count], refs[2 * count :]):
        rows = out_ref.shape[0]
        out_ref[...] = kept_ref[:rows, :] + got_ref[:rows, :].astype(jnp.float32)


def add_all(kept, got, rows):
    width = kept[0].shape[1]
    block = width // 4
    count = len(kept)
    spec = pl.BlockSpec((kept[0].shape[0], block), lambda i: (0, i))
    return pl.pallas_call(
        add_kernel,
        grid=(4,),
        in_specs=[spec] * (2 * count),
        out_specs=[pl.BlockSpec((rows, block), lambda i: (0, i))] * count,
        out_shape=[jax.ShapeDtypeStruct((rows, width), jnp.float32)] * count,
        compiler_params=pltpu.CompilerParams(vmem_limit_bytes=40 * 2**20),
        cost_estimate=FREE,
        name="add_all",
    )(*kept, *got)


def copy_kernel(dp_ref, in_ref, out_ref):
    out_ref[...] = in_ref[...]


def own_first(rows, dp):
    block = (rows.shape[0] // 4, rows.shape[1])
    return pl.pallas_call(
        copy_kernel,
        grid_spec=pltpu.PrefetchScalarGridSpec(
            num_scalar_prefetch=1,
            grid=(4,),
            in_specs=[pl.BlockSpec(block, lambda i, dp: (dp[0] ^ (2 * (i % 2) + i // 2), 0))],
            out_specs=pl.BlockSpec(block, lambda i, dp: (i, 0)),
        ),
        out_shape=jax.ShapeDtypeStruct(rows.shape, rows.dtype),
        compiler_params=pltpu.CompilerParams(vmem_limit_bytes=16 * 2**20),
        cost_estimate=FREE,
        name="own_first",
    )(dp.reshape(1).astype(jnp.int32), rows)


class ColumnGrads:
    def __init__(self, dp):
        self.dp = dp
        self.y, self.c = dp // 2, dp % 2

    def gain_core(self, gain, *gate):
        gain = gain.reshape(2, 2, -1)
        kept = lax.dynamic_index_in_dim(gain, self.c, 1, keepdims=False)
        given = lax.dynamic_index_in_dim(gain, 1 - self.c, 1, keepdims=False)
        self.gain = kept + core_swap(after(given, *gate))
        return [given]

    def gain_y(self, *gate):
        gain = after(self.gain, *gate)
        kept = lax.dynamic_index_in_dim(gain, self.y, 0, keepdims=False)
        given = lax.dynamic_index_in_dim(gain, 1 - self.y, 0, keepdims=False)
        self.gain = kept + y_swap(given)
        return [given]

    def along_core(self, sources, hiddens, d_queries, d_pairs):
        count, width = sources[0].shape
        block = width // 4
        mine = d_queries.shape[1]
        rows = d_queries.shape[0]

        def of_step(i):
            return 2 * (i % 2) + 1 - i // 2

        by_block = pl.BlockSpec((count, block), lambda i, dp: (0, dp[0] ^ of_step(i)))
        given, self.kept = pl.pallas_call(
            column_grads_kernel,
            grid_spec=pltpu.PrefetchScalarGridSpec(
                num_scalar_prefetch=1,
                grid=(4,),
                in_specs=[by_block] * 8
                + [
                    pl.BlockSpec((rows, mine), lambda i, dp: (0, 0)),
                    pl.BlockSpec((rows, 2 * mine), lambda i, dp: (0, 0)),
                ],
                out_specs=[
                    pl.BlockSpec((1, block, 3 * mine), lambda i, dp: (jnp.minimum(i, 1), 0, 0)),
                    pl.BlockSpec((1, block, 3 * mine), lambda i, dp: (jnp.maximum(i, 2) - 2, 0, 0)),
                ],
            ),
            out_shape=[
                jax.ShapeDtypeStruct((2, block, 3 * mine), jnp.bfloat16),
                jax.ShapeDtypeStruct((2, block, 3 * mine), jnp.float32),
            ],
            compiler_params=pltpu.CompilerParams(vmem_limit_bytes=40 * 2**20),
            cost_estimate=pl.CostEstimate(
                flops=rows * width, bytes_accessed=2**20, transcendentals=0
            ),
            name="column_grads",
        )(self.dp.reshape(1).astype(jnp.int32), *sources, *hiddens, d_queries, d_pairs)
        self.from_core = core_swap(given)
        return [given]

    def along_y(self, *gate):
        given = self.kept[1] + after(self.from_core, *gate)[1].astype(jnp.float32)
        given = given.astype(jnp.bfloat16)
        self.from_y = y_swap(given)
        return [given]

    def along_fsdp(self, *gate):
        total = self.kept[0] + self.from_core[0].astype(jnp.float32)
        total = (total + after(self.from_y, *gate).astype(jnp.float32)).astype(jnp.bfloat16)
        each, columns = total.shape[0] // 8, total.shape[1]
        gain = self.gain.astype(jnp.bfloat16).reshape(8, 1, each)
        gain = jnp.pad(gain, ((0, 0), (0, 7), (0, columns - each)))
        given = jnp.concatenate([total.reshape(8, each, columns), gain], axis=1)
        self.got = lax.all_to_all(given, "fsdp", 0, 0, tiled=True)
        return [given], [self.got]

    def whole(self, weights, *gate):
        each, width = weights[0].shape
        got = after(self.got, *gate)
        flat = jax.ShapeDtypeStruct((each, width), jnp.float32)
        column = jax.ShapeDtypeStruct((each, 1), jnp.float32)
        out = pl.pallas_call(
            own_grads_kernel,
            out_shape=[flat, flat, flat, column, column],
            compiler_params=pltpu.CompilerParams(vmem_limit_bytes=32 * 2**20),
            cost_estimate=pl.CostEstimate(flops=0, bytes_accessed=2**20, transcendentals=0),
            name="own_grads",
        )(got, *weights)
        gain = jnp.sum(got[:, each, :each].astype(jnp.float32), axis=0)
        return out, gain


def out_rows(own, x, y, c, before, late):
    head = in_order(x, own, x_swap(own))
    pairs = [(place, place ^ 16) for place in range(32) if place // 16 == place % 2]
    got = lax.ppermute(after(head, *before), ("dp", "fsdp"), pairs)
    mine = jnp.where(x == y, head, after(got, *late))
    return in_order(c, mine, core_swap(mine))


class OutGrads:
    def __init__(self, grad, x, y, c):
        self.grad, self.x, self.y, self.c = grad, x, y, c

    def along_core(self, *gate):
        head, width = self.grad.shape[0] // 2, self.grad.shape[1]
        kept = lax.dynamic_slice(self.grad, (head * self.c, 0), (head, width))
        given = lax.dynamic_slice(self.grad, (head * (1 - self.c), 0), (head, width))
        given = after(given.astype(jnp.bfloat16), *gate)
        self.total = kept + core_swap(given).astype(jnp.float32)
        return [given]

    def along_y(self, *gate):
        pairs = [(place, place ^ 16) for place in range(32) if place // 16 != place % 2]
        given = after(self.total.astype(jnp.bfloat16), *gate)
        self.from_y = lax.ppermute(given, ("dp", "fsdp"), pairs)
        return [given]

    def along_x(self, *gate):
        total = self.total + after(self.from_y, *gate).astype(jnp.float32)
        each, width = total.shape[0] // 2, total.shape[1]
        self.kept = lax.dynamic_slice(total, (each * self.x, 0), (each, width))
        given = lax.dynamic_slice(total, (each * (1 - self.x), 0), (each, width))
        pairs = [(place, place ^ 1) for place in range(32) if place // 16 == place % 2]
        self.from_x = lax.ppermute(given.astype(jnp.bfloat16), ("dp", "fsdp"), pairs)

    def whole(self, *gate):
        got = after(self.from_x, *gate)
        return jnp.where(self.x == self.y, self.kept, got.astype(jnp.float32))


def hidden_units(own, padded, dp, *gate):
    rows = jnp.pad(own, ((0, padded - own.shape[0]), (0, 0)))
    return own_first(lax.all_gather(after(rows, *gate), "dp", axis=0, tiled=True), dp)


class HiddenGrads:
    def along_core(self, units, rows):
        self.units, self.rows = units, rows
        half = units.shape[1] // 2
        given = columns_by_columns(units[:, half:], rows).astype(jnp.bfloat16)
        self.from_core = core_swap(given)
        return [given]

    def along_y(self, *gate):
        half = self.units.shape[1] // 2
        units, got = after((self.units, self.from_core), *gate)
        total = columns_by_columns(units[:, :half], self.rows) + got.astype(jnp.float32)
        given = total[half // 2 :].astype(jnp.bfloat16)
        self.kept = total[: half // 2]
        self.from_y = y_swap(given)
        return [given]


def fast_body(
    hidden,
    source,
    cotangent,
    row_counts,
    seq_lengths,
    kv_gain,
    w_key,
    w_value,
    attn_gain,
    w_query,
    w_out,
    ffn_gain,
    w_gate,
    w_up,
    w_down,
):
    local_rows, width = hidden.shape
    head = width // HEADS
    dp = lax.axis_index("dp")
    fsdp = lax.axis_index("fsdp")
    y, c = dp // 2, dp % 2
    z, x = fsdp // 2, fsdp % 2
    me = 8 * dp + fsdp

    each = kv_gain.shape[0]
    inputs = Gather(jnp.concatenate([source, hidden], axis=0))
    columns = Columns(
        [w_query, w_key, w_value], jnp.concatenate([kv_gain, attn_gain, ffn_gain]), dp
    )
    wa = columns.along_fsdp()
    s1 = move([inputs])
    wy = columns.along_y(*wa)
    s2 = move([inputs], *s1, *wa)
    wc = columns.along_core(*wy)
    s3 = move([inputs], *s2, *wy)
    wq, w_kv, gains = columns.whole()
    kv_gain_full, attn_gain_full, ffn_gain_full = (
        gains[:, which * each : (which + 1) * each].reshape(1, width) for which in range(3)
    )
    units = w_gate.shape[0]
    padded = -(-units // 64) * 64
    wg, wu, wd = (hidden_units(own, padded, dp, *s1, *wa) for own in (w_gate, w_up, w_down))

    order = z ^ (z >> 1)
    devices = []
    for step in range(4):
        place = (order - step) % 4
        for side in range(2):
            devices.append(2 * (place ^ (place >> 1)) + (x ^ side))
    slots = (
        jnp.stack(devices).astype(jnp.int32)[:, None] * local_rows
        + jnp.arange(local_rows, dtype=jnp.int32)[None, :]
    ).reshape(-1)
    live, position, sequence = slot_layout(row_counts, seq_lengths, slots, local_rows)
    starts = jnp.concatenate([jnp.zeros((1,), jnp.int32), jnp.cumsum(seq_lengths[0])])
    first = jnp.sum(
        jnp.where(
            sequence[:, None] == jnp.arange(starts.shape[0], dtype=jnp.int32)[None, :],
            starts[None, :],
            0,
        ),
        axis=1,
    )
    first, last = first[:, None], position[:, None]
    place_of_key = jnp.where(live, position, -1)[None, :]
    own_live = live[:local_rows].astype(jnp.float32)[:, None]

    hidden_f = hidden.astype(jnp.float32)
    d_out = cotangent.astype(jnp.float32) * own_live
    projected = []

    def project_piece(step):
        piece = after(tuple(inputs.pieces[step]), *(value[3] for value in projected[-1:]))
        projected.append(project(piece, kv_gain_full, attn_gain_full, w_kv, wq))

    project_piece(0)
    project_piece(1)
    s4 = move([inputs], *s3)
    project_piece(2)
    cots = Gather(d_out.astype(jnp.bfloat16))
    c1 = move([cots], *s4)
    project_piece(3)
    src_low, hid_low, pairs, queries = zip(*projected)
    queries = jnp.concatenate(queries, axis=0)
    pairs = jnp.concatenate(pairs, axis=0)
    attended_f, attended_low, lse = attend(queries, pairs, first, last, place_of_key, head)
    wo = out_rows(after(w_out, *s3), x, y, c, s4, [attended_low])

    def rows_of(array, step):
        return array[2 * step * local_rows : 2 * (step + 1) * local_rows]

    def branch_terms(step, *gate):
        return product(after(rows_of(attended_low, step), *gate), wo).astype(jnp.bfloat16)

    branch = Scatter()
    b1 = move([branch.of(branch_terms(1)), cots], *c1)
    b2 = move([branch.of(branch_terms(2)), cots], *b1)
    b3 = move([branch.of(branch_terms(3, *b1)), cots], *b2)
    b4 = move([branch.of(branch_terms(0, *b2))], *b3)
    middle = hidden_f + branch.total()
    middle_scale = inverse_scale(middle)
    middle_unit = middle * middle_scale
    mids = Gather((middle_unit * ffn_gain_full).astype(jnp.bfloat16))

    inners, d_gates, d_ups = [], [], []

    def feed(step):
        mid = mids.piece(step)
        gate_value = rows_by_rows(mid, wg)
        up_value = rows_by_rows(mid, wu)
        sigmoid_gate = jax.nn.sigmoid(gate_value)
        swished = gate_value * sigmoid_gate
        d_inner = rows_by_rows(cots.piece(step), wd)
        inners.append((swished * up_value).astype(jnp.bfloat16))
        d_gates.append(
            (d_inner * up_value * sigmoid_gate * (1.0 + gate_value * (1.0 - sigmoid_gate))).astype(
                jnp.bfloat16
            )
        )
        d_ups.append((d_inner * swished).astype(jnp.bfloat16))
        return (product(d_gates[step], wg) + product(d_ups[step], wu)).astype(jnp.bfloat16)

    m1 = move([mids])
    m2 = move([mids], *m1)
    t0 = feed(0)
    m3 = move([mids], *m2, t0)
    t1 = feed(1)
    back = Scatter()
    d1 = move([mids, back.of(t1)], *m3)
    t2 = feed(2)
    d2 = move([back.of(t2)], *d1)
    t3 = feed(3)
    d3 = move([back.of(t3)], *d2)
    d_gates, d_ups, inners = (jnp.concatenate(value, axis=0) for value in (d_gates, d_ups, inners))
    all_mids = jnp.concatenate([mids.piece(step) for step in range(4)], axis=0)
    all_cots = jnp.concatenate([cots.piece(step) for step in range(4)], axis=0)
    gate_sums, up_sums, down_sums = (HiddenGrads() for which in range(3))
    h1 = gate_sums.along_core(after(d_gates, *d2), all_mids)
    d4 = move([back.of(t0)], *d3, *h1)
    h2 = up_sums.along_core(after(d_ups, *d3), all_mids)
    d_normed = after(back.total(), *h2)
    d_middle = d_out + norm_backward(middle, middle_scale, ffn_gain_full, d_normed)
    d_branch_low = d_middle.astype(jnp.bfloat16)
    outs = Gather(d_branch_low)
    e1 = move([outs])
    h1 = gate_sums.along_y(d_branch_low)
    e2 = move([outs], *e1, *h1)
    h2 = up_sums.along_y(*e1)
    h3 = down_sums.along_core(after(inners, *e1), all_cots)
    e3 = move([outs], *e2, *h2, *h3)
    ffn_gain_part = jnp.sum(after(d_normed * middle_unit, *e2), axis=0)
    h3 = down_sums.along_y(*e2)

    def result_terms(step, *gate):
        return product(after(rows_of(inners, step), *gate), wd).astype(jnp.bfloat16)

    result = Scatter()
    e4 = move([outs, result.of(result_terms(1, *e2))], *e3, *h3, gate_sums.from_y)
    column_grads = ColumnGrads(dp)
    column_grads.gain_core(ffn_gain_part, *e3)
    column_grads.gain_y(*e4)
    d_branches = [outs.piece(step) for step in range(4)]
    d_attended = jnp.concatenate(
        [rows_by_rows(rows, wo).astype(jnp.bfloat16) for rows in d_branches], axis=0
    )
    o2 = move([result.of(result_terms(2, *e3))], *e4)
    d_queries, d_pairs = attend_back(
        queries, pairs, first, last, place_of_key, lse, attended_f, d_attended, head
    )
    d_queries, d_pairs = after((d_queries, d_pairs), *o2)
    d_src, d_hid = Scatter(), Scatter()

    def terms(step, *gate):
        rows = input_terms(step, *after((d_pairs, d_queries), *gate), w_kv, wq)
        return [d_src.of(rows[0]), d_hid.of(rows[1])]

    first_terms = terms(1)
    started = d_hid.terms
    i1 = move(first_terms, *o2, up_sums.from_y, column_grads.gain)
    sources, hiddens = after((tuple(src_low), tuple(hid_low)), started)
    column_grads.along_core(sources, hiddens, d_queries, d_pairs)
    py = column_grads.along_y()
    i2 = move(
        terms(2, started) + [result.of(result_terms(3, started))],
        *i1,
        down_sums.from_y,
    )
    out_grads = OutGrads(
        columns_by_columns(after(attended_low, *i1, *py), jnp.concatenate(d_branches, axis=0)), x, y, c
    )
    out_grads.along_core()
    oy = out_grads.along_y(column_grads.from_y)
    pz, got_z = column_grads.along_fsdp(*i2)
    i3 = move(terms(3, *i1) + [result.of(result_terms(0, *i1))], *i2, *oy)
    out_grads.along_x(*i2)
    i4 = move(terms(0, *i2), *i3)
    grad_gate, grad_up, grad_down = add_all(
        *zip(
            *(
                (sums.kept, after(sums.from_y, *i3))
                for sums in (gate_sums, up_sums, down_sums)
            )
        ),
        units,
    )
    output = ((middle + after(result.total(), *i3)) * own_live).astype(jnp.bfloat16)
    d_src, d_hid = d_src.total(), d_hid.total()

    grad_out = out_grads.whole(*i3)
    own_grads, grad_ffn_gain = column_grads.whole([w_query, w_key, w_value], *i3)
    grad_query, grad_key, grad_value, query_sum, pair_sum = own_grads
    grad_attn_gain = query_sum[:, 0] / attn_gain.astype(jnp.float32)
    grad_kv_gain = pair_sum[:, 0] / kv_gain.astype(jnp.float32)

    grad_hidden = (
        d_middle + norm_backward(hidden_f, inverse_scale(hidden_f), attn_gain_full, d_hid)
    ).astype(jnp.bfloat16)
    source_f = source.astype(jnp.float32)
    grad_source = norm_backward(source_f, inverse_scale(source_f), kv_gain_full, d_src).astype(
        jnp.bfloat16
    )
    return (
        output,
        grad_hidden,
        grad_source,
        grad_kv_gain,
        grad_key,
        grad_value,
        grad_attn_gain,
        grad_query,
        grad_out,
        grad_ffn_gain,
        grad_gate,
        grad_up,
        grad_down,
    )


def solution(mesh):
    in_specs = (
        P(("dp", "fsdp"), None),
        P(("dp", "fsdp"), None),
        P(("dp", "fsdp"), None),
        P("dp", None),
        P("dp", None),
        P(("dp", "fsdp")),
        P(("dp", "fsdp"), None),
        P(("dp", "fsdp"), None),
        P(("dp", "fsdp")),
        P(("dp", "fsdp"), None),
        P(("dp", "fsdp"), None),
        P(("dp", "fsdp")),
        P(("dp", "fsdp"), None),
        P(("dp", "fsdp"), None),
        P(("dp", "fsdp"), None),
    )
    out_specs = (
        P(("dp", "fsdp"), None),
        P(("dp", "fsdp"), None),
        P(("dp", "fsdp"), None),
        P(("dp", "fsdp")),
        P(("dp", "fsdp"), None),
        P(("dp", "fsdp"), None),
        P(("dp", "fsdp")),
        P(("dp", "fsdp"), None),
        P(("dp", "fsdp"), None),
        P(("dp", "fsdp")),
        P(("dp", "fsdp"), None),
        P(("dp", "fsdp"), None),
        P(("dp", "fsdp"), None),
    )
    placed = (
        mesh.shape["dp"] == 4 and mesh.shape["fsdp"] == 8 and HEADS == 2 * mesh.shape["fsdp"]
    )
    chosen = fast_body if placed else body
    return jax.shard_map(chosen, mesh=mesh, in_specs=in_specs, out_specs=out_specs, check_vma=False)
```

```python
import functools
import math

import jax
import jax.numpy as jnp
from jax import lax
from jax.experimental import pallas as pl
from jax.experimental.pallas import tpu as pltpu
from jax.sharding import PartitionSpec as P

HEADS = 16


EPSILON = 1e-06
MASKED = -1000000000.0


def product(left, right):
    return jnp.dot(left, right, preferred_element_type=jnp.float32)


def rows_by_rows(left, right):
    return lax.dot_general(
        left, right, (((1,), (1,)), ((), ())), preferred_element_type=jnp.float32
    )


def columns_by_columns(left, right):
    return lax.dot_general(
        left, right, (((0,), (0,)), ((), ())), preferred_element_type=jnp.float32
    )


def inverse_scale(values):
    return lax.rsqrt(jnp.mean(values * values, axis=-1, keepdims=True) + EPSILON)


def norm_backward(values, scale, gain, d_normed):
    weighted = d_normed * gain
    return scale * weighted - values * scale**3 * jnp.mean(
        values * weighted, axis=-1, keepdims=True
    )


def slot_layout(row_counts, seq_lengths, slots, per_device):
    counts = row_counts[0]
    offsets = jnp.cumsum(counts) - counts
    device_of = slots // per_device
    within = slots - device_of * per_device
    picker = device_of[:, None] == jnp.arange(counts.shape[0], dtype=jnp.int32)[None, :]
    count_here = jnp.sum(jnp.where(picker, counts[None, :], 0), axis=1)
    offset_here = jnp.sum(jnp.where(picker, offsets[None, :], 0), axis=1)
    position = offset_here + within
    ends = jnp.cumsum(seq_lengths[0])
    sequence = jnp.sum((ends[None, :] <= position[:, None]).astype(jnp.int32), axis=1)
    return (within < count_here, position, sequence)


def body(
    hidden,
    source,
    cotangent,
    row_counts,
    seq_lengths,
    kv_gain,
    w_key,
    w_value,
    attn_gain,
    w_query,
    w_out,
    ffn_gain,
    w_gate,
    w_up,
    w_down,
):
    local_rows, model_width = hidden.shape
    group_rows = local_rows * lax.axis_size("fsdp")
    head_size = model_width // HEADS
    factor = 1.0 / math.sqrt(head_size)
    block_rows = math.gcd(group_rows, 512)
    block_count = group_rows // block_rows
    own_slots = lax.axis_index("fsdp") * local_rows + jnp.arange(local_rows, dtype=jnp.int32)
    query_live, query_position, query_sequence = slot_layout(
        row_counts, seq_lengths, own_slots, local_rows
    )
    key_live, key_position, key_sequence = slot_layout(
        row_counts, seq_lengths, jnp.arange(group_rows, dtype=jnp.int32), local_rows
    )
    live_column = query_live.astype(jnp.float32)[:, None]
    source_f = source.astype(jnp.float32)
    hidden_f = hidden.astype(jnp.float32)
    source_scale = inverse_scale(source_f)
    hidden_scale = inverse_scale(hidden_f)
    source_unit = source_f * source_scale
    hidden_unit = hidden_f * hidden_scale
    piece_kv_gain = lax.all_gather(kv_gain, ("dp", "fsdp"), axis=0, tiled=True)
    piece_key = lax.all_gather(w_key, ("dp", "fsdp"), axis=0, tiled=True)
    piece_value = lax.all_gather(w_value, ("dp", "fsdp"), axis=0, tiled=True)
    piece_attn_gain = lax.all_gather(attn_gain, ("dp", "fsdp"), axis=0, tiled=True)
    piece_query = lax.all_gather(w_query, ("dp", "fsdp"), axis=0, tiled=True)
    piece_ffn_gain = lax.all_gather(ffn_gain, ("dp", "fsdp"), axis=0, tiled=True)
    source_cols = (source_unit * piece_kv_gain.astype(jnp.float32)[None, :]).astype(jnp.bfloat16)
    hidden_cols = (hidden_unit * piece_attn_gain.astype(jnp.float32)[None, :]).astype(jnp.bfloat16)
    key_sum = product(source_cols, piece_key)
    value_sum = product(source_cols, piece_value)
    query_sum = product(hidden_cols, piece_query)
    stacked = jnp.stack([piece_kv_gain, piece_attn_gain, piece_ffn_gain]).astype(jnp.float32)
    gains = stacked
    key_sum, value_sum, query_sum, gains = (key_sum, value_sum, query_sum, gains)
    kv_gain_full, attn_gain_full, ffn_gain_full = (gains[0], gains[1], gains[2])
    keys_low = key_sum.astype(jnp.bfloat16)
    values_low = value_sum.astype(jnp.bfloat16)
    queries_low = query_sum.astype(jnp.bfloat16)
    group_keys, group_values = (
        lax.all_gather(keys_low, "fsdp", axis=0, tiled=True),
        lax.all_gather(values_low, "fsdp", axis=0, tiled=True),
    )
    blocks = (
        group_keys.reshape(block_count, block_rows, HEADS, head_size),
        group_values.reshape(block_count, block_rows, HEADS, head_size),
        key_live.reshape(block_count, block_rows),
        key_position.reshape(block_count, block_rows),
        key_sequence.reshape(block_count, block_rows),
    )
    query_heads = queries_low.reshape(local_rows, HEADS, head_size)

    def block_scores(key_block, live_block, position_block, sequence_block):
        scores = (
            jnp.einsum("qhd,khd->hqk", query_heads, key_block, preferred_element_type=jnp.float32)
            * factor
        )
        allowed = (
            live_block[None, :]
            & (sequence_block[None, :] == query_sequence[:, None])
            & (position_block[None, :] <= query_position[:, None])
        )
        return jnp.where(allowed[None], scores, MASKED)

    def running_total(running, key_block_set):
        largest, summed = running
        key_block, value_block, live_block, position_block, sequence_block = key_block_set
        masked = block_scores(key_block, live_block, position_block, sequence_block)
        new_largest = jnp.maximum(largest, jnp.max(masked, axis=-1))
        summed = summed * jnp.exp(largest - new_largest) + jnp.sum(
            jnp.exp(masked - new_largest[:, :, None]), axis=-1
        )
        return ((new_largest, summed), None)

    (largest, summed), unused = lax.scan(
        running_total,
        (
            jnp.full((HEADS, local_rows), MASKED, jnp.float32),
            jnp.zeros((HEADS, local_rows), jnp.float32),
        ),
        blocks,
    )
    log_total = largest + jnp.log(summed)

    def weighted_sum(running, key_block_set):
        key_block, value_block, live_block, position_block, sequence_block = key_block_set
        probs_low = jnp.exp(
            block_scores(key_block, live_block, position_block, sequence_block)
            - log_total[:, :, None]
        ).astype(jnp.bfloat16)
        return (
            running
            + jnp.einsum(
                "hqk,khd->qhd", probs_low, value_block, preferred_element_type=jnp.float32
            ),
            None,
        )

    attended_f, unused = lax.scan(
        weighted_sum, jnp.zeros((local_rows, HEADS, head_size), jnp.float32), blocks
    )
    attended_low = attended_f.reshape(local_rows, model_width).astype(jnp.bfloat16)
    branch = product(attended_low, lax.all_gather(w_out, ("dp", "fsdp"), axis=0, tiled=True))
    middle = hidden_f + branch
    middle_scale = inverse_scale(middle)
    middle_unit = middle * middle_scale
    middle_low = (middle_unit * ffn_gain_full).astype(jnp.bfloat16)
    piece_gate = lax.all_gather(w_gate, ("dp", "fsdp"), axis=0, tiled=True)
    piece_up = lax.all_gather(w_up, ("dp", "fsdp"), axis=0, tiled=True)
    piece_down = lax.all_gather(w_down, ("dp", "fsdp"), axis=0, tiled=True)
    gate_value = rows_by_rows(middle_low, piece_gate)
    up_value = rows_by_rows(middle_low, piece_up)
    inner = (jax.nn.silu(gate_value) * up_value).astype(jnp.bfloat16)
    ffn_result = product(inner, piece_down)
    output = ((middle + ffn_result) * live_column).astype(jnp.bfloat16)
    d_out = cotangent.astype(jnp.float32) * live_column
    d_out_low = d_out.astype(jnp.bfloat16)
    piece_gate = lax.all_gather(w_gate, ("dp", "fsdp"), axis=0, tiled=True)
    piece_up = lax.all_gather(w_up, ("dp", "fsdp"), axis=0, tiled=True)
    piece_down = lax.all_gather(w_down, ("dp", "fsdp"), axis=0, tiled=True)
    gate_value = rows_by_rows(middle_low, piece_gate)
    up_value = rows_by_rows(middle_low, piece_up)
    sigmoid_gate = jax.nn.sigmoid(gate_value)
    swished = gate_value * sigmoid_gate
    inner = (swished * up_value).astype(jnp.bfloat16)
    d_inner = rows_by_rows(d_out_low, piece_down)
    d_gate = (d_inner * up_value * sigmoid_gate * (1.0 + gate_value * (1.0 - sigmoid_gate))).astype(
        jnp.bfloat16
    )
    d_up = (d_inner * swished).astype(jnp.bfloat16)
    d_normed = product(d_gate, piece_gate) + product(d_up, piece_up)
    ffn_grads = lax.psum_scatter(
        jnp.stack(
            [
                columns_by_columns(d_gate, middle_low),
                columns_by_columns(d_up, middle_low),
                columns_by_columns(inner, d_out_low),
            ],
            axis=1,
        ),
        ("dp", "fsdp"),
        scatter_dimension=0,
        tiled=True,
    )
    ffn_gain_part = jnp.sum(d_normed * middle_unit, axis=0)
    d_middle = d_out + norm_backward(middle, middle_scale, ffn_gain_full, d_normed)
    d_branch_low = d_middle.astype(jnp.bfloat16)
    d_attended = rows_by_rows(
        d_branch_low, lax.all_gather(w_out, ("dp", "fsdp"), axis=0, tiled=True)
    )
    d_heads = d_attended.astype(jnp.bfloat16).reshape(local_rows, HEADS, head_size)
    delta = jnp.sum(d_heads.astype(jnp.float32) * attended_f, axis=-1).T

    def attention_backward(d_query_sum, key_block_set):
        key_block, value_block, live_block, position_block, sequence_block = key_block_set
        probs = jnp.exp(
            block_scores(key_block, live_block, position_block, sequence_block)
            - log_total[:, :, None]
        )
        probs_low = probs.astype(jnp.bfloat16)
        d_values = jnp.einsum(
            "hqk,qhd->khd", probs_low, d_heads, preferred_element_type=jnp.float32
        )
        d_probs = jnp.einsum(
            "qhd,khd->hqk", d_heads, value_block, preferred_element_type=jnp.float32
        )
        d_scores = (probs * (d_probs - delta[:, :, None])).astype(jnp.bfloat16)
        d_query_sum = d_query_sum + jnp.einsum(
            "hqk,khd->qhd", d_scores, key_block, preferred_element_type=jnp.float32
        )
        d_keys = (
            jnp.einsum("hqk,qhd->khd", d_scores, query_heads, preferred_element_type=jnp.float32)
            * factor
        )
        return (d_query_sum, jnp.stack([d_keys, d_values], axis=1))

    d_query_sum, key_terms = lax.scan(
        attention_backward, jnp.zeros((local_rows, HEADS, head_size), jnp.float32), blocks
    )
    key_grads = lax.psum_scatter(
        key_terms.reshape(group_rows, 2, model_width).astype(jnp.bfloat16),
        "fsdp",
        scatter_dimension=0,
        tiled=True,
    ).astype(jnp.float32)
    d_keys_low = key_grads[:, 0].astype(jnp.bfloat16)
    d_values_low = key_grads[:, 1].astype(jnp.bfloat16)
    d_queries_low = (d_query_sum * factor).reshape(local_rows, model_width).astype(jnp.bfloat16)
    piece_query = lax.all_gather(w_query, ("dp", "fsdp"), axis=0, tiled=True)
    piece_key = lax.all_gather(w_key, ("dp", "fsdp"), axis=0, tiled=True)
    piece_value = lax.all_gather(w_value, ("dp", "fsdp"), axis=0, tiled=True)
    hidden_part = rows_by_rows(d_queries_low, piece_query)
    source_part = rows_by_rows(d_keys_low, piece_key) + rows_by_rows(d_values_low, piece_value)
    input_back = jnp.stack([hidden_part, source_part])
    grad_hidden = (
        d_middle + norm_backward(hidden_f, hidden_scale, attn_gain_full, input_back[0])
    ).astype(jnp.bfloat16)
    grad_source = norm_backward(source_f, source_scale, kv_gain_full, input_back[1]).astype(
        jnp.bfloat16
    )
    attn_gain_part = jnp.sum(input_back[0] * hidden_unit, axis=0)
    kv_gain_part = jnp.sum(input_back[1] * source_unit, axis=0)
    source_low = (source_unit * kv_gain_full).astype(jnp.bfloat16)
    hidden_low = (hidden_unit * attn_gain_full).astype(jnp.bfloat16)
    hidden_part = hidden_low
    source_part = source_low
    layer_stack = lax.psum_scatter(
        jnp.stack(
            [
                columns_by_columns(hidden_part, d_queries_low),
                columns_by_columns(source_part, d_keys_low),
                columns_by_columns(source_part, d_values_low),
                columns_by_columns(attended_low, d_branch_low),
            ],
            axis=1,
        ),
        ("dp", "fsdp"),
        scatter_dimension=0,
        tiled=True,
    )
    grad_query, grad_key, grad_value, grad_out = (
        layer_stack[:, 0],
        layer_stack[:, 1],
        layer_stack[:, 2],
        layer_stack[:, 3],
    )
    grad_kv_gain, grad_attn_gain, grad_ffn_gain = (
        lax.psum_scatter(kv_gain_part, ("dp", "fsdp"), scatter_dimension=0, tiled=True),
        lax.psum_scatter(attn_gain_part, ("dp", "fsdp"), scatter_dimension=0, tiled=True),
        lax.psum_scatter(ffn_gain_part, ("dp", "fsdp"), scatter_dimension=0, tiled=True),
    )
    return (
        output,
        grad_hidden,
        grad_source,
        grad_kv_gain,
        grad_key,
        grad_value,
        grad_attn_gain,
        grad_query,
        grad_out,
        grad_ffn_gain,
        ffn_grads[:, 0],
        ffn_grads[:, 1],
        ffn_grads[:, 2],
    )


RING = (0, 1, 3, 2)
BLOCK = 256


def swap_pairs(size, mask):
    return [(place, place ^ mask) for place in range(size)]


def ring_pairs():
    return [
        (2 * RING[place] + x, 2 * RING[(place + 1) % 4] + x) for place in range(4) for x in range(2)
    ]


def x_swap(value):
    return lax.ppermute(value, "fsdp", swap_pairs(8, 1))


def ring_step(value):
    return lax.ppermute(value, "fsdp", ring_pairs())


def y_swap(value):
    return lax.ppermute(value, "dp", swap_pairs(4, 2))


def core_swap(value):
    return lax.ppermute(value, "dp", swap_pairs(4, 1))


def in_order(flag, first, second):
    swapped = flag == 1
    return jnp.concatenate(
        [jnp.where(swapped, second, first), jnp.where(swapped, first, second)], axis=0
    )


def after(value, *earlier):
    if not earlier:
        return value
    return lax.optimization_barrier((value, *earlier))[0]


FREE = pl.CostEstimate(flops=0, bytes_accessed=0, transcendentals=0)
LONG = pl.CostEstimate(flops=2 * 10**10, bytes_accessed=0, transcendentals=0)


class Rows:
    def __init__(self, array, start, count):
        self.array, self.start, self.count = array, start, count

    def part(self, start, count):
        return Rows(self.array, self.start + start, count)

    def value(self):
        if self.count == self.array.shape[0]:
            return self.array
        return self.array[self.start : self.start + self.count]


def rows_in(array):
    return Rows(array, 0, array.shape[0])


class Gather:
    def __init__(self, own):
        self.held = rows_in(own)
        self.pieces = []

    def send(self):
        if len(self.pieces) < 3:
            return [[self.held]], [[self.held]]
        half = self.held.count // 2
        return [[self.held.part(0, half)]], [[self.pieces[2][1].part(half, half)]]

    def take(self, from_x, from_ring):
        if len(self.pieces) < 3:
            self.pieces.append((self.held, from_x))
            self.held = from_ring
        else:
            self.pieces.append((self.held, from_x, from_ring))

    def arrays(self, step):
        return tuple(rows.value() for rows in self.pieces[step])

    def piece(self, step):
        return jnp.concatenate(self.arrays(step), axis=0)


class Scatter:
    def __init__(self):
        self.stage = 0

    def of(self, terms):
        rows = terms.shape[0] // 2
        return self.of_rows(Rows(terms, 0, rows), Rows(terms, rows, rows))

    def of_rows(self, own, other):
        self.own, self.other = own, other
        return self

    def send(self):
        own, other = self.own, self.other
        half = own.count // 2
        if self.stage == 0:
            given = [[other.part(0, half)]], [[other.part(half, half)]]
        elif self.stage == 1:
            kept, (from_x, from_ring) = self.kept, self.got
            given = (
                [[other.part(0, half)], [other.part(half, half), from_ring]],
                [[kept.part(0, half), from_x], [kept.part(half, half)]],
            )
        else:
            given = [[other]], [[self.kept, *self.got]]
        self.stage += 1
        self.kept = own
        return given

    def take(self, from_x, from_ring):
        self.got = (from_x, from_ring)

    def total(self):
        return sum(rows.value().astype(jnp.float32) for rows in (self.kept, *self.got))


def mix_kernel(plans, *refs):
    for plan, out_ref in zip(plans, refs[-len(plans) :]):
        first = 0
        for places, count in plan:
            values = [refs[index][start : start + count, :] for index, start in places]
            if len(values) > 1:
                values = [sum(value.astype(jnp.float32) for value in values)]
            out_ref[first : first + count, :] = values[0].astype(out_ref.dtype)
            first += count


def only_array(sums):
    array = sums[0][0].array
    first = 0
    for rows in sums:
        if len(rows) > 1 or rows[0].array is not array or rows[0].start != first:
            return None
        first += rows[0].count
    return array if first == array.shape[0] else None


def mixed(*all_sums):
    arrays = []
    plans = []
    for sums in all_sums:
        plan = []
        for rows in sums:
            places = []
            for part in rows:
                index = next((n for n, held in enumerate(arrays) if held is part.array), None)
                if index is None:
                    index = len(arrays)
                    arrays.append(part.array)
                places.append((index, part.start))
            plan.append((tuple(places), rows[0].count))
        plans.append(tuple(plan))
    width = arrays[0].shape[1]
    counts = [sum(count for places, count in plan) for plan in plans]
    return pl.pallas_call(
        functools.partial(mix_kernel, tuple(plans)),
        out_shape=[jax.ShapeDtypeStruct((count, width), jnp.bfloat16) for count in counts],
        compiler_params=pltpu.CompilerParams(vmem_limit_bytes=32 * 2**20),
        cost_estimate=FREE,
        name="mix",
    )(*arrays)


def move(parts, *gate):
    sent = [part.send() for part in parts]
    x_sums, ring_sums = (sum((given[way] for given in sent), []) for way in range(2))
    along_x, along_ring = only_array(x_sums), only_array(ring_sums)
    if along_x is None and along_ring is None:
        along_x, along_ring = mixed(x_sums, ring_sums)
    elif along_x is None:
        (along_x,) = mixed(x_sums)
    elif along_ring is None:
        (along_ring,) = mixed(ring_sums)
    along_x, along_ring = after((along_x, along_ring), *gate)
    from_x, from_ring = x_swap(along_x), ring_step(along_ring)
    x_row = ring_row = 0
    for part, given in zip(parts, sent):
        x_count, ring_count = (sum(rows[0].count for rows in sums) for sums in given)
        part.take(Rows(from_x, x_row, x_count), Rows(from_ring, ring_row, ring_count))
        x_row, ring_row = x_row + x_count, ring_row + ring_count
    return [from_x, from_ring]


def attend_kernel(
    factor, q_ref, k_ref, v_ref, first_ref, last_ref, place_ref, att_ref, low_ref, lse_ref
):
    scores = rows_by_rows(q_ref[...], k_ref[...]) * factor
    places = place_ref[...]
    allowed = (places >= first_ref[...]) & (places <= last_ref[...])
    masked = jnp.where(allowed, scores, MASKED)
    largest = jnp.max(masked, axis=-1, keepdims=True)
    raised = jnp.exp(masked - largest)
    summed = jnp.sum(raised, axis=-1, keepdims=True)
    probs_low = (raised * (1.0 / summed)).astype(jnp.bfloat16)
    attended = product(probs_low, v_ref[...])
    att_ref[...] = attended
    low_ref[...] = attended.astype(jnp.bfloat16)
    lse_ref[...] = (largest + jnp.log(summed))[None]


def attend_back_kernel(
    factor,
    q_ref,
    k_ref,
    v_ref,
    first_ref,
    last_ref,
    place_ref,
    lse_ref,
    att_ref,
    d_att_ref,
    dq_ref,
    dkv_ref,
    dk_sum,
    dv_sum,
):
    head = pl.program_id(0)
    step = pl.program_id(1)
    size = q_ref.shape[1]
    mine = dkv_ref.shape[1] // 2

    @pl.when(step == 0)
    def _():
        dk_sum[...] = jnp.zeros_like(dk_sum)
        dv_sum[...] = jnp.zeros_like(dv_sum)

    queries = q_ref[...]
    keys = k_ref[...]
    d_att = d_att_ref[...]
    scores = rows_by_rows(queries, keys) * factor
    places = place_ref[...]
    allowed = (places >= first_ref[...]) & (places <= last_ref[...])
    probs = jnp.exp(jnp.where(allowed, scores, MASKED) - lse_ref[0])
    delta = jnp.sum(d_att.astype(jnp.float32) * att_ref[...], axis=-1, keepdims=True)
    d_probs = rows_by_rows(d_att, v_ref[...])
    d_scores = (probs * (d_probs - delta)).astype(jnp.bfloat16)
    dq_ref[...] = (product(d_scores, keys) * factor).astype(jnp.bfloat16)
    dk_sum[...] += columns_by_columns(d_scores, queries)
    dv_sum[...] += columns_by_columns(probs.astype(jnp.bfloat16), d_att)

    @pl.when(step == pl.num_programs(1) - 1)
    def _():
        first = pl.multiple_of(size * head, size)
        dkv_ref[:, pl.ds(first, size)] = (dk_sum[...] * factor).astype(jnp.bfloat16)
        dkv_ref[:, pl.ds(mine + first, size)] = dv_sum[...].astype(jnp.bfloat16)


def attend_specs(count, head):
    by_query = pl.BlockSpec((BLOCK, head), lambda h, i: (i, h))
    keys = pl.BlockSpec((count, head), lambda h, i: (0, h))
    values = pl.BlockSpec((count, head), lambda h, i: (0, 2 + h))
    bound = pl.BlockSpec((BLOCK, 1), lambda h, i: (i, 0))
    place = pl.BlockSpec((1, count), lambda h, i: (0, 0))
    lse = pl.BlockSpec((1, BLOCK, 1), lambda h, i: (h, i, 0))
    return by_query, keys, values, bound, place, lse


def attend(queries, pairs, first, last, place, head):
    count, width = queries.shape
    by_query, keys, values, bound, places, lse = attend_specs(count, head)
    return pl.pallas_call(
        functools.partial(attend_kernel, 1.0 / math.sqrt(head)),
        grid=(width // head, count // BLOCK),
        in_specs=[by_query, keys, values, bound, bound, places],
        out_specs=[by_query, by_query, lse],
        out_shape=[
            jax.ShapeDtypeStruct((count, width), jnp.float32),
            jax.ShapeDtypeStruct((count, width), jnp.bfloat16),
            jax.ShapeDtypeStruct((width // head, count, 1), jnp.float32),
        ],
        compiler_params=pltpu.CompilerParams(vmem_limit_bytes=40 * 2**20),
        cost_estimate=LONG,
        name="attend",
    )(queries, pairs, pairs, first, last, place)


def attend_back(queries, pairs, first, last, place, lse, attended, d_attended, head):
    count, width = queries.shape
    by_query, keys, values, bound, places, by_lse = attend_specs(count, head)
    return pl.pallas_call(
        functools.partial(attend_back_kernel, 1.0 / math.sqrt(head)),
        grid=(width // head, count // BLOCK),
        in_specs=[
            by_query,
            keys,
            values,
            bound,
            bound,
            places,
            by_lse,
            by_query,
            by_query,
        ],
        out_specs=[by_query, pl.BlockSpec((count, 2 * width), lambda h, i: (0, 0))],
        out_shape=[
            jax.ShapeDtypeStruct((count, width), jnp.bfloat16),
            jax.ShapeDtypeStruct((count, 2 * width), jnp.bfloat16),
        ],
        scratch_shapes=[pltpu.VMEM((count, head), jnp.float32)] * 2,
        compiler_params=pltpu.CompilerParams(vmem_limit_bytes=40 * 2**20),
        cost_estimate=LONG,
        name="attend_back",
    )(queries, pairs, pairs, first, last, place, lse, attended, d_attended)


def as_rows(values, columns):
    rows = 8 * -(-values.shape[0] // (8 * columns))
    return jnp.pad(values, (0, rows * columns - values.shape[0])).reshape(rows, columns)


def from_rows(rows, count):
    return rows.reshape(-1)[:count]


def heads_of(device, head):
    z, x = device // 2, device % 2
    return [slice(head * (8 * x + 4 * j + z), head * (8 * x + 4 * j + z + 1)) for j in range(2)]


def columns_kernel(dp_ref, held_ref, q_ref, kv_ref, gain_ref):
    each = q_ref.shape[0] // 8
    mine = q_ref.shape[1]
    rows = held_ref.shape[2] // 8
    for device in range(8):
        first = rows * device
        here = slice(each * device, each * (device + 1))
        q_ref[here, :] = held_ref[0, 0, first : first + each, :]
        kv_ref[here, :mine] = held_ref[0, 0, first + each : first + 2 * each, :]
        kv_ref[here, mine:] = held_ref[0, 0, first + 2 * each : first + 3 * each, :]
        extra = rows - 3 * each
        gain_ref[0, extra * device : extra * (device + 1), :] = held_ref[
            0, 0, first + 3 * each : first + rows, :
        ]


def payload_kernel(q_ref, k_ref, v_ref, gain_ref, out_ref):
    each = q_ref.shape[0]
    head = q_ref.shape[1] // 16
    rows = out_ref.shape[0] // 8
    for device in range(8):
        for which, w_ref in enumerate((q_ref, k_ref, v_ref)):
            first = rows * device + each * which
            for j, columns in enumerate(heads_of(device, head)):
                out_ref[first : first + each, head * j : head * (j + 1)] = w_ref[:, columns]
        out_ref[rows * device + 3 * each : rows * (device + 1), :] = gain_ref[...]


class Columns:
    def __init__(self, weights, gains, dp):
        self.weights, self.gains, self.dp = weights, gains, dp

    def along_fsdp(self, *gate):
        each, width = self.weights[0].shape
        extra = as_rows(self.gains, width // 8)
        given = pl.pallas_call(
            payload_kernel,
            out_shape=jax.ShapeDtypeStruct(
                (8 * (3 * each + extra.shape[0]), width // 8), self.weights[0].dtype
            ),
            compiler_params=pltpu.CompilerParams(vmem_limit_bytes=16 * 2**20),
            cost_estimate=LONG,
            name="payload",
        )(*self.weights, extra)
        self.held = lax.all_to_all(after(given, *gate), "fsdp", 0, 0, tiled=True)
        return [self.held]

    def along_y(self, *gate):
        held = after(self.held, *gate)
        got, other = y_swap(held), core_swap(held)
        self.held = [held, got, other]
        return [got, other]

    def along_core(self, *gate):
        held, got, other = after(tuple(self.held), *gate)
        last = core_swap(got)
        self.held = jnp.stack([held, got, other, last]).reshape(2, 2, *held.shape)
        return [last]

    def whole(self):
        each, width = self.weights[0].shape
        rows, mine = self.held.shape[2:]
        extra = rows - 24 * each
        block = 8 * each
        low = self.held.dtype
        wq, w_kv, gains = pl.pallas_call(
            columns_kernel,
            grid_spec=pltpu.PrefetchScalarGridSpec(
                num_scalar_prefetch=1,
                grid=(4,),
                in_specs=[
                    pl.BlockSpec(
                        (1, 1, rows, mine),
                        lambda i, dp: ((dp[0] ^ i) % 2, (dp[0] ^ i) // 2, 0, 0),
                    )
                ],
                out_specs=[
                    pl.BlockSpec((block, mine), lambda i, dp: (i, 0)),
                    pl.BlockSpec((block, 2 * mine), lambda i, dp: (i, 0)),
                    pl.BlockSpec((1, extra, mine), lambda i, dp: (i, 0, 0)),
                ],
            ),
            out_shape=[
                jax.ShapeDtypeStruct((4 * block, mine), low),
                jax.ShapeDtypeStruct((4 * block, 2 * mine), low),
                jax.ShapeDtypeStruct((4, extra, mine), low),
            ],
            compiler_params=pltpu.CompilerParams(vmem_limit_bytes=32 * 2**20),
            cost_estimate=FREE,
            name="columns",
        )(self.dp.reshape(1).astype(jnp.int32), self.held)
        gains = gains.reshape(32, -1)[:, : self.gains.shape[0]].astype(jnp.float32)
        return wq, w_kv, gains


def column_grads_kernel(dp_ref, *refs):
    sources, hiddens = refs[:4], refs[4:8]
    dq_ref, dkv_ref, given_ref, kept_ref = refs[8:]
    count = sources[0].shape[0]
    mine = dq_ref.shape[1]
    for_q, for_kv = 0.0, 0.0
    for step in range(4):
        here = slice(count * step, count * (step + 1))
        for_q = for_q + columns_by_columns(hiddens[step][...], dq_ref[here, :])
        for_kv = for_kv + columns_by_columns(sources[step][...], dkv_ref[here, :])

    @pl.when(pl.program_id(0) < 2)
    def _():
        given_ref[0, :, :mine] = for_q.astype(jnp.bfloat16)
        given_ref[0, :, mine:] = for_kv.astype(jnp.bfloat16)

    @pl.when(pl.program_id(0) >= 2)
    def _():
        kept_ref[0, :, :mine] = for_q
        kept_ref[0, :, mine:] = for_kv


def own_grads_kernel(
    got_ref,
    wq_ref,
    wk_ref,
    wv_ref,
    flag_ref,
    out_kept_ref,
    out_got_ref,
    q_ref,
    k_ref,
    v_ref,
    q_sum_ref,
    kv_sum_ref,
    gain_ref,
    out_ref,
):
    each = wq_ref.shape[0]
    gain = 0.0
    for device in range(8):
        gain = gain + got_ref[device, each : each + 8, :128].astype(jnp.float32)
    gain_ref[...] = gain
    out_ref[...] = jnp.where(
        flag_ref[...] != 0, out_kept_ref[...], out_got_ref[...].astype(jnp.float32)
    )
    head = wq_ref.shape[1] // 16
    sums = []
    for which, (w_ref, out_ref) in enumerate(((wq_ref, q_ref), (wk_ref, k_ref), (wv_ref, v_ref))):
        total = jnp.zeros((each, head), jnp.float32)
        for device in range(8):
            for j, columns in enumerate(heads_of(device, head)):
                first = head * (2 * which + j)
                grad = got_ref[device, :each, first : first + head].astype(jnp.float32)
                out_ref[:, columns] = grad
                total = total + grad * w_ref[:, columns].astype(jnp.float32)
        sums.append(jnp.sum(total, axis=1, keepdims=True))
    q_sum_ref[...] = sums[0]
    kv_sum_ref[...] = sums[1] + sums[2]


def whole_block(array):
    return pl.BlockSpec(array.shape, lambda *place: (0,) * array.ndim)


def project_kernel(held_ref, *refs):
    others = refs[:-8]
    kv_gain_ref, attn_gain_ref, w_kv_ref, wq_ref, src_ref, hid_ref, pair_ref, query_ref = refs[-8:]
    rows = src_ref.shape[0] // 2

    def other_rows(which):
        if len(others) == 1:
            return others[0][rows * which : rows * (which + 1), :]
        return others[which][...]

    for which, gain_ref, w_ref, low_ref, out_ref in (
        (0, kv_gain_ref, w_kv_ref, src_ref, pair_ref),
        (1, attn_gain_ref, wq_ref, hid_ref, query_ref),
    ):
        for side in range(2):
            here = slice(rows * side, rows * (side + 1))
            values = other_rows(which) if side else held_ref[rows * which : rows * (which + 1), :]
            values = values.astype(jnp.float32)
            low_ref[here, :] = (values * inverse_scale(values) * gain_ref[...]).astype(jnp.bfloat16)
        out_ref[...] = product(low_ref[...], w_ref[...]).astype(jnp.bfloat16)


def project(piece, kv_gain, attn_gain, w_kv, wq, cost):
    rows, width = piece[0].shape
    low = piece[0].dtype
    return pl.pallas_call(
        project_kernel,
        out_shape=[
            jax.ShapeDtypeStruct((rows, width), low),
            jax.ShapeDtypeStruct((rows, width), low),
            jax.ShapeDtypeStruct((rows, w_kv.shape[1]), low),
            jax.ShapeDtypeStruct((rows, wq.shape[1]), low),
        ],
        compiler_params=pltpu.CompilerParams(vmem_limit_bytes=40 * 2**20),
        cost_estimate=cost,
        name="project",
    )(*piece, kv_gain, attn_gain, w_kv, wq)


def terms_kernel(step, result_step, pair_ref, query_ref, w_kv_ref, wq_ref, *refs):
    own_ref, other_ref = refs[-2:]
    count = pair_ref.shape[0] // 4
    here = slice(count * step, count * (step + 1))
    found = [
        rows_by_rows(pair_ref[here, :], w_kv_ref[...]),
        rows_by_rows(query_ref[here, :], wq_ref[...]),
    ]
    if len(refs) > 2:
        there = slice(count * result_step, count * (result_step + 1))
        found.append(product(refs[0][there, :], refs[1][...]))
    rows = count // 2
    for place, value in enumerate(found):
        value = value.astype(jnp.bfloat16)
        own_ref[rows * place : rows * (place + 1), :] = value[:rows]
        other_ref[rows * place : rows * (place + 1), :] = value[rows:]


def back_terms(parts, step, d_pairs, d_queries, w_kv, wq, result=()):
    rows, width = d_pairs.shape[0] // 4, w_kv.shape[0]
    result_step, *weights = result or (None,)
    count = rows // 2
    out = jax.ShapeDtypeStruct((count * len(parts), width), jnp.bfloat16)
    own, other = pl.pallas_call(
        functools.partial(terms_kernel, step, result_step),
        out_shape=[out, out],
        compiler_params=pltpu.CompilerParams(vmem_limit_bytes=40 * 2**20),
        cost_estimate=FREE,
        name="back_terms",
    )(d_pairs, d_queries, w_kv, wq, *weights)
    return [
        part.of_rows(Rows(own, count * place, count), Rows(other, count * place, count))
        for place, part in enumerate(parts)
    ]


def row_blocks(rows, count):
    first = rows.start // count
    return pl.BlockSpec((count, rows.array.shape[1]), lambda i: (first + i, 0))


def result_kernel(middle_ref, live_ref, kept_ref, x_ref, ring_ref, out_ref):
    total = middle_ref[...] + kept_ref[...].astype(jnp.float32)
    total = total + x_ref[...].astype(jnp.float32) + ring_ref[...].astype(jnp.float32)
    out_ref[...] = (total * live_ref[...]).astype(jnp.bfloat16)


def result_of(middle, live, scatter):
    sums = [scatter.kept, *scatter.got]
    rows, width = middle.shape
    block = rows // 4
    return pl.pallas_call(
        result_kernel,
        grid=(4,),
        in_specs=[
            pl.BlockSpec((block, width), lambda i: (i, 0)),
            pl.BlockSpec((block, 1), lambda i: (i, 0)),
        ]
        + [row_blocks(part, block) for part in sums],
        out_specs=pl.BlockSpec((block, width), lambda i: (i, 0)),
        out_shape=jax.ShapeDtypeStruct((rows, width), jnp.bfloat16),
        compiler_params=pltpu.CompilerParams(vmem_limit_bytes=16 * 2**20),
        cost_estimate=FREE,
        name="result",
    )(middle, live, *(part.array for part in sums))


def input_grads_kernel(hidden_ref, source_ref, d_middle_ref, attn_gain_ref, kv_gain_ref, *refs):
    d_hid, d_src = (
        sum(ref[...].astype(jnp.float32) for ref in refs[first : first + 3]) for first in (0, 3)
    )
    hidden = hidden_ref[...].astype(jnp.float32)
    source = source_ref[...].astype(jnp.float32)
    refs[6][...] = (
        d_middle_ref[...] + norm_backward(hidden, inverse_scale(hidden), attn_gain_ref[...], d_hid)
    ).astype(jnp.bfloat16)
    refs[7][...] = norm_backward(
        source, inverse_scale(source), kv_gain_ref[...], d_src
    ).astype(jnp.bfloat16)


def input_grads(hidden, source, d_middle, attn_gain, kv_gain, d_hid, d_src):
    sums = [d_hid.kept, *d_hid.got, d_src.kept, *d_src.got]
    rows, width = hidden.shape
    block = rows // 4
    spec = pl.BlockSpec((block, width), lambda i: (i, 0))
    return pl.pallas_call(
        input_grads_kernel,
        grid=(4,),
        in_specs=[spec] * 3
        + [whole_block(attn_gain), whole_block(kv_gain)]
        + [row_blocks(part, block) for part in sums],
        out_specs=[spec, spec],
        out_shape=[jax.ShapeDtypeStruct((rows, width), jnp.bfloat16)] * 2,
        compiler_params=pltpu.CompilerParams(vmem_limit_bytes=16 * 2**20),
        cost_estimate=FREE,
        name="input_grads",
    )(hidden, source, d_middle, attn_gain, kv_gain, *(part.array for part in sums))


def add_kernel(*refs):
    count = len(refs) // 3
    for kept_ref, got_ref, out_ref in zip(refs[:count], refs[count : 2 * count], refs[2 * count :]):
        rows = out_ref.shape[0]
        out_ref[...] = kept_ref[:rows, :] + got_ref[:rows, :].astype(jnp.float32)


def add_all(kept, got, rows):
    width = kept[0].shape[1]
    block = width // 4
    count = len(kept)
    spec = pl.BlockSpec((got[0].shape[0], block), lambda i: (0, i))
    return pl.pallas_call(
        add_kernel,
        grid=(4,),
        in_specs=[spec] * (2 * count),
        out_specs=[pl.BlockSpec((rows, block), lambda i: (0, i))] * count,
        out_shape=[jax.ShapeDtypeStruct((rows, width), jnp.float32)] * count,
        compiler_params=pltpu.CompilerParams(vmem_limit_bytes=40 * 2**20),
        cost_estimate=LONG,
        name="add_all",
    )(*kept, *got)


def copy_kernel(dp_ref, in_ref, out_ref):
    out_ref[...] = in_ref[...]


def own_first(rows, dp):
    block = (rows.shape[0] // 4, rows.shape[1])
    return pl.pallas_call(
        copy_kernel,
        grid_spec=pltpu.PrefetchScalarGridSpec(
            num_scalar_prefetch=1,
            grid=(4,),
            in_specs=[pl.BlockSpec(block, lambda i, dp: (dp[0] ^ (2 * (i % 2) + i // 2), 0))],
            out_specs=pl.BlockSpec(block, lambda i, dp: (i, 0)),
        ),
        out_shape=jax.ShapeDtypeStruct(rows.shape, rows.dtype),
        compiler_params=pltpu.CompilerParams(vmem_limit_bytes=16 * 2**20),
        cost_estimate=FREE,
        name="own_first",
    )(dp.reshape(1).astype(jnp.int32), rows)


class ColumnGrads:
    def __init__(self, dp):
        self.dp = dp
        self.y, self.c = dp // 2, dp % 2

    def gain_core(self, gain, *gate):
        gain = gain.reshape(2, 2, -1)
        kept = lax.dynamic_index_in_dim(gain, self.c, 1, keepdims=False)
        given = lax.dynamic_index_in_dim(gain, 1 - self.c, 1, keepdims=False)
        self.gain = kept + core_swap(after(given, *gate))
        return [given]

    def gain_y(self, *gate):
        gain = after(self.gain, *gate)
        kept = lax.dynamic_index_in_dim(gain, self.y, 0, keepdims=False)
        given = lax.dynamic_index_in_dim(gain, 1 - self.y, 0, keepdims=False)
        self.gain = kept + y_swap(given)
        return [given]

    def along_core(self, sources, hiddens, d_queries, d_pairs):
        count, width = sources[0].shape
        block = width // 4
        mine = d_queries.shape[1]
        rows = d_queries.shape[0]

        def of_step(i):
            return 2 * (i % 2) + 1 - i // 2

        by_block = pl.BlockSpec((count, block), lambda i, dp: (0, dp[0] ^ of_step(i)))
        given, self.kept = pl.pallas_call(
            column_grads_kernel,
            grid_spec=pltpu.PrefetchScalarGridSpec(
                num_scalar_prefetch=1,
                grid=(4,),
                in_specs=[by_block] * 8
                + [
                    pl.BlockSpec((rows, mine), lambda i, dp: (0, 0)),
                    pl.BlockSpec((rows, 2 * mine), lambda i, dp: (0, 0)),
                ],
                out_specs=[
                    pl.BlockSpec((1, block, 3 * mine), lambda i, dp: (jnp.minimum(i, 1), 0, 0)),
                    pl.BlockSpec((1, block, 3 * mine), lambda i, dp: (jnp.maximum(i, 2) - 2, 0, 0)),
                ],
            ),
            out_shape=[
                jax.ShapeDtypeStruct((2, block, 3 * mine), jnp.bfloat16),
                jax.ShapeDtypeStruct((2, block, 3 * mine), jnp.float32),
            ],
            compiler_params=pltpu.CompilerParams(vmem_limit_bytes=40 * 2**20),
            cost_estimate=LONG,
            name="column_grads",
        )(self.dp.reshape(1).astype(jnp.int32), *sources, *hiddens, d_queries, d_pairs)
        self.from_core = core_swap(given)
        return [given]

    def along_y(self, *gate):
        given = self.kept[1] + after(self.from_core, *gate)[1].astype(jnp.float32)
        given = given.astype(jnp.bfloat16)
        self.from_y = y_swap(given)
        return [given]

    def along_fsdp(self, *gate):
        total = self.kept[0] + self.from_core[0].astype(jnp.float32)
        total = (total + after(self.from_y, *gate).astype(jnp.float32)).astype(jnp.bfloat16)
        each, columns = total.shape[0] // 8, total.shape[1]
        gain = self.gain.astype(jnp.bfloat16).reshape(8, 1, each)
        gain = jnp.pad(gain, ((0, 0), (0, 7), (0, columns - each)))
        given = jnp.concatenate([total.reshape(8, each, columns), gain], axis=1)
        self.got = lax.all_to_all(given, "fsdp", 0, 0, tiled=True)
        return [given], [self.got]

    def whole(self, weights, out_grads, *gate):
        each, width = weights[0].shape
        got, out_got = after((self.got, out_grads.from_x), *gate)
        flag = (out_grads.x == out_grads.y).astype(jnp.int32).reshape(1, 1)
        flat = jax.ShapeDtypeStruct((each, width), jnp.float32)
        column = jax.ShapeDtypeStruct((each, 1), jnp.float32)
        out = pl.pallas_call(
            own_grads_kernel,
            out_shape=[
                flat,
                flat,
                flat,
                column,
                column,
                jax.ShapeDtypeStruct((8, 128), jnp.float32),
                flat,
            ],
            compiler_params=pltpu.CompilerParams(vmem_limit_bytes=32 * 2**20),
            cost_estimate=FREE,
            name="own_grads",
        )(got, *weights, flag, out_grads.kept, out_got)
        return out, out[5][0, :each]


def out_rows(own, x, y, c, before, late):
    head = in_order(x, own, x_swap(own))
    pairs = [(place, place ^ 16) for place in range(32) if place // 16 == place % 2]
    got = lax.ppermute(after(head, *before), ("dp", "fsdp"), pairs)
    mine = jnp.where(x == y, head, after(got, *late))
    return in_order(c, mine, core_swap(mine))


class OutGrads:
    def __init__(self, grad, x, y, c):
        self.grad, self.x, self.y, self.c = grad, x, y, c

    def along_core(self, *gate):
        head, width = self.grad.shape[0] // 2, self.grad.shape[1]
        kept = lax.dynamic_slice(self.grad, (head * self.c, 0), (head, width))
        given = lax.dynamic_slice(self.grad, (head * (1 - self.c), 0), (head, width))
        given = after(given.astype(jnp.bfloat16), *gate)
        self.total = kept + core_swap(given).astype(jnp.float32)
        return [given]

    def along_y(self, *gate):
        pairs = [(place, place ^ 16) for place in range(32) if place // 16 != place % 2]
        given = after(self.total.astype(jnp.bfloat16), *gate)
        self.from_y = lax.ppermute(given, ("dp", "fsdp"), pairs)
        return [given]

    def along_x(self, *gate):
        total = self.total + after(self.from_y, *gate).astype(jnp.float32)
        each, width = total.shape[0] // 2, total.shape[1]
        self.kept = lax.dynamic_slice(total, (each * self.x, 0), (each, width))
        given = lax.dynamic_slice(total, (each * (1 - self.x), 0), (each, width))
        pairs = [(place, place ^ 1) for place in range(32) if place // 16 == place % 2]
        self.from_x = lax.ppermute(given.astype(jnp.bfloat16), ("dp", "fsdp"), pairs)


def hidden_units(own, padded, dp, *gate):
    rows = jnp.pad(own, ((0, padded - own.shape[0]), (0, 0)))
    return own_first(lax.all_gather(after(rows, *gate), "dp", axis=0, tiled=True), dp)


class HiddenGrads:
    def along_core(self, units, rows):
        self.units, self.rows = units, rows
        half = units.shape[1] // 2
        given = columns_by_columns(units[:, half:], rows).astype(jnp.bfloat16)
        self.from_core = core_swap(given)
        return [given]

    def along_y(self, *gate):
        half = self.units.shape[1] // 2
        units, got = after((self.units, self.from_core), *gate)
        total = columns_by_columns(units[:, :half], self.rows) + got.astype(jnp.float32)
        given = total[half // 2 :].astype(jnp.bfloat16)
        self.kept = total
        self.from_y = y_swap(given)
        return [given]


def fast_body(
    hidden,
    source,
    cotangent,
    row_counts,
    seq_lengths,
    kv_gain,
    w_key,
    w_value,
    attn_gain,
    w_query,
    w_out,
    ffn_gain,
    w_gate,
    w_up,
    w_down,
):
    local_rows, width = hidden.shape
    head = width // HEADS
    dp = lax.axis_index("dp")
    fsdp = lax.axis_index("fsdp")
    y, c = dp // 2, dp % 2
    z, x = fsdp // 2, fsdp % 2
    me = 8 * dp + fsdp

    order = z ^ (z >> 1)
    devices = []
    for step in range(4):
        place = (order - step) % 4
        for side in range(2):
            devices.append(2 * (place ^ (place >> 1)) + (x ^ side))
    slots = (
        jnp.stack(devices).astype(jnp.int32)[:, None] * local_rows
        + jnp.arange(local_rows, dtype=jnp.int32)[None, :]
    ).reshape(-1)
    live, position, sequence = slot_layout(row_counts, seq_lengths, slots, local_rows)
    starts = jnp.concatenate([jnp.zeros((1,), jnp.int32), jnp.cumsum(seq_lengths[0])])
    first = jnp.sum(
        jnp.where(
            sequence[:, None] == jnp.arange(starts.shape[0], dtype=jnp.int32)[None, :],
            starts[None, :],
            0,
        ),
        axis=1,
    )
    first, last = first[:, None], position[:, None]
    place_of_key = jnp.where(live, position, -1)[None, :]
    own_live = live[:local_rows].astype(jnp.float32)[:, None]

    def layout():
        return first, last, place_of_key, own_live

    each = kv_gain.shape[0]
    inputs = Gather(jnp.concatenate([source, hidden], axis=0))
    columns = Columns(
        [w_query, w_key, w_value], jnp.concatenate([kv_gain, attn_gain, ffn_gain]), dp
    )
    wa = columns.along_fsdp()
    s1 = move([inputs])
    wy = columns.along_y(*s1)
    s2 = move([inputs], *s1, *wa, *layout())
    wc = columns.along_core(*wy)
    s3 = move([inputs], *s2)
    wq, w_kv, gains = columns.whole()
    kv_gain_full, attn_gain_full, ffn_gain_full = (
        gains[:, which * each : (which + 1) * each].reshape(1, width) for which in range(3)
    )
    units = w_gate.shape[0]
    padded = -(-units // 64) * 64
    wg, wu, wd = (hidden_units(own, padded, dp, *s2, *wy) for own in (w_gate, w_up, w_down))

    hidden_f = hidden.astype(jnp.float32)
    d_out = cotangent.astype(jnp.float32) * own_live
    projected = []

    def project_piece(step, cost, *gate):
        piece = after(inputs.arrays(step), *(value[3] for value in projected[-1:]), *gate)
        projected.append(project(piece, kv_gain_full, attn_gain_full, w_kv, wq, cost))

    project_piece(0, FREE)
    project_piece(1, FREE)
    s4 = move([inputs], *s3)
    project_piece(2, LONG, *s3)
    cots = Gather(d_out.astype(jnp.bfloat16))
    c1 = move([cots], *s4, projected[2][3])
    project_piece(3, LONG)
    src_low, hid_low, pairs, queries = zip(*projected)
    queries = jnp.concatenate(queries, axis=0)
    pairs = jnp.concatenate(pairs, axis=0)
    c2 = move([cots], *c1, pairs, queries)
    attended_f, attended_low, lse = attend(
        *after((queries, pairs), *c1), first, last, place_of_key, head
    )
    wo = out_rows(after(w_out, *s3), x, y, c, s4, c1)

    def rows_of(array, step):
        return array[2 * step * local_rows : 2 * (step + 1) * local_rows]

    def branch_terms(step, *gate):
        return product(after(rows_of(attended_low, step), *gate), wo).astype(jnp.bfloat16)

    branch = Scatter()
    b1 = move([branch.of(branch_terms(1)), cots], *c2)
    b2 = move([branch.of(branch_terms(2)), cots], *b1)
    b3 = move([branch.of(branch_terms(3, *b1))], *b2)
    b4 = move([branch.of(branch_terms(0, *b2))], *b3)
    middle = hidden_f + branch.total()
    middle_scale = inverse_scale(middle)
    middle_unit = middle * middle_scale
    mids = Gather((middle_unit * ffn_gain_full).astype(jnp.bfloat16))

    inners, d_gates, d_ups = [], [], []

    def feed(step):
        mid = mids.piece(step)
        gate_value = rows_by_rows(mid, wg)
        up_value = rows_by_rows(mid, wu)
        sigmoid_gate = jax.nn.sigmoid(gate_value)
        swished = gate_value * sigmoid_gate
        d_inner = rows_by_rows(cots.piece(step), wd)
        inners.append((swished * up_value).astype(jnp.bfloat16))
        d_gates.append(
            (d_inner * up_value * sigmoid_gate * (1.0 + gate_value * (1.0 - sigmoid_gate))).astype(
                jnp.bfloat16
            )
        )
        d_ups.append((d_inner * swished).astype(jnp.bfloat16))
        return (product(d_gates[step], wg) + product(d_ups[step], wu)).astype(jnp.bfloat16)

    m1 = move([mids])
    m2 = move([mids], *m1)
    t0 = feed(0)
    m3 = move([mids], *m2, t0)
    t1 = feed(1)
    back = Scatter()
    d1 = move([mids, back.of(t1)], *m3)
    t2 = feed(2)
    d2 = move([back.of(t2)], *d1)
    t3 = feed(3)
    d3 = move([back.of(t3)], *d2)
    d_gates, d_ups, inners = (jnp.concatenate(value, axis=0) for value in (d_gates, d_ups, inners))
    all_mids = jnp.concatenate([mids.piece(step) for step in range(4)], axis=0)
    all_cots = jnp.concatenate([cots.piece(step) for step in range(4)], axis=0)
    gate_sums, up_sums, down_sums = (HiddenGrads() for which in range(3))
    h1 = gate_sums.along_core(after(d_gates, *d2), all_mids)
    d4 = move([back.of(t0)], *d3, *h1)
    h2 = up_sums.along_core(after(d_ups, *d3), all_mids)
    h3 = down_sums.along_core(after(inners, *d3), all_cots)
    d_normed = after(back.total(), *h2, *h3)
    d_middle = d_out + norm_backward(middle, middle_scale, ffn_gain_full, d_normed)
    d_branch_low = d_middle.astype(jnp.bfloat16)
    outs = Gather(d_branch_low)
    e1 = move([outs])
    h1 = gate_sums.along_y(d_branch_low)
    e2 = move([outs], *e1, *h1)
    h2 = up_sums.along_y(*e1)
    e3 = move([outs], *e2, *h2)
    h3 = down_sums.along_y(*e2)

    def result_terms(step, *gate):
        return product(after(rows_of(inners, step), *gate), wd).astype(jnp.bfloat16)

    result = Scatter()
    first_result = result_terms(1, *e2, *h3)
    ffn_gain_part = jnp.sum(after(d_normed * middle_unit, first_result), axis=0)
    e4 = move([outs, result.of(first_result)], *e3, ffn_gain_part, gate_sums.from_y)
    column_grads = ColumnGrads(dp)
    column_grads.gain_core(ffn_gain_part, *e3)
    column_grads.gain_y(*e4)
    d_branches = [outs.piece(step) for step in range(4)]
    d_attended = jnp.concatenate(
        [rows_by_rows(rows, wo).astype(jnp.bfloat16) for rows in d_branches], axis=0
    )
    o2 = move([result.of(result_terms(2, *e3))], *e4, up_sums.from_y, down_sums.from_y, column_grads.gain)
    d_queries, d_pairs = attend_back(
        queries, pairs, first, last, place_of_key, lse, attended_f, d_attended, head
    )
    d_queries, d_pairs = after((d_queries, d_pairs), *o2)
    d_src, d_hid = Scatter(), Scatter()

    def terms(step, *gate, result=()):
        parts = [d_src, d_hid, *result[:1]]
        rows = after((d_pairs, d_queries), *gate)
        weights = (*result[1:], inners, wd) if result else ()
        return back_terms(parts, step, *rows, w_kv, wq, weights)

    first_terms = terms(1)
    started = d_hid.own.array
    i1 = move(first_terms, *o2)
    sources, hiddens = after((tuple(src_low), tuple(hid_low)), started)
    column_grads.along_core(sources, hiddens, d_queries, d_pairs)
    py = column_grads.along_y()
    i2 = move(terms(2, started, result=(result, 3)), *i1)
    out_grads = OutGrads(
        columns_by_columns(after(attended_low, *i1), jnp.concatenate(d_branches, axis=0)), x, y, c
    )
    out_grads.along_core()
    oy = out_grads.along_y(column_grads.from_y)
    pz, got_z = column_grads.along_fsdp()
    i3 = move(terms(3, *i1, result=(result, 0)), *i2, *oy, *pz)
    out_grads.along_x(*i2)
    i4 = move(terms(0, *i2), *i3)
    grad_gate, grad_up, grad_down = add_all(
        *zip(
            *(
                (sums.kept, after(sums.from_y, *i3))
                for sums in (gate_sums, up_sums, down_sums)
            )
        ),
        units,
    )
    output = result_of(after(middle, grad_gate), own_live, result)
    own_grads, grad_ffn_gain = column_grads.whole([w_query, w_key, w_value], out_grads, grad_gate)
    grad_query, grad_key, grad_value, query_sum, pair_sum, gain_sum, grad_out = own_grads
    grad_attn_gain = query_sum[:, 0] / attn_gain.astype(jnp.float32)
    grad_kv_gain = pair_sum[:, 0] / kv_gain.astype(jnp.float32)

    grad_hidden, grad_source = input_grads(
        hidden, source, d_middle, attn_gain_full, kv_gain_full, d_hid, d_src
    )
    return (
        output,
        grad_hidden,
        grad_source,
        grad_kv_gain,
        grad_key,
        grad_value,
        grad_attn_gain,
        grad_query,
        grad_out,
        grad_ffn_gain,
        grad_gate,
        grad_up,
        grad_down,
    )


def solution(mesh):
    in_specs = (
        P(("dp", "fsdp"), None),
        P(("dp", "fsdp"), None),
        P(("dp", "fsdp"), None),
        P("dp", None),
        P("dp", None),
        P(("dp", "fsdp")),
        P(("dp", "fsdp"), None),
        P(("dp", "fsdp"), None),
        P(("dp", "fsdp")),
        P(("dp", "fsdp"), None),
        P(("dp", "fsdp"), None),
        P(("dp", "fsdp")),
        P(("dp", "fsdp"), None),
        P(("dp", "fsdp"), None),
        P(("dp", "fsdp"), None),
    )
    out_specs = (
        P(("dp", "fsdp"), None),
        P(("dp", "fsdp"), None),
        P(("dp", "fsdp"), None),
        P(("dp", "fsdp")),
        P(("dp", "fsdp"), None),
        P(("dp", "fsdp"), None),
        P(("dp", "fsdp")),
        P(("dp", "fsdp"), None),
        P(("dp", "fsdp"), None),
        P(("dp", "fsdp")),
        P(("dp", "fsdp"), None),
        P(("dp", "fsdp"), None),
        P(("dp", "fsdp"), None),
    )
    placed = (
        mesh.shape["dp"] == 4 and mesh.shape["fsdp"] == 8 and HEADS == 2 * mesh.shape["fsdp"]
    )
    chosen = fast_body if placed else body
    return jax.shard_map(chosen, mesh=mesh, in_specs=in_specs, out_specs=out_specs, check_vma=False)
```

```python
import functools
import math

import jax
import jax.numpy as jnp
from jax import lax
from jax.experimental import pallas as pl
from jax.experimental.pallas import tpu as pltpu
from jax.sharding import PartitionSpec as P

HEADS = 16


EPSILON = 1e-06
MASKED = -1000000000.0


def product(left, right):
    return jnp.dot(left, right, preferred_element_type=jnp.float32)


def rows_by_rows(left, right):
    return lax.dot_general(
        left, right, (((1,), (1,)), ((), ())), preferred_element_type=jnp.float32
    )


def columns_by_columns(left, right):
    return lax.dot_general(
        left, right, (((0,), (0,)), ((), ())), preferred_element_type=jnp.float32
    )


def inverse_scale(values):
    return lax.rsqrt(jnp.mean(values * values, axis=-1, keepdims=True) + EPSILON)


def norm_backward(values, scale, gain, d_normed):
    weighted = d_normed * gain
    return scale * weighted - values * scale**3 * jnp.mean(
        values * weighted, axis=-1, keepdims=True
    )


def slot_layout(row_counts, seq_lengths, slots, per_device):
    counts = row_counts[0]
    offsets = jnp.cumsum(counts) - counts
    device_of = slots // per_device
    within = slots - device_of * per_device
    picker = device_of[:, None] == jnp.arange(counts.shape[0], dtype=jnp.int32)[None, :]
    count_here = jnp.sum(jnp.where(picker, counts[None, :], 0), axis=1)
    offset_here = jnp.sum(jnp.where(picker, offsets[None, :], 0), axis=1)
    position = offset_here + within
    ends = jnp.cumsum(seq_lengths[0])
    sequence = jnp.sum((ends[None, :] <= position[:, None]).astype(jnp.int32), axis=1)
    return (within < count_here, position, sequence)


def body(
    hidden,
    source,
    cotangent,
    row_counts,
    seq_lengths,
    kv_gain,
    w_key,
    w_value,
    attn_gain,
    w_query,
    w_out,
    ffn_gain,
    w_gate,
    w_up,
    w_down,
):
    local_rows, model_width = hidden.shape
    group_rows = local_rows * lax.axis_size("fsdp")
    head_size = model_width // HEADS
    factor = 1.0 / math.sqrt(head_size)
    block_rows = math.gcd(group_rows, 512)
    block_count = group_rows // block_rows
    own_slots = lax.axis_index("fsdp") * local_rows + jnp.arange(local_rows, dtype=jnp.int32)
    query_live, query_position, query_sequence = slot_layout(
        row_counts, seq_lengths, own_slots, local_rows
    )
    key_live, key_position, key_sequence = slot_layout(
        row_counts, seq_lengths, jnp.arange(group_rows, dtype=jnp.int32), local_rows
    )
    live_column = query_live.astype(jnp.float32)[:, None]
    source_f = source.astype(jnp.float32)
    hidden_f = hidden.astype(jnp.float32)
    source_scale = inverse_scale(source_f)
    hidden_scale = inverse_scale(hidden_f)
    source_unit = source_f * source_scale
    hidden_unit = hidden_f * hidden_scale
    piece_kv_gain = lax.all_gather(kv_gain, ("dp", "fsdp"), axis=0, tiled=True)
    piece_key = lax.all_gather(w_key, ("dp", "fsdp"), axis=0, tiled=True)
    piece_value = lax.all_gather(w_value, ("dp", "fsdp"), axis=0, tiled=True)
    piece_attn_gain = lax.all_gather(attn_gain, ("dp", "fsdp"), axis=0, tiled=True)
    piece_query = lax.all_gather(w_query, ("dp", "fsdp"), axis=0, tiled=True)
    piece_ffn_gain = lax.all_gather(ffn_gain, ("dp", "fsdp"), axis=0, tiled=True)
    source_cols = (source_unit * piece_kv_gain.astype(jnp.float32)[None, :]).astype(jnp.bfloat16)
    hidden_cols = (hidden_unit * piece_attn_gain.astype(jnp.float32)[None, :]).astype(jnp.bfloat16)
    key_sum = product(source_cols, piece_key)
    value_sum = product(source_cols, piece_value)
    query_sum = product(hidden_cols, piece_query)
    stacked = jnp.stack([piece_kv_gain, piece_attn_gain, piece_ffn_gain]).astype(jnp.float32)
    gains = stacked
    key_sum, value_sum, query_sum, gains = (key_sum, value_sum, query_sum, gains)
    kv_gain_full, attn_gain_full, ffn_gain_full = (gains[0], gains[1], gains[2])
    keys_low = key_sum.astype(jnp.bfloat16)
    values_low = value_sum.astype(jnp.bfloat16)
    queries_low = query_sum.astype(jnp.bfloat16)
    group_keys, group_values = (
        lax.all_gather(keys_low, "fsdp", axis=0, tiled=True),
        lax.all_gather(values_low, "fsdp", axis=0, tiled=True),
    )
    blocks = (
        group_keys.reshape(block_count, block_rows, HEADS, head_size),
        group_values.reshape(block_count, block_rows, HEADS, head_size),
        key_live.reshape(block_count, block_rows),
        key_position.reshape(block_count, block_rows),
        key_sequence.reshape(block_count, block_rows),
    )
    query_heads = queries_low.reshape(local_rows, HEADS, head_size)

    def block_scores(key_block, live_block, position_block, sequence_block):
        scores = (
            jnp.einsum("qhd,khd->hqk", query_heads, key_block, preferred_element_type=jnp.float32)
            * factor
        )
        allowed = (
            live_block[None, :]
            & (sequence_block[None, :] == query_sequence[:, None])
            & (position_block[None, :] <= query_position[:, None])
        )
        return jnp.where(allowed[None], scores, MASKED)

    def running_total(running, key_block_set):
        largest, summed = running
        key_block, value_block, live_block, position_block, sequence_block = key_block_set
        masked = block_scores(key_block, live_block, position_block, sequence_block)
        new_largest = jnp.maximum(largest, jnp.max(masked, axis=-1))
        summed = summed * jnp.exp(largest - new_largest) + jnp.sum(
            jnp.exp(masked - new_largest[:, :, None]), axis=-1
        )
        return ((new_largest, summed), None)

    (largest, summed), unused = lax.scan(
        running_total,
        (
            jnp.full((HEADS, local_rows), MASKED, jnp.float32),
            jnp.zeros((HEADS, local_rows), jnp.float32),
        ),
        blocks,
    )
    log_total = largest + jnp.log(summed)

    def weighted_sum(running, key_block_set):
        key_block, value_block, live_block, position_block, sequence_block = key_block_set
        probs_low = jnp.exp(
            block_scores(key_block, live_block, position_block, sequence_block)
            - log_total[:, :, None]
        ).astype(jnp.bfloat16)
        return (
            running
            + jnp.einsum(
                "hqk,khd->qhd", probs_low, value_block, preferred_element_type=jnp.float32
            ),
            None,
        )

    attended_f, unused = lax.scan(
        weighted_sum, jnp.zeros((local_rows, HEADS, head_size), jnp.float32), blocks
    )
    attended_low = attended_f.reshape(local_rows, model_width).astype(jnp.bfloat16)
    branch = product(attended_low, lax.all_gather(w_out, ("dp", "fsdp"), axis=0, tiled=True))
    middle = hidden_f + branch
    middle_scale = inverse_scale(middle)
    middle_unit = middle * middle_scale
    middle_low = (middle_unit * ffn_gain_full).astype(jnp.bfloat16)
    piece_gate = lax.all_gather(w_gate, ("dp", "fsdp"), axis=0, tiled=True)
    piece_up = lax.all_gather(w_up, ("dp", "fsdp"), axis=0, tiled=True)
    piece_down = lax.all_gather(w_down, ("dp", "fsdp"), axis=0, tiled=True)
    gate_value = rows_by_rows(middle_low, piece_gate)
    up_value = rows_by_rows(middle_low, piece_up)
    inner = (jax.nn.silu(gate_value) * up_value).astype(jnp.bfloat16)
    ffn_result = product(inner, piece_down)
    output = ((middle + ffn_result) * live_column).astype(jnp.bfloat16)
    d_out = cotangent.astype(jnp.float32) * live_column
    d_out_low = d_out.astype(jnp.bfloat16)
    piece_gate = lax.all_gather(w_gate, ("dp", "fsdp"), axis=0, tiled=True)
    piece_up = lax.all_gather(w_up, ("dp", "fsdp"), axis=0, tiled=True)
    piece_down = lax.all_gather(w_down, ("dp", "fsdp"), axis=0, tiled=True)
    gate_value = rows_by_rows(middle_low, piece_gate)
    up_value = rows_by_rows(middle_low, piece_up)
    sigmoid_gate = jax.nn.sigmoid(gate_value)
    swished = gate_value * sigmoid_gate
    inner = (swished * up_value).astype(jnp.bfloat16)
    d_inner = rows_by_rows(d_out_low, piece_down)
    d_gate = (d_inner * up_value * sigmoid_gate * (1.0 + gate_value * (1.0 - sigmoid_gate))).astype(
        jnp.bfloat16
    )
    d_up = (d_inner * swished).astype(jnp.bfloat16)
    d_normed = product(d_gate, piece_gate) + product(d_up, piece_up)
    ffn_grads = lax.psum_scatter(
        jnp.stack(
            [
                columns_by_columns(d_gate, middle_low),
                columns_by_columns(d_up, middle_low),
                columns_by_columns(inner, d_out_low),
            ],
            axis=1,
        ),
        ("dp", "fsdp"),
        scatter_dimension=0,
        tiled=True,
    )
    ffn_gain_part = jnp.sum(d_normed * middle_unit, axis=0)
    d_middle = d_out + norm_backward(middle, middle_scale, ffn_gain_full, d_normed)
    d_branch_low = d_middle.astype(jnp.bfloat16)
    d_attended = rows_by_rows(
        d_branch_low, lax.all_gather(w_out, ("dp", "fsdp"), axis=0, tiled=True)
    )
    d_heads = d_attended.astype(jnp.bfloat16).reshape(local_rows, HEADS, head_size)
    delta = jnp.sum(d_heads.astype(jnp.float32) * attended_f, axis=-1).T

    def attention_backward(d_query_sum, key_block_set):
        key_block, value_block, live_block, position_block, sequence_block = key_block_set
        probs = jnp.exp(
            block_scores(key_block, live_block, position_block, sequence_block)
            - log_total[:, :, None]
        )
        probs_low = probs.astype(jnp.bfloat16)
        d_values = jnp.einsum(
            "hqk,qhd->khd", probs_low, d_heads, preferred_element_type=jnp.float32
        )
        d_probs = jnp.einsum(
            "qhd,khd->hqk", d_heads, value_block, preferred_element_type=jnp.float32
        )
        d_scores = (probs * (d_probs - delta[:, :, None])).astype(jnp.bfloat16)
        d_query_sum = d_query_sum + jnp.einsum(
            "hqk,khd->qhd", d_scores, key_block, preferred_element_type=jnp.float32
        )
        d_keys = (
            jnp.einsum("hqk,qhd->khd", d_scores, query_heads, preferred_element_type=jnp.float32)
            * factor
        )
        return (d_query_sum, jnp.stack([d_keys, d_values], axis=1))

    d_query_sum, key_terms = lax.scan(
        attention_backward, jnp.zeros((local_rows, HEADS, head_size), jnp.float32), blocks
    )
    key_grads = lax.psum_scatter(
        key_terms.reshape(group_rows, 2, model_width).astype(jnp.bfloat16),
        "fsdp",
        scatter_dimension=0,
        tiled=True,
    ).astype(jnp.float32)
    d_keys_low = key_grads[:, 0].astype(jnp.bfloat16)
    d_values_low = key_grads[:, 1].astype(jnp.bfloat16)
    d_queries_low = (d_query_sum * factor).reshape(local_rows, model_width).astype(jnp.bfloat16)
    piece_query = lax.all_gather(w_query, ("dp", "fsdp"), axis=0, tiled=True)
    piece_key = lax.all_gather(w_key, ("dp", "fsdp"), axis=0, tiled=True)
    piece_value = lax.all_gather(w_value, ("dp", "fsdp"), axis=0, tiled=True)
    hidden_part = rows_by_rows(d_queries_low, piece_query)
    source_part = rows_by_rows(d_keys_low, piece_key) + rows_by_rows(d_values_low, piece_value)
    input_back = jnp.stack([hidden_part, source_part])
    grad_hidden = (
        d_middle + norm_backward(hidden_f, hidden_scale, attn_gain_full, input_back[0])
    ).astype(jnp.bfloat16)
    grad_source = norm_backward(source_f, source_scale, kv_gain_full, input_back[1]).astype(
        jnp.bfloat16
    )
    attn_gain_part = jnp.sum(input_back[0] * hidden_unit, axis=0)
    kv_gain_part = jnp.sum(input_back[1] * source_unit, axis=0)
    source_low = (source_unit * kv_gain_full).astype(jnp.bfloat16)
    hidden_low = (hidden_unit * attn_gain_full).astype(jnp.bfloat16)
    hidden_part = hidden_low
    source_part = source_low
    layer_stack = lax.psum_scatter(
        jnp.stack(
            [
                columns_by_columns(hidden_part, d_queries_low),
                columns_by_columns(source_part, d_keys_low),
                columns_by_columns(source_part, d_values_low),
                columns_by_columns(attended_low, d_branch_low),
            ],
            axis=1,
        ),
        ("dp", "fsdp"),
        scatter_dimension=0,
        tiled=True,
    )
    grad_query, grad_key, grad_value, grad_out = (
        layer_stack[:, 0],
        layer_stack[:, 1],
        layer_stack[:, 2],
        layer_stack[:, 3],
    )
    grad_kv_gain, grad_attn_gain, grad_ffn_gain = (
        lax.psum_scatter(kv_gain_part, ("dp", "fsdp"), scatter_dimension=0, tiled=True),
        lax.psum_scatter(attn_gain_part, ("dp", "fsdp"), scatter_dimension=0, tiled=True),
        lax.psum_scatter(ffn_gain_part, ("dp", "fsdp"), scatter_dimension=0, tiled=True),
    )
    return (
        output,
        grad_hidden,
        grad_source,
        grad_kv_gain,
        grad_key,
        grad_value,
        grad_attn_gain,
        grad_query,
        grad_out,
        grad_ffn_gain,
        ffn_grads[:, 0],
        ffn_grads[:, 1],
        ffn_grads[:, 2],
    )


RING = (0, 1, 3, 2)
BLOCK = 256


def swap_pairs(size, mask):
    return [(place, place ^ mask) for place in range(size)]


def ring_pairs():
    return [
        (2 * RING[place] + x, 2 * RING[(place + 1) % 4] + x) for place in range(4) for x in range(2)
    ]


def x_swap(value):
    return lax.ppermute(value, "fsdp", swap_pairs(8, 1))


def ring_step(value):
    return lax.ppermute(value, "fsdp", ring_pairs())


def y_swap(value):
    return lax.ppermute(value, "dp", swap_pairs(4, 2))


def core_swap(value):
    return lax.ppermute(value, "dp", swap_pairs(4, 1))


def in_order(flag, first, second):
    swapped = flag == 1
    return jnp.concatenate(
        [jnp.where(swapped, second, first), jnp.where(swapped, first, second)], axis=0
    )


def after(value, *earlier):
    if not earlier:
        return value
    return lax.optimization_barrier((value, *earlier))[0]


FREE = pl.CostEstimate(flops=0, bytes_accessed=0, transcendentals=0)
LONG = pl.CostEstimate(flops=2 * 10**10, bytes_accessed=0, transcendentals=0)


class Rows:
    def __init__(self, array, start, count):
        self.array, self.start, self.count = array, start, count

    def part(self, start, count):
        return Rows(self.array, self.start + start, count)

    def value(self):
        if self.count == self.array.shape[0]:
            return self.array
        return self.array[self.start : self.start + self.count]


def rows_in(array):
    return Rows(array, 0, array.shape[0])


class Gather:
    def __init__(self, own):
        self.held = rows_in(own)
        self.pieces = []

    def send(self):
        if len(self.pieces) < 3:
            return [[self.held]], [[self.held]]
        half = self.held.count // 2
        return [[self.held.part(0, half)]], [[self.pieces[2][1].part(half, half)]]

    def take(self, from_x, from_ring):
        if len(self.pieces) < 3:
            self.pieces.append((self.held, from_x))
            self.held = from_ring
        else:
            self.pieces.append((self.held, from_x, from_ring))

    def arrays(self, step):
        return tuple(rows.value() for rows in self.pieces[step])

    def piece(self, step):
        return jnp.concatenate(self.arrays(step), axis=0)


class Scatter:
    def __init__(self):
        self.stage = 0

    def of(self, terms):
        rows = terms.shape[0] // 2
        return self.of_rows(Rows(terms, 0, rows), Rows(terms, rows, rows))

    def of_rows(self, own, other):
        self.own, self.other = own, other
        return self

    def send(self):
        own, other = self.own, self.other
        half = own.count // 2
        if self.stage == 0:
            given = [[other.part(0, half)]], [[other.part(half, half)]]
        elif self.stage == 1:
            kept, (from_x, from_ring) = self.kept, self.got
            given = (
                [[other.part(0, half)], [other.part(half, half), from_ring]],
                [[kept.part(0, half), from_x], [kept.part(half, half)]],
            )
        else:
            given = [[other]], [[self.kept, *self.got]]
        self.stage += 1
        self.kept = own
        return given

    def take(self, from_x, from_ring):
        self.got = (from_x, from_ring)

    def total(self):
        return sum(rows.value().astype(jnp.float32) for rows in (self.kept, *self.got))


def mix_kernel(plans, *refs):
    for plan, out_ref in zip(plans, refs[-len(plans) :]):
        first = 0
        for places, count in plan:
            values = [refs[index][start : start + count, :] for index, start in places]
            if len(values) > 1:
                values = [sum(value.astype(jnp.float32) for value in values)]
            out_ref[first : first + count, :] = values[0].astype(out_ref.dtype)
            first += count


def only_array(sums):
    array = sums[0][0].array
    first = 0
    for rows in sums:
        if len(rows) > 1 or rows[0].array is not array or rows[0].start != first:
            return None
        first += rows[0].count
    return array if first == array.shape[0] else None


def mixed(*all_sums):
    arrays = []
    plans = []
    for sums in all_sums:
        plan = []
        for rows in sums:
            places = []
            for part in rows:
                index = next((n for n, held in enumerate(arrays) if held is part.array), None)
                if index is None:
                    index = len(arrays)
                    arrays.append(part.array)
                places.append((index, part.start))
            plan.append((tuple(places), rows[0].count))
        plans.append(tuple(plan))
    width = arrays[0].shape[1]
    counts = [sum(count for places, count in plan) for plan in plans]
    return pl.pallas_call(
        functools.partial(mix_kernel, tuple(plans)),
        out_shape=[jax.ShapeDtypeStruct((count, width), jnp.bfloat16) for count in counts],
        compiler_params=pltpu.CompilerParams(vmem_limit_bytes=16 * 2**20),
        cost_estimate=FREE,
        name="mix",
    )(*arrays)


def move(parts, *gate, payload=None):
    sent = [part.send() for part in parts]
    x_sums, ring_sums = (sum((given[way] for given in sent), []) for way in range(2))
    along_x, along_ring = only_array(x_sums), only_array(ring_sums)
    if along_x is None and along_ring is None:
        along_x, along_ring = mixed(x_sums, ring_sums)
    elif along_x is None:
        (along_x,) = mixed(x_sums)
    elif along_ring is None:
        (along_ring,) = mixed(ring_sums)
    along_x, along_ring = after((along_x, along_ring), *gate)
    if payload is not None:
        payload += [along_x, along_ring]
    from_x, from_ring = x_swap(along_x), ring_step(along_ring)
    x_row = ring_row = 0
    for part, given in zip(parts, sent):
        x_count, ring_count = (sum(rows[0].count for rows in sums) for sums in given)
        part.take(Rows(from_x, x_row, x_count), Rows(from_ring, ring_row, ring_count))
        x_row, ring_row = x_row + x_count, ring_row + ring_count
    return [from_x, from_ring]


def attend_kernel(
    factor, q_ref, k_ref, v_ref, first_ref, last_ref, place_ref, att_ref, low_ref, lse_ref
):
    scores = rows_by_rows(q_ref[...], k_ref[...]) * factor
    places = place_ref[...]
    allowed = (places >= first_ref[...]) & (places <= last_ref[...])
    masked = jnp.where(allowed, scores, MASKED)
    largest = jnp.max(masked, axis=-1, keepdims=True)
    raised = jnp.exp(masked - largest)
    summed = jnp.sum(raised, axis=-1, keepdims=True)
    probs_low = (raised * (1.0 / summed)).astype(jnp.bfloat16)
    attended = product(probs_low, v_ref[...])
    att_ref[...] = attended
    low_ref[...] = attended.astype(jnp.bfloat16)
    lse_ref[...] = (largest + jnp.log(summed))[None]


def attend_back_kernel(
    factor,
    q_ref,
    k_ref,
    v_ref,
    first_ref,
    last_ref,
    place_ref,
    lse_ref,
    att_ref,
    d_att_ref,
    dq_ref,
    dkv_ref,
    dk_sum,
    dv_sum,
):
    head = pl.program_id(0)
    step = pl.program_id(1)
    size = q_ref.shape[1]
    mine = dkv_ref.shape[1] // 2

    @pl.when(step == 0)
    def _():
        dk_sum[...] = jnp.zeros_like(dk_sum)
        dv_sum[...] = jnp.zeros_like(dv_sum)

    queries = q_ref[...]
    keys = k_ref[...]
    d_att = d_att_ref[...]
    scores = rows_by_rows(queries, keys) * factor
    places = place_ref[...]
    allowed = (places >= first_ref[...]) & (places <= last_ref[...])
    probs = jnp.exp(jnp.where(allowed, scores, MASKED) - lse_ref[0])
    delta = jnp.sum(d_att.astype(jnp.float32) * att_ref[...], axis=-1, keepdims=True)
    d_probs = rows_by_rows(d_att, v_ref[...])
    d_scores = (probs * (d_probs - delta)).astype(jnp.bfloat16)
    dq_ref[...] = (product(d_scores, keys) * factor).astype(jnp.bfloat16)
    dk_sum[...] += columns_by_columns(d_scores, queries)
    dv_sum[...] += columns_by_columns(probs.astype(jnp.bfloat16), d_att)

    @pl.when(step == pl.num_programs(1) - 1)
    def _():
        first = pl.multiple_of(size * head, size)
        dkv_ref[:, pl.ds(first, size)] = (dk_sum[...] * factor).astype(jnp.bfloat16)
        dkv_ref[:, pl.ds(mine + first, size)] = dv_sum[...].astype(jnp.bfloat16)


def attend_specs(count, head):
    by_query = pl.BlockSpec((BLOCK, head), lambda h, i: (i, h))
    keys = pl.BlockSpec((count, head), lambda h, i: (0, h))
    values = pl.BlockSpec((count, head), lambda h, i: (0, 2 + h))
    bound = pl.BlockSpec((BLOCK, 1), lambda h, i: (i, 0))
    place = pl.BlockSpec((1, count), lambda h, i: (0, 0))
    lse = pl.BlockSpec((1, BLOCK, 1), lambda h, i: (h, i, 0))
    return by_query, keys, values, bound, place, lse


def attend(queries, pairs, first, last, place, head):
    count, width = queries.shape
    by_query, keys, values, bound, places, lse = attend_specs(count, head)
    return pl.pallas_call(
        functools.partial(attend_kernel, 1.0 / math.sqrt(head)),
        grid=(width // head, count // BLOCK),
        in_specs=[by_query, keys, values, bound, bound, places],
        out_specs=[by_query, by_query, lse],
        out_shape=[
            jax.ShapeDtypeStruct((count, width), jnp.float32),
            jax.ShapeDtypeStruct((count, width), jnp.bfloat16),
            jax.ShapeDtypeStruct((width // head, count, 1), jnp.float32),
        ],
        compiler_params=pltpu.CompilerParams(vmem_limit_bytes=20 * 2**20),
        cost_estimate=LONG,
        name="attend",
    )(queries, pairs, pairs, first, last, place)


def attend_back(queries, pairs, first, last, place, lse, attended, d_attended, head):
    count, width = queries.shape
    by_query, keys, values, bound, places, by_lse = attend_specs(count, head)
    return pl.pallas_call(
        functools.partial(attend_back_kernel, 1.0 / math.sqrt(head)),
        grid=(width // head, count // BLOCK),
        in_specs=[
            by_query,
            keys,
            values,
            bound,
            bound,
            places,
            by_lse,
            by_query,
            by_query,
        ],
        out_specs=[by_query, pl.BlockSpec((count, 2 * width), lambda h, i: (0, 0))],
        out_shape=[
            jax.ShapeDtypeStruct((count, width), jnp.bfloat16),
            jax.ShapeDtypeStruct((count, 2 * width), jnp.bfloat16),
        ],
        scratch_shapes=[pltpu.VMEM((count, head), jnp.float32)] * 2,
        compiler_params=pltpu.CompilerParams(vmem_limit_bytes=20 * 2**20),
        cost_estimate=LONG,
        name="attend_back",
    )(queries, pairs, pairs, first, last, place, lse, attended, d_attended)


def as_rows(values, columns):
    rows = 16 * -(-values.shape[0] // (16 * columns))
    return jnp.pad(values, (0, rows * columns - values.shape[0])).reshape(rows, columns)


def from_rows(rows, count):
    return rows.reshape(-1)[:count]


def heads_of(device, head):
    z, x = device // 2, device % 2
    return [slice(head * (8 * x + 4 * j + z), head * (8 * x + 4 * j + z + 1)) for j in range(2)]


def columns_kernel(dp_ref, *refs):
    held_refs = refs[:4]
    q_ref, kv_ref, gain_ref = refs[4:]
    each = q_ref.shape[0] // 8
    mine = q_ref.shape[1]
    rows = held_refs[0].shape[0] // 8
    extra = rows - 3 * each
    for mask, held_ref in enumerate(held_refs):

        @pl.when((dp_ref[0] ^ pl.program_id(0)) == mask)
        def _():
            for device in range(8):
                first = rows * device
                here = slice(each * device, each * (device + 1))
                q_ref[here, :] = held_ref[first : first + each, :]
                kv_ref[here, :mine] = held_ref[first + each : first + 2 * each, :]
                kv_ref[here, mine:] = held_ref[first + 2 * each : first + 3 * each, :]
                gain_ref[0, extra * device : extra * (device + 1), :] = held_ref[
                    first + 3 * each : first + rows, :
                ]


def payload_kernel(q_ref, k_ref, v_ref, gain_ref, out_ref):
    each = q_ref.shape[0]
    head = q_ref.shape[1] // 16
    rows = out_ref.shape[0] // 8
    for device in range(8):
        for which, w_ref in enumerate((q_ref, k_ref, v_ref)):
            first = rows * device + each * which
            for j, columns in enumerate(heads_of(device, head)):
                out_ref[first : first + each, head * j : head * (j + 1)] = w_ref[:, columns]
        out_ref[rows * device + 3 * each : rows * (device + 1), :] = gain_ref[...]


class Columns:
    def __init__(self, weights, gains, dp):
        self.weights, self.gains, self.dp = weights, gains, dp

    def along_fsdp(self, *gate):
        each, width = self.weights[0].shape
        extra = as_rows(self.gains, width // 8)
        given = pl.pallas_call(
            payload_kernel,
            out_shape=jax.ShapeDtypeStruct(
                (8 * (3 * each + extra.shape[0]), width // 8), self.weights[0].dtype
            ),
            compiler_params=pltpu.CompilerParams(vmem_limit_bytes=8 * 2**20),
            cost_estimate=LONG,
            name="payload",
        )(*self.weights, extra)
        self.held = lax.all_to_all(after(given, *gate), "fsdp", 0, 0, tiled=True)
        return [self.held]

    def along_y(self, *gate):
        held = after(self.held, *gate)
        got, other = y_swap(held), core_swap(held)
        self.held = [held, got, other]
        return [got, other]

    def along_core(self, *gate):
        held, got, other = after(tuple(self.held), *gate)
        last = core_swap(got)
        self.held = [held, other, got, last]
        return [last]

    def whole(self):
        each, width = self.weights[0].shape
        rows, mine = self.held[0].shape
        extra = rows - 24 * each
        block = 8 * each
        low = self.held[0].dtype
        wq, w_kv, gains = pl.pallas_call(
            columns_kernel,
            grid_spec=pltpu.PrefetchScalarGridSpec(
                num_scalar_prefetch=1,
                grid=(4,),
                in_specs=[pl.BlockSpec((rows, mine), lambda i, dp: (0, 0))] * 4,
                out_specs=[
                    pl.BlockSpec((block, mine), lambda i, dp: (i, 0)),
                    pl.BlockSpec((block, 2 * mine), lambda i, dp: (i, 0)),
                    pl.BlockSpec((1, extra, mine), lambda i, dp: (i, 0, 0)),
                ],
            ),
            out_shape=[
                jax.ShapeDtypeStruct((4 * block, mine), low),
                jax.ShapeDtypeStruct((4 * block, 2 * mine), low),
                jax.ShapeDtypeStruct((4, extra, mine), low),
            ],
            compiler_params=pltpu.CompilerParams(vmem_limit_bytes=16 * 2**20),
            cost_estimate=FREE,
            name="columns",
        )(self.dp.reshape(1).astype(jnp.int32), *self.held)
        gains = gains.reshape(32, -1)[:, : self.gains.shape[0]].astype(jnp.float32)
        return wq, w_kv, gains


def column_grads_kernel(dp_ref, *refs):
    sources, hiddens = refs[:4], refs[4:8]
    dq_ref, dkv_ref, *given_refs, kept_ref = refs[8:]
    count = sources[0].shape[0]
    mine = dq_ref.shape[1]
    for_q, for_kv = 0.0, 0.0
    for step in range(4):
        here = slice(count * step, count * (step + 1))
        for_q = for_q + columns_by_columns(hiddens[step][...], dq_ref[here, :])
        for_kv = for_kv + columns_by_columns(sources[step][...], dkv_ref[here, :])

    for place in range(2):

        @pl.when(pl.program_id(0) == place)
        def _():
            given_refs[2 * place][...] = for_q.astype(jnp.bfloat16)
            given_refs[2 * place + 1][...] = for_kv.astype(jnp.bfloat16)

    @pl.when(pl.program_id(0) >= 2)
    def _():
        kept_ref[0, :, :mine] = for_q
        kept_ref[0, :, mine:] = for_kv


def own_grads_kernel(
    got_ref,
    wq_ref,
    wk_ref,
    wv_ref,
    flag_ref,
    out_kept_ref,
    out_got_ref,
    q_ref,
    k_ref,
    v_ref,
    q_sum_ref,
    kv_sum_ref,
    gain_ref,
    out_ref,
):
    each = wq_ref.shape[0]
    gain = 0.0
    for device in range(8):
        gain = gain + got_ref[device, each : each + 16, :128].astype(jnp.float32)
    gain_ref[...] = gain
    out_ref[...] = jnp.where(
        flag_ref[...] != 0, out_kept_ref[...], out_got_ref[...].astype(jnp.float32)
    )
    head = wq_ref.shape[1] // 16
    sums = []
    for which, (w_ref, out_ref) in enumerate(((wq_ref, q_ref), (wk_ref, k_ref), (wv_ref, v_ref))):
        total = jnp.zeros((each, head), jnp.float32)
        for device in range(8):
            for j, columns in enumerate(heads_of(device, head)):
                first = head * (2 * which + j)
                grad = got_ref[device, :each, first : first + head].astype(jnp.float32)
                out_ref[:, columns] = grad
                total = total + grad * w_ref[:, columns].astype(jnp.float32)
        sums.append(jnp.sum(total, axis=1, keepdims=True))
    q_sum_ref[...] = sums[0]
    kv_sum_ref[...] = sums[1] + sums[2]


def whole_block(array):
    return pl.BlockSpec(array.shape, lambda *place: (0,) * array.ndim)


def project_kernel(held_ref, *refs):
    others = refs[:-8]
    kv_gain_ref, attn_gain_ref, w_kv_ref, wq_ref, src_ref, hid_ref, pair_ref, query_ref = refs[-8:]
    rows = src_ref.shape[0] // 2

    def other_rows(which):
        if len(others) == 1:
            return others[0][rows * which : rows * (which + 1), :]
        return others[which][...]

    for which, gain_ref, w_ref, low_ref, out_ref in (
        (0, kv_gain_ref, w_kv_ref, src_ref, pair_ref),
        (1, attn_gain_ref, wq_ref, hid_ref, query_ref),
    ):
        for side in range(2):
            here = slice(rows * side, rows * (side + 1))
            values = other_rows(which) if side else held_ref[rows * which : rows * (which + 1), :]
            values = values.astype(jnp.float32)
            low_ref[here, :] = (values * inverse_scale(values) * gain_ref[...]).astype(jnp.bfloat16)
        out_ref[...] = product(low_ref[...], w_ref[...]).astype(jnp.bfloat16)


def project(piece, kv_gain, attn_gain, w_kv, wq, cost):
    rows, width = piece[0].shape
    low = piece[0].dtype
    return pl.pallas_call(
        project_kernel,
        out_shape=[
            jax.ShapeDtypeStruct((rows, width), low),
            jax.ShapeDtypeStruct((rows, width), low),
            jax.ShapeDtypeStruct((rows, w_kv.shape[1]), low),
            jax.ShapeDtypeStruct((rows, wq.shape[1]), low),
        ],
        compiler_params=pltpu.CompilerParams(vmem_limit_bytes=16 * 2**20),
        cost_estimate=cost,
        name="project",
    )(*piece, kv_gain, attn_gain, w_kv, wq)


def terms_kernel(step, pair_ref, query_ref, w_kv_ref, wq_ref, *refs):
    own_ref, other_ref = refs[-2:]
    count = pair_ref.shape[0] // 4
    here = slice(count * step, count * (step + 1))
    found = [
        rows_by_rows(pair_ref[here, :], w_kv_ref[...]),
        rows_by_rows(query_ref[here, :], wq_ref[...]),
    ]
    if len(refs) > 2:
        found.append(product(refs[0][...], refs[1][...]))
    rows = count // 2
    for place, value in enumerate(found):
        value = value.astype(jnp.bfloat16)
        own_ref[rows * place : rows * (place + 1), :] = value[:rows]
        other_ref[rows * place : rows * (place + 1), :] = value[rows:]


def back_terms(parts, step, d_pairs, d_queries, w_kv, wq, result=()):
    rows, width = d_pairs.shape[0] // 4, w_kv.shape[0]
    count = rows // 2
    out = jax.ShapeDtypeStruct((count * len(parts), width), jnp.bfloat16)
    own, other = pl.pallas_call(
        functools.partial(terms_kernel, step),
        out_shape=[out, out],
        compiler_params=pltpu.CompilerParams(vmem_limit_bytes=20 * 2**20),
        cost_estimate=FREE,
        name="back_terms",
    )(d_pairs, d_queries, w_kv, wq, *result)
    return [
        part.of_rows(Rows(own, count * place, count), Rows(other, count * place, count))
        for place, part in enumerate(parts)
    ]


def row_blocks(rows, count):
    first = rows.start // count
    return pl.BlockSpec((count, rows.array.shape[1]), lambda i: (first + i, 0))


def result_kernel(middle_ref, live_ref, kept_ref, x_ref, ring_ref, out_ref):
    total = middle_ref[...] + kept_ref[...].astype(jnp.float32)
    total = total + x_ref[...].astype(jnp.float32) + ring_ref[...].astype(jnp.float32)
    out_ref[...] = (total * live_ref[...]).astype(jnp.bfloat16)


def result_of(middle, live, scatter):
    sums = [scatter.kept, *scatter.got]
    rows, width = middle.shape
    block = rows // 4
    return pl.pallas_call(
        result_kernel,
        grid=(4,),
        in_specs=[
            pl.BlockSpec((block, width), lambda i: (i, 0)),
            pl.BlockSpec((block, 1), lambda i: (i, 0)),
        ]
        + [row_blocks(part, block) for part in sums],
        out_specs=pl.BlockSpec((block, width), lambda i: (i, 0)),
        out_shape=jax.ShapeDtypeStruct((rows, width), jnp.bfloat16),
        compiler_params=pltpu.CompilerParams(vmem_limit_bytes=8 * 2**20),
        cost_estimate=FREE,
        name="result",
    )(middle, live, *(part.array for part in sums))


def input_grads_kernel(hidden_ref, source_ref, d_middle_ref, attn_gain_ref, kv_gain_ref, *refs):
    d_hid, d_src = (
        sum(ref[...].astype(jnp.float32) for ref in refs[first : first + 3]) for first in (0, 3)
    )
    hidden = hidden_ref[...].astype(jnp.float32)
    source = source_ref[...].astype(jnp.float32)
    refs[6][...] = (
        d_middle_ref[...] + norm_backward(hidden, inverse_scale(hidden), attn_gain_ref[...], d_hid)
    ).astype(jnp.bfloat16)
    refs[7][...] = norm_backward(
        source, inverse_scale(source), kv_gain_ref[...], d_src
    ).astype(jnp.bfloat16)


def input_grads(hidden, source, d_middle, attn_gain, kv_gain, d_hid, d_src):
    sums = [d_hid.kept, *d_hid.got, d_src.kept, *d_src.got]
    rows, width = hidden.shape
    block = rows // 4
    spec = pl.BlockSpec((block, width), lambda i: (i, 0))
    return pl.pallas_call(
        input_grads_kernel,
        grid=(4,),
        in_specs=[spec] * 3
        + [whole_block(attn_gain), whole_block(kv_gain)]
        + [row_blocks(part, block) for part in sums],
        out_specs=[spec, spec],
        out_shape=[jax.ShapeDtypeStruct((rows, width), jnp.bfloat16)] * 2,
        compiler_params=pltpu.CompilerParams(vmem_limit_bytes=56 * 2**20),
        cost_estimate=FREE,
        name="input_grads",
    )(hidden, source, d_middle, attn_gain, kv_gain, *(part.array for part in sums))


def feed_kernel(mid_plan, cot_plan, *refs):
    arrays = refs[:-10]
    wg_ref, wu_ref, wd_ref, inner_ref, d_gate_ref, d_up_ref, own_ref, other_ref = refs[-10:-2]
    for plan, rows_ref in ((mid_plan, refs[-2]), (cot_plan, refs[-1])):
        first = 0
        for index, start, count in plan:
            rows_ref[first : first + count, :] = arrays[index][start : start + count, :]
            first += count
    mid_ref, cot_ref = refs[-2:]
    hidden, width = wg_ref.shape
    for first in range(0, hidden, 256):
        here = slice(first, min(first + 256, hidden))
        gate_value = rows_by_rows(mid_ref[...], wg_ref[here, :])
        up_value = rows_by_rows(mid_ref[...], wu_ref[here, :])
        d_inner = rows_by_rows(cot_ref[...], wd_ref[here, :])
        sigmoid_gate = jax.nn.sigmoid(gate_value)
        swished = gate_value * sigmoid_gate
        inner_ref[:, here] = (swished * up_value).astype(jnp.bfloat16)
        d_gate_ref[:, here] = (
            d_inner * up_value * sigmoid_gate * (1.0 + gate_value * (1.0 - sigmoid_gate))
        ).astype(jnp.bfloat16)
        d_up_ref[:, here] = (d_inner * swished).astype(jnp.bfloat16)
    rows = own_ref.shape[0]
    for first in range(0, width, 512):
        here = slice(first, first + 512)
        terms = product(d_gate_ref[...], wg_ref[:, here]) + product(d_up_ref[...], wu_ref[:, here])
        terms = terms.astype(jnp.bfloat16)
        own_ref[:, here] = terms[:rows]
        other_ref[:, here] = terms[rows:]


def feed(mid, cot, wg, wu, wd):
    arrays = []
    plans = []
    for pieces in (mid, cot):
        plan = []
        for rows in pieces:
            index = next((n for n, held in enumerate(arrays) if held is rows.array), None)
            if index is None:
                index = len(arrays)
                arrays.append(rows.array)
            plan.append((index, rows.start, rows.count))
        plans.append(tuple(plan))
    count = sum(rows.count for rows in mid)
    hidden, width = wg.shape
    low = jax.ShapeDtypeStruct((count, hidden), jnp.bfloat16)
    terms = jax.ShapeDtypeStruct((count // 2, width), jnp.bfloat16)
    return pl.pallas_call(
        functools.partial(feed_kernel, *plans),
        out_shape=[low, low, low, terms, terms]
        + [jax.ShapeDtypeStruct((count, width), jnp.bfloat16)] * 2,
        compiler_params=pltpu.CompilerParams(vmem_limit_bytes=24 * 2**20),
        cost_estimate=LONG,
        name="feed",
    )(*arrays, wg, wu, wd)


def add_kernel(*refs):
    count = len(refs) // 3
    for kept_ref, got_ref, out_ref in zip(refs[:count], refs[count : 2 * count], refs[2 * count :]):
        total = kept_ref[...] + got_ref[...].astype(jnp.float32)
        out_ref[...] = total[: out_ref.shape[0]]


def add_all(kept, got, rows):
    width = kept[0].shape[1]
    block = width // 4
    count = len(kept)
    spec = pl.BlockSpec((got[0].shape[0], block), lambda i: (0, i))
    return pl.pallas_call(
        add_kernel,
        grid=(4,),
        in_specs=[spec] * (2 * count),
        out_specs=[pl.BlockSpec((rows, block), lambda i: (0, i))] * count,
        out_shape=[jax.ShapeDtypeStruct((rows, width), jnp.float32)] * count,
        compiler_params=pltpu.CompilerParams(vmem_limit_bytes=20 * 2**20),
        cost_estimate=LONG,
        name="add_all",
    )(*kept, *got)


def copy_kernel(dp_ref, in_ref, out_ref):
    out_ref[...] = in_ref[...]


def own_first(rows, dp):
    block = (rows.shape[0] // 4, rows.shape[1])
    return pl.pallas_call(
        copy_kernel,
        grid_spec=pltpu.PrefetchScalarGridSpec(
            num_scalar_prefetch=1,
            grid=(4,),
            in_specs=[pl.BlockSpec(block, lambda i, dp: (dp[0] ^ (2 * (i % 2) + i // 2), 0))],
            out_specs=pl.BlockSpec(block, lambda i, dp: (i, 0)),
        ),
        out_shape=jax.ShapeDtypeStruct(rows.shape, rows.dtype),
        compiler_params=pltpu.CompilerParams(vmem_limit_bytes=8 * 2**20),
        cost_estimate=FREE,
        name="own_first",
    )(dp.reshape(1).astype(jnp.int32), rows)


class ColumnGrads:
    def __init__(self, dp):
        self.dp = dp
        self.y, self.c = dp // 2, dp % 2

    def gain_core(self, gain, *gate):
        gain = gain.reshape(2, 2, -1)
        kept = lax.dynamic_index_in_dim(gain, self.c, 1, keepdims=False)
        given = lax.dynamic_index_in_dim(gain, 1 - self.c, 1, keepdims=False)
        self.gain = kept + core_swap(after(given, *gate))
        return [given]

    def gain_y(self, *gate):
        gain = after(self.gain, *gate)
        kept = lax.dynamic_index_in_dim(gain, self.y, 0, keepdims=False)
        given = lax.dynamic_index_in_dim(gain, 1 - self.y, 0, keepdims=False)
        self.gain = kept + y_swap(given)
        return [given]

    def along_core(self, sources, hiddens, d_queries, d_pairs):
        count, width = sources[0].shape
        block = width // 4
        mine = d_queries.shape[1]
        rows = d_queries.shape[0]

        def of_step(i):
            return 2 * (i % 2) + 1 - i // 2

        by_block = pl.BlockSpec((count, block), lambda i, dp: (0, dp[0] ^ of_step(i)))
        *given, self.kept = pl.pallas_call(
            column_grads_kernel,
            grid_spec=pltpu.PrefetchScalarGridSpec(
                num_scalar_prefetch=1,
                grid=(4,),
                in_specs=[by_block] * 8
                + [
                    pl.BlockSpec((rows, mine), lambda i, dp: (0, 0)),
                    pl.BlockSpec((rows, 2 * mine), lambda i, dp: (0, 0)),
                ],
                out_specs=[
                    *(
                        pl.BlockSpec((block, width_of * mine), lambda i, dp: (0, 0))
                        for width_of in (1, 2, 1, 2)
                    ),
                    pl.BlockSpec((1, block, 3 * mine), lambda i, dp: (jnp.maximum(i, 2) - 2, 0, 0)),
                ],
            ),
            out_shape=[
                *(
                    jax.ShapeDtypeStruct((block, width_of * mine), jnp.bfloat16)
                    for width_of in (1, 2, 1, 2)
                ),
                jax.ShapeDtypeStruct((2, block, 3 * mine), jnp.float32),
            ],
            compiler_params=pltpu.CompilerParams(vmem_limit_bytes=20 * 2**20),
            cost_estimate=LONG,
            name="column_grads",
        )(self.dp.reshape(1).astype(jnp.int32), *sources, *hiddens, d_queries, d_pairs)
        self.from_core = [core_swap(value) for value in given]
        return given

    def along_y(self, *gate):
        got = after(tuple(self.from_core[2:]), *gate)
        given = self.kept[1] + jnp.concatenate(got, axis=1).astype(jnp.float32)
        given = given.astype(jnp.bfloat16)
        self.from_y = y_swap(given)
        return [given]

    def along_fsdp(self, *gate):
        total = self.kept[0] + jnp.concatenate(self.from_core[:2], axis=1).astype(jnp.float32)
        total = (total + after(self.from_y, *gate).astype(jnp.float32)).astype(jnp.bfloat16)
        each, columns = total.shape[0] // 8, total.shape[1]
        gain = self.gain.astype(jnp.bfloat16).reshape(8, 1, each)
        gain = jnp.pad(gain, ((0, 0), (0, 15), (0, columns - each)))
        given = jnp.concatenate([total.reshape(8, each, columns), gain], axis=1)
        self.got = lax.all_to_all(given, "fsdp", 0, 0, tiled=True)
        return [given], [self.got]

    def whole(self, weights, out_grads, *gate):
        each, width = weights[0].shape
        got, out_got = after((self.got, out_grads.from_x), *gate)
        flag = (out_grads.x == out_grads.y).astype(jnp.int32).reshape(1, 1)
        flat = jax.ShapeDtypeStruct((each, width), jnp.float32)
        column = jax.ShapeDtypeStruct((each, 1), jnp.float32)
        out = pl.pallas_call(
            own_grads_kernel,
            out_shape=[
                flat,
                flat,
                flat,
                column,
                column,
                jax.ShapeDtypeStruct((16, 128), jnp.float32),
                flat,
            ],
            compiler_params=pltpu.CompilerParams(vmem_limit_bytes=8 * 2**20),
            cost_estimate=FREE,
            name="own_grads",
        )(got, *weights, flag, out_grads.kept, out_got)
        return out, out[5][0, :each]


def out_rows(own, x, y, c, before, late):
    head = in_order(x, own, x_swap(own))
    pairs = [(place, place ^ 16) for place in range(32) if place // 16 == place % 2]
    got = lax.ppermute(after(head, *before), ("dp", "fsdp"), pairs)
    mine = jnp.where(x == y, head, after(got, *late))
    return in_order(c, mine, core_swap(mine))


class OutGrads:
    def __init__(self, grad, x, y, c):
        self.grad, self.x, self.y, self.c = grad, x, y, c

    def along_core(self, *gate):
        head, width = self.grad.shape[0] // 2, self.grad.shape[1]
        kept = lax.dynamic_slice(self.grad, (head * self.c, 0), (head, width))
        given = lax.dynamic_slice(self.grad, (head * (1 - self.c), 0), (head, width))
        given = after(given.astype(jnp.bfloat16), *gate)
        self.total = kept + core_swap(given).astype(jnp.float32)
        return [given]

    def along_y(self, *gate):
        pairs = [(place, place ^ 16) for place in range(32) if place // 16 != place % 2]
        given = after(self.total.astype(jnp.bfloat16), *gate)
        self.from_y = lax.ppermute(given, ("dp", "fsdp"), pairs)
        return [given]

    def along_x(self, *gate):
        total = self.total + after(self.from_y, *gate).astype(jnp.float32)
        each, width = total.shape[0] // 2, total.shape[1]
        self.kept = lax.dynamic_slice(total, (each * self.x, 0), (each, width))
        given = lax.dynamic_slice(total, (each * (1 - self.x), 0), (each, width))
        pairs = [(place, place ^ 1) for place in range(32) if place // 16 == place % 2]
        self.from_x = lax.ppermute(given.astype(jnp.bfloat16), ("dp", "fsdp"), pairs)


def hidden_units(rows, dp, *gate):
    return own_first(lax.all_gather(after(rows, *gate), "dp", axis=0, tiled=True), dp)


def hidden_core_kernel(count, *refs):
    units, rows, out_refs = refs[:count], refs[count : 2 * count], refs[2 * count :]
    half = units[0].shape[1] // 2
    total = sum(
        columns_by_columns(unit_ref[:, half:], row_ref[...]) for unit_ref, row_ref in zip(units, rows)
    ).astype(jnp.bfloat16)
    out_refs[0][...] = total[: half // 2]
    out_refs[1][...] = total[half // 2 :]


def hidden_y_kernel(count, *refs):
    units, rows = refs[:count], refs[count : 2 * count]
    own_got_ref, y_got_ref, kept_ref, given_ref = refs[2 * count :]
    half = units[0].shape[1] // 2
    total = sum(
        columns_by_columns(unit_ref[:, :half], row_ref[...]) for unit_ref, row_ref in zip(units, rows)
    )
    kept_ref[...] = total[: half // 2] + own_got_ref[...].astype(jnp.float32)
    given = total[half // 2 :] + y_got_ref[...].astype(jnp.float32)
    given_ref[...] = given.astype(jnp.bfloat16)


def out_grad_kernel(att_ref, *refs):
    *rows, out_ref = refs
    count = rows[0].shape[0]
    out_ref[...] = sum(
        columns_by_columns(att_ref[count * place : count * (place + 1), :], row_ref[...])
        for place, row_ref in enumerate(rows)
    )


def out_grad(attended, pieces):
    width = pieces[0].shape[1]
    block = width // 2
    return pl.pallas_call(
        out_grad_kernel,
        grid=(2,),
        in_specs=[whole_block(attended)]
        + [pl.BlockSpec((rows.shape[0], block), lambda i: (0, i)) for rows in pieces],
        out_specs=pl.BlockSpec((attended.shape[1], block), lambda i: (0, i)),
        out_shape=jax.ShapeDtypeStruct((attended.shape[1], width), jnp.float32),
        compiler_params=pltpu.CompilerParams(vmem_limit_bytes=20 * 2**20),
        cost_estimate=FREE,
        name="out_grad",
    )(attended, *pieces)


class HiddenGrads:
    def __init__(self, units, rows):
        self.units, self.rows = list(units), list(rows)

    def call(self, kernel, got, outs, *gate):
        width = self.rows[0].shape[1]
        block = width // 2
        units = after(tuple(self.units), *gate)

        def spec(rows):
            return pl.BlockSpec((rows, block), lambda i: (0, i))

        return pl.pallas_call(
            functools.partial(kernel, len(self.units)),
            grid=(2,),
            in_specs=[whole_block(unit) for unit in units]
            + [spec(rows.shape[0]) for rows in self.rows]
            + [spec(rows.shape[0]) for rows in got],
            out_specs=[spec(rows) for rows, dtype in outs],
            out_shape=[jax.ShapeDtypeStruct((rows, width), dtype) for rows, dtype in outs],
            compiler_params=pltpu.CompilerParams(vmem_limit_bytes=24 * 2**20),
            cost_estimate=LONG,
            name="hidden_grads",
        )(*units, *self.rows, *got)

    def along_core(self, *gate):
        half = self.units[0].shape[1] // 2
        given = self.call(hidden_core_kernel, [], [(half // 2, jnp.bfloat16)] * 2, *gate)
        self.from_core = [core_swap(value) for value in given]
        return given

    def along_y(self, *gate):
        half = self.units[0].shape[1] // 2
        self.kept, given = self.call(
            hidden_y_kernel,
            self.from_core,
            [(half // 2, jnp.float32), (half // 2, jnp.bfloat16)],
            *gate,
        )
        self.from_y = y_swap(given)
        return [given]


def fast_body(
    hidden,
    source,
    cotangent,
    row_counts,
    seq_lengths,
    kv_gain,
    w_key,
    w_value,
    attn_gain,
    w_query,
    w_out,
    ffn_gain,
    w_gate,
    w_up,
    w_down,
):
    local_rows, width = hidden.shape
    head = width // HEADS
    dp = lax.axis_index("dp")
    fsdp = lax.axis_index("fsdp")
    y, c = dp // 2, dp % 2
    z, x = fsdp // 2, fsdp % 2
    me = 8 * dp + fsdp

    order = z ^ (z >> 1)
    devices = []
    for step in range(4):
        place = (order - step) % 4
        for side in range(2):
            devices.append(2 * (place ^ (place >> 1)) + (x ^ side))
    slots = (
        jnp.stack(devices).astype(jnp.int32)[:, None] * local_rows
        + jnp.arange(local_rows, dtype=jnp.int32)[None, :]
    ).reshape(-1)
    live, position, sequence = slot_layout(row_counts, seq_lengths, slots, local_rows)
    starts = jnp.concatenate([jnp.zeros((1,), jnp.int32), jnp.cumsum(seq_lengths[0])])
    first = jnp.sum(
        jnp.where(
            sequence[:, None] == jnp.arange(starts.shape[0], dtype=jnp.int32)[None, :],
            starts[None, :],
            0,
        ),
        axis=1,
    )
    first, last = first[:, None], position[:, None]
    place_of_key = jnp.where(live, position, -1)[None, :]
    own_live = live[:local_rows].astype(jnp.float32)[:, None]

    def layout():
        return first, last, place_of_key, own_live

    each = kv_gain.shape[0]
    inputs = Gather(jnp.concatenate([source, hidden], axis=0))
    columns = Columns(
        [w_query, w_key, w_value], jnp.concatenate([kv_gain, attn_gain, ffn_gain]), dp
    )
    wa = columns.along_fsdp()
    s1 = move([inputs])
    wy = columns.along_y(*s1)
    units = w_gate.shape[0]
    padded = -(-units // 64) * 64
    own_units = [
        jnp.pad(own, ((0, padded - units), (0, 0))) for own in (w_gate, w_up, w_down)
    ]
    s2 = move([inputs], *s1, *wa, *layout(), *own_units)
    wc = columns.along_core(*wy)
    s3 = move([inputs], *s2)
    wq, w_kv, gains = columns.whole()
    kv_gain_full, attn_gain_full, ffn_gain_full = (
        gains[:, which * each : (which + 1) * each].reshape(1, width) for which in range(3)
    )
    wg, wu, wd = (hidden_units(own, dp, *s2, *wy) for own in own_units)

    hidden_f = hidden.astype(jnp.float32)
    d_out = cotangent.astype(jnp.float32) * own_live
    projected = []

    def project_piece(step, cost, *gate):
        piece = after(inputs.arrays(step), *(value[3] for value in projected[-1:]), *gate)
        projected.append(project(piece, kv_gain_full, attn_gain_full, w_kv, wq, cost))

    project_piece(0, FREE)
    project_piece(1, FREE)
    s4 = move([inputs], *s3)
    project_piece(2, LONG, *s3)
    cots = Gather(d_out.astype(jnp.bfloat16))
    c1 = move([cots], *s4, projected[2][3])
    project_piece(3, LONG)
    src_low, hid_low, pairs, queries = zip(*projected)
    queries = jnp.concatenate(queries, axis=0)
    pairs = jnp.concatenate(pairs, axis=0)
    c2 = move([cots], *c1, pairs, queries)
    attended_f, attended_low, lse = attend(
        *after((queries, pairs), *c1), first, last, place_of_key, head
    )
    wo = out_rows(after(w_out, *s2), x, y, c, s3, c1)

    def rows_of(array, step):
        return array[2 * step * local_rows : 2 * (step + 1) * local_rows]

    def branch_terms(step, *gate):
        return product(after(rows_of(attended_low, step), *gate), wo).astype(jnp.bfloat16)

    branch = Scatter()
    b1 = move([branch.of(branch_terms(1)), cots], *c2)
    b2 = move([branch.of(branch_terms(2)), cots], *b1)
    b3 = move([branch.of(branch_terms(3, *b1))], *b2)
    b4 = move([branch.of(branch_terms(0, *b2))], *b3)
    middle = hidden_f + branch.total()
    middle_scale = inverse_scale(middle)
    middle_unit = middle * middle_scale
    mids = Gather((middle_unit * ffn_gain_full).astype(jnp.bfloat16))

    fed = []

    def feed_piece(step, *gate):
        weights = after((wg, wu, wd), *gate)
        fed.append(feed(mids.pieces[step], cots.pieces[step], *weights))

    def terms_of(step):
        own, other = fed[step][3:5]
        return back.of_rows(rows_in(own), rows_in(other))

    back = Scatter()
    m1 = move([mids])
    m2 = move([mids], *m1)
    feed_piece(0)
    m3 = move([mids], *m2, fed[0][0])
    feed_piece(1, *m2)
    d1 = move([mids, terms_of(1)], *m3)
    feed_piece(2, *m3)
    d2 = move([terms_of(2)], *d1)
    feed_piece(3, *d1)
    d3 = move([terms_of(3)], *d2)
    inners, d_gates, d_ups, _, _, all_mids, all_cots = zip(*fed)
    gate_sums = HiddenGrads(d_gates, all_mids)
    up_sums = HiddenGrads(d_ups, all_mids)
    down_sums = HiddenGrads(inners, all_cots)
    h1 = gate_sums.along_core(*d2)
    d4 = move([terms_of(0)], *d3, *h1)
    h2 = up_sums.along_core(*d3)
    d_normed = after(back.total(), *h2)
    d_middle = d_out + norm_backward(middle, middle_scale, ffn_gain_full, d_normed)
    d_branch_low = d_middle.astype(jnp.bfloat16)
    outs = Gather(d_branch_low)
    e1 = move([outs])
    def result_terms(step, *gate):
        return product(after(inners[step], *gate), wd).astype(jnp.bfloat16)

    h1 = gate_sums.along_y(d_branch_low)
    h3 = down_sums.along_core(*h1)
    e2 = move([outs], *e1, *h3)
    h2 = up_sums.along_y(*e1)
    first_result = result_terms(1, *e1, *h2)
    ffn_gain_part = jnp.sum(after(d_normed * middle_unit, first_result), axis=0)
    column_grads = ColumnGrads(dp)
    column_grads.gain_core(ffn_gain_part)
    column_grads.gain_y()
    e3 = move([outs], *e2, *h2, ffn_gain_part)
    h3 = down_sums.along_y(*e2)

    result = Scatter()
    e4 = move([outs, result.of(first_result)], *e3, *h3, gate_sums.from_y, column_grads.gain)
    d_branches = [outs.piece(step) for step in range(4)]
    d_attended = jnp.concatenate(
        [rows_by_rows(rows, wo).astype(jnp.bfloat16) for rows in d_branches], axis=0
    )
    o2 = move([result.of(result_terms(2, *e3))], *e4)
    d_queries, d_pairs = attend_back(
        queries, pairs, first, last, place_of_key, lse, attended_f, d_attended, head
    )
    d_queries, d_pairs = after((d_queries, d_pairs), *o2)
    d_src, d_hid = Scatter(), Scatter()

    def terms(step, *gate, result=()):
        parts = [d_src, d_hid, *result[:1]]
        rows = after((d_pairs, d_queries), *gate)
        weights = (inners[result[1]], wd) if result else ()
        return back_terms(parts, step, *rows, w_kv, wq, weights)

    first_terms = terms(1)
    started = d_hid.own.array
    sent = []
    i1 = move(first_terms, *o2, up_sums.from_y, down_sums.from_y, payload=sent)
    sources, hiddens = after((tuple(src_low), tuple(hid_low)), *sent)
    column_grads.along_core(sources, hiddens, d_queries, d_pairs)
    second_terms = terms(2, started, result=(result, 3))
    i2 = move(second_terms, *i1)
    py = column_grads.along_y()
    next_terms = terms(3, *py, result=(result, 0))
    out_grads = OutGrads(
        out_grad(after(attended_low, *py), d_branches),
        x,
        y,
        c,
    )
    out_grads.along_core()
    oy = out_grads.along_y(column_grads.from_y)
    pz, got_z = column_grads.along_fsdp()
    i3 = move(next_terms, *i2, *oy)
    out_grads.along_x(*i2)
    i4 = move(terms(0, *i2), *i3)
    grad_gate, grad_up, grad_down = add_all(
        *zip(
            *(
                (sums.kept, after(sums.from_y, *i3))
                for sums in (gate_sums, up_sums, down_sums)
            )
        ),
        units,
    )
    output = result_of(after(middle, grad_gate), own_live, result)
    own_grads, grad_ffn_gain = column_grads.whole([w_query, w_key, w_value], out_grads, grad_gate)
    grad_query, grad_key, grad_value, query_sum, pair_sum, gain_sum, grad_out = own_grads
    grad_attn_gain = query_sum[:, 0] / attn_gain.astype(jnp.float32)
    grad_kv_gain = pair_sum[:, 0] / kv_gain.astype(jnp.float32)

    grad_hidden, grad_source = input_grads(
        hidden, source, d_middle, attn_gain_full, kv_gain_full, d_hid, d_src
    )
    return (
        output,
        grad_hidden,
        grad_source,
        grad_kv_gain,
        grad_key,
        grad_value,
        grad_attn_gain,
        grad_query,
        grad_out,
        grad_ffn_gain,
        grad_gate,
        grad_up,
        grad_down,
    )


def solution(mesh):
    in_specs = (
        P(("dp", "fsdp"), None),
        P(("dp", "fsdp"), None),
        P(("dp", "fsdp"), None),
        P("dp", None),
        P("dp", None),
        P(("dp", "fsdp")),
        P(("dp", "fsdp"), None),
        P(("dp", "fsdp"), None),
        P(("dp", "fsdp")),
        P(("dp", "fsdp"), None),
        P(("dp", "fsdp"), None),
        P(("dp", "fsdp")),
        P(("dp", "fsdp"), None),
        P(("dp", "fsdp"), None),
        P(("dp", "fsdp"), None),
    )
    out_specs = (
        P(("dp", "fsdp"), None),
        P(("dp", "fsdp"), None),
        P(("dp", "fsdp"), None),
        P(("dp", "fsdp")),
        P(("dp", "fsdp"), None),
        P(("dp", "fsdp"), None),
        P(("dp", "fsdp")),
        P(("dp", "fsdp"), None),
        P(("dp", "fsdp"), None),
        P(("dp", "fsdp")),
        P(("dp", "fsdp"), None),
        P(("dp", "fsdp"), None),
        P(("dp", "fsdp"), None),
    )
    placed = (
        mesh.shape["dp"] == 4 and mesh.shape["fsdp"] == 8 and HEADS == 2 * mesh.shape["fsdp"]
    )
    chosen = fast_body if placed else body
    return jax.shard_map(chosen, mesh=mesh, in_specs=in_specs, out_specs=out_specs, check_vma=False)
```

```python
import functools
import math

import jax
import jax.numpy as jnp
from jax import lax
from jax.experimental import pallas as pl
from jax.experimental.pallas import tpu as pltpu
from jax.sharding import PartitionSpec as P

HEADS = 16


EPSILON = 1e-06
MASKED = -1000000000.0


def product(left, right):
    return jnp.dot(left, right, preferred_element_type=jnp.float32)


def rows_by_rows(left, right):
    return lax.dot_general(
        left, right, (((1,), (1,)), ((), ())), preferred_element_type=jnp.float32
    )


def columns_by_columns(left, right):
    return lax.dot_general(
        left, right, (((0,), (0,)), ((), ())), preferred_element_type=jnp.float32
    )


def inverse_scale(values):
    return lax.rsqrt(jnp.mean(values * values, axis=-1, keepdims=True) + EPSILON)


def norm_backward(values, scale, gain, d_normed):
    weighted = d_normed * gain
    return scale * weighted - values * scale**3 * jnp.mean(
        values * weighted, axis=-1, keepdims=True
    )


def slot_layout(row_counts, seq_lengths, slots, per_device):
    counts = row_counts[0]
    offsets = jnp.cumsum(counts) - counts
    device_of = slots // per_device
    within = slots - device_of * per_device
    picker = device_of[:, None] == jnp.arange(counts.shape[0], dtype=jnp.int32)[None, :]
    count_here = jnp.sum(jnp.where(picker, counts[None, :], 0), axis=1)
    offset_here = jnp.sum(jnp.where(picker, offsets[None, :], 0), axis=1)
    position = offset_here + within
    ends = jnp.cumsum(seq_lengths[0])
    sequence = jnp.sum((ends[None, :] <= position[:, None]).astype(jnp.int32), axis=1)
    return (within < count_here, position, sequence)


def body(
    hidden,
    source,
    cotangent,
    row_counts,
    seq_lengths,
    kv_gain,
    w_key,
    w_value,
    attn_gain,
    w_query,
    w_out,
    ffn_gain,
    w_gate,
    w_up,
    w_down,
):
    local_rows, model_width = hidden.shape
    group_rows = local_rows * lax.axis_size("fsdp")
    head_size = model_width // HEADS
    factor = 1.0 / math.sqrt(head_size)
    block_rows = math.gcd(group_rows, 512)
    block_count = group_rows // block_rows
    own_slots = lax.axis_index("fsdp") * local_rows + jnp.arange(local_rows, dtype=jnp.int32)
    query_live, query_position, query_sequence = slot_layout(
        row_counts, seq_lengths, own_slots, local_rows
    )
    key_live, key_position, key_sequence = slot_layout(
        row_counts, seq_lengths, jnp.arange(group_rows, dtype=jnp.int32), local_rows
    )
    live_column = query_live.astype(jnp.float32)[:, None]
    source_f = source.astype(jnp.float32)
    hidden_f = hidden.astype(jnp.float32)
    source_scale = inverse_scale(source_f)
    hidden_scale = inverse_scale(hidden_f)
    source_unit = source_f * source_scale
    hidden_unit = hidden_f * hidden_scale
    piece_kv_gain = lax.all_gather(kv_gain, ("dp", "fsdp"), axis=0, tiled=True)
    piece_key = lax.all_gather(w_key, ("dp", "fsdp"), axis=0, tiled=True)
    piece_value = lax.all_gather(w_value, ("dp", "fsdp"), axis=0, tiled=True)
    piece_attn_gain = lax.all_gather(attn_gain, ("dp", "fsdp"), axis=0, tiled=True)
    piece_query = lax.all_gather(w_query, ("dp", "fsdp"), axis=0, tiled=True)
    piece_ffn_gain = lax.all_gather(ffn_gain, ("dp", "fsdp"), axis=0, tiled=True)
    source_cols = (source_unit * piece_kv_gain.astype(jnp.float32)[None, :]).astype(jnp.bfloat16)
    hidden_cols = (hidden_unit * piece_attn_gain.astype(jnp.float32)[None, :]).astype(jnp.bfloat16)
    key_sum = product(source_cols, piece_key)
    value_sum = product(source_cols, piece_value)
    query_sum = product(hidden_cols, piece_query)
    stacked = jnp.stack([piece_kv_gain, piece_attn_gain, piece_ffn_gain]).astype(jnp.float32)
    gains = stacked
    key_sum, value_sum, query_sum, gains = (key_sum, value_sum, query_sum, gains)
    kv_gain_full, attn_gain_full, ffn_gain_full = (gains[0], gains[1], gains[2])
    keys_low = key_sum.astype(jnp.bfloat16)
    values_low = value_sum.astype(jnp.bfloat16)
    queries_low = query_sum.astype(jnp.bfloat16)
    group_keys, group_values = (
        lax.all_gather(keys_low, "fsdp", axis=0, tiled=True),
        lax.all_gather(values_low, "fsdp", axis=0, tiled=True),
    )
    blocks = (
        group_keys.reshape(block_count, block_rows, HEADS, head_size),
        group_values.reshape(block_count, block_rows, HEADS, head_size),
        key_live.reshape(block_count, block_rows),
        key_position.reshape(block_count, block_rows),
        key_sequence.reshape(block_count, block_rows),
    )
    query_heads = queries_low.reshape(local_rows, HEADS, head_size)

    def block_scores(key_block, live_block, position_block, sequence_block):
        scores = (
            jnp.einsum("qhd,khd->hqk", query_heads, key_block, preferred_element_type=jnp.float32)
            * factor
        )
        allowed = (
            live_block[None, :]
            & (sequence_block[None, :] == query_sequence[:, None])
            & (position_block[None, :] <= query_position[:, None])
        )
        return jnp.where(allowed[None], scores, MASKED)

    def running_total(running, key_block_set):
        largest, summed = running
        key_block, value_block, live_block, position_block, sequence_block = key_block_set
        masked = block_scores(key_block, live_block, position_block, sequence_block)
        new_largest = jnp.maximum(largest, jnp.max(masked, axis=-1))
        summed = summed * jnp.exp(largest - new_largest) + jnp.sum(
            jnp.exp(masked - new_largest[:, :, None]), axis=-1
        )
        return ((new_largest, summed), None)

    (largest, summed), unused = lax.scan(
        running_total,
        (
            jnp.full((HEADS, local_rows), MASKED, jnp.float32),
            jnp.zeros((HEADS, local_rows), jnp.float32),
        ),
        blocks,
    )
    log_total = largest + jnp.log(summed)

    def weighted_sum(running, key_block_set):
        key_block, value_block, live_block, position_block, sequence_block = key_block_set
        probs_low = jnp.exp(
            block_scores(key_block, live_block, position_block, sequence_block)
            - log_total[:, :, None]
        ).astype(jnp.bfloat16)
        return (
            running
            + jnp.einsum(
                "hqk,khd->qhd", probs_low, value_block, preferred_element_type=jnp.float32
            ),
            None,
        )

    attended_f, unused = lax.scan(
        weighted_sum, jnp.zeros((local_rows, HEADS, head_size), jnp.float32), blocks
    )
    attended_low = attended_f.reshape(local_rows, model_width).astype(jnp.bfloat16)
    branch = product(attended_low, lax.all_gather(w_out, ("dp", "fsdp"), axis=0, tiled=True))
    middle = hidden_f + branch
    middle_scale = inverse_scale(middle)
    middle_unit = middle * middle_scale
    middle_low = (middle_unit * ffn_gain_full).astype(jnp.bfloat16)
    piece_gate = lax.all_gather(w_gate, ("dp", "fsdp"), axis=0, tiled=True)
    piece_up = lax.all_gather(w_up, ("dp", "fsdp"), axis=0, tiled=True)
    piece_down = lax.all_gather(w_down, ("dp", "fsdp"), axis=0, tiled=True)
    gate_value = rows_by_rows(middle_low, piece_gate)
    up_value = rows_by_rows(middle_low, piece_up)
    inner = (jax.nn.silu(gate_value) * up_value).astype(jnp.bfloat16)
    ffn_result = product(inner, piece_down)
    output = ((middle + ffn_result) * live_column).astype(jnp.bfloat16)
    d_out = cotangent.astype(jnp.float32) * live_column
    d_out_low = d_out.astype(jnp.bfloat16)
    piece_gate = lax.all_gather(w_gate, ("dp", "fsdp"), axis=0, tiled=True)
    piece_up = lax.all_gather(w_up, ("dp", "fsdp"), axis=0, tiled=True)
    piece_down = lax.all_gather(w_down, ("dp", "fsdp"), axis=0, tiled=True)
    gate_value = rows_by_rows(middle_low, piece_gate)
    up_value = rows_by_rows(middle_low, piece_up)
    sigmoid_gate = jax.nn.sigmoid(gate_value)
    swished = gate_value * sigmoid_gate
    inner = (swished * up_value).astype(jnp.bfloat16)
    d_inner = rows_by_rows(d_out_low, piece_down)
    d_gate = (d_inner * up_value * sigmoid_gate * (1.0 + gate_value * (1.0 - sigmoid_gate))).astype(
        jnp.bfloat16
    )
    d_up = (d_inner * swished).astype(jnp.bfloat16)
    d_normed = product(d_gate, piece_gate) + product(d_up, piece_up)
    ffn_grads = lax.psum_scatter(
        jnp.stack(
            [
                columns_by_columns(d_gate, middle_low),
                columns_by_columns(d_up, middle_low),
                columns_by_columns(inner, d_out_low),
            ],
            axis=1,
        ),
        ("dp", "fsdp"),
        scatter_dimension=0,
        tiled=True,
    )
    ffn_gain_part = jnp.sum(d_normed * middle_unit, axis=0)
    d_middle = d_out + norm_backward(middle, middle_scale, ffn_gain_full, d_normed)
    d_branch_low = d_middle.astype(jnp.bfloat16)
    d_attended = rows_by_rows(
        d_branch_low, lax.all_gather(w_out, ("dp", "fsdp"), axis=0, tiled=True)
    )
    d_heads = d_attended.astype(jnp.bfloat16).reshape(local_rows, HEADS, head_size)
    delta = jnp.sum(d_heads.astype(jnp.float32) * attended_f, axis=-1).T

    def attention_backward(d_query_sum, key_block_set):
        key_block, value_block, live_block, position_block, sequence_block = key_block_set
        probs = jnp.exp(
            block_scores(key_block, live_block, position_block, sequence_block)
            - log_total[:, :, None]
        )
        probs_low = probs.astype(jnp.bfloat16)
        d_values = jnp.einsum(
            "hqk,qhd->khd", probs_low, d_heads, preferred_element_type=jnp.float32
        )
        d_probs = jnp.einsum(
            "qhd,khd->hqk", d_heads, value_block, preferred_element_type=jnp.float32
        )
        d_scores = (probs * (d_probs - delta[:, :, None])).astype(jnp.bfloat16)
        d_query_sum = d_query_sum + jnp.einsum(
            "hqk,khd->qhd", d_scores, key_block, preferred_element_type=jnp.float32
        )
        d_keys = (
            jnp.einsum("hqk,qhd->khd", d_scores, query_heads, preferred_element_type=jnp.float32)
            * factor
        )
        return (d_query_sum, jnp.stack([d_keys, d_values], axis=1))

    d_query_sum, key_terms = lax.scan(
        attention_backward, jnp.zeros((local_rows, HEADS, head_size), jnp.float32), blocks
    )
    key_grads = lax.psum_scatter(
        key_terms.reshape(group_rows, 2, model_width).astype(jnp.bfloat16),
        "fsdp",
        scatter_dimension=0,
        tiled=True,
    ).astype(jnp.float32)
    d_keys_low = key_grads[:, 0].astype(jnp.bfloat16)
    d_values_low = key_grads[:, 1].astype(jnp.bfloat16)
    d_queries_low = (d_query_sum * factor).reshape(local_rows, model_width).astype(jnp.bfloat16)
    piece_query = lax.all_gather(w_query, ("dp", "fsdp"), axis=0, tiled=True)
    piece_key = lax.all_gather(w_key, ("dp", "fsdp"), axis=0, tiled=True)
    piece_value = lax.all_gather(w_value, ("dp", "fsdp"), axis=0, tiled=True)
    hidden_part = rows_by_rows(d_queries_low, piece_query)
    source_part = rows_by_rows(d_keys_low, piece_key) + rows_by_rows(d_values_low, piece_value)
    input_back = jnp.stack([hidden_part, source_part])
    grad_hidden = (
        d_middle + norm_backward(hidden_f, hidden_scale, attn_gain_full, input_back[0])
    ).astype(jnp.bfloat16)
    grad_source = norm_backward(source_f, source_scale, kv_gain_full, input_back[1]).astype(
        jnp.bfloat16
    )
    attn_gain_part = jnp.sum(input_back[0] * hidden_unit, axis=0)
    kv_gain_part = jnp.sum(input_back[1] * source_unit, axis=0)
    source_low = (source_unit * kv_gain_full).astype(jnp.bfloat16)
    hidden_low = (hidden_unit * attn_gain_full).astype(jnp.bfloat16)
    hidden_part = hidden_low
    source_part = source_low
    layer_stack = lax.psum_scatter(
        jnp.stack(
            [
                columns_by_columns(hidden_part, d_queries_low),
                columns_by_columns(source_part, d_keys_low),
                columns_by_columns(source_part, d_values_low),
                columns_by_columns(attended_low, d_branch_low),
            ],
            axis=1,
        ),
        ("dp", "fsdp"),
        scatter_dimension=0,
        tiled=True,
    )
    grad_query, grad_key, grad_value, grad_out = (
        layer_stack[:, 0],
        layer_stack[:, 1],
        layer_stack[:, 2],
        layer_stack[:, 3],
    )
    grad_kv_gain, grad_attn_gain, grad_ffn_gain = (
        lax.psum_scatter(kv_gain_part, ("dp", "fsdp"), scatter_dimension=0, tiled=True),
        lax.psum_scatter(attn_gain_part, ("dp", "fsdp"), scatter_dimension=0, tiled=True),
        lax.psum_scatter(ffn_gain_part, ("dp", "fsdp"), scatter_dimension=0, tiled=True),
    )
    return (
        output,
        grad_hidden,
        grad_source,
        grad_kv_gain,
        grad_key,
        grad_value,
        grad_attn_gain,
        grad_query,
        grad_out,
        grad_ffn_gain,
        ffn_grads[:, 0],
        ffn_grads[:, 1],
        ffn_grads[:, 2],
    )


RING = (0, 1, 3, 2)
BLOCK = 256


def swap_pairs(size, mask):
    return [(place, place ^ mask) for place in range(size)]


def ring_pairs():
    return [
        (2 * RING[place] + x, 2 * RING[(place + 1) % 4] + x) for place in range(4) for x in range(2)
    ]


def x_swap(value):
    return lax.ppermute(value, "fsdp", swap_pairs(8, 1))


def ring_step(value):
    return lax.ppermute(value, "fsdp", ring_pairs())


def y_swap(value):
    return lax.ppermute(value, "dp", swap_pairs(4, 2))


def core_swap(value):
    return lax.ppermute(value, "dp", swap_pairs(4, 1))


def in_order(flag, first, second):
    swapped = flag == 1
    return jnp.concatenate(
        [jnp.where(swapped, second, first), jnp.where(swapped, first, second)], axis=0
    )


def after(value, *earlier):
    if not earlier:
        return value
    return lax.optimization_barrier((value, *earlier))[0]


FREE = pl.CostEstimate(flops=0, bytes_accessed=0, transcendentals=0)
LONG = pl.CostEstimate(flops=2 * 10**10, bytes_accessed=0, transcendentals=0)


class Rows:
    def __init__(self, array, start, count):
        self.array, self.start, self.count = array, start, count

    def part(self, start, count):
        return Rows(self.array, self.start + start, count)

    def value(self):
        if self.count == self.array.shape[0]:
            return self.array
        return self.array[self.start : self.start + self.count]


def rows_in(array):
    return Rows(array, 0, array.shape[0])


class Gather:
    def __init__(self, own):
        self.held = rows_in(own)
        self.pieces = []

    def send(self):
        if len(self.pieces) < 3:
            return [[self.held]], [[self.held]]
        half = self.held.count // 2
        return [[self.held.part(0, half)]], [[self.pieces[2][1].part(half, half)]]

    def take(self, from_x, from_ring):
        if len(self.pieces) < 3:
            self.pieces.append((self.held, from_x))
            self.held = from_ring
        else:
            self.pieces.append((self.held, from_x, from_ring))

    def arrays(self, step):
        return tuple(rows.value() for rows in self.pieces[step])

    def piece(self, step):
        return jnp.concatenate(self.arrays(step), axis=0)


class Scatter:
    def __init__(self):
        self.stage = 0

    def of(self, terms):
        rows = terms.shape[0] // 2
        return self.of_rows(Rows(terms, 0, rows), Rows(terms, rows, rows))

    def of_rows(self, own, other):
        self.own, self.other = own, other
        return self

    def send(self):
        own, other = self.own, self.other
        half = own.count // 2
        if self.stage == 0:
            given = [[other.part(0, half)]], [[other.part(half, half)]]
        elif self.stage == 1:
            kept, (from_x, from_ring) = self.kept, self.got
            given = (
                [[other.part(0, half)], [other.part(half, half), from_ring]],
                [[kept.part(0, half), from_x], [kept.part(half, half)]],
            )
        else:
            given = [[other]], [[self.kept, *self.got]]
        self.stage += 1
        self.kept = own
        return given

    def take(self, from_x, from_ring):
        self.got = (from_x, from_ring)

    def total(self):
        return sum(rows.value().astype(jnp.float32) for rows in (self.kept, *self.got))


def mix_kernel(plans, *refs):
    for plan, out_ref in zip(plans, refs[-len(plans) :]):
        first = 0
        for places, count in plan:
            values = [refs[index][start : start + count, :] for index, start in places]
            if len(values) > 1:
                values = [sum(value.astype(jnp.float32) for value in values)]
            out_ref[first : first + count, :] = values[0].astype(out_ref.dtype)
            first += count


def only_array(sums):
    array = sums[0][0].array
    first = 0
    for rows in sums:
        if len(rows) > 1 or rows[0].array is not array or rows[0].start != first:
            return None
        first += rows[0].count
    return array if first == array.shape[0] else None


def mixed(*all_sums):
    arrays = []
    plans = []
    for sums in all_sums:
        plan = []
        for rows in sums:
            places = []
            for part in rows:
                index = next((n for n, held in enumerate(arrays) if held is part.array), None)
                if index is None:
                    index = len(arrays)
                    arrays.append(part.array)
                places.append((index, part.start))
            plan.append((tuple(places), rows[0].count))
        plans.append(tuple(plan))
    width = arrays[0].shape[1]
    counts = [sum(count for places, count in plan) for plan in plans]
    return pl.pallas_call(
        functools.partial(mix_kernel, tuple(plans)),
        out_shape=[jax.ShapeDtypeStruct((count, width), jnp.bfloat16) for count in counts],
        compiler_params=pltpu.CompilerParams(vmem_limit_bytes=16 * 2**20),
        cost_estimate=FREE,
        name="mix",
    )(*arrays)


def move(parts, *gate, payload=None):
    sent = [part.send() for part in parts]
    x_sums, ring_sums = (sum((given[way] for given in sent), []) for way in range(2))
    along_x, along_ring = only_array(x_sums), only_array(ring_sums)
    if along_x is None and along_ring is None:
        along_x, along_ring = mixed(x_sums, ring_sums)
    elif along_x is None:
        (along_x,) = mixed(x_sums)
    elif along_ring is None:
        (along_ring,) = mixed(ring_sums)
    along_x, along_ring = after((along_x, along_ring), *gate)
    if payload is not None:
        payload += [along_x, along_ring]
    from_x, from_ring = x_swap(along_x), ring_step(along_ring)
    x_row = ring_row = 0
    for part, given in zip(parts, sent):
        x_count, ring_count = (sum(rows[0].count for rows in sums) for sums in given)
        part.take(Rows(from_x, x_row, x_count), Rows(from_ring, ring_row, ring_count))
        x_row, ring_row = x_row + x_count, ring_row + ring_count
    return [from_x, from_ring]


def attend_kernel(
    factor, q_ref, k_ref, v_ref, first_ref, last_ref, place_ref, att_ref, low_ref, lse_ref
):
    scores = rows_by_rows(q_ref[...], k_ref[...]) * factor
    places = place_ref[...]
    allowed = (places >= first_ref[...]) & (places <= last_ref[...])
    masked = jnp.where(allowed, scores, MASKED)
    largest = jnp.max(masked, axis=-1, keepdims=True)
    raised = jnp.exp(masked - largest)
    summed = jnp.sum(raised, axis=-1, keepdims=True)
    probs_low = (raised * (1.0 / summed)).astype(jnp.bfloat16)
    attended = product(probs_low, v_ref[...])
    att_ref[...] = attended
    low_ref[...] = attended.astype(jnp.bfloat16)
    lse_ref[...] = (largest + jnp.log(summed))[None]


def attend_back_kernel(
    factor,
    q_ref,
    k_ref,
    v_ref,
    first_ref,
    last_ref,
    place_ref,
    lse_ref,
    att_ref,
    d_att_ref,
    dq_ref,
    dkv_ref,
    dk_sum,
    dv_sum,
):
    head = pl.program_id(0)
    step = pl.program_id(1)
    size = q_ref.shape[1]
    mine = dkv_ref.shape[1] // 2

    @pl.when(step == 0)
    def _():
        dk_sum[...] = jnp.zeros_like(dk_sum)
        dv_sum[...] = jnp.zeros_like(dv_sum)

    queries = q_ref[...]
    keys = k_ref[...]
    d_att = d_att_ref[...]
    scores = rows_by_rows(queries, keys) * factor
    places = place_ref[...]
    allowed = (places >= first_ref[...]) & (places <= last_ref[...])
    probs = jnp.exp(jnp.where(allowed, scores, MASKED) - lse_ref[0])
    delta = jnp.sum(d_att.astype(jnp.float32) * att_ref[...], axis=-1, keepdims=True)
    d_probs = rows_by_rows(d_att, v_ref[...])
    d_scores = (probs * (d_probs - delta)).astype(jnp.bfloat16)
    dq_ref[...] = (product(d_scores, keys) * factor).astype(jnp.bfloat16)
    dk_sum[...] += columns_by_columns(d_scores, queries)
    dv_sum[...] += columns_by_columns(probs.astype(jnp.bfloat16), d_att)

    @pl.when(step == pl.num_programs(1) - 1)
    def _():
        first = pl.multiple_of(size * head, size)
        dkv_ref[:, pl.ds(first, size)] = (dk_sum[...] * factor).astype(jnp.bfloat16)
        dkv_ref[:, pl.ds(mine + first, size)] = dv_sum[...].astype(jnp.bfloat16)


def attend_specs(count, head):
    by_query = pl.BlockSpec((BLOCK, head), lambda h, i: (i, h))
    keys = pl.BlockSpec((count, head), lambda h, i: (0, h))
    values = pl.BlockSpec((count, head), lambda h, i: (0, 2 + h))
    bound = pl.BlockSpec((BLOCK, 1), lambda h, i: (i, 0))
    place = pl.BlockSpec((1, count), lambda h, i: (0, 0))
    lse = pl.BlockSpec((1, BLOCK, 1), lambda h, i: (h, i, 0))
    return by_query, keys, values, bound, place, lse


def attend(queries, pairs, first, last, place, head):
    count, width = queries.shape
    by_query, keys, values, bound, places, lse = attend_specs(count, head)
    return pl.pallas_call(
        functools.partial(attend_kernel, 1.0 / math.sqrt(head)),
        grid=(width // head, count // BLOCK),
        in_specs=[by_query, keys, values, bound, bound, places],
        out_specs=[by_query, by_query, lse],
        out_shape=[
            jax.ShapeDtypeStruct((count, width), jnp.float32),
            jax.ShapeDtypeStruct((count, width), jnp.bfloat16),
            jax.ShapeDtypeStruct((width // head, count, 1), jnp.float32),
        ],
        compiler_params=pltpu.CompilerParams(vmem_limit_bytes=20 * 2**20),
        cost_estimate=LONG,
        name="attend",
    )(queries, pairs, pairs, first, last, place)


def attend_back(queries, pairs, first, last, place, lse, attended, d_attended, head):
    count, width = queries.shape
    by_query, keys, values, bound, places, by_lse = attend_specs(count, head)
    return pl.pallas_call(
        functools.partial(attend_back_kernel, 1.0 / math.sqrt(head)),
        grid=(width // head, count // BLOCK),
        in_specs=[
            by_query,
            keys,
            values,
            bound,
            bound,
            places,
            by_lse,
            by_query,
            by_query,
        ],
        out_specs=[by_query, pl.BlockSpec((count, 2 * width), lambda h, i: (0, 0))],
        out_shape=[
            jax.ShapeDtypeStruct((count, width), jnp.bfloat16),
            jax.ShapeDtypeStruct((count, 2 * width), jnp.bfloat16),
        ],
        scratch_shapes=[pltpu.VMEM((count, head), jnp.float32)] * 2,
        compiler_params=pltpu.CompilerParams(vmem_limit_bytes=20 * 2**20),
        cost_estimate=LONG,
        name="attend_back",
    )(queries, pairs, pairs, first, last, place, lse, attended, d_attended)


def as_rows(values, columns):
    rows = 16 * -(-values.shape[0] // (16 * columns))
    return jnp.pad(values, (0, rows * columns - values.shape[0])).reshape(rows, columns)


def from_rows(rows, count):
    return rows.reshape(-1)[:count]


def heads_of(device, head):
    z, x = device // 2, device % 2
    return [slice(head * (8 * x + 4 * j + z), head * (8 * x + 4 * j + z + 1)) for j in range(2)]


def columns_kernel(dp_ref, *refs):
    held_refs = refs[:4]
    q_ref, kv_ref, gain_ref = refs[4:]
    each = q_ref.shape[0] // 8
    mine = q_ref.shape[1]
    rows = held_refs[0].shape[0] // 8
    extra = rows - 3 * each
    for mask, held_ref in enumerate(held_refs):

        @pl.when((dp_ref[0] ^ pl.program_id(0)) == mask)
        def _():
            for device in range(8):
                first = rows * device
                here = slice(each * device, each * (device + 1))
                q_ref[here, :] = held_ref[first : first + each, :]
                kv_ref[here, :mine] = held_ref[first + each : first + 2 * each, :]
                kv_ref[here, mine:] = held_ref[first + 2 * each : first + 3 * each, :]
                gain_ref[0, extra * device : extra * (device + 1), :] = held_ref[
                    first + 3 * each : first + rows, :
                ]


def payload_kernel(q_ref, k_ref, v_ref, gain_ref, out_ref):
    each = q_ref.shape[0]
    head = q_ref.shape[1] // 16
    rows = out_ref.shape[0] // 8
    for device in range(8):
        for which, w_ref in enumerate((q_ref, k_ref, v_ref)):
            first = rows * device + each * which
            for j, columns in enumerate(heads_of(device, head)):
                out_ref[first : first + each, head * j : head * (j + 1)] = w_ref[:, columns]
        out_ref[rows * device + 3 * each : rows * (device + 1), :] = gain_ref[...]


class Columns:
    def __init__(self, weights, gains, dp):
        self.weights, self.gains, self.dp = weights, gains, dp

    def along_fsdp(self, *gate):
        each, width = self.weights[0].shape
        extra = as_rows(self.gains, width // 8)
        given = pl.pallas_call(
            payload_kernel,
            out_shape=jax.ShapeDtypeStruct(
                (8 * (3 * each + extra.shape[0]), width // 8), self.weights[0].dtype
            ),
            compiler_params=pltpu.CompilerParams(vmem_limit_bytes=8 * 2**20),
            cost_estimate=LONG,
            name="payload",
        )(*self.weights, extra)
        self.held = lax.all_to_all(after(given, *gate), "fsdp", 0, 0, tiled=True)
        return [self.held]

    def along_y(self, *gate):
        held = after(self.held, *gate)
        got, other = y_swap(held), core_swap(held)
        self.held = [held, got, other]
        return [got, other]

    def along_core(self, *gate):
        held, got, other = after(tuple(self.held), *gate)
        last = core_swap(got)
        self.held = [held, other, got, last]
        return [last]

    def whole(self):
        each, width = self.weights[0].shape
        rows, mine = self.held[0].shape
        extra = rows - 24 * each
        block = 8 * each
        low = self.held[0].dtype
        wq, w_kv, gains = pl.pallas_call(
            columns_kernel,
            grid_spec=pltpu.PrefetchScalarGridSpec(
                num_scalar_prefetch=1,
                grid=(4,),
                in_specs=[pl.BlockSpec((rows, mine), lambda i, dp: (0, 0))] * 4,
                out_specs=[
                    pl.BlockSpec((block, mine), lambda i, dp: (i, 0)),
                    pl.BlockSpec((block, 2 * mine), lambda i, dp: (i, 0)),
                    pl.BlockSpec((1, extra, mine), lambda i, dp: (i, 0, 0)),
                ],
            ),
            out_shape=[
                jax.ShapeDtypeStruct((4 * block, mine), low),
                jax.ShapeDtypeStruct((4 * block, 2 * mine), low),
                jax.ShapeDtypeStruct((4, extra, mine), low),
            ],
            compiler_params=pltpu.CompilerParams(vmem_limit_bytes=16 * 2**20),
            cost_estimate=FREE,
            name="columns",
        )(self.dp.reshape(1).astype(jnp.int32), *self.held)
        gains = gains.reshape(32, -1)[:, : self.gains.shape[0]].astype(jnp.float32)
        return wq, w_kv, gains


def column_grads_kernel(dp_ref, *refs):
    sources, hiddens = refs[:4], refs[4:8]
    dq_ref, dkv_ref, *given_refs, kept_ref = refs[8:]
    count = sources[0].shape[0]
    mine = dq_ref.shape[1]
    for_q, for_kv = 0.0, 0.0
    for step in range(4):
        here = slice(count * step, count * (step + 1))
        for_q = for_q + columns_by_columns(hiddens[step][...], dq_ref[here, :])
        for_kv = for_kv + columns_by_columns(sources[step][...], dkv_ref[here, :])

    for place in range(2):

        @pl.when(pl.program_id(0) == place)
        def _():
            given_refs[2 * place][...] = for_q.astype(jnp.bfloat16)
            given_refs[2 * place + 1][...] = for_kv.astype(jnp.bfloat16)

    @pl.when(pl.program_id(0) >= 2)
    def _():
        kept_ref[0, :, :mine] = for_q
        kept_ref[0, :, mine:] = for_kv


def own_grads_kernel(
    got_ref,
    wq_ref,
    wk_ref,
    wv_ref,
    flag_ref,
    out_kept_ref,
    out_got_ref,
    q_ref,
    k_ref,
    v_ref,
    q_sum_ref,
    kv_sum_ref,
    gain_ref,
    out_ref,
):
    each = wq_ref.shape[0]
    gain = 0.0
    for device in range(8):
        gain = gain + got_ref[device, each : each + 16, :128].astype(jnp.float32)
    gain_ref[...] = gain
    out_ref[...] = jnp.where(
        flag_ref[...] != 0, out_kept_ref[...], out_got_ref[...].astype(jnp.float32)
    )
    head = wq_ref.shape[1] // 16
    sums = []
    for which, (w_ref, out_ref) in enumerate(((wq_ref, q_ref), (wk_ref, k_ref), (wv_ref, v_ref))):
        total = jnp.zeros((each, head), jnp.float32)
        for device in range(8):
            for j, columns in enumerate(heads_of(device, head)):
                first = head * (2 * which + j)
                grad = got_ref[device, :each, first : first + head].astype(jnp.float32)
                out_ref[:, columns] = grad
                total = total + grad * w_ref[:, columns].astype(jnp.float32)
        sums.append(jnp.sum(total, axis=1, keepdims=True))
    q_sum_ref[...] = sums[0]
    kv_sum_ref[...] = sums[1] + sums[2]


def whole_block(array):
    return pl.BlockSpec(array.shape, lambda *place: (0,) * array.ndim)


def project_kernel(held_ref, *refs):
    others = refs[:-8]
    kv_gain_ref, attn_gain_ref, w_kv_ref, wq_ref, src_ref, hid_ref, pair_ref, query_ref = refs[-8:]
    rows = src_ref.shape[0] // 2

    def other_rows(which):
        if len(others) == 1:
            return others[0][rows * which : rows * (which + 1), :]
        return others[which][...]

    for which, gain_ref, w_ref, low_ref, out_ref in (
        (0, kv_gain_ref, w_kv_ref, src_ref, pair_ref),
        (1, attn_gain_ref, wq_ref, hid_ref, query_ref),
    ):
        for side in range(2):
            here = slice(rows * side, rows * (side + 1))
            values = other_rows(which) if side else held_ref[rows * which : rows * (which + 1), :]
            values = values.astype(jnp.float32)
            low_ref[here, :] = (values * inverse_scale(values) * gain_ref[...]).astype(jnp.bfloat16)
        out_ref[...] = product(low_ref[...], w_ref[...]).astype(jnp.bfloat16)


def project(piece, kv_gain, attn_gain, w_kv, wq, cost):
    rows, width = piece[0].shape
    low = piece[0].dtype
    return pl.pallas_call(
        project_kernel,
        out_shape=[
            jax.ShapeDtypeStruct((rows, width), low),
            jax.ShapeDtypeStruct((rows, width), low),
            jax.ShapeDtypeStruct((rows, w_kv.shape[1]), low),
            jax.ShapeDtypeStruct((rows, wq.shape[1]), low),
        ],
        compiler_params=pltpu.CompilerParams(vmem_limit_bytes=16 * 2**20),
        cost_estimate=cost,
        name="project",
    )(*piece, kv_gain, attn_gain, w_kv, wq)


def terms_kernel(step, pair_ref, query_ref, w_kv_ref, wq_ref, *refs):
    own_ref, other_ref = refs[-2:]
    count = pair_ref.shape[0] // 4
    here = slice(count * step, count * (step + 1))
    found = [
        rows_by_rows(pair_ref[here, :], w_kv_ref[...]),
        rows_by_rows(query_ref[here, :], wq_ref[...]),
    ]
    if len(refs) > 2:
        found.append(product(refs[0][...], refs[1][...]))
    rows = count // 2
    for place, value in enumerate(found):
        value = value.astype(jnp.bfloat16)
        own_ref[rows * place : rows * (place + 1), :] = value[:rows]
        other_ref[rows * place : rows * (place + 1), :] = value[rows:]


def back_terms(parts, step, d_pairs, d_queries, w_kv, wq, result=()):
    rows, width = d_pairs.shape[0] // 4, w_kv.shape[0]
    count = rows // 2
    out = jax.ShapeDtypeStruct((count * len(parts), width), jnp.bfloat16)
    own, other = pl.pallas_call(
        functools.partial(terms_kernel, step),
        out_shape=[out, out],
        compiler_params=pltpu.CompilerParams(vmem_limit_bytes=20 * 2**20),
        cost_estimate=FREE,
        name="back_terms",
    )(d_pairs, d_queries, w_kv, wq, *result)
    return [
        part.of_rows(Rows(own, count * place, count), Rows(other, count * place, count))
        for place, part in enumerate(parts)
    ]


def row_blocks(rows, count):
    first = rows.start // count
    return pl.BlockSpec((count, rows.array.shape[1]), lambda i: (first + i, 0))


def result_kernel(middle_ref, live_ref, kept_ref, x_ref, ring_ref, out_ref):
    total = middle_ref[...] + kept_ref[...].astype(jnp.float32)
    total = total + x_ref[...].astype(jnp.float32) + ring_ref[...].astype(jnp.float32)
    out_ref[...] = (total * live_ref[...]).astype(jnp.bfloat16)


def result_of(middle, live, scatter):
    sums = [scatter.kept, *scatter.got]
    rows, width = middle.shape
    block = rows // 4
    return pl.pallas_call(
        result_kernel,
        grid=(4,),
        in_specs=[
            pl.BlockSpec((block, width), lambda i: (i, 0)),
            pl.BlockSpec((block, 1), lambda i: (i, 0)),
        ]
        + [row_blocks(part, block) for part in sums],
        out_specs=pl.BlockSpec((block, width), lambda i: (i, 0)),
        out_shape=jax.ShapeDtypeStruct((rows, width), jnp.bfloat16),
        compiler_params=pltpu.CompilerParams(vmem_limit_bytes=8 * 2**20),
        cost_estimate=FREE,
        name="result",
    )(middle, live, *(part.array for part in sums))


def input_grads_kernel(hidden_ref, source_ref, d_middle_ref, attn_gain_ref, kv_gain_ref, *refs):
    d_hid, d_src = (
        sum(ref[...].astype(jnp.float32) for ref in refs[first : first + 3]) for first in (0, 3)
    )
    hidden = hidden_ref[...].astype(jnp.float32)
    source = source_ref[...].astype(jnp.float32)
    refs[6][...] = (
        d_middle_ref[...] + norm_backward(hidden, inverse_scale(hidden), attn_gain_ref[...], d_hid)
    ).astype(jnp.bfloat16)
    refs[7][...] = norm_backward(
        source, inverse_scale(source), kv_gain_ref[...], d_src
    ).astype(jnp.bfloat16)


def input_grads(hidden, source, d_middle, attn_gain, kv_gain, d_hid, d_src):
    sums = [d_hid.kept, *d_hid.got, d_src.kept, *d_src.got]
    rows, width = hidden.shape
    block = rows // 4
    spec = pl.BlockSpec((block, width), lambda i: (i, 0))
    return pl.pallas_call(
        input_grads_kernel,
        grid=(4,),
        in_specs=[spec] * 3
        + [whole_block(attn_gain), whole_block(kv_gain)]
        + [row_blocks(part, block) for part in sums],
        out_specs=[spec, spec],
        out_shape=[jax.ShapeDtypeStruct((rows, width), jnp.bfloat16)] * 2,
        compiler_params=pltpu.CompilerParams(vmem_limit_bytes=56 * 2**20),
        cost_estimate=FREE,
        name="input_grads",
    )(hidden, source, d_middle, attn_gain, kv_gain, *(part.array for part in sums))


def feed_kernel(mid_plan, cot_plan, *refs):
    arrays = refs[:-10]
    wg_ref, wu_ref, wd_ref, inner_ref, d_gate_ref, d_up_ref, own_ref, other_ref = refs[-10:-2]
    for plan, rows_ref in ((mid_plan, refs[-2]), (cot_plan, refs[-1])):
        first = 0
        for index, start, count in plan:
            rows_ref[first : first + count, :] = arrays[index][start : start + count, :]
            first += count
    mid_ref, cot_ref = refs[-2:]
    hidden, width = wg_ref.shape
    for first in range(0, hidden, 256):
        here = slice(first, min(first + 256, hidden))
        gate_value = rows_by_rows(mid_ref[...], wg_ref[here, :])
        up_value = rows_by_rows(mid_ref[...], wu_ref[here, :])
        d_inner = rows_by_rows(cot_ref[...], wd_ref[here, :])
        sigmoid_gate = jax.nn.sigmoid(gate_value)
        swished = gate_value * sigmoid_gate
        inner_ref[:, here] = (swished * up_value).astype(jnp.bfloat16)
        d_gate_ref[:, here] = (
            d_inner * up_value * sigmoid_gate * (1.0 + gate_value * (1.0 - sigmoid_gate))
        ).astype(jnp.bfloat16)
        d_up_ref[:, here] = (d_inner * swished).astype(jnp.bfloat16)
    rows = own_ref.shape[0]
    for first in range(0, width, 512):
        here = slice(first, first + 512)
        terms = product(d_gate_ref[...], wg_ref[:, here]) + product(d_up_ref[...], wu_ref[:, here])
        terms = terms.astype(jnp.bfloat16)
        own_ref[:, here] = terms[:rows]
        other_ref[:, here] = terms[rows:]


def feed(mid, cot, wg, wu, wd):
    arrays = []
    plans = []
    for pieces in (mid, cot):
        plan = []
        for rows in pieces:
            index = next((n for n, held in enumerate(arrays) if held is rows.array), None)
            if index is None:
                index = len(arrays)
                arrays.append(rows.array)
            plan.append((index, rows.start, rows.count))
        plans.append(tuple(plan))
    count = sum(rows.count for rows in mid)
    hidden, width = wg.shape
    low = jax.ShapeDtypeStruct((count, hidden), jnp.bfloat16)
    terms = jax.ShapeDtypeStruct((count // 2, width), jnp.bfloat16)
    return pl.pallas_call(
        functools.partial(feed_kernel, *plans),
        out_shape=[low, low, low, terms, terms]
        + [jax.ShapeDtypeStruct((count, width), jnp.bfloat16)] * 2,
        compiler_params=pltpu.CompilerParams(vmem_limit_bytes=24 * 2**20),
        cost_estimate=LONG,
        name="feed",
    )(*arrays, wg, wu, wd)


def branch_back_kernel(plan, *refs):
    *arrays, wo_ref, rows_ref, att_ref = refs
    first = 0
    for (start, count), array in zip(plan, arrays):
        rows_ref[first : first + count, :] = array[start : start + count, :]
        first += count
    att_ref[...] = rows_by_rows(rows_ref[...], wo_ref[...]).astype(jnp.bfloat16)


def branch_back(pieces, wo):
    count = sum(rows.count for rows in pieces)
    return pl.pallas_call(
        functools.partial(branch_back_kernel, tuple((rows.start, rows.count) for rows in pieces)),
        out_shape=[
            jax.ShapeDtypeStruct((count, wo.shape[1]), jnp.bfloat16),
            jax.ShapeDtypeStruct((count, wo.shape[0]), jnp.bfloat16),
        ],
        compiler_params=pltpu.CompilerParams(vmem_limit_bytes=16 * 2**20),
        cost_estimate=FREE,
        name="branch_back",
    )(*(rows.array for rows in pieces), wo)


def add_kernel(*refs):
    count = len(refs) // 3
    for kept_ref, got_ref, out_ref in zip(refs[:count], refs[count : 2 * count], refs[2 * count :]):
        total = kept_ref[...] + got_ref[...].astype(jnp.float32)
        out_ref[...] = total[: out_ref.shape[0]]


def add_all(kept, got, rows):
    width = kept[0].shape[1]
    block = width // 4
    count = len(kept)
    spec = pl.BlockSpec((got[0].shape[0], block), lambda i: (0, i))
    return pl.pallas_call(
        add_kernel,
        grid=(4,),
        in_specs=[spec] * (2 * count),
        out_specs=[pl.BlockSpec((rows, block), lambda i: (0, i))] * count,
        out_shape=[jax.ShapeDtypeStruct((rows, width), jnp.float32)] * count,
        compiler_params=pltpu.CompilerParams(vmem_limit_bytes=20 * 2**20),
        cost_estimate=LONG,
        name="add_all",
    )(*kept, *got)


def copy_kernel(dp_ref, in_ref, out_ref):
    out_ref[...] = in_ref[...]


def own_first(rows, dp):
    block = (rows.shape[0] // 4, rows.shape[1])
    return pl.pallas_call(
        copy_kernel,
        grid_spec=pltpu.PrefetchScalarGridSpec(
            num_scalar_prefetch=1,
            grid=(4,),
            in_specs=[pl.BlockSpec(block, lambda i, dp: (dp[0] ^ (2 * (i % 2) + i // 2), 0))],
            out_specs=pl.BlockSpec(block, lambda i, dp: (i, 0)),
        ),
        out_shape=jax.ShapeDtypeStruct(rows.shape, rows.dtype),
        compiler_params=pltpu.CompilerParams(vmem_limit_bytes=8 * 2**20),
        cost_estimate=FREE,
        name="own_first",
    )(dp.reshape(1).astype(jnp.int32), rows)


class ColumnGrads:
    def __init__(self, dp):
        self.dp = dp
        self.y, self.c = dp // 2, dp % 2

    def gain_core(self, gain, *gate):
        gain = gain.reshape(2, 2, -1)
        kept = lax.dynamic_index_in_dim(gain, self.c, 1, keepdims=False)
        given = lax.dynamic_index_in_dim(gain, 1 - self.c, 1, keepdims=False)
        self.gain = kept + core_swap(after(given, *gate))
        return [given]

    def gain_y(self, *gate):
        gain = after(self.gain, *gate)
        kept = lax.dynamic_index_in_dim(gain, self.y, 0, keepdims=False)
        given = lax.dynamic_index_in_dim(gain, 1 - self.y, 0, keepdims=False)
        self.gain = kept + y_swap(given)
        return [given]

    def along_core(self, sources, hiddens, d_queries, d_pairs):
        count, width = sources[0].shape
        block = width // 4
        mine = d_queries.shape[1]
        rows = d_queries.shape[0]

        def of_step(i):
            return 2 * (i % 2) + 1 - i // 2

        by_block = pl.BlockSpec((count, block), lambda i, dp: (0, dp[0] ^ of_step(i)))
        *given, self.kept = pl.pallas_call(
            column_grads_kernel,
            grid_spec=pltpu.PrefetchScalarGridSpec(
                num_scalar_prefetch=1,
                grid=(4,),
                in_specs=[by_block] * 8
                + [
                    pl.BlockSpec((rows, mine), lambda i, dp: (0, 0)),
                    pl.BlockSpec((rows, 2 * mine), lambda i, dp: (0, 0)),
                ],
                out_specs=[
                    *(
                        pl.BlockSpec((block, width_of * mine), lambda i, dp: (0, 0))
                        for width_of in (1, 2, 1, 2)
                    ),
                    pl.BlockSpec((1, block, 3 * mine), lambda i, dp: (jnp.maximum(i, 2) - 2, 0, 0)),
                ],
            ),
            out_shape=[
                *(
                    jax.ShapeDtypeStruct((block, width_of * mine), jnp.bfloat16)
                    for width_of in (1, 2, 1, 2)
                ),
                jax.ShapeDtypeStruct((2, block, 3 * mine), jnp.float32),
            ],
            compiler_params=pltpu.CompilerParams(vmem_limit_bytes=20 * 2**20),
            cost_estimate=LONG,
            name="column_grads",
        )(self.dp.reshape(1).astype(jnp.int32), *sources, *hiddens, d_queries, d_pairs)
        self.from_core = [core_swap(value) for value in given]
        return given

    def along_y(self, *gate):
        got = after(tuple(self.from_core[2:]), *gate)
        given = self.kept[1] + jnp.concatenate(got, axis=1).astype(jnp.float32)
        given = given.astype(jnp.bfloat16)
        self.from_y = y_swap(given)
        return [given]

    def along_fsdp(self, *gate):
        total = self.kept[0] + jnp.concatenate(self.from_core[:2], axis=1).astype(jnp.float32)
        total = (total + after(self.from_y, *gate).astype(jnp.float32)).astype(jnp.bfloat16)
        each, columns = total.shape[0] // 8, total.shape[1]
        gain = self.gain.astype(jnp.bfloat16).reshape(8, 1, each)
        gain = jnp.pad(gain, ((0, 0), (0, 15), (0, columns - each)))
        given = jnp.concatenate([total.reshape(8, each, columns), gain], axis=1)
        self.got = lax.all_to_all(given, "fsdp", 0, 0, tiled=True)
        return [given], [self.got]

    def whole(self, weights, out_grads, *gate):
        each, width = weights[0].shape
        got, out_got = after((self.got, out_grads.from_x), *gate)
        flag = (out_grads.x == out_grads.y).astype(jnp.int32).reshape(1, 1)
        flat = jax.ShapeDtypeStruct((each, width), jnp.float32)
        column = jax.ShapeDtypeStruct((each, 1), jnp.float32)
        out = pl.pallas_call(
            own_grads_kernel,
            out_shape=[
                flat,
                flat,
                flat,
                column,
                column,
                jax.ShapeDtypeStruct((16, 128), jnp.float32),
                flat,
            ],
            compiler_params=pltpu.CompilerParams(vmem_limit_bytes=8 * 2**20),
            cost_estimate=FREE,
            name="own_grads",
        )(got, *weights, flag, out_grads.kept, out_got)
        return out, out[5][0, :each]


def out_rows(own, x, y, c, before, late):
    head = in_order(x, own, x_swap(own))
    pairs = [(place, place ^ 16) for place in range(32) if place // 16 == place % 2]
    got = lax.ppermute(after(head, *before), ("dp", "fsdp"), pairs)
    mine = jnp.where(x == y, head, after(got, *late))
    return in_order(c, mine, core_swap(mine))


class OutGrads:
    def __init__(self, grad, x, y, c):
        self.grad, self.x, self.y, self.c = grad, x, y, c

    def along_core(self, *gate):
        head, width = self.grad.shape[0] // 2, self.grad.shape[1]
        kept = lax.dynamic_slice(self.grad, (head * self.c, 0), (head, width))
        given = lax.dynamic_slice(self.grad, (head * (1 - self.c), 0), (head, width))
        given = after(given.astype(jnp.bfloat16), *gate)
        self.total = kept + core_swap(given).astype(jnp.float32)
        return [given]

    def along_y(self, *gate):
        pairs = [(place, place ^ 16) for place in range(32) if place // 16 != place % 2]
        given = after(self.total.astype(jnp.bfloat16), *gate)
        self.from_y = lax.ppermute(given, ("dp", "fsdp"), pairs)
        return [given]

    def along_x(self, *gate):
        total = self.total + after(self.from_y, *gate).astype(jnp.float32)
        each, width = total.shape[0] // 2, total.shape[1]
        self.kept = lax.dynamic_slice(total, (each * self.x, 0), (each, width))
        given = lax.dynamic_slice(total, (each * (1 - self.x), 0), (each, width))
        pairs = [(place, place ^ 1) for place in range(32) if place // 16 == place % 2]
        self.from_x = lax.ppermute(given.astype(jnp.bfloat16), ("dp", "fsdp"), pairs)


def hidden_units(rows, dp, *gate):
    return own_first(lax.all_gather(after(rows, *gate), "dp", axis=0, tiled=True), dp)


def hidden_core_kernel(count, *refs):
    units, rows, out_refs = refs[:count], refs[count : 2 * count], refs[2 * count :]
    half = units[0].shape[1] // 2
    total = sum(
        columns_by_columns(unit_ref[:, half:], row_ref[...]) for unit_ref, row_ref in zip(units, rows)
    ).astype(jnp.bfloat16)
    out_refs[0][...] = total[: half // 2]
    out_refs[1][...] = total[half // 2 :]


def hidden_y_kernel(count, *refs):
    units, rows = refs[:count], refs[count : 2 * count]
    own_got_ref, y_got_ref, kept_ref, given_ref = refs[2 * count :]
    half = units[0].shape[1] // 2
    total = sum(
        columns_by_columns(unit_ref[:, :half], row_ref[...]) for unit_ref, row_ref in zip(units, rows)
    )
    kept_ref[...] = total[: half // 2] + own_got_ref[...].astype(jnp.float32)
    given = total[half // 2 :] + y_got_ref[...].astype(jnp.float32)
    given_ref[...] = given.astype(jnp.bfloat16)


def out_grad_kernel(att_ref, *refs):
    *rows, out_ref = refs
    count = rows[0].shape[0]
    out_ref[...] = sum(
        columns_by_columns(att_ref[count * place : count * (place + 1), :], row_ref[...])
        for place, row_ref in enumerate(rows)
    )


def out_grad(attended, pieces):
    width = pieces[0].shape[1]
    block = width // 2
    return pl.pallas_call(
        out_grad_kernel,
        grid=(2,),
        in_specs=[whole_block(attended)]
        + [pl.BlockSpec((rows.shape[0], block), lambda i: (0, i)) for rows in pieces],
        out_specs=pl.BlockSpec((attended.shape[1], block), lambda i: (0, i)),
        out_shape=jax.ShapeDtypeStruct((attended.shape[1], width), jnp.float32),
        compiler_params=pltpu.CompilerParams(vmem_limit_bytes=20 * 2**20),
        cost_estimate=FREE,
        name="out_grad",
    )(attended, *pieces)


class HiddenGrads:
    def __init__(self, units, rows):
        self.units, self.rows = list(units), list(rows)

    def call(self, kernel, got, outs, *gate):
        width = self.rows[0].shape[1]
        block = width // 2
        units = after(tuple(self.units), *gate)

        def spec(rows):
            return pl.BlockSpec((rows, block), lambda i: (0, i))

        return pl.pallas_call(
            functools.partial(kernel, len(self.units)),
            grid=(2,),
            in_specs=[whole_block(unit) for unit in units]
            + [spec(rows.shape[0]) for rows in self.rows]
            + [spec(rows.shape[0]) for rows in got],
            out_specs=[spec(rows) for rows, dtype in outs],
            out_shape=[jax.ShapeDtypeStruct((rows, width), dtype) for rows, dtype in outs],
            compiler_params=pltpu.CompilerParams(vmem_limit_bytes=24 * 2**20),
            cost_estimate=LONG,
            name="hidden_grads",
        )(*units, *self.rows, *got)

    def along_core(self, *gate):
        half = self.units[0].shape[1] // 2
        given = self.call(hidden_core_kernel, [], [(half // 2, jnp.bfloat16)] * 2, *gate)
        self.from_core = [core_swap(value) for value in given]
        return given

    def along_y(self, *gate):
        half = self.units[0].shape[1] // 2
        self.kept, given = self.call(
            hidden_y_kernel,
            self.from_core,
            [(half // 2, jnp.float32), (half // 2, jnp.bfloat16)],
            *gate,
        )
        self.from_y = y_swap(given)
        return [given]


def fast_body(
    hidden,
    source,
    cotangent,
    row_counts,
    seq_lengths,
    kv_gain,
    w_key,
    w_value,
    attn_gain,
    w_query,
    w_out,
    ffn_gain,
    w_gate,
    w_up,
    w_down,
):
    local_rows, width = hidden.shape
    head = width // HEADS
    dp = lax.axis_index("dp")
    fsdp = lax.axis_index("fsdp")
    y, c = dp // 2, dp % 2
    z, x = fsdp // 2, fsdp % 2
    me = 8 * dp + fsdp

    order = z ^ (z >> 1)
    devices = []
    for step in range(4):
        place = (order - step) % 4
        for side in range(2):
            devices.append(2 * (place ^ (place >> 1)) + (x ^ side))
    slots = (
        jnp.stack(devices).astype(jnp.int32)[:, None] * local_rows
        + jnp.arange(local_rows, dtype=jnp.int32)[None, :]
    ).reshape(-1)
    live, position, sequence = slot_layout(row_counts, seq_lengths, slots, local_rows)
    starts = jnp.concatenate([jnp.zeros((1,), jnp.int32), jnp.cumsum(seq_lengths[0])])
    first = jnp.sum(
        jnp.where(
            sequence[:, None] == jnp.arange(starts.shape[0], dtype=jnp.int32)[None, :],
            starts[None, :],
            0,
        ),
        axis=1,
    )
    first, last = first[:, None], position[:, None]
    place_of_key = jnp.where(live, position, -1)[None, :]
    own_live = live[:local_rows].astype(jnp.float32)[:, None]

    d_out = cotangent.astype(jnp.float32) * own_live
    d_out_low = d_out.astype(jnp.bfloat16)
    layout = lax.optimization_barrier((first, last, place_of_key, own_live, d_out_low))
    first, last, place_of_key, own_live, d_out_low = layout

    each = kv_gain.shape[0]
    inputs = Gather(jnp.concatenate([source, hidden], axis=0))
    columns = Columns(
        [w_query, w_key, w_value], jnp.concatenate([kv_gain, attn_gain, ffn_gain]), dp
    )
    wa = columns.along_fsdp()
    s1 = move([inputs])
    wy = columns.along_y(*s1)
    units = w_gate.shape[0]
    padded = -(-units // 64) * 64
    own_units = [
        jnp.pad(own, ((0, padded - units), (0, 0))) for own in (w_gate, w_up, w_down)
    ]
    s2 = move([inputs], *s1, *wa, *layout, *own_units)
    wc = columns.along_core(*wy)
    s3 = move([inputs], *s2)
    wq, w_kv, gains = columns.whole()
    kv_gain_full, attn_gain_full, ffn_gain_full = (
        gains[:, which * each : (which + 1) * each].reshape(1, width) for which in range(3)
    )
    wg, wu, wd = (hidden_units(own, dp, *s2, *wy) for own in own_units)

    hidden_f = hidden.astype(jnp.float32)
    projected = []

    def project_piece(step, cost, *gate):
        piece = after(inputs.arrays(step), *(value[3] for value in projected[-1:]), *gate)
        projected.append(project(piece, kv_gain_full, attn_gain_full, w_kv, wq, cost))

    project_piece(0, FREE)
    project_piece(1, FREE)
    s4 = move([inputs], *s3)
    project_piece(2, LONG, *s3)
    cots = Gather(d_out_low)
    c1 = move([cots], *s4, projected[2][3])
    project_piece(3, LONG)
    src_low, hid_low, pairs, queries = zip(*projected)
    queries = jnp.concatenate(queries, axis=0)
    pairs = jnp.concatenate(pairs, axis=0)
    c2 = move([cots], *c1, pairs, queries)
    attended_f, attended_low, lse = attend(
        *after((queries, pairs), *c1), first, last, place_of_key, head
    )
    wo = out_rows(after(w_out, *s2), x, y, c, s3, c1)

    def rows_of(array, step):
        return array[2 * step * local_rows : 2 * (step + 1) * local_rows]

    def branch_terms(step, *gate):
        return product(after(rows_of(attended_low, step), *gate), wo).astype(jnp.bfloat16)

    branch = Scatter()
    b1 = move([branch.of(branch_terms(1)), cots], *c2)
    b2 = move([branch.of(branch_terms(2)), cots], *b1)
    b3 = move([branch.of(branch_terms(3, *b1))], *b2)
    b4 = move([branch.of(branch_terms(0, *b2))], *b3)
    middle = hidden_f + branch.total()
    middle_scale = inverse_scale(middle)
    middle_unit = middle * middle_scale
    mids = Gather((middle_unit * ffn_gain_full).astype(jnp.bfloat16))

    fed = []

    def feed_piece(step, *gate):
        weights = after((wg, wu, wd), *gate)
        fed.append(feed(mids.pieces[step], cots.pieces[step], *weights))

    def terms_of(step):
        own, other = fed[step][3:5]
        return back.of_rows(rows_in(own), rows_in(other))

    back = Scatter()
    m1 = move([mids])
    m2 = move([mids], *m1)
    feed_piece(0)
    m3 = move([mids], *m2, fed[0][0])
    feed_piece(1, *m2)
    d1 = move([mids, terms_of(1)], *m3)
    feed_piece(2, *m3)
    d2 = move([terms_of(2)], *d1)
    feed_piece(3, *d1)
    d3 = move([terms_of(3)], *d2)
    inners, d_gates, d_ups, _, _, all_mids, all_cots = zip(*fed)
    gate_sums = HiddenGrads(d_gates, all_mids)
    up_sums = HiddenGrads(d_ups, all_mids)
    down_sums = HiddenGrads(inners, all_cots)
    h1 = gate_sums.along_core(*d2)
    d4 = move([terms_of(0)], *d3, *h1)
    h2 = up_sums.along_core(*d3)
    d_normed = after(back.total(), *h2)
    d_middle = d_out + norm_backward(middle, middle_scale, ffn_gain_full, d_normed)
    d_branch_low = d_middle.astype(jnp.bfloat16)
    outs = Gather(d_branch_low)
    e1 = move([outs])
    def result_terms(step, *gate):
        return product(after(inners[step], *gate), wd).astype(jnp.bfloat16)

    h1 = gate_sums.along_y(d_branch_low)
    h3 = down_sums.along_core(*h1)
    e2 = move([outs], *e1, *h3)
    h2 = up_sums.along_y(*e1)
    first_result = result_terms(1, *e1, *h2)
    ffn_gain_part = jnp.sum(after(d_normed * middle_unit, first_result), axis=0)
    column_grads = ColumnGrads(dp)
    column_grads.gain_core(ffn_gain_part)
    column_grads.gain_y()
    e3 = move([outs], *e2, *h2, ffn_gain_part)
    h3 = down_sums.along_y(*e2)

    result = Scatter()
    e4 = move([outs, result.of(first_result)], *e3, *h3, gate_sums.from_y, column_grads.gain)
    d_branches, d_attended = zip(*(branch_back(outs.pieces[step], wo) for step in range(4)))
    d_attended = jnp.concatenate(d_attended, axis=0)
    o2 = move([result.of(result_terms(2, *e3))], *e4)
    d_queries, d_pairs = attend_back(
        queries, pairs, first, last, place_of_key, lse, attended_f, d_attended, head
    )
    d_queries, d_pairs = after((d_queries, d_pairs), *o2)
    d_src, d_hid = Scatter(), Scatter()

    def terms(step, *gate, result=()):
        parts = [d_src, d_hid, *result[:1]]
        rows = after((d_pairs, d_queries), *gate)
        weights = (inners[result[1]], wd) if result else ()
        return back_terms(parts, step, *rows, w_kv, wq, weights)

    first_terms = terms(1)
    started = d_hid.own.array
    sent = []
    i1 = move(first_terms, *o2, up_sums.from_y, payload=sent)
    second_terms = terms(2, started, result=(result, 3))
    sources, hiddens = after((tuple(src_low), tuple(hid_low)), *sent, result.own.array)
    column_grads.along_core(sources, hiddens, d_queries, d_pairs)
    i2 = move(second_terms, *i1, down_sums.from_y)
    py = column_grads.along_y()
    next_terms = terms(3, *py, result=(result, 0))
    out_grads = OutGrads(
        out_grad(after(attended_low, *py), d_branches),
        x,
        y,
        c,
    )
    out_grads.along_core()
    oy = out_grads.along_y(column_grads.from_y)
    pz, got_z = column_grads.along_fsdp()
    i3 = move(next_terms, *i2, *oy)
    out_grads.along_x(*i2)
    i4 = move(terms(0, *i2), *i3)
    grad_gate, grad_up, grad_down = add_all(
        *zip(
            *(
                (sums.kept, after(sums.from_y, *i3))
                for sums in (gate_sums, up_sums, down_sums)
            )
        ),
        units,
    )
    output = result_of(after(middle, grad_gate), own_live, result)
    own_grads, grad_ffn_gain = column_grads.whole([w_query, w_key, w_value], out_grads, grad_gate)
    grad_query, grad_key, grad_value, query_sum, pair_sum, gain_sum, grad_out = own_grads
    grad_attn_gain = query_sum[:, 0] / attn_gain.astype(jnp.float32)
    grad_kv_gain = pair_sum[:, 0] / kv_gain.astype(jnp.float32)

    grad_hidden, grad_source = input_grads(
        hidden, source, d_middle, attn_gain_full, kv_gain_full, d_hid, d_src
    )
    return (
        output,
        grad_hidden,
        grad_source,
        grad_kv_gain,
        grad_key,
        grad_value,
        grad_attn_gain,
        grad_query,
        grad_out,
        grad_ffn_gain,
        grad_gate,
        grad_up,
        grad_down,
    )


def solution(mesh):
    in_specs = (
        P(("dp", "fsdp"), None),
        P(("dp", "fsdp"), None),
        P(("dp", "fsdp"), None),
        P("dp", None),
        P("dp", None),
        P(("dp", "fsdp")),
        P(("dp", "fsdp"), None),
        P(("dp", "fsdp"), None),
        P(("dp", "fsdp")),
        P(("dp", "fsdp"), None),
        P(("dp", "fsdp"), None),
        P(("dp", "fsdp")),
        P(("dp", "fsdp"), None),
        P(("dp", "fsdp"), None),
        P(("dp", "fsdp"), None),
    )
    out_specs = (
        P(("dp", "fsdp"), None),
        P(("dp", "fsdp"), None),
        P(("dp", "fsdp"), None),
        P(("dp", "fsdp")),
        P(("dp", "fsdp"), None),
        P(("dp", "fsdp"), None),
        P(("dp", "fsdp")),
        P(("dp", "fsdp"), None),
        P(("dp", "fsdp"), None),
        P(("dp", "fsdp")),
        P(("dp", "fsdp"), None),
        P(("dp", "fsdp"), None),
        P(("dp", "fsdp"), None),
    )
    placed = (
        mesh.shape["dp"] == 4 and mesh.shape["fsdp"] == 8 and HEADS == 2 * mesh.shape["fsdp"]
    )
    chosen = fast_body if placed else body
    return jax.shard_map(chosen, mesh=mesh, in_specs=in_specs, out_specs=out_specs, check_vma=False)
```

```python
import functools
import math

import jax
import jax.numpy as jnp
from jax import lax
from jax.experimental import pallas as pl
from jax.experimental.pallas import tpu as pltpu
from jax.sharding import PartitionSpec as P

HEADS = 16


EPSILON = 1e-06
MASKED = -1000000000.0


def product(left, right):
    return jnp.dot(left, right, preferred_element_type=jnp.float32)


def rows_by_rows(left, right):
    return lax.dot_general(
        left, right, (((1,), (1,)), ((), ())), preferred_element_type=jnp.float32
    )


def columns_by_columns(left, right):
    return lax.dot_general(
        left, right, (((0,), (0,)), ((), ())), preferred_element_type=jnp.float32
    )


def inverse_scale(values):
    return lax.rsqrt(jnp.mean(values * values, axis=-1, keepdims=True) + EPSILON)


def norm_backward(values, scale, gain, d_normed):
    weighted = d_normed * gain
    return scale * weighted - values * scale**3 * jnp.mean(
        values * weighted, axis=-1, keepdims=True
    )


def slot_layout(row_counts, seq_lengths, slots, per_device):
    counts = row_counts[0]
    offsets = jnp.cumsum(counts) - counts
    device_of = slots // per_device
    within = slots - device_of * per_device
    picker = device_of[:, None] == jnp.arange(counts.shape[0], dtype=jnp.int32)[None, :]
    count_here = jnp.sum(jnp.where(picker, counts[None, :], 0), axis=1)
    offset_here = jnp.sum(jnp.where(picker, offsets[None, :], 0), axis=1)
    position = offset_here + within
    ends = jnp.cumsum(seq_lengths[0])
    sequence = jnp.sum((ends[None, :] <= position[:, None]).astype(jnp.int32), axis=1)
    return (within < count_here, position, sequence)


def body(
    hidden,
    source,
    cotangent,
    row_counts,
    seq_lengths,
    kv_gain,
    w_key,
    w_value,
    attn_gain,
    w_query,
    w_out,
    ffn_gain,
    w_gate,
    w_up,
    w_down,
):
    local_rows, model_width = hidden.shape
    group_rows = local_rows * lax.axis_size("fsdp")
    head_size = model_width // HEADS
    factor = 1.0 / math.sqrt(head_size)
    block_rows = math.gcd(group_rows, 512)
    block_count = group_rows // block_rows
    own_slots = lax.axis_index("fsdp") * local_rows + jnp.arange(local_rows, dtype=jnp.int32)
    query_live, query_position, query_sequence = slot_layout(
        row_counts, seq_lengths, own_slots, local_rows
    )
    key_live, key_position, key_sequence = slot_layout(
        row_counts, seq_lengths, jnp.arange(group_rows, dtype=jnp.int32), local_rows
    )
    live_column = query_live.astype(jnp.float32)[:, None]
    source_f = source.astype(jnp.float32)
    hidden_f = hidden.astype(jnp.float32)
    source_scale = inverse_scale(source_f)
    hidden_scale = inverse_scale(hidden_f)
    source_unit = source_f * source_scale
    hidden_unit = hidden_f * hidden_scale
    piece_kv_gain = lax.all_gather(kv_gain, ("dp", "fsdp"), axis=0, tiled=True)
    piece_key = lax.all_gather(w_key, ("dp", "fsdp"), axis=0, tiled=True)
    piece_value = lax.all_gather(w_value, ("dp", "fsdp"), axis=0, tiled=True)
    piece_attn_gain = lax.all_gather(attn_gain, ("dp", "fsdp"), axis=0, tiled=True)
    piece_query = lax.all_gather(w_query, ("dp", "fsdp"), axis=0, tiled=True)
    piece_ffn_gain = lax.all_gather(ffn_gain, ("dp", "fsdp"), axis=0, tiled=True)
    source_cols = (source_unit * piece_kv_gain.astype(jnp.float32)[None, :]).astype(jnp.bfloat16)
    hidden_cols = (hidden_unit * piece_attn_gain.astype(jnp.float32)[None, :]).astype(jnp.bfloat16)
    key_sum = product(source_cols, piece_key)
    value_sum = product(source_cols, piece_value)
    query_sum = product(hidden_cols, piece_query)
    stacked = jnp.stack([piece_kv_gain, piece_attn_gain, piece_ffn_gain]).astype(jnp.float32)
    gains = stacked
    key_sum, value_sum, query_sum, gains = (key_sum, value_sum, query_sum, gains)
    kv_gain_full, attn_gain_full, ffn_gain_full = (gains[0], gains[1], gains[2])
    keys_low = key_sum.astype(jnp.bfloat16)
    values_low = value_sum.astype(jnp.bfloat16)
    queries_low = query_sum.astype(jnp.bfloat16)
    group_keys, group_values = (
        lax.all_gather(keys_low, "fsdp", axis=0, tiled=True),
        lax.all_gather(values_low, "fsdp", axis=0, tiled=True),
    )
    blocks = (
        group_keys.reshape(block_count, block_rows, HEADS, head_size),
        group_values.reshape(block_count, block_rows, HEADS, head_size),
        key_live.reshape(block_count, block_rows),
        key_position.reshape(block_count, block_rows),
        key_sequence.reshape(block_count, block_rows),
    )
    query_heads = queries_low.reshape(local_rows, HEADS, head_size)

    def block_scores(key_block, live_block, position_block, sequence_block):
        scores = (
            jnp.einsum("qhd,khd->hqk", query_heads, key_block, preferred_element_type=jnp.float32)
            * factor
        )
        allowed = (
            live_block[None, :]
            & (sequence_block[None, :] == query_sequence[:, None])
            & (position_block[None, :] <= query_position[:, None])
        )
        return jnp.where(allowed[None], scores, MASKED)

    def running_total(running, key_block_set):
        largest, summed = running
        key_block, value_block, live_block, position_block, sequence_block = key_block_set
        masked = block_scores(key_block, live_block, position_block, sequence_block)
        new_largest = jnp.maximum(largest, jnp.max(masked, axis=-1))
        summed = summed * jnp.exp(largest - new_largest) + jnp.sum(
            jnp.exp(masked - new_largest[:, :, None]), axis=-1
        )
        return ((new_largest, summed), None)

    (largest, summed), unused = lax.scan(
        running_total,
        (
            jnp.full((HEADS, local_rows), MASKED, jnp.float32),
            jnp.zeros((HEADS, local_rows), jnp.float32),
        ),
        blocks,
    )
    log_total = largest + jnp.log(summed)

    def weighted_sum(running, key_block_set):
        key_block, value_block, live_block, position_block, sequence_block = key_block_set
        probs_low = jnp.exp(
            block_scores(key_block, live_block, position_block, sequence_block)
            - log_total[:, :, None]
        ).astype(jnp.bfloat16)
        return (
            running
            + jnp.einsum(
                "hqk,khd->qhd", probs_low, value_block, preferred_element_type=jnp.float32
            ),
            None,
        )

    attended_f, unused = lax.scan(
        weighted_sum, jnp.zeros((local_rows, HEADS, head_size), jnp.float32), blocks
    )
    attended_low = attended_f.reshape(local_rows, model_width).astype(jnp.bfloat16)
    branch = product(attended_low, lax.all_gather(w_out, ("dp", "fsdp"), axis=0, tiled=True))
    middle = hidden_f + branch
    middle_scale = inverse_scale(middle)
    middle_unit = middle * middle_scale
    middle_low = (middle_unit * ffn_gain_full).astype(jnp.bfloat16)
    piece_gate = lax.all_gather(w_gate, ("dp", "fsdp"), axis=0, tiled=True)
    piece_up = lax.all_gather(w_up, ("dp", "fsdp"), axis=0, tiled=True)
    piece_down = lax.all_gather(w_down, ("dp", "fsdp"), axis=0, tiled=True)
    gate_value = rows_by_rows(middle_low, piece_gate)
    up_value = rows_by_rows(middle_low, piece_up)
    inner = (jax.nn.silu(gate_value) * up_value).astype(jnp.bfloat16)
    ffn_result = product(inner, piece_down)
    output = ((middle + ffn_result) * live_column).astype(jnp.bfloat16)
    d_out = cotangent.astype(jnp.float32) * live_column
    d_out_low = d_out.astype(jnp.bfloat16)
    piece_gate = lax.all_gather(w_gate, ("dp", "fsdp"), axis=0, tiled=True)
    piece_up = lax.all_gather(w_up, ("dp", "fsdp"), axis=0, tiled=True)
    piece_down = lax.all_gather(w_down, ("dp", "fsdp"), axis=0, tiled=True)
    gate_value = rows_by_rows(middle_low, piece_gate)
    up_value = rows_by_rows(middle_low, piece_up)
    sigmoid_gate = jax.nn.sigmoid(gate_value)
    swished = gate_value * sigmoid_gate
    inner = (swished * up_value).astype(jnp.bfloat16)
    d_inner = rows_by_rows(d_out_low, piece_down)
    d_gate = (d_inner * up_value * sigmoid_gate * (1.0 + gate_value * (1.0 - sigmoid_gate))).astype(
        jnp.bfloat16
    )
    d_up = (d_inner * swished).astype(jnp.bfloat16)
    d_normed = product(d_gate, piece_gate) + product(d_up, piece_up)
    ffn_grads = lax.psum_scatter(
        jnp.stack(
            [
                columns_by_columns(d_gate, middle_low),
                columns_by_columns(d_up, middle_low),
                columns_by_columns(inner, d_out_low),
            ],
            axis=1,
        ),
        ("dp", "fsdp"),
        scatter_dimension=0,
        tiled=True,
    )
    ffn_gain_part = jnp.sum(d_normed * middle_unit, axis=0)
    d_middle = d_out + norm_backward(middle, middle_scale, ffn_gain_full, d_normed)
    d_branch_low = d_middle.astype(jnp.bfloat16)
    d_attended = rows_by_rows(
        d_branch_low, lax.all_gather(w_out, ("dp", "fsdp"), axis=0, tiled=True)
    )
    d_heads = d_attended.astype(jnp.bfloat16).reshape(local_rows, HEADS, head_size)
    delta = jnp.sum(d_heads.astype(jnp.float32) * attended_f, axis=-1).T

    def attention_backward(d_query_sum, key_block_set):
        key_block, value_block, live_block, position_block, sequence_block = key_block_set
        probs = jnp.exp(
            block_scores(key_block, live_block, position_block, sequence_block)
            - log_total[:, :, None]
        )
        probs_low = probs.astype(jnp.bfloat16)
        d_values = jnp.einsum(
            "hqk,qhd->khd", probs_low, d_heads, preferred_element_type=jnp.float32
        )
        d_probs = jnp.einsum(
            "qhd,khd->hqk", d_heads, value_block, preferred_element_type=jnp.float32
        )
        d_scores = (probs * (d_probs - delta[:, :, None])).astype(jnp.bfloat16)
        d_query_sum = d_query_sum + jnp.einsum(
            "hqk,khd->qhd", d_scores, key_block, preferred_element_type=jnp.float32
        )
        d_keys = (
            jnp.einsum("hqk,qhd->khd", d_scores, query_heads, preferred_element_type=jnp.float32)
            * factor
        )
        return (d_query_sum, jnp.stack([d_keys, d_values], axis=1))

    d_query_sum, key_terms = lax.scan(
        attention_backward, jnp.zeros((local_rows, HEADS, head_size), jnp.float32), blocks
    )
    key_grads = lax.psum_scatter(
        key_terms.reshape(group_rows, 2, model_width).astype(jnp.bfloat16),
        "fsdp",
        scatter_dimension=0,
        tiled=True,
    ).astype(jnp.float32)
    d_keys_low = key_grads[:, 0].astype(jnp.bfloat16)
    d_values_low = key_grads[:, 1].astype(jnp.bfloat16)
    d_queries_low = (d_query_sum * factor).reshape(local_rows, model_width).astype(jnp.bfloat16)
    piece_query = lax.all_gather(w_query, ("dp", "fsdp"), axis=0, tiled=True)
    piece_key = lax.all_gather(w_key, ("dp", "fsdp"), axis=0, tiled=True)
    piece_value = lax.all_gather(w_value, ("dp", "fsdp"), axis=0, tiled=True)
    hidden_part = rows_by_rows(d_queries_low, piece_query)
    source_part = rows_by_rows(d_keys_low, piece_key) + rows_by_rows(d_values_low, piece_value)
    input_back = jnp.stack([hidden_part, source_part])
    grad_hidden = (
        d_middle + norm_backward(hidden_f, hidden_scale, attn_gain_full, input_back[0])
    ).astype(jnp.bfloat16)
    grad_source = norm_backward(source_f, source_scale, kv_gain_full, input_back[1]).astype(
        jnp.bfloat16
    )
    attn_gain_part = jnp.sum(input_back[0] * hidden_unit, axis=0)
    kv_gain_part = jnp.sum(input_back[1] * source_unit, axis=0)
    source_low = (source_unit * kv_gain_full).astype(jnp.bfloat16)
    hidden_low = (hidden_unit * attn_gain_full).astype(jnp.bfloat16)
    hidden_part = hidden_low
    source_part = source_low
    layer_stack = lax.psum_scatter(
        jnp.stack(
            [
                columns_by_columns(hidden_part, d_queries_low),
                columns_by_columns(source_part, d_keys_low),
                columns_by_columns(source_part, d_values_low),
                columns_by_columns(attended_low, d_branch_low),
            ],
            axis=1,
        ),
        ("dp", "fsdp"),
        scatter_dimension=0,
        tiled=True,
    )
    grad_query, grad_key, grad_value, grad_out = (
        layer_stack[:, 0],
        layer_stack[:, 1],
        layer_stack[:, 2],
        layer_stack[:, 3],
    )
    grad_kv_gain, grad_attn_gain, grad_ffn_gain = (
        lax.psum_scatter(kv_gain_part, ("dp", "fsdp"), scatter_dimension=0, tiled=True),
        lax.psum_scatter(attn_gain_part, ("dp", "fsdp"), scatter_dimension=0, tiled=True),
        lax.psum_scatter(ffn_gain_part, ("dp", "fsdp"), scatter_dimension=0, tiled=True),
    )
    return (
        output,
        grad_hidden,
        grad_source,
        grad_kv_gain,
        grad_key,
        grad_value,
        grad_attn_gain,
        grad_query,
        grad_out,
        grad_ffn_gain,
        ffn_grads[:, 0],
        ffn_grads[:, 1],
        ffn_grads[:, 2],
    )


RING = (0, 1, 3, 2)
BLOCK = 256


def swap_pairs(size, mask):
    return [(place, place ^ mask) for place in range(size)]


def ring_pairs():
    return [
        (2 * RING[place] + x, 2 * RING[(place + 1) % 4] + x) for place in range(4) for x in range(2)
    ]


def x_swap(value):
    return lax.ppermute(value, "fsdp", swap_pairs(8, 1))


def ring_step(value):
    return lax.ppermute(value, "fsdp", ring_pairs())


def y_swap(value):
    return lax.ppermute(value, "dp", swap_pairs(4, 2))


def core_swap(value):
    return lax.ppermute(value, "dp", swap_pairs(4, 1))


def in_order(flag, first, second):
    swapped = flag == 1
    return jnp.concatenate(
        [jnp.where(swapped, second, first), jnp.where(swapped, first, second)], axis=0
    )


def after(value, *earlier):
    if not earlier:
        return value
    return lax.optimization_barrier((value, *earlier))[0]


FREE = pl.CostEstimate(flops=0, bytes_accessed=0, transcendentals=0)
LONG = pl.CostEstimate(flops=2 * 10**10, bytes_accessed=0, transcendentals=0)


class Rows:
    def __init__(self, array, start, count):
        self.array, self.start, self.count = array, start, count

    def part(self, start, count):
        return Rows(self.array, self.start + start, count)

    def value(self):
        if self.count == self.array.shape[0]:
            return self.array
        return self.array[self.start : self.start + self.count]


def rows_in(array):
    return Rows(array, 0, array.shape[0])


class Gather:
    def __init__(self, own):
        self.held = rows_in(own)
        self.pieces = []

    def send(self):
        if len(self.pieces) < 3:
            return [[self.held]], [[self.held]]
        half = self.held.count // 2
        return [[self.held.part(0, half)]], [[self.pieces[2][1].part(half, half)]]

    def take(self, from_x, from_ring):
        if len(self.pieces) < 3:
            self.pieces.append((self.held, from_x))
            self.held = from_ring
        else:
            self.pieces.append((self.held, from_x, from_ring))

    def arrays(self, step):
        return tuple(rows.value() for rows in self.pieces[step])

    def piece(self, step):
        return jnp.concatenate(self.arrays(step), axis=0)


class Scatter:
    def __init__(self):
        self.stage = 0

    def of(self, terms):
        rows = terms.shape[0] // 2
        return self.of_rows(Rows(terms, 0, rows), Rows(terms, rows, rows))

    def of_rows(self, own, other):
        self.own, self.other = own, other
        return self

    def send(self):
        own, other = self.own, self.other
        half = own.count // 2
        if self.stage == 0:
            given = [[other.part(0, half)]], [[other.part(half, half)]]
        elif self.stage == 1:
            kept, (from_x, from_ring) = self.kept, self.got
            given = (
                [[other.part(0, half)], [other.part(half, half), from_ring]],
                [[kept.part(0, half), from_x], [kept.part(half, half)]],
            )
        else:
            given = [[other]], [[self.kept, *self.got]]
        self.stage += 1
        self.kept = own
        return given

    def take(self, from_x, from_ring):
        self.got = (from_x, from_ring)

    def total(self):
        return sum(rows.value().astype(jnp.float32) for rows in (self.kept, *self.got))


def mix_kernel(plans, *refs):
    for plan, out_ref in zip(plans, refs[-len(plans) :]):
        first = 0
        for places, count in plan:
            values = [refs[index][start : start + count, :] for index, start in places]
            if len(values) > 1:
                values = [sum(value.astype(jnp.float32) for value in values)]
            out_ref[first : first + count, :] = values[0].astype(out_ref.dtype)
            first += count


def only_array(sums):
    array = sums[0][0].array
    first = 0
    for rows in sums:
        if len(rows) > 1 or rows[0].array is not array or rows[0].start != first:
            return None
        first += rows[0].count
    return array if first == array.shape[0] else None


def mixed(*all_sums):
    arrays = []
    plans = []
    for sums in all_sums:
        plan = []
        for rows in sums:
            places = []
            for part in rows:
                index = next((n for n, held in enumerate(arrays) if held is part.array), None)
                if index is None:
                    index = len(arrays)
                    arrays.append(part.array)
                places.append((index, part.start))
            plan.append((tuple(places), rows[0].count))
        plans.append(tuple(plan))
    width = arrays[0].shape[1]
    counts = [sum(count for places, count in plan) for plan in plans]
    return pl.pallas_call(
        functools.partial(mix_kernel, tuple(plans)),
        out_shape=[jax.ShapeDtypeStruct((count, width), jnp.bfloat16) for count in counts],
        compiler_params=pltpu.CompilerParams(vmem_limit_bytes=10 * 2**20),
        cost_estimate=FREE,
        name="mix",
    )(*arrays)


def move(parts, *gate, payload=None):
    sent = [part.send() for part in parts]
    x_sums, ring_sums = (sum((given[way] for given in sent), []) for way in range(2))
    along_x, along_ring = only_array(x_sums), only_array(ring_sums)
    if along_x is None and along_ring is None:
        along_x, along_ring = mixed(x_sums, ring_sums)
    elif along_x is None:
        (along_x,) = mixed(x_sums)
    elif along_ring is None:
        (along_ring,) = mixed(ring_sums)
    along_x, along_ring = after((along_x, along_ring), *gate)
    if payload is not None:
        payload += [along_x, along_ring]
    from_x, from_ring = x_swap(along_x), ring_step(along_ring)
    x_row = ring_row = 0
    for part, given in zip(parts, sent):
        x_count, ring_count = (sum(rows[0].count for rows in sums) for sums in given)
        part.take(Rows(from_x, x_row, x_count), Rows(from_ring, ring_row, ring_count))
        x_row, ring_row = x_row + x_count, ring_row + ring_count
    return [from_x, from_ring]


def attend_kernel(
    factor, q_ref, k_ref, v_ref, first_ref, last_ref, place_ref, att_ref, low_ref, lse_ref
):
    scores = rows_by_rows(q_ref[...], k_ref[...]) * factor
    places = place_ref[...]
    allowed = (places >= first_ref[...]) & (places <= last_ref[...])
    masked = jnp.where(allowed, scores, MASKED)
    largest = jnp.max(masked, axis=-1, keepdims=True)
    raised = jnp.exp(masked - largest)
    summed = jnp.sum(raised, axis=-1, keepdims=True)
    probs_low = (raised * (1.0 / summed)).astype(jnp.bfloat16)
    attended = product(probs_low, v_ref[...])
    att_ref[...] = attended
    low_ref[...] = attended.astype(jnp.bfloat16)
    lse_ref[...] = (largest + jnp.log(summed))[None]


def attend_back_kernel(
    factor,
    q_ref,
    k_ref,
    v_ref,
    first_ref,
    last_ref,
    place_ref,
    lse_ref,
    att_ref,
    d_att_ref,
    dq_ref,
    dkv_ref,
    dk_sum,
    dv_sum,
):
    head = pl.program_id(0)
    step = pl.program_id(1)
    size = q_ref.shape[1]
    mine = dkv_ref.shape[1] // 2

    @pl.when(step == 0)
    def _():
        dk_sum[...] = jnp.zeros_like(dk_sum)
        dv_sum[...] = jnp.zeros_like(dv_sum)

    queries = q_ref[...]
    keys = k_ref[...]
    d_att = d_att_ref[...]
    scores = rows_by_rows(queries, keys) * factor
    places = place_ref[...]
    allowed = (places >= first_ref[...]) & (places <= last_ref[...])
    probs = jnp.exp(jnp.where(allowed, scores, MASKED) - lse_ref[0])
    delta = jnp.sum(d_att.astype(jnp.float32) * att_ref[...], axis=-1, keepdims=True)
    d_probs = rows_by_rows(d_att, v_ref[...])
    d_scores = (probs * (d_probs - delta)).astype(jnp.bfloat16)
    dq_ref[...] = (product(d_scores, keys) * factor).astype(jnp.bfloat16)
    dk_sum[...] += columns_by_columns(d_scores, queries)
    dv_sum[...] += columns_by_columns(probs.astype(jnp.bfloat16), d_att)

    @pl.when(step == pl.num_programs(1) - 1)
    def _():
        first = pl.multiple_of(size * head, size)
        dkv_ref[:, pl.ds(first, size)] = (dk_sum[...] * factor).astype(jnp.bfloat16)
        dkv_ref[:, pl.ds(mine + first, size)] = dv_sum[...].astype(jnp.bfloat16)


def attend_specs(count, head):
    by_query = pl.BlockSpec((BLOCK, head), lambda h, i: (i, h))
    keys = pl.BlockSpec((count, head), lambda h, i: (0, h))
    values = pl.BlockSpec((count, head), lambda h, i: (0, 2 + h))
    bound = pl.BlockSpec((BLOCK, 1), lambda h, i: (i, 0))
    place = pl.BlockSpec((1, count), lambda h, i: (0, 0))
    lse = pl.BlockSpec((1, BLOCK, 1), lambda h, i: (h, i, 0))
    return by_query, keys, values, bound, place, lse


def attend(queries, pairs, first, last, place, head):
    count, width = queries.shape
    by_query, keys, values, bound, places, lse = attend_specs(count, head)
    return pl.pallas_call(
        functools.partial(attend_kernel, 1.0 / math.sqrt(head)),
        grid=(width // head, count // BLOCK),
        in_specs=[by_query, keys, values, bound, bound, places],
        out_specs=[by_query, by_query, lse],
        out_shape=[
            jax.ShapeDtypeStruct((count, width), jnp.float32),
            jax.ShapeDtypeStruct((count, width), jnp.bfloat16),
            jax.ShapeDtypeStruct((width // head, count, 1), jnp.float32),
        ],
        compiler_params=pltpu.CompilerParams(vmem_limit_bytes=20 * 2**20),
        cost_estimate=LONG,
        name="attend",
    )(queries, pairs, pairs, first, last, place)


def attend_back(queries, pairs, first, last, place, lse, attended, d_attended, head):
    count, width = queries.shape
    by_query, keys, values, bound, places, by_lse = attend_specs(count, head)
    return pl.pallas_call(
        functools.partial(attend_back_kernel, 1.0 / math.sqrt(head)),
        grid=(width // head, count // BLOCK),
        in_specs=[
            by_query,
            keys,
            values,
            bound,
            bound,
            places,
            by_lse,
            by_query,
            by_query,
        ],
        out_specs=[by_query, pl.BlockSpec((count, 2 * width), lambda h, i: (0, 0))],
        out_shape=[
            jax.ShapeDtypeStruct((count, width), jnp.bfloat16),
            jax.ShapeDtypeStruct((count, 2 * width), jnp.bfloat16),
        ],
        scratch_shapes=[pltpu.VMEM((count, head), jnp.float32)] * 2,
        compiler_params=pltpu.CompilerParams(vmem_limit_bytes=14 * 2**20),
        cost_estimate=LONG,
        name="attend_back",
    )(queries, pairs, pairs, first, last, place, lse, attended, d_attended)


def as_rows(values, columns):
    rows = 16 * -(-values.shape[0] // (16 * columns))
    return jnp.pad(values, (0, rows * columns - values.shape[0])).reshape(rows, columns)


def from_rows(rows, count):
    return rows.reshape(-1)[:count]


def heads_of(device, head):
    z, x = device // 2, device % 2
    return [slice(head * (8 * x + 4 * j + z), head * (8 * x + 4 * j + z + 1)) for j in range(2)]


def columns_kernel(dp_ref, *refs):
    held_refs = refs[:4]
    q_ref, kv_ref, gain_ref = refs[4:]
    each = q_ref.shape[0] // 8
    mine = q_ref.shape[1]
    rows = held_refs[0].shape[0] // 8
    extra = rows - 3 * each
    for mask, held_ref in enumerate(held_refs):

        @pl.when((dp_ref[0] ^ pl.program_id(0)) == mask)
        def _():
            for device in range(8):
                first = rows * device
                here = slice(each * device, each * (device + 1))
                q_ref[here, :] = held_ref[first : first + each, :]
                kv_ref[here, :mine] = held_ref[first + each : first + 2 * each, :]
                kv_ref[here, mine:] = held_ref[first + 2 * each : first + 3 * each, :]
                gain_ref[0, extra * device : extra * (device + 1), :] = held_ref[
                    first + 3 * each : first + rows, :
                ]


def payload_kernel(q_ref, k_ref, v_ref, gain_ref, out_ref):
    each = q_ref.shape[0]
    head = q_ref.shape[1] // 16
    rows = out_ref.shape[0] // 8
    for device in range(8):
        for which, w_ref in enumerate((q_ref, k_ref, v_ref)):
            first = rows * device + each * which
            for j, columns in enumerate(heads_of(device, head)):
                out_ref[first : first + each, head * j : head * (j + 1)] = w_ref[:, columns]
        out_ref[rows * device + 3 * each : rows * (device + 1), :] = gain_ref[...]


class Columns:
    def __init__(self, weights, gains, dp):
        self.weights, self.gains, self.dp = weights, gains, dp

    def along_fsdp(self, *gate):
        each, width = self.weights[0].shape
        extra = as_rows(self.gains, width // 8)
        given = pl.pallas_call(
            payload_kernel,
            out_shape=jax.ShapeDtypeStruct(
                (8 * (3 * each + extra.shape[0]), width // 8), self.weights[0].dtype
            ),
            compiler_params=pltpu.CompilerParams(vmem_limit_bytes=8 * 2**20),
            cost_estimate=LONG,
            name="payload",
        )(*self.weights, extra)
        self.held = lax.all_to_all(after(given, *gate), "fsdp", 0, 0, tiled=True)
        return [self.held]

    def along_y(self, *gate):
        held = after(self.held, *gate)
        got, other = y_swap(held), core_swap(held)
        self.held = [held, got, other]
        return [got, other]

    def along_core(self, *gate):
        held, got, other = after(tuple(self.held), *gate)
        last = core_swap(got)
        self.held = [held, other, got, last]
        return [last]

    def whole(self):
        each, width = self.weights[0].shape
        rows, mine = self.held[0].shape
        extra = rows - 24 * each
        block = 8 * each
        low = self.held[0].dtype
        wq, w_kv, gains = pl.pallas_call(
            columns_kernel,
            grid_spec=pltpu.PrefetchScalarGridSpec(
                num_scalar_prefetch=1,
                grid=(4,),
                in_specs=[pl.BlockSpec((rows, mine), lambda i, dp: (0, 0))] * 4,
                out_specs=[
                    pl.BlockSpec((block, mine), lambda i, dp: (i, 0)),
                    pl.BlockSpec((block, 2 * mine), lambda i, dp: (i, 0)),
                    pl.BlockSpec((1, extra, mine), lambda i, dp: (i, 0, 0)),
                ],
            ),
            out_shape=[
                jax.ShapeDtypeStruct((4 * block, mine), low),
                jax.ShapeDtypeStruct((4 * block, 2 * mine), low),
                jax.ShapeDtypeStruct((4, extra, mine), low),
            ],
            compiler_params=pltpu.CompilerParams(vmem_limit_bytes=16 * 2**20),
            cost_estimate=FREE,
            name="columns",
        )(self.dp.reshape(1).astype(jnp.int32), *self.held)
        gains = gains.reshape(32, -1)[:, : self.gains.shape[0]].astype(jnp.float32)
        return wq, w_kv, gains


def column_grads_kernel(dp_ref, *refs):
    sources, hiddens = refs[:4], refs[4:8]
    dq_ref, dkv_ref, *given_refs, kept_ref = refs[8:]
    count = sources[0].shape[0]
    mine = dq_ref.shape[1]
    for_q, for_kv = 0.0, 0.0
    for step in range(4):
        here = slice(count * step, count * (step + 1))
        for_q = for_q + columns_by_columns(hiddens[step][...], dq_ref[here, :])
        for_kv = for_kv + columns_by_columns(sources[step][...], dkv_ref[here, :])

    for place in range(2):

        @pl.when(pl.program_id(0) == place)
        def _():
            given_refs[2 * place][...] = for_q.astype(jnp.bfloat16)
            given_refs[2 * place + 1][...] = for_kv.astype(jnp.bfloat16)

    @pl.when(pl.program_id(0) >= 2)
    def _():
        kept_ref[0, :, :mine] = for_q
        kept_ref[0, :, mine:] = for_kv


def own_grads_kernel(
    got_ref,
    wq_ref,
    wk_ref,
    wv_ref,
    flag_ref,
    out_kept_ref,
    out_got_ref,
    q_ref,
    k_ref,
    v_ref,
    q_sum_ref,
    kv_sum_ref,
    gain_ref,
    out_ref,
):
    each = wq_ref.shape[0]
    gain = 0.0
    for device in range(8):
        gain = gain + got_ref[device, each : each + 16, :128].astype(jnp.float32)
    gain_ref[...] = gain
    out_ref[...] = jnp.where(
        flag_ref[...] != 0, out_kept_ref[...], out_got_ref[...].astype(jnp.float32)
    )
    head = wq_ref.shape[1] // 16
    sums = []
    for which, (w_ref, out_ref) in enumerate(((wq_ref, q_ref), (wk_ref, k_ref), (wv_ref, v_ref))):
        total = jnp.zeros((each, head), jnp.float32)
        for device in range(8):
            for j, columns in enumerate(heads_of(device, head)):
                first = head * (2 * which + j)
                grad = got_ref[device, :each, first : first + head].astype(jnp.float32)
                out_ref[:, columns] = grad
                total = total + grad * w_ref[:, columns].astype(jnp.float32)
        sums.append(jnp.sum(total, axis=1, keepdims=True))
    q_sum_ref[...] = sums[0]
    kv_sum_ref[...] = sums[1] + sums[2]


def whole_block(array):
    return pl.BlockSpec(array.shape, lambda *place: (0,) * array.ndim)


def project_kernel(held_ref, *refs):
    others = refs[:-8]
    kv_gain_ref, attn_gain_ref, w_kv_ref, wq_ref, src_ref, hid_ref, pair_ref, query_ref = refs[-8:]
    rows = src_ref.shape[0] // 2

    def other_rows(which):
        if len(others) == 1:
            return others[0][rows * which : rows * (which + 1), :]
        return others[which][...]

    for which, gain_ref, w_ref, low_ref, out_ref in (
        (0, kv_gain_ref, w_kv_ref, src_ref, pair_ref),
        (1, attn_gain_ref, wq_ref, hid_ref, query_ref),
    ):
        for side in range(2):
            here = slice(rows * side, rows * (side + 1))
            values = other_rows(which) if side else held_ref[rows * which : rows * (which + 1), :]
            values = values.astype(jnp.float32)
            low_ref[here, :] = (values * inverse_scale(values) * gain_ref[...]).astype(jnp.bfloat16)
        out_ref[...] = product(low_ref[...], w_ref[...]).astype(jnp.bfloat16)


def project(piece, kv_gain, attn_gain, w_kv, wq, cost):
    rows, width = piece[0].shape
    low = piece[0].dtype
    return pl.pallas_call(
        project_kernel,
        out_shape=[
            jax.ShapeDtypeStruct((rows, width), low),
            jax.ShapeDtypeStruct((rows, width), low),
            jax.ShapeDtypeStruct((rows, w_kv.shape[1]), low),
            jax.ShapeDtypeStruct((rows, wq.shape[1]), low),
        ],
        compiler_params=pltpu.CompilerParams(vmem_limit_bytes=12 * 2**20),
        cost_estimate=cost,
        name="project",
    )(*piece, kv_gain, attn_gain, w_kv, wq)


def terms_kernel(step, pair_ref, query_ref, w_kv_ref, wq_ref, *refs):
    own_ref, other_ref = refs[-2:]
    count = pair_ref.shape[0] // 4
    here = slice(count * step, count * (step + 1))
    found = [
        rows_by_rows(pair_ref[here, :], w_kv_ref[...]),
        rows_by_rows(query_ref[here, :], wq_ref[...]),
    ]
    if len(refs) > 2:
        found.append(product(refs[0][...], refs[1][...]))
    rows = count // 2
    for place, value in enumerate(found):
        value = value.astype(jnp.bfloat16)
        own_ref[rows * place : rows * (place + 1), :] = value[:rows]
        other_ref[rows * place : rows * (place + 1), :] = value[rows:]


def back_terms(parts, step, d_pairs, d_queries, w_kv, wq, result=()):
    rows, width = d_pairs.shape[0] // 4, w_kv.shape[0]
    count = rows // 2
    out = jax.ShapeDtypeStruct((count * len(parts), width), jnp.bfloat16)
    own, other = pl.pallas_call(
        functools.partial(terms_kernel, step),
        out_shape=[out, out],
        compiler_params=pltpu.CompilerParams(vmem_limit_bytes=14 * 2**20),
        cost_estimate=FREE,
        name="back_terms",
    )(d_pairs, d_queries, w_kv, wq, *result)
    return [
        part.of_rows(Rows(own, count * place, count), Rows(other, count * place, count))
        for place, part in enumerate(parts)
    ]


def row_blocks(rows, count):
    first = rows.start // count
    return pl.BlockSpec((count, rows.array.shape[1]), lambda i: (first + i, 0))


def result_kernel(middle_ref, live_ref, kept_ref, x_ref, ring_ref, out_ref):
    total = middle_ref[...] + kept_ref[...].astype(jnp.float32)
    total = total + x_ref[...].astype(jnp.float32) + ring_ref[...].astype(jnp.float32)
    out_ref[...] = (total * live_ref[...]).astype(jnp.bfloat16)


def result_of(middle, live, scatter):
    sums = [scatter.kept, *scatter.got]
    rows, width = middle.shape
    block = rows // 4
    return pl.pallas_call(
        result_kernel,
        grid=(4,),
        in_specs=[
            pl.BlockSpec((block, width), lambda i: (i, 0)),
            pl.BlockSpec((block, 1), lambda i: (i, 0)),
        ]
        + [row_blocks(part, block) for part in sums],
        out_specs=pl.BlockSpec((block, width), lambda i: (i, 0)),
        out_shape=jax.ShapeDtypeStruct((rows, width), jnp.bfloat16),
        compiler_params=pltpu.CompilerParams(vmem_limit_bytes=6 * 2**20),
        cost_estimate=FREE,
        name="result",
    )(middle, live, *(part.array for part in sums))


def input_grads_kernel(hidden_ref, source_ref, d_middle_ref, attn_gain_ref, kv_gain_ref, *refs):
    d_hid, d_src = (
        sum(ref[...].astype(jnp.float32) for ref in refs[first : first + 3]) for first in (0, 3)
    )
    hidden = hidden_ref[...].astype(jnp.float32)
    source = source_ref[...].astype(jnp.float32)
    refs[6][...] = (
        d_middle_ref[...] + norm_backward(hidden, inverse_scale(hidden), attn_gain_ref[...], d_hid)
    ).astype(jnp.bfloat16)
    refs[7][...] = norm_backward(
        source, inverse_scale(source), kv_gain_ref[...], d_src
    ).astype(jnp.bfloat16)


def input_grads(hidden, source, d_middle, attn_gain, kv_gain, d_hid, d_src):
    sums = [d_hid.kept, *d_hid.got, d_src.kept, *d_src.got]
    rows, width = hidden.shape
    block = rows // 4
    spec = pl.BlockSpec((block, width), lambda i: (i, 0))
    return pl.pallas_call(
        input_grads_kernel,
        grid=(4,),
        in_specs=[spec] * 3
        + [whole_block(attn_gain), whole_block(kv_gain)]
        + [row_blocks(part, block) for part in sums],
        out_specs=[spec, spec],
        out_shape=[jax.ShapeDtypeStruct((rows, width), jnp.bfloat16)] * 2,
        compiler_params=pltpu.CompilerParams(vmem_limit_bytes=8 * 2**20),
        cost_estimate=FREE,
        name="input_grads",
    )(hidden, source, d_middle, attn_gain, kv_gain, *(part.array for part in sums))


def feed_kernel(mid_plan, cot_plan, *refs):
    arrays = refs[:-10]
    wg_ref, wu_ref, wd_ref, inner_ref, d_gate_ref, d_up_ref, own_ref, other_ref = refs[-10:-2]
    for plan, rows_ref in ((mid_plan, refs[-2]), (cot_plan, refs[-1])):
        first = 0
        for index, start, count in plan:
            rows_ref[first : first + count, :] = arrays[index][start : start + count, :]
            first += count
    mid_ref, cot_ref = refs[-2:]
    hidden, width = wg_ref.shape
    for first in range(0, hidden, 256):
        here = slice(first, min(first + 256, hidden))
        gate_value = rows_by_rows(mid_ref[...], wg_ref[here, :])
        up_value = rows_by_rows(mid_ref[...], wu_ref[here, :])
        d_inner = rows_by_rows(cot_ref[...], wd_ref[here, :])
        sigmoid_gate = jax.nn.sigmoid(gate_value)
        swished = gate_value * sigmoid_gate
        inner_ref[:, here] = (swished * up_value).astype(jnp.bfloat16)
        d_gate_ref[:, here] = (
            d_inner * up_value * sigmoid_gate * (1.0 + gate_value * (1.0 - sigmoid_gate))
        ).astype(jnp.bfloat16)
        d_up_ref[:, here] = (d_inner * swished).astype(jnp.bfloat16)
    rows = own_ref.shape[0]
    for first in range(0, width, 512):
        here = slice(first, first + 512)
        terms = product(d_gate_ref[...], wg_ref[:, here]) + product(d_up_ref[...], wu_ref[:, here])
        terms = terms.astype(jnp.bfloat16)
        own_ref[:, here] = terms[:rows]
        other_ref[:, here] = terms[rows:]


def feed(mid, cot, wg, wu, wd):
    arrays = []
    plans = []
    for pieces in (mid, cot):
        plan = []
        for rows in pieces:
            index = next((n for n, held in enumerate(arrays) if held is rows.array), None)
            if index is None:
                index = len(arrays)
                arrays.append(rows.array)
            plan.append((index, rows.start, rows.count))
        plans.append(tuple(plan))
    count = sum(rows.count for rows in mid)
    hidden, width = wg.shape
    low = jax.ShapeDtypeStruct((count, hidden), jnp.bfloat16)
    terms = jax.ShapeDtypeStruct((count // 2, width), jnp.bfloat16)
    return pl.pallas_call(
        functools.partial(feed_kernel, *plans),
        out_shape=[low, low, low, terms, terms]
        + [jax.ShapeDtypeStruct((count, width), jnp.bfloat16)] * 2,
        compiler_params=pltpu.CompilerParams(vmem_limit_bytes=20 * 2**20),
        cost_estimate=LONG,
        name="feed",
    )(*arrays, wg, wu, wd)


def branch_back_kernel(plan, *refs):
    *arrays, wo_ref, rows_ref, att_ref = refs
    first = 0
    for (start, count), array in zip(plan, arrays):
        rows_ref[first : first + count, :] = array[start : start + count, :]
        first += count
    att_ref[...] = rows_by_rows(rows_ref[...], wo_ref[...]).astype(jnp.bfloat16)


def branch_back(pieces, wo):
    count = sum(rows.count for rows in pieces)
    return pl.pallas_call(
        functools.partial(branch_back_kernel, tuple((rows.start, rows.count) for rows in pieces)),
        out_shape=[
            jax.ShapeDtypeStruct((count, wo.shape[1]), jnp.bfloat16),
            jax.ShapeDtypeStruct((count, wo.shape[0]), jnp.bfloat16),
        ],
        compiler_params=pltpu.CompilerParams(vmem_limit_bytes=16 * 2**20),
        cost_estimate=FREE,
        name="branch_back",
    )(*(rows.array for rows in pieces), wo)


def add_kernel(*refs):
    count = len(refs) // 3
    for kept_ref, got_ref, out_ref in zip(refs[:count], refs[count : 2 * count], refs[2 * count :]):
        total = kept_ref[...] + got_ref[...].astype(jnp.float32)
        out_ref[...] = total[: out_ref.shape[0]]


def add_all(kept, got, rows):
    width = kept[0].shape[1]
    block = width // 4
    count = len(kept)
    spec = pl.BlockSpec((got[0].shape[0], block), lambda i: (0, i))
    return pl.pallas_call(
        add_kernel,
        grid=(4,),
        in_specs=[spec] * (2 * count),
        out_specs=[pl.BlockSpec((rows, block), lambda i: (0, i))] * count,
        out_shape=[jax.ShapeDtypeStruct((rows, width), jnp.float32)] * count,
        compiler_params=pltpu.CompilerParams(vmem_limit_bytes=8 * 2**20),
        cost_estimate=LONG,
        name="add_all",
    )(*kept, *got)


def copy_kernel(dp_ref, in_ref, out_ref):
    out_ref[...] = in_ref[...]


def own_first(rows, dp):
    block = (rows.shape[0] // 4, rows.shape[1])
    return pl.pallas_call(
        copy_kernel,
        grid_spec=pltpu.PrefetchScalarGridSpec(
            num_scalar_prefetch=1,
            grid=(4,),
            in_specs=[pl.BlockSpec(block, lambda i, dp: (dp[0] ^ (2 * (i % 2) + i // 2), 0))],
            out_specs=pl.BlockSpec(block, lambda i, dp: (i, 0)),
        ),
        out_shape=jax.ShapeDtypeStruct(rows.shape, rows.dtype),
        compiler_params=pltpu.CompilerParams(vmem_limit_bytes=8 * 2**20),
        cost_estimate=FREE,
        name="own_first",
    )(dp.reshape(1).astype(jnp.int32), rows)


class ColumnGrads:
    def __init__(self, dp):
        self.dp = dp
        self.y, self.c = dp // 2, dp % 2

    def gain_core(self, gain, *gate):
        gain = gain.reshape(2, 2, -1)
        kept = lax.dynamic_index_in_dim(gain, self.c, 1, keepdims=False)
        given = lax.dynamic_index_in_dim(gain, 1 - self.c, 1, keepdims=False)
        self.gain = kept + core_swap(after(given, *gate))
        return [given]

    def gain_y(self, *gate):
        gain = after(self.gain, *gate)
        kept = lax.dynamic_index_in_dim(gain, self.y, 0, keepdims=False)
        given = lax.dynamic_index_in_dim(gain, 1 - self.y, 0, keepdims=False)
        self.gain = kept + y_swap(given)
        return [given]

    def along_core(self, sources, hiddens, d_queries, d_pairs):
        count, width = sources[0].shape
        block = width // 4
        mine = d_queries.shape[1]
        rows = d_queries.shape[0]

        def of_step(i):
            return 2 * (i % 2) + 1 - i // 2

        by_block = pl.BlockSpec((count, block), lambda i, dp: (0, dp[0] ^ of_step(i)))
        *given, self.kept = pl.pallas_call(
            column_grads_kernel,
            grid_spec=pltpu.PrefetchScalarGridSpec(
                num_scalar_prefetch=1,
                grid=(4,),
                in_specs=[by_block] * 8
                + [
                    pl.BlockSpec((rows, mine), lambda i, dp: (0, 0)),
                    pl.BlockSpec((rows, 2 * mine), lambda i, dp: (0, 0)),
                ],
                out_specs=[
                    *(
                        pl.BlockSpec((block, width_of * mine), lambda i, dp: (0, 0))
                        for width_of in (1, 2, 1, 2)
                    ),
                    pl.BlockSpec((1, block, 3 * mine), lambda i, dp: (jnp.maximum(i, 2) - 2, 0, 0)),
                ],
            ),
            out_shape=[
                *(
                    jax.ShapeDtypeStruct((block, width_of * mine), jnp.bfloat16)
                    for width_of in (1, 2, 1, 2)
                ),
                jax.ShapeDtypeStruct((2, block, 3 * mine), jnp.float32),
            ],
            compiler_params=pltpu.CompilerParams(vmem_limit_bytes=16 * 2**20),
            cost_estimate=LONG,
            name="column_grads",
        )(self.dp.reshape(1).astype(jnp.int32), *sources, *hiddens, d_queries, d_pairs)
        self.from_core = [core_swap(value) for value in given]
        return given

    def along_y(self, *gate):
        got = after(tuple(self.from_core[2:]), *gate)
        given = self.kept[1] + jnp.concatenate(got, axis=1).astype(jnp.float32)
        given = given.astype(jnp.bfloat16)
        self.from_y = y_swap(given)
        return [given]

    def along_fsdp(self, *gate):
        total = self.kept[0] + jnp.concatenate(self.from_core[:2], axis=1).astype(jnp.float32)
        total = (total + after(self.from_y, *gate).astype(jnp.float32)).astype(jnp.bfloat16)
        each, columns = total.shape[0] // 8, total.shape[1]
        gain = self.gain.astype(jnp.bfloat16).reshape(8, 1, each)
        gain = jnp.pad(gain, ((0, 0), (0, 15), (0, columns - each)))
        given = jnp.concatenate([total.reshape(8, each, columns), gain], axis=1)
        self.got = lax.all_to_all(given, "fsdp", 0, 0, tiled=True)
        return [given], [self.got]

    def whole(self, weights, out_grads, *gate):
        each, width = weights[0].shape
        got, out_got = after((self.got, out_grads.from_x), *gate)
        flag = (out_grads.x == out_grads.y).astype(jnp.int32).reshape(1, 1)
        flat = jax.ShapeDtypeStruct((each, width), jnp.float32)
        column = jax.ShapeDtypeStruct((each, 1), jnp.float32)
        out = pl.pallas_call(
            own_grads_kernel,
            out_shape=[
                flat,
                flat,
                flat,
                column,
                column,
                jax.ShapeDtypeStruct((16, 128), jnp.float32),
                flat,
            ],
            compiler_params=pltpu.CompilerParams(vmem_limit_bytes=6 * 2**20),
            cost_estimate=FREE,
            name="own_grads",
        )(got, *weights, flag, out_grads.kept, out_got)
        return out, out[5][0, :each]


def out_rows(own, x, y, c, before, late):
    head = in_order(x, own, x_swap(own))
    pairs = [(place, place ^ 16) for place in range(32) if place // 16 == place % 2]
    got = lax.ppermute(after(head, *before), ("dp", "fsdp"), pairs)
    mine = jnp.where(x == y, head, after(got, *late))
    return in_order(c, mine, core_swap(mine))


class OutGrads:
    def __init__(self, grad, x, y, c):
        self.grad, self.x, self.y, self.c = grad, x, y, c

    def along_core(self, *gate):
        head, width = self.grad.shape[0] // 2, self.grad.shape[1]
        kept = lax.dynamic_slice(self.grad, (head * self.c, 0), (head, width))
        given = lax.dynamic_slice(self.grad, (head * (1 - self.c), 0), (head, width))
        given = after(given.astype(jnp.bfloat16), *gate)
        self.total = kept + core_swap(given).astype(jnp.float32)
        return [given]

    def along_y(self, *gate):
        pairs = [(place, place ^ 16) for place in range(32) if place // 16 != place % 2]
        given = after(self.total.astype(jnp.bfloat16), *gate)
        self.from_y = lax.ppermute(given, ("dp", "fsdp"), pairs)
        return [given]

    def along_x(self, *gate):
        total = self.total + after(self.from_y, *gate).astype(jnp.float32)
        each, width = total.shape[0] // 2, total.shape[1]
        self.kept = lax.dynamic_slice(total, (each * self.x, 0), (each, width))
        given = lax.dynamic_slice(total, (each * (1 - self.x), 0), (each, width))
        pairs = [(place, place ^ 1) for place in range(32) if place // 16 == place % 2]
        self.from_x = lax.ppermute(given.astype(jnp.bfloat16), ("dp", "fsdp"), pairs)


def hidden_units(rows, dp, *gate):
    return own_first(lax.all_gather(after(rows, *gate), "dp", axis=0, tiled=True), dp)


def hidden_core_kernel(count, *refs):
    units, rows, out_refs = refs[:count], refs[count : 2 * count], refs[2 * count :]
    half = units[0].shape[1] // 2
    total = sum(
        columns_by_columns(unit_ref[:, half:], row_ref[...]) for unit_ref, row_ref in zip(units, rows)
    ).astype(jnp.bfloat16)
    out_refs[0][...] = total[: half // 2]
    out_refs[1][...] = total[half // 2 :]


def hidden_y_kernel(count, *refs):
    units, rows = refs[:count], refs[count : 2 * count]
    own_got_ref, y_got_ref, kept_ref, given_ref = refs[2 * count :]
    half = units[0].shape[1] // 2
    total = sum(
        columns_by_columns(unit_ref[:, :half], row_ref[...]) for unit_ref, row_ref in zip(units, rows)
    )
    kept_ref[...] = total[: half // 2] + own_got_ref[...].astype(jnp.float32)
    given = total[half // 2 :] + y_got_ref[...].astype(jnp.float32)
    given_ref[...] = given.astype(jnp.bfloat16)


def out_grad_kernel(att_ref, *refs):
    *rows, out_ref = refs
    count = rows[0].shape[0]
    out_ref[...] = sum(
        columns_by_columns(att_ref[count * place : count * (place + 1), :], row_ref[...])
        for place, row_ref in enumerate(rows)
    )


def out_grad(attended, pieces):
    width = pieces[0].shape[1]
    block = width // 2
    return pl.pallas_call(
        out_grad_kernel,
        grid=(2,),
        in_specs=[whole_block(attended)]
        + [pl.BlockSpec((rows.shape[0], block), lambda i: (0, i)) for rows in pieces],
        out_specs=pl.BlockSpec((attended.shape[1], block), lambda i: (0, i)),
        out_shape=jax.ShapeDtypeStruct((attended.shape[1], width), jnp.float32),
        compiler_params=pltpu.CompilerParams(vmem_limit_bytes=10 * 2**20),
        cost_estimate=FREE,
        name="out_grad",
    )(attended, *pieces)


class HiddenGrads:
    def __init__(self, units, rows):
        self.units, self.rows = list(units), list(rows)

    def call(self, kernel, got, outs, *gate):
        width = self.rows[0].shape[1]
        block = width // 2
        units = after(tuple(self.units), *gate)

        def spec(rows):
            return pl.BlockSpec((rows, block), lambda i: (0, i))

        return pl.pallas_call(
            functools.partial(kernel, len(self.units)),
            grid=(2,),
            in_specs=[whole_block(unit) for unit in units]
            + [spec(rows.shape[0]) for rows in self.rows]
            + [spec(rows.shape[0]) for rows in got],
            out_specs=[spec(rows) for rows, dtype in outs],
            out_shape=[jax.ShapeDtypeStruct((rows, width), dtype) for rows, dtype in outs],
            compiler_params=pltpu.CompilerParams(vmem_limit_bytes=14 * 2**20),
            cost_estimate=LONG,
            name="hidden_grads",
        )(*units, *self.rows, *got)

    def along_core(self, *gate):
        half = self.units[0].shape[1] // 2
        given = self.call(hidden_core_kernel, [], [(half // 2, jnp.bfloat16)] * 2, *gate)
        self.from_core = [core_swap(value) for value in given]
        return given

    def along_y(self, *gate):
        half = self.units[0].shape[1] // 2
        self.kept, given = self.call(
            hidden_y_kernel,
            self.from_core,
            [(half // 2, jnp.float32), (half // 2, jnp.bfloat16)],
            *gate,
        )
        self.from_y = y_swap(given)
        return [given]


def fast_body(
    hidden,
    source,
    cotangent,
    row_counts,
    seq_lengths,
    kv_gain,
    w_key,
    w_value,
    attn_gain,
    w_query,
    w_out,
    ffn_gain,
    w_gate,
    w_up,
    w_down,
):
    local_rows, width = hidden.shape
    head = width // HEADS
    dp = lax.axis_index("dp")
    fsdp = lax.axis_index("fsdp")
    y, c = dp // 2, dp % 2
    z, x = fsdp // 2, fsdp % 2
    me = 8 * dp + fsdp

    order = z ^ (z >> 1)
    devices = []
    for step in range(4):
        place = (order - step) % 4
        for side in range(2):
            devices.append(2 * (place ^ (place >> 1)) + (x ^ side))
    slots = (
        jnp.stack(devices).astype(jnp.int32)[:, None] * local_rows
        + jnp.arange(local_rows, dtype=jnp.int32)[None, :]
    ).reshape(-1)
    live, position, sequence = slot_layout(row_counts, seq_lengths, slots, local_rows)
    starts = jnp.concatenate([jnp.zeros((1,), jnp.int32), jnp.cumsum(seq_lengths[0])])
    first = jnp.sum(
        jnp.where(
            sequence[:, None] == jnp.arange(starts.shape[0], dtype=jnp.int32)[None, :],
            starts[None, :],
            0,
        ),
        axis=1,
    )
    first, last = first[:, None], position[:, None]
    place_of_key = jnp.where(live, position, -1)[None, :]
    own_live = live[:local_rows].astype(jnp.float32)[:, None]

    d_out = cotangent.astype(jnp.float32) * own_live
    d_out_low = d_out.astype(jnp.bfloat16)
    layout = lax.optimization_barrier((first, last, place_of_key, own_live, d_out_low))
    first, last, place_of_key, own_live, d_out_low = layout

    each = kv_gain.shape[0]
    inputs = Gather(jnp.concatenate([source, hidden], axis=0))
    columns = Columns(
        [w_query, w_key, w_value], jnp.concatenate([kv_gain, attn_gain, ffn_gain]), dp
    )
    wa = columns.along_fsdp()
    s1 = move([inputs])
    wy = columns.along_y(*s1)
    units = w_gate.shape[0]
    padded = -(-units // 64) * 64
    own_units = [
        jnp.pad(own, ((0, padded - units), (0, 0))) for own in (w_gate, w_up, w_down)
    ]
    s2 = move([inputs], *s1, *wa, *layout, *own_units)
    wc = columns.along_core(*wy)
    s3 = move([inputs], *s2)
    wq, w_kv, gains = columns.whole()
    kv_gain_full, attn_gain_full, ffn_gain_full = (
        gains[:, which * each : (which + 1) * each].reshape(1, width) for which in range(3)
    )
    wg, wu, wd = (hidden_units(own, dp, *s2, *wy) for own in own_units)

    hidden_f = hidden.astype(jnp.float32)
    projected = []

    def project_piece(step, cost, *gate):
        piece = after(inputs.arrays(step), *(value[3] for value in projected[-1:]), *gate)
        projected.append(project(piece, kv_gain_full, attn_gain_full, w_kv, wq, cost))

    project_piece(0, FREE)
    project_piece(1, FREE)
    s4 = move([inputs], *s3)
    project_piece(2, LONG, *s3)
    cots = Gather(d_out_low)
    c1 = move([cots], *s4, projected[2][3])
    project_piece(3, LONG)
    src_low, hid_low, pairs, queries = zip(*projected)
    queries = jnp.concatenate(queries, axis=0)
    pairs = jnp.concatenate(pairs, axis=0)
    c2 = move([cots], *c1, pairs, queries)
    attended_f, attended_low, lse = attend(
        *after((queries, pairs), *c1), first, last, place_of_key, head
    )
    wo = out_rows(after(w_out, *s2), x, y, c, s3, c1)

    def rows_of(array, step):
        return array[2 * step * local_rows : 2 * (step + 1) * local_rows]

    def branch_terms(step, *gate):
        return product(after(rows_of(attended_low, step), *gate), wo).astype(jnp.bfloat16)

    branch = Scatter()
    b1 = move([branch.of(branch_terms(1)), cots], *c2)
    b2 = move([branch.of(branch_terms(2)), cots], *b1)
    b3 = move([branch.of(branch_terms(3, *b1))], *b2)
    b4 = move([branch.of(branch_terms(0, *b2))], *b3)
    middle = hidden_f + branch.total()
    middle_scale = inverse_scale(middle)
    middle_unit = middle * middle_scale
    mids = Gather((middle_unit * ffn_gain_full).astype(jnp.bfloat16))

    fed = []

    def feed_piece(step, *gate):
        weights = after((wg, wu, wd), *gate)
        fed.append(feed(mids.pieces[step], cots.pieces[step], *weights))

    def terms_of(step):
        own, other = fed[step][3:5]
        return back.of_rows(rows_in(own), rows_in(other))

    back = Scatter()
    m1 = move([mids])
    m2 = move([mids], *m1)
    feed_piece(0)
    m3 = move([mids], *m2, fed[0][0])
    feed_piece(1, *m2)
    d1 = move([mids, terms_of(1)], *m3)
    feed_piece(2, *m3)
    d2 = move([terms_of(2)], *d1)
    feed_piece(3, *d1)
    d3 = move([terms_of(3)], *d2)
    inners, d_gates, d_ups, _, _, all_mids, all_cots = zip(*fed)
    gate_sums = HiddenGrads(d_gates, all_mids)
    up_sums = HiddenGrads(d_ups, all_mids)
    down_sums = HiddenGrads(inners, all_cots)
    h1 = gate_sums.along_core(*d2)
    d4 = move([terms_of(0)], *d3, *h1)
    h2 = up_sums.along_core(*d3)
    d_normed = after(back.total(), *h2)
    d_middle = d_out + norm_backward(middle, middle_scale, ffn_gain_full, d_normed)
    d_branch_low = d_middle.astype(jnp.bfloat16)
    outs = Gather(d_branch_low)
    e1 = move([outs])
    def result_terms(step, *gate):
        return product(after(inners[step], *gate), wd).astype(jnp.bfloat16)

    h1 = gate_sums.along_y(d_branch_low)
    h3 = down_sums.along_core(*h1)
    e2 = move([outs], *e1, *h3)
    h2 = up_sums.along_y(*e1)
    first_result = result_terms(1, *e1, *h2)
    ffn_gain_part = jnp.sum(after(d_normed * middle_unit, first_result), axis=0)
    column_grads = ColumnGrads(dp)
    column_grads.gain_core(ffn_gain_part)
    column_grads.gain_y()
    e3 = move([outs], *e2, *h2, ffn_gain_part)
    h3 = down_sums.along_y(*e2)

    result = Scatter()
    e4 = move([outs, result.of(first_result)], *e3, *h3, gate_sums.from_y, column_grads.gain)
    d_branches, d_attended = zip(*(branch_back(outs.pieces[step], wo) for step in range(4)))
    d_attended = jnp.concatenate(d_attended, axis=0)
    o2 = move([result.of(result_terms(2, *e3))], *e4)
    d_queries, d_pairs = attend_back(
        queries, pairs, first, last, place_of_key, lse, attended_f, d_attended, head
    )
    d_queries, d_pairs = after((d_queries, d_pairs), *o2)
    d_src, d_hid = Scatter(), Scatter()

    def terms(step, *gate, result=()):
        parts = [d_src, d_hid, *result[:1]]
        rows = after((d_pairs, d_queries), *gate)
        weights = (inners[result[1]], wd) if result else ()
        return back_terms(parts, step, *rows, w_kv, wq, weights)

    first_terms = terms(1)
    started = d_hid.own.array
    sent = []
    i1 = move(first_terms, *o2, up_sums.from_y, payload=sent)
    second_terms = terms(2, started, result=(result, 3))
    sources, hiddens = after((tuple(src_low), tuple(hid_low)), *sent, result.own.array)
    column_grads.along_core(sources, hiddens, d_queries, d_pairs)
    i2 = move(second_terms, *i1, down_sums.from_y)
    py = column_grads.along_y()
    next_terms = terms(3, *py, result=(result, 0))
    out_grads = OutGrads(
        out_grad(after(attended_low, *py), d_branches),
        x,
        y,
        c,
    )
    out_grads.along_core()
    oy = out_grads.along_y(column_grads.from_y)
    pz, got_z = column_grads.along_fsdp()
    i3 = move(next_terms, *i2, *oy)
    out_grads.along_x(*i2)
    i4 = move(terms(0, *i2), *i3)
    grad_gate, grad_up, grad_down = add_all(
        *zip(
            *(
                (sums.kept, after(sums.from_y, *i3))
                for sums in (gate_sums, up_sums, down_sums)
            )
        ),
        units,
    )
    output = result_of(after(middle, grad_gate), own_live, result)
    own_grads, grad_ffn_gain = column_grads.whole([w_query, w_key, w_value], out_grads, grad_gate)
    grad_query, grad_key, grad_value, query_sum, pair_sum, gain_sum, grad_out = own_grads
    grad_attn_gain = query_sum[:, 0] / attn_gain.astype(jnp.float32)
    grad_kv_gain = pair_sum[:, 0] / kv_gain.astype(jnp.float32)

    grad_hidden, grad_source = input_grads(
        hidden, source, d_middle, attn_gain_full, kv_gain_full, d_hid, d_src
    )
    return (
        output,
        grad_hidden,
        grad_source,
        grad_kv_gain,
        grad_key,
        grad_value,
        grad_attn_gain,
        grad_query,
        grad_out,
        grad_ffn_gain,
        grad_gate,
        grad_up,
        grad_down,
    )


def solution(mesh):
    in_specs = (
        P(("dp", "fsdp"), None),
        P(("dp", "fsdp"), None),
        P(("dp", "fsdp"), None),
        P("dp", None),
        P("dp", None),
        P(("dp", "fsdp")),
        P(("dp", "fsdp"), None),
        P(("dp", "fsdp"), None),
        P(("dp", "fsdp")),
        P(("dp", "fsdp"), None),
        P(("dp", "fsdp"), None),
        P(("dp", "fsdp")),
        P(("dp", "fsdp"), None),
        P(("dp", "fsdp"), None),
        P(("dp", "fsdp"), None),
    )
    out_specs = (
        P(("dp", "fsdp"), None),
        P(("dp", "fsdp"), None),
        P(("dp", "fsdp"), None),
        P(("dp", "fsdp")),
        P(("dp", "fsdp"), None),
        P(("dp", "fsdp"), None),
        P(("dp", "fsdp")),
        P(("dp", "fsdp"), None),
        P(("dp", "fsdp"), None),
        P(("dp", "fsdp")),
        P(("dp", "fsdp"), None),
        P(("dp", "fsdp"), None),
        P(("dp", "fsdp"), None),
    )
    placed = (
        mesh.shape["dp"] == 4 and mesh.shape["fsdp"] == 8 and HEADS == 2 * mesh.shape["fsdp"]
    )
    chosen = fast_body if placed else body
    return jax.shard_map(chosen, mesh=mesh, in_specs=in_specs, out_specs=out_specs, check_vma=False)
```

```python
import functools
import math

import jax
import jax.numpy as jnp
from jax import lax
from jax.experimental import pallas as pl
from jax.experimental.pallas import tpu as pltpu
from jax.sharding import PartitionSpec as P

HEADS = 16


EPSILON = 1e-06
MASKED = -1000000000.0


def product(left, right):
    return jnp.dot(left, right, preferred_element_type=jnp.float32)


def rows_by_rows(left, right):
    return lax.dot_general(
        left, right, (((1,), (1,)), ((), ())), preferred_element_type=jnp.float32
    )


def columns_by_columns(left, right):
    return lax.dot_general(
        left, right, (((0,), (0,)), ((), ())), preferred_element_type=jnp.float32
    )


def inverse_scale(values):
    return lax.rsqrt(jnp.mean(values * values, axis=-1, keepdims=True) + EPSILON)


def norm_backward(values, scale, gain, d_normed):
    weighted = d_normed * gain
    return scale * weighted - values * scale**3 * jnp.mean(
        values * weighted, axis=-1, keepdims=True
    )


def slot_layout(row_counts, seq_lengths, slots, per_device):
    counts = row_counts[0]
    offsets = jnp.cumsum(counts) - counts
    device_of = slots // per_device
    within = slots - device_of * per_device
    picker = device_of[:, None] == jnp.arange(counts.shape[0], dtype=jnp.int32)[None, :]
    count_here = jnp.sum(jnp.where(picker, counts[None, :], 0), axis=1)
    offset_here = jnp.sum(jnp.where(picker, offsets[None, :], 0), axis=1)
    position = offset_here + within
    ends = jnp.cumsum(seq_lengths[0])
    sequence = jnp.sum((ends[None, :] <= position[:, None]).astype(jnp.int32), axis=1)
    return (within < count_here, position, sequence)


def body(
    hidden,
    source,
    cotangent,
    row_counts,
    seq_lengths,
    kv_gain,
    w_key,
    w_value,
    attn_gain,
    w_query,
    w_out,
    ffn_gain,
    w_gate,
    w_up,
    w_down,
):
    local_rows, model_width = hidden.shape
    group_rows = local_rows * lax.axis_size("fsdp")
    head_size = model_width // HEADS
    factor = 1.0 / math.sqrt(head_size)
    block_rows = math.gcd(group_rows, 512)
    block_count = group_rows // block_rows
    own_slots = lax.axis_index("fsdp") * local_rows + jnp.arange(local_rows, dtype=jnp.int32)
    query_live, query_position, query_sequence = slot_layout(
        row_counts, seq_lengths, own_slots, local_rows
    )
    key_live, key_position, key_sequence = slot_layout(
        row_counts, seq_lengths, jnp.arange(group_rows, dtype=jnp.int32), local_rows
    )
    live_column = query_live.astype(jnp.float32)[:, None]
    source_f = source.astype(jnp.float32)
    hidden_f = hidden.astype(jnp.float32)
    source_scale = inverse_scale(source_f)
    hidden_scale = inverse_scale(hidden_f)
    source_unit = source_f * source_scale
    hidden_unit = hidden_f * hidden_scale
    piece_kv_gain = lax.all_gather(kv_gain, ("dp", "fsdp"), axis=0, tiled=True)
    piece_key = lax.all_gather(w_key, ("dp", "fsdp"), axis=0, tiled=True)
    piece_value = lax.all_gather(w_value, ("dp", "fsdp"), axis=0, tiled=True)
    piece_attn_gain = lax.all_gather(attn_gain, ("dp", "fsdp"), axis=0, tiled=True)
    piece_query = lax.all_gather(w_query, ("dp", "fsdp"), axis=0, tiled=True)
    piece_ffn_gain = lax.all_gather(ffn_gain, ("dp", "fsdp"), axis=0, tiled=True)
    source_cols = (source_unit * piece_kv_gain.astype(jnp.float32)[None, :]).astype(jnp.bfloat16)
    hidden_cols = (hidden_unit * piece_attn_gain.astype(jnp.float32)[None, :]).astype(jnp.bfloat16)
    key_sum = product(source_cols, piece_key)
    value_sum = product(source_cols, piece_value)
    query_sum = product(hidden_cols, piece_query)
    stacked = jnp.stack([piece_kv_gain, piece_attn_gain, piece_ffn_gain]).astype(jnp.float32)
    gains = stacked
    key_sum, value_sum, query_sum, gains = (key_sum, value_sum, query_sum, gains)
    kv_gain_full, attn_gain_full, ffn_gain_full = (gains[0], gains[1], gains[2])
    keys_low = key_sum.astype(jnp.bfloat16)
    values_low = value_sum.astype(jnp.bfloat16)
    queries_low = query_sum.astype(jnp.bfloat16)
    group_keys, group_values = (
        lax.all_gather(keys_low, "fsdp", axis=0, tiled=True),
        lax.all_gather(values_low, "fsdp", axis=0, tiled=True),
    )
    blocks = (
        group_keys.reshape(block_count, block_rows, HEADS, head_size),
        group_values.reshape(block_count, block_rows, HEADS, head_size),
        key_live.reshape(block_count, block_rows),
        key_position.reshape(block_count, block_rows),
        key_sequence.reshape(block_count, block_rows),
    )
    query_heads = queries_low.reshape(local_rows, HEADS, head_size)

    def block_scores(key_block, live_block, position_block, sequence_block):
        scores = (
            jnp.einsum("qhd,khd->hqk", query_heads, key_block, preferred_element_type=jnp.float32)
            * factor
        )
        allowed = (
            live_block[None, :]
            & (sequence_block[None, :] == query_sequence[:, None])
            & (position_block[None, :] <= query_position[:, None])
        )
        return jnp.where(allowed[None], scores, MASKED)

    def running_total(running, key_block_set):
        largest, summed = running
        key_block, value_block, live_block, position_block, sequence_block = key_block_set
        masked = block_scores(key_block, live_block, position_block, sequence_block)
        new_largest = jnp.maximum(largest, jnp.max(masked, axis=-1))
        summed = summed * jnp.exp(largest - new_largest) + jnp.sum(
            jnp.exp(masked - new_largest[:, :, None]), axis=-1
        )
        return ((new_largest, summed), None)

    (largest, summed), unused = lax.scan(
        running_total,
        (
            jnp.full((HEADS, local_rows), MASKED, jnp.float32),
            jnp.zeros((HEADS, local_rows), jnp.float32),
        ),
        blocks,
    )
    log_total = largest + jnp.log(summed)

    def weighted_sum(running, key_block_set):
        key_block, value_block, live_block, position_block, sequence_block = key_block_set
        probs_low = jnp.exp(
            block_scores(key_block, live_block, position_block, sequence_block)
            - log_total[:, :, None]
        ).astype(jnp.bfloat16)
        return (
            running
            + jnp.einsum(
                "hqk,khd->qhd", probs_low, value_block, preferred_element_type=jnp.float32
            ),
            None,
        )

    attended_f, unused = lax.scan(
        weighted_sum, jnp.zeros((local_rows, HEADS, head_size), jnp.float32), blocks
    )
    attended_low = attended_f.reshape(local_rows, model_width).astype(jnp.bfloat16)
    branch = product(attended_low, lax.all_gather(w_out, ("dp", "fsdp"), axis=0, tiled=True))
    middle = hidden_f + branch
    middle_scale = inverse_scale(middle)
    middle_unit = middle * middle_scale
    middle_low = (middle_unit * ffn_gain_full).astype(jnp.bfloat16)
    piece_gate = lax.all_gather(w_gate, ("dp", "fsdp"), axis=0, tiled=True)
    piece_up = lax.all_gather(w_up, ("dp", "fsdp"), axis=0, tiled=True)
    piece_down = lax.all_gather(w_down, ("dp", "fsdp"), axis=0, tiled=True)
    gate_value = rows_by_rows(middle_low, piece_gate)
    up_value = rows_by_rows(middle_low, piece_up)
    inner = (jax.nn.silu(gate_value) * up_value).astype(jnp.bfloat16)
    ffn_result = product(inner, piece_down)
    output = ((middle + ffn_result) * live_column).astype(jnp.bfloat16)
    d_out = cotangent.astype(jnp.float32) * live_column
    d_out_low = d_out.astype(jnp.bfloat16)
    piece_gate = lax.all_gather(w_gate, ("dp", "fsdp"), axis=0, tiled=True)
    piece_up = lax.all_gather(w_up, ("dp", "fsdp"), axis=0, tiled=True)
    piece_down = lax.all_gather(w_down, ("dp", "fsdp"), axis=0, tiled=True)
    gate_value = rows_by_rows(middle_low, piece_gate)
    up_value = rows_by_rows(middle_low, piece_up)
    sigmoid_gate = jax.nn.sigmoid(gate_value)
    swished = gate_value * sigmoid_gate
    inner = (swished * up_value).astype(jnp.bfloat16)
    d_inner = rows_by_rows(d_out_low, piece_down)
    d_gate = (d_inner * up_value * sigmoid_gate * (1.0 + gate_value * (1.0 - sigmoid_gate))).astype(
        jnp.bfloat16
    )
    d_up = (d_inner * swished).astype(jnp.bfloat16)
    d_normed = product(d_gate, piece_gate) + product(d_up, piece_up)
    ffn_grads = lax.psum_scatter(
        jnp.stack(
            [
                columns_by_columns(d_gate, middle_low),
                columns_by_columns(d_up, middle_low),
                columns_by_columns(inner, d_out_low),
            ],
            axis=1,
        ),
        ("dp", "fsdp"),
        scatter_dimension=0,
        tiled=True,
    )
    ffn_gain_part = jnp.sum(d_normed * middle_unit, axis=0)
    d_middle = d_out + norm_backward(middle, middle_scale, ffn_gain_full, d_normed)
    d_branch_low = d_middle.astype(jnp.bfloat16)
    d_attended = rows_by_rows(
        d_branch_low, lax.all_gather(w_out, ("dp", "fsdp"), axis=0, tiled=True)
    )
    d_heads = d_attended.astype(jnp.bfloat16).reshape(local_rows, HEADS, head_size)
    delta = jnp.sum(d_heads.astype(jnp.float32) * attended_f, axis=-1).T

    def attention_backward(d_query_sum, key_block_set):
        key_block, value_block, live_block, position_block, sequence_block = key_block_set
        probs = jnp.exp(
            block_scores(key_block, live_block, position_block, sequence_block)
            - log_total[:, :, None]
        )
        probs_low = probs.astype(jnp.bfloat16)
        d_values = jnp.einsum(
            "hqk,qhd->khd", probs_low, d_heads, preferred_element_type=jnp.float32
        )
        d_probs = jnp.einsum(
            "qhd,khd->hqk", d_heads, value_block, preferred_element_type=jnp.float32
        )
        d_scores = (probs * (d_probs - delta[:, :, None])).astype(jnp.bfloat16)
        d_query_sum = d_query_sum + jnp.einsum(
            "hqk,khd->qhd", d_scores, key_block, preferred_element_type=jnp.float32
        )
        d_keys = (
            jnp.einsum("hqk,qhd->khd", d_scores, query_heads, preferred_element_type=jnp.float32)
            * factor
        )
        return (d_query_sum, jnp.stack([d_keys, d_values], axis=1))

    d_query_sum, key_terms = lax.scan(
        attention_backward, jnp.zeros((local_rows, HEADS, head_size), jnp.float32), blocks
    )
    key_grads = lax.psum_scatter(
        key_terms.reshape(group_rows, 2, model_width).astype(jnp.bfloat16),
        "fsdp",
        scatter_dimension=0,
        tiled=True,
    ).astype(jnp.float32)
    d_keys_low = key_grads[:, 0].astype(jnp.bfloat16)
    d_values_low = key_grads[:, 1].astype(jnp.bfloat16)
    d_queries_low = (d_query_sum * factor).reshape(local_rows, model_width).astype(jnp.bfloat16)
    piece_query = lax.all_gather(w_query, ("dp", "fsdp"), axis=0, tiled=True)
    piece_key = lax.all_gather(w_key, ("dp", "fsdp"), axis=0, tiled=True)
    piece_value = lax.all_gather(w_value, ("dp", "fsdp"), axis=0, tiled=True)
    hidden_part = rows_by_rows(d_queries_low, piece_query)
    source_part = rows_by_rows(d_keys_low, piece_key) + rows_by_rows(d_values_low, piece_value)
    input_back = jnp.stack([hidden_part, source_part])
    grad_hidden = (
        d_middle + norm_backward(hidden_f, hidden_scale, attn_gain_full, input_back[0])
    ).astype(jnp.bfloat16)
    grad_source = norm_backward(source_f, source_scale, kv_gain_full, input_back[1]).astype(
        jnp.bfloat16
    )
    attn_gain_part = jnp.sum(input_back[0] * hidden_unit, axis=0)
    kv_gain_part = jnp.sum(input_back[1] * source_unit, axis=0)
    source_low = (source_unit * kv_gain_full).astype(jnp.bfloat16)
    hidden_low = (hidden_unit * attn_gain_full).astype(jnp.bfloat16)
    hidden_part = hidden_low
    source_part = source_low
    layer_stack = lax.psum_scatter(
        jnp.stack(
            [
                columns_by_columns(hidden_part, d_queries_low),
                columns_by_columns(source_part, d_keys_low),
                columns_by_columns(source_part, d_values_low),
                columns_by_columns(attended_low, d_branch_low),
            ],
            axis=1,
        ),
        ("dp", "fsdp"),
        scatter_dimension=0,
        tiled=True,
    )
    grad_query, grad_key, grad_value, grad_out = (
        layer_stack[:, 0],
        layer_stack[:, 1],
        layer_stack[:, 2],
        layer_stack[:, 3],
    )
    grad_kv_gain, grad_attn_gain, grad_ffn_gain = (
        lax.psum_scatter(kv_gain_part, ("dp", "fsdp"), scatter_dimension=0, tiled=True),
        lax.psum_scatter(attn_gain_part, ("dp", "fsdp"), scatter_dimension=0, tiled=True),
        lax.psum_scatter(ffn_gain_part, ("dp", "fsdp"), scatter_dimension=0, tiled=True),
    )
    return (
        output,
        grad_hidden,
        grad_source,
        grad_kv_gain,
        grad_key,
        grad_value,
        grad_attn_gain,
        grad_query,
        grad_out,
        grad_ffn_gain,
        ffn_grads[:, 0],
        ffn_grads[:, 1],
        ffn_grads[:, 2],
    )


RING = (0, 1, 3, 2)
BLOCK = 256


def swap_pairs(size, mask):
    return [(place, place ^ mask) for place in range(size)]


def ring_pairs():
    return [
        (2 * RING[place] + x, 2 * RING[(place + 1) % 4] + x) for place in range(4) for x in range(2)
    ]


def x_swap(value):
    return lax.ppermute(value, "fsdp", swap_pairs(8, 1))


def ring_step(value):
    return lax.ppermute(value, "fsdp", ring_pairs())


def y_swap(value):
    return lax.ppermute(value, "dp", swap_pairs(4, 2))


def core_swap(value):
    return lax.ppermute(value, "dp", swap_pairs(4, 1))


def in_order(flag, first, second):
    swapped = flag == 1
    return jnp.concatenate(
        [jnp.where(swapped, second, first), jnp.where(swapped, first, second)], axis=0
    )


def after(value, *earlier):
    if not earlier:
        return value
    return lax.optimization_barrier((value, *earlier))[0]


FREE = pl.CostEstimate(flops=0, bytes_accessed=0, transcendentals=0)
LONG = pl.CostEstimate(flops=2 * 10**10, bytes_accessed=0, transcendentals=0)


class Rows:
    def __init__(self, array, start, count):
        self.array, self.start, self.count = array, start, count

    def part(self, start, count):
        return Rows(self.array, self.start + start, count)

    def value(self):
        if self.count == self.array.shape[0]:
            return self.array
        return self.array[self.start : self.start + self.count]


def rows_in(array):
    return Rows(array, 0, array.shape[0])


class Gather:
    def __init__(self, own):
        self.held = rows_in(own)
        self.pieces = []

    def send(self):
        if len(self.pieces) < 3:
            return [[self.held]], [[self.held]]
        half = self.held.count // 2
        return [[self.held.part(0, half)]], [[self.pieces[2][1].part(half, half)]]

    def take(self, from_x, from_ring):
        if len(self.pieces) < 3:
            self.pieces.append((self.held, from_x))
            self.held = from_ring
        else:
            self.pieces.append((self.held, from_x, from_ring))

    def arrays(self, step):
        return tuple(rows.value() for rows in self.pieces[step])

    def piece(self, step):
        return jnp.concatenate(self.arrays(step), axis=0)


class Scatter:
    def __init__(self):
        self.stage = 0

    def of(self, terms):
        rows = terms.shape[0] // 2
        return self.of_rows(Rows(terms, 0, rows), Rows(terms, rows, rows))

    def of_rows(self, own, other):
        self.own, self.other = own, other
        return self

    def send(self):
        own, other = self.own, self.other
        half = own.count // 2
        if self.stage == 0:
            given = [[other.part(0, half)]], [[other.part(half, half)]]
        elif self.stage == 1:
            kept, (from_x, from_ring) = self.kept, self.got
            given = (
                [[other.part(0, half)], [other.part(half, half), from_ring]],
                [[kept.part(0, half), from_x], [kept.part(half, half)]],
            )
        else:
            given = [[other]], [[self.kept, *self.got]]
        self.stage += 1
        self.kept = own
        return given

    def take(self, from_x, from_ring):
        self.got = (from_x, from_ring)

    def total(self):
        return sum(rows.value().astype(jnp.float32) for rows in (self.kept, *self.got))


def mix_kernel(plans, *refs):
    for plan, out_ref in zip(plans, refs[-len(plans) :]):
        first = 0
        for places, count in plan:
            values = [refs[index][start : start + count, :] for index, start in places]
            if len(values) > 1:
                values = [sum(value.astype(jnp.float32) for value in values)]
            out_ref[first : first + count, :] = values[0].astype(out_ref.dtype)
            first += count


def only_array(sums):
    array = sums[0][0].array
    first = 0
    for rows in sums:
        if len(rows) > 1 or rows[0].array is not array or rows[0].start != first:
            return None
        first += rows[0].count
    return array if first == array.shape[0] else None


def mixed(*all_sums):
    arrays = []
    plans = []
    for sums in all_sums:
        plan = []
        for rows in sums:
            places = []
            for part in rows:
                index = next((n for n, held in enumerate(arrays) if held is part.array), None)
                if index is None:
                    index = len(arrays)
                    arrays.append(part.array)
                places.append((index, part.start))
            plan.append((tuple(places), rows[0].count))
        plans.append(tuple(plan))
    width = arrays[0].shape[1]
    counts = [sum(count for places, count in plan) for plan in plans]
    return pl.pallas_call(
        functools.partial(mix_kernel, tuple(plans)),
        out_shape=[jax.ShapeDtypeStruct((count, width), jnp.bfloat16) for count in counts],
        compiler_params=pltpu.CompilerParams(vmem_limit_bytes=10 * 2**20),
        cost_estimate=FREE,
        name="mix",
    )(*arrays)


def move(parts, *gate, payload=None):
    sent = [part.send() for part in parts]
    x_sums, ring_sums = (sum((given[way] for given in sent), []) for way in range(2))
    along_x, along_ring = only_array(x_sums), only_array(ring_sums)
    if along_x is None and along_ring is None:
        along_x, along_ring = mixed(x_sums, ring_sums)
    elif along_x is None:
        (along_x,) = mixed(x_sums)
    elif along_ring is None:
        (along_ring,) = mixed(ring_sums)
    along_x, along_ring = after((along_x, along_ring), *gate)
    if payload is not None:
        payload += [along_x, along_ring]
    from_x, from_ring = x_swap(along_x), ring_step(along_ring)
    x_row = ring_row = 0
    for part, given in zip(parts, sent):
        x_count, ring_count = (sum(rows[0].count for rows in sums) for sums in given)
        part.take(Rows(from_x, x_row, x_count), Rows(from_ring, ring_row, ring_count))
        x_row, ring_row = x_row + x_count, ring_row + ring_count
    return [from_x, from_ring]


def attend_kernel(
    factor, q_ref, k_ref, v_ref, first_ref, last_ref, place_ref, att_ref, low_ref, lse_ref
):
    scores = rows_by_rows(q_ref[...], k_ref[...]) * factor
    places = place_ref[...]
    allowed = (places >= first_ref[...]) & (places <= last_ref[...])
    masked = jnp.where(allowed, scores, MASKED)
    largest = jnp.max(masked, axis=-1, keepdims=True)
    raised = jnp.exp(masked - largest)
    summed = jnp.sum(raised, axis=-1, keepdims=True)
    probs_low = (raised * (1.0 / summed)).astype(jnp.bfloat16)
    attended = product(probs_low, v_ref[...])
    att_ref[...] = attended
    low_ref[...] = attended.astype(jnp.bfloat16)
    lse_ref[...] = (largest + jnp.log(summed))[None]


def attend_back_kernel(
    factor,
    q_ref,
    k_ref,
    v_ref,
    first_ref,
    last_ref,
    place_ref,
    lse_ref,
    att_ref,
    d_att_ref,
    dq_ref,
    dkv_ref,
    dk_sum,
    dv_sum,
):
    head = pl.program_id(0)
    step = pl.program_id(1)
    size = q_ref.shape[1]
    mine = dkv_ref.shape[1] // 2

    @pl.when(step == 0)
    def _():
        dk_sum[...] = jnp.zeros_like(dk_sum)
        dv_sum[...] = jnp.zeros_like(dv_sum)

    queries = q_ref[...]
    keys = k_ref[...]
    d_att = d_att_ref[...]
    scores = rows_by_rows(queries, keys) * factor
    places = place_ref[...]
    allowed = (places >= first_ref[...]) & (places <= last_ref[...])
    probs = jnp.exp(jnp.where(allowed, scores, MASKED) - lse_ref[0])
    delta = jnp.sum(d_att.astype(jnp.float32) * att_ref[...], axis=-1, keepdims=True)
    d_probs = rows_by_rows(d_att, v_ref[...])
    d_scores = (probs * (d_probs - delta)).astype(jnp.bfloat16)
    dq_ref[...] = (product(d_scores, keys) * factor).astype(jnp.bfloat16)
    dk_sum[...] += columns_by_columns(d_scores, queries)
    dv_sum[...] += columns_by_columns(probs.astype(jnp.bfloat16), d_att)

    @pl.when(step == pl.num_programs(1) - 1)
    def _():
        first = pl.multiple_of(size * head, size)
        dkv_ref[:, pl.ds(first, size)] = (dk_sum[...] * factor).astype(jnp.bfloat16)
        dkv_ref[:, pl.ds(mine + first, size)] = dv_sum[...].astype(jnp.bfloat16)


def attend_specs(count, head):
    by_query = pl.BlockSpec((BLOCK, head), lambda h, i: (i, h))
    keys = pl.BlockSpec((count, head), lambda h, i: (0, h))
    values = pl.BlockSpec((count, head), lambda h, i: (0, 2 + h))
    bound = pl.BlockSpec((BLOCK, 1), lambda h, i: (i, 0))
    place = pl.BlockSpec((1, count), lambda h, i: (0, 0))
    lse = pl.BlockSpec((1, BLOCK, 1), lambda h, i: (h, i, 0))
    return by_query, keys, values, bound, place, lse


def attend(queries, pairs, first, last, place, head):
    count, width = queries.shape
    by_query, keys, values, bound, places, lse = attend_specs(count, head)
    return pl.pallas_call(
        functools.partial(attend_kernel, 1.0 / math.sqrt(head)),
        grid=(width // head, count // BLOCK),
        in_specs=[by_query, keys, values, bound, bound, places],
        out_specs=[by_query, by_query, lse],
        out_shape=[
            jax.ShapeDtypeStruct((count, width), jnp.float32),
            jax.ShapeDtypeStruct((count, width), jnp.bfloat16),
            jax.ShapeDtypeStruct((width // head, count, 1), jnp.float32),
        ],
        compiler_params=pltpu.CompilerParams(vmem_limit_bytes=20 * 2**20),
        cost_estimate=LONG,
        name="attend",
    )(queries, pairs, pairs, first, last, place)


def attend_back(queries, pairs, first, last, place, lse, attended, d_attended, head):
    count, width = queries.shape
    by_query, keys, values, bound, places, by_lse = attend_specs(count, head)
    return pl.pallas_call(
        functools.partial(attend_back_kernel, 1.0 / math.sqrt(head)),
        grid=(width // head, count // BLOCK),
        in_specs=[
            by_query,
            keys,
            values,
            bound,
            bound,
            places,
            by_lse,
            by_query,
            by_query,
        ],
        out_specs=[by_query, pl.BlockSpec((count, 2 * width), lambda h, i: (0, 0))],
        out_shape=[
            jax.ShapeDtypeStruct((count, width), jnp.bfloat16),
            jax.ShapeDtypeStruct((count, 2 * width), jnp.bfloat16),
        ],
        scratch_shapes=[pltpu.VMEM((count, head), jnp.float32)] * 2,
        compiler_params=pltpu.CompilerParams(vmem_limit_bytes=14 * 2**20),
        cost_estimate=LONG,
        name="attend_back",
    )(queries, pairs, pairs, first, last, place, lse, attended, d_attended)


def as_rows(values, columns):
    rows = 16 * -(-values.shape[0] // (16 * columns))
    return jnp.pad(values, (0, rows * columns - values.shape[0])).reshape(rows, columns)


def from_rows(rows, count):
    return rows.reshape(-1)[:count]


def heads_of(device, head):
    z, x = device // 2, device % 2
    return [slice(head * (8 * x + 4 * j + z), head * (8 * x + 4 * j + z + 1)) for j in range(2)]


def columns_kernel(dp_ref, *refs):
    held_refs = refs[:4]
    q_ref, kv_ref, gain_ref = refs[4:]
    each = q_ref.shape[0] // 8
    mine = q_ref.shape[1]
    rows = held_refs[0].shape[0] // 8
    extra = rows - 3 * each
    for mask, held_ref in enumerate(held_refs):

        @pl.when((dp_ref[0] ^ pl.program_id(0)) == mask)
        def _():
            for device in range(8):
                first = rows * device
                here = slice(each * device, each * (device + 1))
                q_ref[here, :] = held_ref[first : first + each, :]
                kv_ref[here, :mine] = held_ref[first + each : first + 2 * each, :]
                kv_ref[here, mine:] = held_ref[first + 2 * each : first + 3 * each, :]
                gain_ref[0, extra * device : extra * (device + 1), :] = held_ref[
                    first + 3 * each : first + rows, :
                ]


def payload_kernel(q_ref, k_ref, v_ref, gain_ref, out_ref):
    each = q_ref.shape[0]
    head = q_ref.shape[1] // 16
    rows = out_ref.shape[0] // 8
    for device in range(8):
        for which, w_ref in enumerate((q_ref, k_ref, v_ref)):
            first = rows * device + each * which
            for j, columns in enumerate(heads_of(device, head)):
                out_ref[first : first + each, head * j : head * (j + 1)] = w_ref[:, columns]
        out_ref[rows * device + 3 * each : rows * (device + 1), :] = gain_ref[...]


class Columns:
    def __init__(self, weights, gains, dp):
        self.weights, self.gains, self.dp = weights, gains, dp

    def along_fsdp(self, *gate):
        each, width = self.weights[0].shape
        extra = as_rows(self.gains, width // 8)
        given = pl.pallas_call(
            payload_kernel,
            out_shape=jax.ShapeDtypeStruct(
                (8 * (3 * each + extra.shape[0]), width // 8), self.weights[0].dtype
            ),
            compiler_params=pltpu.CompilerParams(vmem_limit_bytes=8 * 2**20),
            cost_estimate=LONG,
            name="payload",
        )(*self.weights, extra)
        self.held = lax.all_to_all(after(given, *gate), "fsdp", 0, 0, tiled=True)
        return [self.held]

    def along_y(self, *gate):
        held = after(self.held, *gate)
        got, other = y_swap(held), core_swap(held)
        self.held = [held, got, other]
        return [got, other]

    def along_core(self, *gate):
        held, got, other = after(tuple(self.held), *gate)
        last = core_swap(got)
        self.held = [held, other, got, last]
        return [last]

    def whole(self):
        each, width = self.weights[0].shape
        rows, mine = self.held[0].shape
        extra = rows - 24 * each
        block = 8 * each
        low = self.held[0].dtype
        wq, w_kv, gains = pl.pallas_call(
            columns_kernel,
            grid_spec=pltpu.PrefetchScalarGridSpec(
                num_scalar_prefetch=1,
                grid=(4,),
                in_specs=[pl.BlockSpec((rows, mine), lambda i, dp: (0, 0))] * 4,
                out_specs=[
                    pl.BlockSpec((block, mine), lambda i, dp: (i, 0)),
                    pl.BlockSpec((block, 2 * mine), lambda i, dp: (i, 0)),
                    pl.BlockSpec((1, extra, mine), lambda i, dp: (i, 0, 0)),
                ],
            ),
            out_shape=[
                jax.ShapeDtypeStruct((4 * block, mine), low),
                jax.ShapeDtypeStruct((4 * block, 2 * mine), low),
                jax.ShapeDtypeStruct((4, extra, mine), low),
            ],
            compiler_params=pltpu.CompilerParams(vmem_limit_bytes=16 * 2**20),
            cost_estimate=FREE,
            name="columns",
        )(self.dp.reshape(1).astype(jnp.int32), *self.held)
        gains = gains.reshape(32, -1)[:, : self.gains.shape[0]].astype(jnp.float32)
        return wq, w_kv, gains


def column_grads_kernel(dp_ref, *refs):
    sources, hiddens = refs[:4], refs[4:8]
    dq_ref, dkv_ref, *given_refs, kept_ref = refs[8:]
    count = sources[0].shape[0]
    mine = dq_ref.shape[1]
    for_q, for_kv = 0.0, 0.0
    for step in range(4):
        here = slice(count * step, count * (step + 1))
        for_q = for_q + columns_by_columns(hiddens[step][...], dq_ref[here, :])
        for_kv = for_kv + columns_by_columns(sources[step][...], dkv_ref[here, :])

    for place in range(2):

        @pl.when(pl.program_id(0) == place)
        def _():
            given_refs[2 * place][...] = for_q.astype(jnp.bfloat16)
            given_refs[2 * place + 1][...] = for_kv.astype(jnp.bfloat16)

    @pl.when(pl.program_id(0) >= 2)
    def _():
        kept_ref[0, :, :mine] = for_q
        kept_ref[0, :, mine:] = for_kv


def own_grads_kernel(
    got_ref,
    wq_ref,
    wk_ref,
    wv_ref,
    flag_ref,
    out_kept_ref,
    out_got_ref,
    q_ref,
    k_ref,
    v_ref,
    q_sum_ref,
    kv_sum_ref,
    gain_ref,
    out_ref,
):
    each = wq_ref.shape[0]
    gain = 0.0
    for device in range(8):
        gain = gain + got_ref[device, each : each + 16, :128].astype(jnp.float32)
    gain_ref[...] = gain
    out_ref[...] = jnp.where(
        flag_ref[...] != 0, out_kept_ref[...], out_got_ref[...].astype(jnp.float32)
    )
    head = wq_ref.shape[1] // 16
    sums = []
    for which, (w_ref, out_ref) in enumerate(((wq_ref, q_ref), (wk_ref, k_ref), (wv_ref, v_ref))):
        total = jnp.zeros((each, head), jnp.float32)
        for device in range(8):
            for j, columns in enumerate(heads_of(device, head)):
                first = head * (2 * which + j)
                grad = got_ref[device, :each, first : first + head].astype(jnp.float32)
                out_ref[:, columns] = grad
                total = total + grad * w_ref[:, columns].astype(jnp.float32)
        sums.append(jnp.sum(total, axis=1, keepdims=True))
    q_sum_ref[...] = sums[0]
    kv_sum_ref[...] = sums[1] + sums[2]


def whole_block(array):
    return pl.BlockSpec(array.shape, lambda *place: (0,) * array.ndim)


def project_kernel(held_ref, *refs):
    others = refs[:-8]
    kv_gain_ref, attn_gain_ref, w_kv_ref, wq_ref, src_ref, hid_ref, pair_ref, query_ref = refs[-8:]
    rows = src_ref.shape[0] // 2

    def other_rows(which):
        if len(others) == 1:
            return others[0][rows * which : rows * (which + 1), :]
        return others[which][...]

    for which, gain_ref, w_ref, low_ref, out_ref in (
        (0, kv_gain_ref, w_kv_ref, src_ref, pair_ref),
        (1, attn_gain_ref, wq_ref, hid_ref, query_ref),
    ):
        for side in range(2):
            here = slice(rows * side, rows * (side + 1))
            values = other_rows(which) if side else held_ref[rows * which : rows * (which + 1), :]
            values = values.astype(jnp.float32)
            low_ref[here, :] = (values * inverse_scale(values) * gain_ref[...]).astype(jnp.bfloat16)
        out_ref[...] = product(low_ref[...], w_ref[...]).astype(jnp.bfloat16)


def project(piece, kv_gain, attn_gain, w_kv, wq, cost):
    rows, width = piece[0].shape
    low = piece[0].dtype
    return pl.pallas_call(
        project_kernel,
        out_shape=[
            jax.ShapeDtypeStruct((rows, width), low),
            jax.ShapeDtypeStruct((rows, width), low),
            jax.ShapeDtypeStruct((rows, w_kv.shape[1]), low),
            jax.ShapeDtypeStruct((rows, wq.shape[1]), low),
        ],
        compiler_params=pltpu.CompilerParams(vmem_limit_bytes=12 * 2**20),
        cost_estimate=cost,
        name="project",
    )(*piece, kv_gain, attn_gain, w_kv, wq)


def terms_kernel(step, pair_ref, query_ref, w_kv_ref, wq_ref, *refs):
    own_ref, other_ref = refs[-2:]
    count = pair_ref.shape[0] // 4
    here = slice(count * step, count * (step + 1))
    found = [
        rows_by_rows(pair_ref[here, :], w_kv_ref[...]),
        rows_by_rows(query_ref[here, :], wq_ref[...]),
    ]
    if len(refs) > 2:
        found.append(product(refs[0][...], refs[1][...]))
    rows = count // 2
    for place, value in enumerate(found):
        value = value.astype(jnp.bfloat16)
        own_ref[rows * place : rows * (place + 1), :] = value[:rows]
        other_ref[rows * place : rows * (place + 1), :] = value[rows:]


def back_terms(parts, step, d_pairs, d_queries, w_kv, wq, result=()):
    rows, width = d_pairs.shape[0] // 4, w_kv.shape[0]
    count = rows // 2
    out = jax.ShapeDtypeStruct((count * len(parts), width), jnp.bfloat16)
    own, other = pl.pallas_call(
        functools.partial(terms_kernel, step),
        out_shape=[out, out],
        compiler_params=pltpu.CompilerParams(vmem_limit_bytes=14 * 2**20),
        cost_estimate=FREE,
        name="back_terms",
    )(d_pairs, d_queries, w_kv, wq, *result)
    return [
        part.of_rows(Rows(own, count * place, count), Rows(other, count * place, count))
        for place, part in enumerate(parts)
    ]


def row_blocks(rows, count):
    first = rows.start // count
    return pl.BlockSpec((count, rows.array.shape[1]), lambda i: (first + i, 0))


def result_kernel(middle_ref, live_ref, kept_ref, x_ref, ring_ref, out_ref):
    total = middle_ref[...] + kept_ref[...].astype(jnp.float32)
    total = total + x_ref[...].astype(jnp.float32) + ring_ref[...].astype(jnp.float32)
    out_ref[...] = (total * live_ref[...]).astype(jnp.bfloat16)


def result_of(middle, live, scatter):
    sums = [scatter.kept, *scatter.got]
    rows, width = middle.shape
    block = rows // 4
    return pl.pallas_call(
        result_kernel,
        grid=(4,),
        in_specs=[
            pl.BlockSpec((block, width), lambda i: (i, 0)),
            pl.BlockSpec((block, 1), lambda i: (i, 0)),
        ]
        + [row_blocks(part, block) for part in sums],
        out_specs=pl.BlockSpec((block, width), lambda i: (i, 0)),
        out_shape=jax.ShapeDtypeStruct((rows, width), jnp.bfloat16),
        compiler_params=pltpu.CompilerParams(vmem_limit_bytes=6 * 2**20),
        cost_estimate=FREE,
        name="result",
    )(middle, live, *(part.array for part in sums))


def input_grads_kernel(hidden_ref, source_ref, d_middle_ref, attn_gain_ref, kv_gain_ref, *refs):
    d_hid, d_src = (
        sum(ref[...].astype(jnp.float32) for ref in refs[first : first + 3]) for first in (0, 3)
    )
    hidden = hidden_ref[...].astype(jnp.float32)
    source = source_ref[...].astype(jnp.float32)
    refs[6][...] = (
        d_middle_ref[...] + norm_backward(hidden, inverse_scale(hidden), attn_gain_ref[...], d_hid)
    ).astype(jnp.bfloat16)
    refs[7][...] = norm_backward(
        source, inverse_scale(source), kv_gain_ref[...], d_src
    ).astype(jnp.bfloat16)


def input_grads(hidden, source, d_middle, attn_gain, kv_gain, d_hid, d_src):
    sums = [d_hid.kept, *d_hid.got, d_src.kept, *d_src.got]
    rows, width = hidden.shape
    block = rows // 4
    spec = pl.BlockSpec((block, width), lambda i: (i, 0))
    return pl.pallas_call(
        input_grads_kernel,
        grid=(4,),
        in_specs=[spec] * 3
        + [whole_block(attn_gain), whole_block(kv_gain)]
        + [row_blocks(part, block) for part in sums],
        out_specs=[spec, spec],
        out_shape=[jax.ShapeDtypeStruct((rows, width), jnp.bfloat16)] * 2,
        compiler_params=pltpu.CompilerParams(vmem_limit_bytes=8 * 2**20),
        cost_estimate=FREE,
        name="input_grads",
    )(hidden, source, d_middle, attn_gain, kv_gain, *(part.array for part in sums))


def feed_kernel(mid_plan, cot_plan, *refs):
    arrays = refs[:-10]
    wg_ref, wu_ref, wd_ref, inner_ref, d_gate_ref, d_up_ref, own_ref, other_ref = refs[-10:-2]
    for plan, rows_ref in ((mid_plan, refs[-2]), (cot_plan, refs[-1])):
        first = 0
        for index, start, count in plan:
            rows_ref[first : first + count, :] = arrays[index][start : start + count, :]
            first += count
    mid_ref, cot_ref = refs[-2:]
    hidden, width = wg_ref.shape
    for first in range(0, hidden, 256):
        here = slice(first, min(first + 256, hidden))
        gate_value = rows_by_rows(mid_ref[...], wg_ref[here, :])
        up_value = rows_by_rows(mid_ref[...], wu_ref[here, :])
        d_inner = rows_by_rows(cot_ref[...], wd_ref[here, :])
        sigmoid_gate = jax.nn.sigmoid(gate_value)
        swished = gate_value * sigmoid_gate
        inner_ref[:, here] = (swished * up_value).astype(jnp.bfloat16)
        d_gate_ref[:, here] = (
            d_inner * up_value * sigmoid_gate * (1.0 + gate_value * (1.0 - sigmoid_gate))
        ).astype(jnp.bfloat16)
        d_up_ref[:, here] = (d_inner * swished).astype(jnp.bfloat16)
    rows = own_ref.shape[0]
    for first in range(0, width, 512):
        here = slice(first, first + 512)
        terms = product(d_gate_ref[...], wg_ref[:, here]) + product(d_up_ref[...], wu_ref[:, here])
        terms = terms.astype(jnp.bfloat16)
        own_ref[:, here] = terms[:rows]
        other_ref[:, here] = terms[rows:]


def feed(mid, cot, wg, wu, wd):
    arrays = []
    plans = []
    for pieces in (mid, cot):
        plan = []
        for rows in pieces:
            index = next((n for n, held in enumerate(arrays) if held is rows.array), None)
            if index is None:
                index = len(arrays)
                arrays.append(rows.array)
            plan.append((index, rows.start, rows.count))
        plans.append(tuple(plan))
    count = sum(rows.count for rows in mid)
    hidden, width = wg.shape
    low = jax.ShapeDtypeStruct((count, hidden), jnp.bfloat16)
    terms = jax.ShapeDtypeStruct((count // 2, width), jnp.bfloat16)
    return pl.pallas_call(
        functools.partial(feed_kernel, *plans),
        out_shape=[low, low, low, terms, terms]
        + [jax.ShapeDtypeStruct((count, width), jnp.bfloat16)] * 2,
        compiler_params=pltpu.CompilerParams(vmem_limit_bytes=20 * 2**20),
        cost_estimate=LONG,
        name="feed",
    )(*arrays, wg, wu, wd)


def branch_back_kernel(plan, *refs):
    *arrays, wo_ref, rows_ref, att_ref = refs
    first = 0
    for (start, count), array in zip(plan, arrays):
        rows_ref[first : first + count, :] = array[start : start + count, :]
        first += count
    att_ref[...] = rows_by_rows(rows_ref[...], wo_ref[...]).astype(jnp.bfloat16)


def branch_back(pieces, wo):
    count = sum(rows.count for rows in pieces)
    return pl.pallas_call(
        functools.partial(branch_back_kernel, tuple((rows.start, rows.count) for rows in pieces)),
        out_shape=[
            jax.ShapeDtypeStruct((count, wo.shape[1]), jnp.bfloat16),
            jax.ShapeDtypeStruct((count, wo.shape[0]), jnp.bfloat16),
        ],
        compiler_params=pltpu.CompilerParams(vmem_limit_bytes=16 * 2**20),
        cost_estimate=FREE,
        name="branch_back",
    )(*(rows.array for rows in pieces), wo)


def result_terms_kernel(inner_ref, weights_ref, out_ref):
    out_ref[...] = product(inner_ref[...], weights_ref[...]).astype(jnp.bfloat16)


def result_terms_of(inner, weights):
    return pl.pallas_call(
        result_terms_kernel,
        out_shape=jax.ShapeDtypeStruct((inner.shape[0], weights.shape[1]), jnp.bfloat16),
        compiler_params=pltpu.CompilerParams(vmem_limit_bytes=12 * 2**20),
        cost_estimate=FREE,
        name="result_terms",
    )(inner, weights)


def add_kernel(*refs):
    count = len(refs) // 3
    for kept_ref, got_ref, out_ref in zip(refs[:count], refs[count : 2 * count], refs[2 * count :]):
        total = kept_ref[...] + got_ref[...].astype(jnp.float32)
        out_ref[...] = total[: out_ref.shape[0]]


def add_all(kept, got, rows):
    width = kept[0].shape[1]
    block = width // 4
    count = len(kept)
    spec = pl.BlockSpec((got[0].shape[0], block), lambda i: (0, i))
    return pl.pallas_call(
        add_kernel,
        grid=(4,),
        in_specs=[spec] * (2 * count),
        out_specs=[pl.BlockSpec((rows, block), lambda i: (0, i))] * count,
        out_shape=[jax.ShapeDtypeStruct((rows, width), jnp.float32)] * count,
        compiler_params=pltpu.CompilerParams(vmem_limit_bytes=8 * 2**20),
        cost_estimate=LONG,
        name="add_all",
    )(*kept, *got)


def copy_kernel(dp_ref, in_ref, out_ref):
    out_ref[...] = in_ref[...]


def own_first(rows, dp):
    block = (rows.shape[0] // 4, rows.shape[1])
    return pl.pallas_call(
        copy_kernel,
        grid_spec=pltpu.PrefetchScalarGridSpec(
            num_scalar_prefetch=1,
            grid=(4,),
            in_specs=[pl.BlockSpec(block, lambda i, dp: (dp[0] ^ (2 * (i % 2) + i // 2), 0))],
            out_specs=pl.BlockSpec(block, lambda i, dp: (i, 0)),
        ),
        out_shape=jax.ShapeDtypeStruct(rows.shape, rows.dtype),
        compiler_params=pltpu.CompilerParams(vmem_limit_bytes=8 * 2**20),
        cost_estimate=FREE,
        name="own_first",
    )(dp.reshape(1).astype(jnp.int32), rows)


class ColumnGrads:
    def __init__(self, dp):
        self.dp = dp
        self.y, self.c = dp // 2, dp % 2

    def gain_core(self, gain, *gate):
        gain = gain.reshape(2, 2, -1)
        kept = lax.dynamic_index_in_dim(gain, self.c, 1, keepdims=False)
        given = lax.dynamic_index_in_dim(gain, 1 - self.c, 1, keepdims=False)
        self.gain = kept + core_swap(after(given, *gate))
        return [given]

    def gain_y(self, *gate):
        gain = after(self.gain, *gate)
        kept = lax.dynamic_index_in_dim(gain, self.y, 0, keepdims=False)
        given = lax.dynamic_index_in_dim(gain, 1 - self.y, 0, keepdims=False)
        self.gain = kept + y_swap(given)
        return [given]

    def along_core(self, sources, hiddens, d_queries, d_pairs):
        count, width = sources[0].shape
        block = width // 4
        mine = d_queries.shape[1]
        rows = d_queries.shape[0]

        def of_step(i):
            return 2 * (i % 2) + 1 - i // 2

        by_block = pl.BlockSpec((count, block), lambda i, dp: (0, dp[0] ^ of_step(i)))
        *given, self.kept = pl.pallas_call(
            column_grads_kernel,
            grid_spec=pltpu.PrefetchScalarGridSpec(
                num_scalar_prefetch=1,
                grid=(4,),
                in_specs=[by_block] * 8
                + [
                    pl.BlockSpec((rows, mine), lambda i, dp: (0, 0)),
                    pl.BlockSpec((rows, 2 * mine), lambda i, dp: (0, 0)),
                ],
                out_specs=[
                    *(
                        pl.BlockSpec((block, width_of * mine), lambda i, dp: (0, 0))
                        for width_of in (1, 2, 1, 2)
                    ),
                    pl.BlockSpec((1, block, 3 * mine), lambda i, dp: (jnp.maximum(i, 2) - 2, 0, 0)),
                ],
            ),
            out_shape=[
                *(
                    jax.ShapeDtypeStruct((block, width_of * mine), jnp.bfloat16)
                    for width_of in (1, 2, 1, 2)
                ),
                jax.ShapeDtypeStruct((2, block, 3 * mine), jnp.float32),
            ],
            compiler_params=pltpu.CompilerParams(vmem_limit_bytes=16 * 2**20),
            cost_estimate=LONG,
            name="column_grads",
        )(self.dp.reshape(1).astype(jnp.int32), *sources, *hiddens, d_queries, d_pairs)
        self.from_core = [core_swap(value) for value in given]
        return given

    def along_y(self, *gate):
        got = after(tuple(self.from_core[2:]), *gate)
        given = self.kept[1] + jnp.concatenate(got, axis=1).astype(jnp.float32)
        given = given.astype(jnp.bfloat16)
        self.from_y = y_swap(given)
        return [given]

    def along_fsdp(self, *gate):
        total = self.kept[0] + jnp.concatenate(self.from_core[:2], axis=1).astype(jnp.float32)
        total = (total + after(self.from_y, *gate).astype(jnp.float32)).astype(jnp.bfloat16)
        each, columns = total.shape[0] // 8, total.shape[1]
        gain = self.gain.astype(jnp.bfloat16).reshape(8, 1, each)
        gain = jnp.pad(gain, ((0, 0), (0, 15), (0, columns - each)))
        given = jnp.concatenate([total.reshape(8, each, columns), gain], axis=1)
        self.got = lax.all_to_all(given, "fsdp", 0, 0, tiled=True)
        return [given], [self.got]

    def whole(self, weights, out_grads, *gate):
        each, width = weights[0].shape
        got, out_got = after((self.got, out_grads.from_x), *gate)
        flag = (out_grads.x == out_grads.y).astype(jnp.int32).reshape(1, 1)
        flat = jax.ShapeDtypeStruct((each, width), jnp.float32)
        column = jax.ShapeDtypeStruct((each, 1), jnp.float32)
        out = pl.pallas_call(
            own_grads_kernel,
            out_shape=[
                flat,
                flat,
                flat,
                column,
                column,
                jax.ShapeDtypeStruct((16, 128), jnp.float32),
                flat,
            ],
            compiler_params=pltpu.CompilerParams(vmem_limit_bytes=6 * 2**20),
            cost_estimate=FREE,
            name="own_grads",
        )(got, *weights, flag, out_grads.kept, out_got)
        return out, out[5][0, :each]


def out_rows(own, x, y, c, before, late):
    head = in_order(x, own, x_swap(own))
    pairs = [(place, place ^ 16) for place in range(32) if place // 16 == place % 2]
    got = lax.ppermute(after(head, *before), ("dp", "fsdp"), pairs)
    mine = jnp.where(x == y, head, after(got, *late))
    return in_order(c, mine, core_swap(mine))


class OutGrads:
    def __init__(self, grad, x, y, c):
        self.grad, self.x, self.y, self.c = grad, x, y, c

    def along_core(self, *gate):
        head, width = self.grad.shape[0] // 2, self.grad.shape[1]
        kept = lax.dynamic_slice(self.grad, (head * self.c, 0), (head, width))
        given = lax.dynamic_slice(self.grad, (head * (1 - self.c), 0), (head, width))
        given = after(given.astype(jnp.bfloat16), *gate)
        self.total = kept + core_swap(given).astype(jnp.float32)
        return [given]

    def along_y(self, *gate):
        pairs = [(place, place ^ 16) for place in range(32) if place // 16 != place % 2]
        given = after(self.total.astype(jnp.bfloat16), *gate)
        self.from_y = lax.ppermute(given, ("dp", "fsdp"), pairs)
        return [given]

    def along_x(self, *gate):
        total = self.total + after(self.from_y, *gate).astype(jnp.float32)
        each, width = total.shape[0] // 2, total.shape[1]
        self.kept = lax.dynamic_slice(total, (each * self.x, 0), (each, width))
        given = lax.dynamic_slice(total, (each * (1 - self.x), 0), (each, width))
        pairs = [(place, place ^ 1) for place in range(32) if place // 16 == place % 2]
        self.from_x = lax.ppermute(given.astype(jnp.bfloat16), ("dp", "fsdp"), pairs)


def hidden_units(rows, dp, *gate):
    return own_first(lax.all_gather(after(rows, *gate), "dp", axis=0, tiled=True), dp)


def hidden_core_kernel(count, *refs):
    units, rows, out_refs = refs[:count], refs[count : 2 * count], refs[2 * count :]
    half = units[0].shape[1] // 2
    total = sum(
        columns_by_columns(unit_ref[:, half:], row_ref[...]) for unit_ref, row_ref in zip(units, rows)
    ).astype(jnp.bfloat16)
    out_refs[0][...] = total[: half // 2]
    out_refs[1][...] = total[half // 2 :]


def hidden_y_kernel(count, *refs):
    units, rows = refs[:count], refs[count : 2 * count]
    own_got_ref, y_got_ref, kept_ref, given_ref = refs[2 * count :]
    half = units[0].shape[1] // 2
    total = sum(
        columns_by_columns(unit_ref[:, :half], row_ref[...]) for unit_ref, row_ref in zip(units, rows)
    )
    kept_ref[...] = total[: half // 2] + own_got_ref[...].astype(jnp.float32)
    given = total[half // 2 :] + y_got_ref[...].astype(jnp.float32)
    given_ref[...] = given.astype(jnp.bfloat16)


def out_grad_kernel(att_ref, *refs):
    *rows, out_ref = refs
    count = rows[0].shape[0]
    out_ref[...] = sum(
        columns_by_columns(att_ref[count * place : count * (place + 1), :], row_ref[...])
        for place, row_ref in enumerate(rows)
    )


def out_grad(attended, pieces):
    width = pieces[0].shape[1]
    block = width // 2
    return pl.pallas_call(
        out_grad_kernel,
        grid=(2,),
        in_specs=[whole_block(attended)]
        + [pl.BlockSpec((rows.shape[0], block), lambda i: (0, i)) for rows in pieces],
        out_specs=pl.BlockSpec((attended.shape[1], block), lambda i: (0, i)),
        out_shape=jax.ShapeDtypeStruct((attended.shape[1], width), jnp.float32),
        compiler_params=pltpu.CompilerParams(vmem_limit_bytes=10 * 2**20),
        cost_estimate=FREE,
        name="out_grad",
    )(attended, *pieces)


class HiddenGrads:
    def __init__(self, units, rows):
        self.units, self.rows = list(units), list(rows)

    def call(self, kernel, got, outs, *gate):
        width = self.rows[0].shape[1]
        block = width // 2
        units = after(tuple(self.units), *gate)

        def spec(rows):
            return pl.BlockSpec((rows, block), lambda i: (0, i))

        return pl.pallas_call(
            functools.partial(kernel, len(self.units)),
            grid=(2,),
            in_specs=[whole_block(unit) for unit in units]
            + [spec(rows.shape[0]) for rows in self.rows]
            + [spec(rows.shape[0]) for rows in got],
            out_specs=[spec(rows) for rows, dtype in outs],
            out_shape=[jax.ShapeDtypeStruct((rows, width), dtype) for rows, dtype in outs],
            compiler_params=pltpu.CompilerParams(vmem_limit_bytes=14 * 2**20),
            cost_estimate=LONG,
            name="hidden_grads",
        )(*units, *self.rows, *got)

    def along_core(self, *gate):
        half = self.units[0].shape[1] // 2
        given = self.call(hidden_core_kernel, [], [(half // 2, jnp.bfloat16)] * 2, *gate)
        self.from_core = [core_swap(value) for value in given]
        return given

    def along_y(self, *gate):
        half = self.units[0].shape[1] // 2
        self.kept, given = self.call(
            hidden_y_kernel,
            self.from_core,
            [(half // 2, jnp.float32), (half // 2, jnp.bfloat16)],
            *gate,
        )
        self.from_y = y_swap(given)
        return [given]


def fast_body(
    hidden,
    source,
    cotangent,
    row_counts,
    seq_lengths,
    kv_gain,
    w_key,
    w_value,
    attn_gain,
    w_query,
    w_out,
    ffn_gain,
    w_gate,
    w_up,
    w_down,
):
    local_rows, width = hidden.shape
    head = width // HEADS
    dp = lax.axis_index("dp")
    fsdp = lax.axis_index("fsdp")
    y, c = dp // 2, dp % 2
    z, x = fsdp // 2, fsdp % 2
    me = 8 * dp + fsdp

    order = z ^ (z >> 1)
    devices = []
    for step in range(4):
        place = (order - step) % 4
        for side in range(2):
            devices.append(2 * (place ^ (place >> 1)) + (x ^ side))
    slots = (
        jnp.stack(devices).astype(jnp.int32)[:, None] * local_rows
        + jnp.arange(local_rows, dtype=jnp.int32)[None, :]
    ).reshape(-1)
    live, position, sequence = slot_layout(row_counts, seq_lengths, slots, local_rows)
    starts = jnp.concatenate([jnp.zeros((1,), jnp.int32), jnp.cumsum(seq_lengths[0])])
    first = jnp.sum(
        jnp.where(
            sequence[:, None] == jnp.arange(starts.shape[0], dtype=jnp.int32)[None, :],
            starts[None, :],
            0,
        ),
        axis=1,
    )
    first, last = first[:, None], position[:, None]
    place_of_key = jnp.where(live, position, -1)[None, :]
    own_live = live[:local_rows].astype(jnp.float32)[:, None]

    d_out = cotangent.astype(jnp.float32) * own_live
    d_out_low = d_out.astype(jnp.bfloat16)
    layout = lax.optimization_barrier((first, last, place_of_key, own_live, d_out_low))
    first, last, place_of_key, own_live, d_out_low = layout

    each = kv_gain.shape[0]
    inputs = Gather(jnp.concatenate([source, hidden], axis=0))
    columns = Columns(
        [w_query, w_key, w_value], jnp.concatenate([kv_gain, attn_gain, ffn_gain]), dp
    )
    wa = columns.along_fsdp()
    s1 = move([inputs])
    wy = columns.along_y(*s1)
    units = w_gate.shape[0]
    padded = -(-units // 64) * 64
    own_units = [
        jnp.pad(own, ((0, padded - units), (0, 0))) for own in (w_gate, w_up, w_down)
    ]
    s2 = move([inputs], *s1, *wa, *layout, *own_units)
    wc = columns.along_core(*wy)
    s3 = move([inputs], *s2)
    wq, w_kv, gains = columns.whole()
    kv_gain_full, attn_gain_full, ffn_gain_full = (
        gains[:, which * each : (which + 1) * each].reshape(1, width) for which in range(3)
    )
    wg, wu, wd = (hidden_units(own, dp, *s2, *wy) for own in own_units)

    hidden_f = hidden.astype(jnp.float32)
    projected = []

    def project_piece(step, cost, *gate):
        piece = after(inputs.arrays(step), *(value[3] for value in projected[-1:]), *gate)
        projected.append(project(piece, kv_gain_full, attn_gain_full, w_kv, wq, cost))

    project_piece(0, FREE)
    project_piece(1, FREE)
    s4 = move([inputs], *s3)
    project_piece(2, LONG, *s3)
    cots = Gather(d_out_low)
    c1 = move([cots], *s4, projected[2][3])
    project_piece(3, LONG)
    src_low, hid_low, pairs, queries = zip(*projected)
    queries = jnp.concatenate(queries, axis=0)
    pairs = jnp.concatenate(pairs, axis=0)
    c2 = move([cots], *c1, pairs, queries)
    attended_f, attended_low, lse = attend(
        *after((queries, pairs), *c1), first, last, place_of_key, head
    )
    wo = out_rows(after(w_out, *s2), x, y, c, s3, c1)

    def rows_of(array, step):
        return array[2 * step * local_rows : 2 * (step + 1) * local_rows]

    def branch_terms(step, *gate):
        return product(after(rows_of(attended_low, step), *gate), wo).astype(jnp.bfloat16)

    branch = Scatter()
    b1 = move([branch.of(branch_terms(1)), cots], *c2)
    b2 = move([branch.of(branch_terms(2)), cots], *b1)
    b3 = move([branch.of(branch_terms(3, *b1))], *b2)
    b4 = move([branch.of(branch_terms(0, *b2))], *b3)
    middle = hidden_f + branch.total()
    middle_scale = inverse_scale(middle)
    middle_unit = middle * middle_scale
    mids = Gather((middle_unit * ffn_gain_full).astype(jnp.bfloat16))

    fed = []

    def feed_piece(step, *gate):
        weights = after((wg, wu, wd), *gate)
        fed.append(feed(mids.pieces[step], cots.pieces[step], *weights))

    def terms_of(step):
        own, other = fed[step][3:5]
        return back.of_rows(rows_in(own), rows_in(other))

    back = Scatter()
    m1 = move([mids])
    m2 = move([mids], *m1)
    feed_piece(0)
    m3 = move([mids], *m2, fed[0][0])
    feed_piece(1, *m2)
    d1 = move([mids, terms_of(1)], *m3)
    feed_piece(2, *m3)
    d2 = move([terms_of(2)], *d1)
    feed_piece(3, *d1)
    d3 = move([terms_of(3)], *d2)
    inners, d_gates, d_ups, _, _, all_mids, all_cots = zip(*fed)
    gate_sums = HiddenGrads(d_gates, all_mids)
    up_sums = HiddenGrads(d_ups, all_mids)
    down_sums = HiddenGrads(inners, all_cots)
    h1 = gate_sums.along_core(*d2)
    d4 = move([terms_of(0)], *d3, *h1)
    h2 = up_sums.along_core(*d3)
    d_normed = after(back.total(), *h2)
    d_middle = d_out + norm_backward(middle, middle_scale, ffn_gain_full, d_normed)
    d_branch_low = d_middle.astype(jnp.bfloat16)
    outs = Gather(d_branch_low)
    e1 = move([outs])
    def result_terms(step, *gate):
        return result_terms_of(after(inners[step], *gate), wd)

    h1 = gate_sums.along_y(d_branch_low)
    h3 = down_sums.along_core(*h1)
    e2 = move([outs], *e1, *h3)
    h2 = up_sums.along_y(*e1)
    first_result = result_terms(1, *e1, *h2)
    ffn_gain_part = jnp.sum(after(d_normed * middle_unit, first_result), axis=0)
    column_grads = ColumnGrads(dp)
    column_grads.gain_core(ffn_gain_part)
    column_grads.gain_y()
    e3 = move([outs], *e2, *h2, ffn_gain_part)
    h3 = down_sums.along_y(*e2)

    result = Scatter()
    e4 = move([outs, result.of(first_result)], *e3, *h3, gate_sums.from_y, column_grads.gain)
    d_branches, d_attended = zip(*(branch_back(outs.pieces[step], wo) for step in range(4)))
    d_attended = jnp.concatenate(d_attended, axis=0)
    o2 = move([result.of(result_terms(2, *e3))], *e4)
    d_queries, d_pairs = attend_back(
        queries, pairs, first, last, place_of_key, lse, attended_f, d_attended, head
    )
    d_queries, d_pairs = after((d_queries, d_pairs), *o2)
    d_src, d_hid = Scatter(), Scatter()

    def terms(step, *gate, result=()):
        parts = [d_src, d_hid, *result[:1]]
        rows = after((d_pairs, d_queries), *gate)
        weights = (inners[result[1]], wd) if result else ()
        return back_terms(parts, step, *rows, w_kv, wq, weights)

    first_terms = terms(1)
    started = d_hid.own.array
    sent = []
    i1 = move(first_terms, *o2, up_sums.from_y, payload=sent)
    second_terms = terms(2, started, result=(result, 3))
    sources, hiddens = after((tuple(src_low), tuple(hid_low)), *sent, result.own.array)
    column_grads.along_core(sources, hiddens, d_queries, d_pairs)
    i2 = move(second_terms, *i1, down_sums.from_y)
    py = column_grads.along_y()
    next_terms = terms(3, *py, result=(result, 0))
    out_grads = OutGrads(
        out_grad(after(attended_low, *py), d_branches),
        x,
        y,
        c,
    )
    out_grads.along_core()
    oy = out_grads.along_y(column_grads.from_y)
    pz, got_z = column_grads.along_fsdp()
    i3 = move(next_terms, *i2, *oy)
    out_grads.along_x(*i2)
    i4 = move(terms(0, *i2), *i3)
    grad_gate, grad_up, grad_down = add_all(
        *zip(
            *(
                (sums.kept, after(sums.from_y, *i3))
                for sums in (gate_sums, up_sums, down_sums)
            )
        ),
        units,
    )
    output = result_of(after(middle, grad_gate), own_live, result)
    own_grads, grad_ffn_gain = column_grads.whole([w_query, w_key, w_value], out_grads, grad_gate)
    grad_query, grad_key, grad_value, query_sum, pair_sum, gain_sum, grad_out = own_grads
    grad_attn_gain = query_sum[:, 0] / attn_gain.astype(jnp.float32)
    grad_kv_gain = pair_sum[:, 0] / kv_gain.astype(jnp.float32)

    grad_hidden, grad_source = input_grads(
        hidden, source, d_middle, attn_gain_full, kv_gain_full, d_hid, d_src
    )
    return (
        output,
        grad_hidden,
        grad_source,
        grad_kv_gain,
        grad_key,
        grad_value,
        grad_attn_gain,
        grad_query,
        grad_out,
        grad_ffn_gain,
        grad_gate,
        grad_up,
        grad_down,
    )


def solution(mesh):
    in_specs = (
        P(("dp", "fsdp"), None),
        P(("dp", "fsdp"), None),
        P(("dp", "fsdp"), None),
        P("dp", None),
        P("dp", None),
        P(("dp", "fsdp")),
        P(("dp", "fsdp"), None),
        P(("dp", "fsdp"), None),
        P(("dp", "fsdp")),
        P(("dp", "fsdp"), None),
        P(("dp", "fsdp"), None),
        P(("dp", "fsdp")),
        P(("dp", "fsdp"), None),
        P(("dp", "fsdp"), None),
        P(("dp", "fsdp"), None),
    )
    out_specs = (
        P(("dp", "fsdp"), None),
        P(("dp", "fsdp"), None),
        P(("dp", "fsdp"), None),
        P(("dp", "fsdp")),
        P(("dp", "fsdp"), None),
        P(("dp", "fsdp"), None),
        P(("dp", "fsdp")),
        P(("dp", "fsdp"), None),
        P(("dp", "fsdp"), None),
        P(("dp", "fsdp")),
        P(("dp", "fsdp"), None),
        P(("dp", "fsdp"), None),
        P(("dp", "fsdp"), None),
    )
    placed = (
        mesh.shape["dp"] == 4 and mesh.shape["fsdp"] == 8 and HEADS == 2 * mesh.shape["fsdp"]
    )
    chosen = fast_body if placed else body
    return jax.shard_map(chosen, mesh=mesh, in_specs=in_specs, out_specs=out_specs, check_vma=False)
```
